32 devices in a mesh: gx: 8 (over z, x), gy: 4 (over y, core).
Axes of the slice: x: 2, y: 2, z: 4, core: 2. Of those that a mesh axis runs over, the one named last changes fastest.
Arguments:
- cotangent: float32 [8, 4, 42, 1024], P('gx', 'gy'), may hold values from -6 to 6
- section_states: bfloat16 [3, 8, 4, 42, 1024], P(None, 'gx', 'gy'), may hold values from -6 to 6
- inverse_area: float32 [8, 4, 1024], P('gx', 'gy'), may hold values from 0.5 to 2
- edge_length: float32 [8, 4, 3, 1024], P('gx', 'gy'), may hold values from 0.5 to 1.5
- roughness: float32 [8, 4, 1024], P('gx', 'gy'), may hold values from 0.5 to 2
- soil_conductance: float32 [8, 4, 1024], P('gx', 'gy'), may hold values from 0.5 to 2
- zone_friction: float32 [128], replicated, may hold values from 0.25 to 1
- zone_conductivity: float32 [128], replicated, may hold values from 0.25 to 1
- wet_mask: int32 [8, 4, 1024], P('gx', 'gy'), may hold values 0 or 1
- element_zone: int32 [8, 4, 1024], P('gx', 'gy'), may hold values from 0 to 127, as said below
- send_face: int32 [8, 4, 8, 256], P('gx', 'gy'), may hold values from 0 to 3071, as said below
- send_count: int32 [8, 4, 8], P('gx', 'gy'), may hold values from 0 to 256, as said below
- face_partner: int32 [8, 4, 3, 1024], P('gx', 'gy'), may hold values from 0 to 4867, as said below
- volume_matrix: float32 [12, 12], replicated, may hold values from -1.75 to 1.75
- flux_in: float32 [8, 8], replicated, may hold values from -2 to 2
- flux_out: float32 [8, 8], replicated, may hold values from -2 to 2
Outputs:
- adjoint: float32 [8, 4, 42, 1024], P('gx', 'gy')
- zone_grads: float32 [2, 128], replicated
The draws below stay inside these ranges and needn't reach their ends.
Inputs may be any that keep to these rules, and one draw needn't show every extreme that they name: `element_zone`: zones lie near their partition: an element of partition (a, b) has a zone among the 8 zones from (a*4+b)*4 on, modulo 128. send_count[a, b, n] equals send_count of the partition at offset n for offset 7 - n; it is 0 where that partition lies outside the grid, 1 to 4 for the four diagonal offsets (4 for some pair in every draw), at least 192 for the others, and 256 for some pair in every draw. `send_face`: the live slots of a partition name distinct faces; slots at or beyond the count hold 0. `face_partner`: the faces are paired: a face sent in slot j to offset n faces entry 3072 + n*256 + j, the other faces face a local face whose partner they are, or themselves.
All inputs are finite; a program needn't handle non-finite values. No bound on the sum of `wet_mask` on one device may be relied on, other than what follows from the above.
Results may differ from the reference program's by a relative error of at most 0.0003.
Values may be sent and summed in bfloat16 or wider, within the bound.
No kernel may reach another device: no remote copies, remote signals or barrier semaphores. Data moves between devices by JAX's collectives and lax.ppermute only.
A program may use at most 64 MiB of HBM per device.

```python
import math
import jax
import jax.numpy as jnp
import numpy as np
from jax import lax

LAYERS = 10
E_DEV = 1024
CAP = 256
ZONE_DEV = 4
GRID_X = 8
GRID_Y = 4
ZONES = 128
STATE_ROWS = 42


def neighbour_counts(key):
    key_x, key_y, key_pick, key_one, key_two = jax.random.split(key, 5)
    least_count = 3 * CAP // 4
    along_x = jax.random.randint(key_x, (GRID_X - 1, GRID_Y), least_count, CAP + 1)
    forced_pair = jax.random.randint(key_pick, (), 0, (GRID_X - 1) * GRID_Y)
    along_x = along_x.reshape(-1).at[forced_pair].set(CAP).reshape(GRID_X - 1, GRID_Y)
    along_y = jax.random.randint(key_y, (GRID_X, GRID_Y - 1), least_count, CAP + 1)
    diag_one = jax.random.randint(key_one, (GRID_X - 1, GRID_Y - 1), 1, 5)
    diag_one = diag_one.at[0, 0].set(4)
    diag_two = jax.random.randint(key_two, (GRID_X - 1, GRID_Y - 1), 1, 5)
    pad_x = jnp.pad(along_x, ((1, 1), (0, 0)))
    pad_y = jnp.pad(along_y, ((0, 0), (1, 1)))
    pad_one = jnp.pad(diag_one, ((1, 1), (1, 1)))
    pad_two = jnp.pad(diag_two, ((1, 1), (1, 1)))
    counts = jnp.stack([pad_one[:-1, :-1], pad_x[:-1], pad_two[:-1, 1:], pad_y[:, :-1], pad_y[:, 1:], pad_two[1:, :-1], pad_x[1:], pad_one[1:, 1:]], axis=-1)
    return counts.astype(jnp.int32)


def partition_tables(key, counts):
    face_total = 3 * E_DEV
    middle = (jax.random.permutation(key, face_total - 2) + 1).astype(jnp.int32)
    ordering = jnp.concatenate([jnp.full((1,), face_total - 1, jnp.int32), middle, jnp.zeros((1,), jnp.int32)])
    upper_bound = jnp.cumsum(counts).astype(jnp.int32)
    lower_bound = upper_bound - counts
    total_sent = upper_bound[-1]
    slot_index = jnp.arange(CAP, dtype=jnp.int32)
    outgoing = jnp.where(slot_index[None, :] < counts[:, None], ordering[jnp.clip(lower_bound[:, None] + slot_index[None, :], 0, face_total - 1)], 0)
    positions = jnp.arange(face_total, dtype=jnp.int32)
    direction = jnp.minimum(jnp.sum((positions[:, None] >= upper_bound[None, :]).astype(jnp.int32), axis=1), 7)
    remote = 3 * E_DEV + direction * CAP + positions - lower_bound[direction]
    shifted = positions - total_sent
    partner_position = total_sent + jnp.bitwise_xor(shifted, 1)
    inside = partner_position < face_total
    local_partner = jnp.where(inside, ordering[jnp.clip(partner_position, 0, face_total - 1)], ordering)
    values = jnp.where(positions < total_sent, remote, local_partner).astype(jnp.int32)
    partner = jnp.zeros((face_total,), jnp.int32).at[ordering].set(values)
    return (outgoing.astype(jnp.int32), partner.reshape(3, E_DEV))


def mesh_tables(key):
    base_key = jax.random.fold_in(key, 31)
    counts = neighbour_counts(jax.random.fold_in(base_key, 1))
    device_keys = jax.random.split(jax.random.fold_in(base_key, 2), GRID_X * GRID_Y)
    outgoing, partner = jax.vmap(partition_tables)(device_keys, counts.reshape(GRID_X * GRID_Y, 8))
    return (counts, outgoing.reshape(GRID_X, GRID_Y, 8, CAP), partner.reshape(GRID_X, GRID_Y, 3, E_DEV))


def draw_send_count(key, part):
    return mesh_tables(key)[0]


def draw_send_face(key, part):
    return mesh_tables(key)[1]


def draw_face_partner(key, part):
    return mesh_tables(key)[2]


def draw_element_zone(key, part):
    offsets = jax.random.randint(jax.random.fold_in(key, 23), (GRID_X, GRID_Y, E_DEV), 0, 2 * ZONE_DEV)
    device_number = jnp.arange(GRID_X, dtype=jnp.int32)[:, None] * GRID_Y + jnp.arange(GRID_Y, dtype=jnp.int32)[None, :]
    return ((device_number[:, :, None] * ZONE_DEV + offsets) % ZONES).astype(jnp.int32)


def with_ends(entries, rng, smallest, largest):
    dims = entries.shape
    place = [jax.random.randint(jax.random.fold_in(rng, axis), (), 0, dims[axis]) for axis in range(len(dims))]
    entries = entries.at[tuple(place)].set(smallest)
    longest = dims.index(max(dims))
    place[longest] = (place[longest] + 1) % dims[longest]
    return entries.at[tuple(place)].set(largest)


def level_of(own_key, shape, cuts, least, largest):
    gain, own = 1.0, jax.random.fold_in(own_key, 6)
    for axis_at, parts in cuts:
        draws = jnp.exp(jax.random.uniform(jax.random.fold_in(own, axis_at), (parts,), jnp.float32, least / len(cuts), largest / len(cuts)))
        gain = gain * jnp.repeat(draws, shape[axis_at] // parts).reshape([-1 if axis == axis_at else 1 for axis in range(len(shape))])
    return gain


def gaussian(own_key, shape, spread, limit, cuts=(), kind=jnp.bfloat16):
    gain = level_of(own_key, shape, cuts, -0.22, 0.18) if cuts else 1.0
    values = jax.random.normal(own_key, shape, jnp.float32) * spread * gain
    return jnp.minimum(jnp.maximum(values, -limit), limit).astype(kind)


def setup_inputs(seed: int = 0) -> dict:
    seeds = jax.random.split(jax.random.key(seed), 17)
    cotangent = gaussian(seeds[0], (GRID_X, GRID_Y, STATE_ROWS, E_DEV), 1.0, 6.0, ((0, 8), (1, 4)), jnp.float32)
    section_states = gaussian(seeds[1], (3, GRID_X, GRID_Y, STATE_ROWS, E_DEV), 1.0, 6.0, ((1, 8), (2, 4)))
    inverse_area = jnp.clip(jnp.exp(math.log(2.0) - 1.3862944 * jax.random.uniform(seeds[2], (GRID_X, GRID_Y, E_DEV), jnp.float32) ** level_of(seeds[2], (GRID_X, GRID_Y, E_DEV), ((0, 8), (1, 4)), -0.2, 0.2)), 0.5, 2.0)
    edge_length = jnp.clip(jnp.exp(math.log(1.5) - 1.0986123 * jax.random.uniform(seeds[3], (GRID_X, GRID_Y, 3, E_DEV), jnp.float32) ** level_of(seeds[3], (GRID_X, GRID_Y, 3, E_DEV), ((0, 8), (1, 4)), -0.2, 0.2)), 0.5, 1.5)
    roughness = jnp.clip(jnp.exp(math.log(2.0) - 1.3862944 * jax.random.uniform(seeds[4], (GRID_X, GRID_Y, E_DEV), jnp.float32) ** level_of(seeds[4], (GRID_X, GRID_Y, E_DEV), ((0, 8), (1, 4)), -0.2, 0.2)), 0.5, 2.0)
    soil_conductance = jnp.clip(jnp.exp(math.log(2.0) - 1.3862944 * jax.random.uniform(seeds[5], (GRID_X, GRID_Y, E_DEV), jnp.float32) ** level_of(seeds[5], (GRID_X, GRID_Y, E_DEV), ((0, 8), (1, 4)), -0.2, 0.2)), 0.5, 2.0)
    zone_friction = jnp.clip(jnp.exp(jax.random.uniform(seeds[6], (ZONES,), jnp.float32, math.log(0.25), math.log(1.0))), 0.25, 1.0)
    zone_conductivity = jnp.clip(jnp.exp(jax.random.uniform(seeds[7], (ZONES,), jnp.float32, math.log(0.25), math.log(1.0))), 0.25, 1.0)
    wet_mask = with_ends((jax.random.randint(seeds[8], (GRID_X, GRID_Y, E_DEV), 0, 4) < 3).astype(jnp.int32), jax.random.fold_in(seeds[8], 1), 0, 1)
    element_zone = draw_element_zone(jax.random.fold_in(seeds[16], 71), 0)
    send_face = draw_send_face(jax.random.fold_in(seeds[16], 71), 0)
    send_count = draw_send_count(jax.random.fold_in(seeds[16], 71), 0)
    face_partner = draw_face_partner(jax.random.fold_in(seeds[16], 71), 0)
    volume_matrix = gaussian(seeds[13], (12, 12), 12 ** -0.5, 1.75, (), jnp.float32)
    flux_in = gaussian(seeds[14], (8, 8), 8 ** -0.5, 2.0, (), jnp.float32)
    flux_out = gaussian(seeds[15], (8, 8), 8 ** -0.5, 2.0, (), jnp.float32)
    return dict(cotangent=cotangent, section_states=section_states, inverse_area=inverse_area, edge_length=edge_length, roughness=roughness, soil_conductance=soil_conductance, zone_friction=zone_friction, zone_conductivity=zone_conductivity, wet_mask=wet_mask, element_zone=element_zone, send_face=send_face, send_count=send_count, face_partner=face_partner, volume_matrix=volume_matrix, flux_in=flux_in, flux_out=flux_out)


TIME_STEP = 0.2
SALT_RETURN = 0.5
LATERAL = 0.5
GRAD_WEIGHT = 1.0 / 64.0
FACE_NODES = ((1, 2), (2, 0), (0, 1))
DIRECTIONS = ((-1, -1), (-1, 0), (-1, 1), (0, -1), (0, 1), (1, -1), (1, 0), (1, 1))
MOMENTUM_ROWS = np.array([0, 0, 0, 1, 1, 1, 1, 1, 1, 0, 0, 0], np.float32)

def trace_rows():
    channels = 8 + 2 * LAYERS
    rows = np.zeros((channels, 3), np.int32)
    for face_no in range(3):
        for end_no in range(2):
            node_no = FACE_NODES[face_no][end_no]
            for comp_no in range(4):
                rows[comp_no * 2 + end_no, face_no] = comp_no * 3 + node_no
            for layer_no in range(LAYERS):
                rows[8 + layer_no * 2 + end_no, face_no] = 12 + layer_no * 3 + node_no
    return rows.reshape(-1)

def take_traces(state, rows):
    channels = rows.shape[0] // 3
    return state[rows].reshape(channels, 3 * state.shape[1])

def lift_back(flux, rows, row_count):
    return jnp.zeros((row_count, flux.shape[-1]), jnp.float32).at[rows].add(flux)

def send_block(flat_traces, send_face, send_count):
    slot_index = jnp.arange(send_face.shape[1])
    live_slots = (slot_index[None, :] < send_count[:, None]).astype(jnp.float32)
    return flat_traces[:, send_face] * live_slots[None]

def section_speed(flat_traces, outer_flat):
    return jnp.sqrt(1.0 + 0.25 * lax.optimization_barrier(jnp.mean(flat_traces[:8] ** 2 + outer_flat[:8] ** 2, axis=0)))

def local_operator(state, received, conductivity, friction, wave_speed, inverse_area, edge_length, wet_mask, partner, volume_matrix, flux_in, flux_out, rows):
    element_count = state.shape[1]
    channels = rows.shape[0] // 3
    flat_traces = take_traces(state, rows)
    trace_table = jnp.concatenate([flat_traces, received.reshape(channels, -1)], axis=1)
    outer_traces = trace_table[:, partner.reshape(-1)].reshape(channels, 3, element_count)
    inner_traces = flat_traces.reshape(channels, 3, element_count)
    surf_inner = inner_traces[:8]
    surf_outer = outer_traces[:8]
    flux_surface = jnp.einsum('ab,bfe->afe', flux_in, surf_inner, precision=lax.Precision.HIGHEST) - jnp.einsum('ab,bfe->afe', flux_out, surf_outer, precision=lax.Precision.HIGHEST) + 0.5 * wave_speed[None] * (surf_inner - surf_outer)
    flux_pore = LATERAL * conductivity[None, None] * (outer_traces[8:] - inner_traces[8:])
    flux_all = jnp.concatenate([flux_surface, flux_pore], axis=0) * edge_length[None]
    lifted = lift_back(flux_all.reshape(channels * 3, element_count), rows, state.shape[0])
    volume = jnp.dot(volume_matrix, state[:12], precision=lax.Precision.HIGHEST)
    top_exchange = conductivity[None] * (state[9:12] - state[12:15])
    momentum = jnp.asarray(MOMENTUM_ROWS, dtype=jnp.float32)[:, None]
    surface = inverse_area[None] * (volume + lifted[:12]) - momentum * friction[None] * state[:12]
    surface = jnp.concatenate([surface[:9], surface[9:12] - SALT_RETURN * top_exchange], axis=0) * wet_mask[None]
    layers = state[12:].reshape(LAYERS, 3, element_count)
    between = conductivity[None, None] * (layers[:-1] - layers[1:])
    from_above = jnp.concatenate([top_exchange[None], between], axis=0)
    to_below = jnp.concatenate([between, jnp.zeros((1, 3, element_count), jnp.float32)], axis=0)
    pore = (from_above - to_below).reshape(3 * LAYERS, element_count) + inverse_area[None] * lifted[12:]
    return jnp.concatenate([surface, pore], axis=0)

def route_whole(blocks):
    size_x = blocks.shape[0]
    size_y = blocks.shape[1]
    padded = jnp.pad(blocks, ((1, 1), (1, 1), (0, 0), (0, 0), (0, 0)))
    pieces = []
    for dir_no in range(8):
        step_x, step_y = DIRECTIONS[dir_no]
        pieces.append(padded[1 + step_x:1 + step_x + size_x, 1 + step_y:1 + step_y + size_y, :, 7 - dir_no])
    return jnp.stack(pieces, axis=3)

def grid_map(function):
    return jax.vmap(jax.vmap(function))

def reference(cotangent, section_states, inverse_area, edge_length, roughness, soil_conductance, zone_friction, zone_conductivity, wet_mask, element_zone, send_face, send_count, face_partner, volume_matrix, flux_in, flux_out):
    rows = jnp.asarray(trace_rows(), dtype=jnp.int32)
    channels = rows.shape[0] // 3
    wetness = wet_mask.astype(jnp.float32)
    traces_of = grid_map(lambda state: take_traces(state, rows))

    def blocks_of(flat_all):
        return grid_map(send_block)(flat_all, send_face, send_count)

    def outer_one(flat_traces, received, partner):
        return jnp.concatenate([flat_traces, received.reshape(channels, -1)], axis=1)[:, partner.reshape(-1)]

    def apply_one(state, received, conductivity, friction, wave_speed, area_one, edges_one, wet_one, partner):
        return local_operator(state, received, conductivity, friction, wave_speed, area_one, edges_one, wet_one, partner, volume_matrix, flux_in, flux_out, rows)
    apply_grid = grid_map(apply_one)

    def section_adjoint(section_no, weight_field):
        forward_state = section_states[section_no].astype(jnp.float32)
        flat_all = traces_of(forward_state)
        received = route_whole(blocks_of(flat_all))
        outer_all = grid_map(outer_one)(flat_all, received, face_partner)
        wave_speed = grid_map(section_speed)(flat_all, outer_all).reshape(forward_state.shape[0], forward_state.shape[1], 3, -1)
        moment = jnp.sqrt(1.0 + lax.optimization_barrier(jnp.mean(forward_state[:, :, 3:9] ** 2, axis=2)))

        def whole_operator(state, friction_zone, conduct_zone):
            conductivity = conduct_zone[element_zone] * soil_conductance
            friction = friction_zone[element_zone] * roughness * moment
            incoming = route_whole(blocks_of(traces_of(state)))
            return apply_grid(state, incoming, conductivity, friction, wave_speed, inverse_area, edge_length, wetness, face_partner)
        unused, pullback = jax.vjp(whole_operator, forward_state, zone_friction, zone_conductivity)
        state_bar, friction_bar, conduct_bar = pullback(TIME_STEP * weight_field)
        return (state_bar, jnp.stack([friction_bar, conduct_bar], axis=0))
    bar_two, grads_two = section_adjoint(2, cotangent)
    lam_two = 2.0 / 3.0 * (cotangent + bar_two)
    bar_one, grads_one = section_adjoint(1, lam_two)
    lam_one = 0.25 * (lam_two + bar_one)
    bar_zero, grads_zero = section_adjoint(0, lam_one)
    adjoint = cotangent / 3.0 + 0.75 * lam_two + lam_one + bar_zero
    zone_grads = GRAD_WEIGHT * (2.0 / 3.0 * grads_two + 0.25 * grads_one + grads_zero)
    return (adjoint, zone_grads)
```

```python
import functools
import jax
import jax.numpy as jnp
from jax import lax
from jax.experimental import pallas as pl
from jax.experimental.pallas import tpu as pltpu
from jax.sharding import PartitionSpec as P

TIME_STEP = 0.2
SALT_RETURN = 0.5
LATERAL = 0.5
GRAD_WEIGHT = 1.0 / 64.0
FACE_NODES = ((1, 2), (2, 0), (0, 1))
NODE_FACES = (((1, 1), (2, 0)), ((0, 0), (2, 1)), ((0, 1), (1, 0)))
SUB = 8
LANES = 128


WET_AREA, KAPPA, HALF_KAPPA_AREA, WET, EDGE, FRICTION_BASE, ZONE_FRICTION, ZONE_ID = (
    0,
    1,
    2,
    3,
    4,
    7,
    10,
    11,
)
STAT_ROWS = 12
OUTER_EDGE, OUTER_ZONE, HALF_SPEED = 0, 3, 6
FACT_ROWS = 15
REMOTE_BLOCKS = (
    (0, 0),
    (0, 1),
    (1, 0),
    (1, 1),
    (2, 0),
    (2, 1),
    (3, 0),
    (3, 1),
    (2, 2),
    (3, 2),
)


def shifted(x, axis, by):
    peers = lax.axis_size(axis)
    pairs = [(i, i + by) for i in range(peers) if 0 <= i + by < peers]
    return lax.ppermute(x, axis, pairs)


def tile(ref, row):
    return ref[row * SUB : (row + 1) * SUB, :]


def put(ref, row, value):
    ref[row * SUB : (row + 1) * SUB, :] = value


def take(row, lane_index):
    return jnp.take_along_axis(row, lane_index, axis=1, mode="promise_in_bounds")


def spread(ref, row):
    return jnp.broadcast_to(ref[pl.ds(row, 1), :], (SUB, LANES))


def rows_to_tiles(read, tiles_ref, count):
    for block in range(SUB):
        tiles_ref[pl.ds(block, count, stride=SUB), :] = read(block)


def lanes_of(block):
    return slice(block * LANES, (block + 1) * LANES)


def gather_tile(src, row, lane_index, sublane_index):
    found = [None] * len(lane_index)
    for sub in range(SUB):
        line = spread(src, row * SUB + sub)
        for d, lane in enumerate(lane_index):
            got = take(line, lane)
            found[d] = got if sub == 0 else jnp.where(sublane_index[d] == sub, got, found[d])
    return found


def pick(face, for_zero, for_one, for_two):
    return jnp.where(face == 0, for_zero, jnp.where(face == 1, for_one, for_two))


def gather_ends(src, row, lane_index, sublane_index, face):
    nodes = [gather_tile(src, row + i, lane_index, sublane_index) for i in range(3)]
    ends = []
    for d, which in enumerate(face):
        n0, n1, n2 = nodes[0][d], nodes[1][d], nodes[2][d]
        ends.append((pick(which, n1, n2, n0), pick(which, n2, n0, n1)))
    return ends


def gather_by_face(src, row, lane_index, sublane_index, face):
    faces = [gather_tile(src, row + i, lane_index, sublane_index) for i in range(3)]
    return [pick(which, faces[0][d], faces[1][d], faces[2][d]) for d, which in enumerate(face)]


def fill_remote(received, row, lane_index, remote_index, values):
    values = list(values)
    for number, (message, block) in enumerate(REMOTE_BLOCKS):
        line = spread(received[message].at[block], row)
        for d, lane in enumerate(lane_index):
            values[d] = jnp.where(remote_index[d] == number, take(line, lane), values[d])
    return values


def partner_index(index_ref):
    return [[tile(index_ref, part * 3 + f) for f in range(3)] for part in range(4)]


def sent_index(index_ref):
    return [[tile(index_ref, 12 + part * 2 + d) for d in range(2)] for part in range(3)]


INDEX_ROWS = 18


def send_states(src, first_comp, comps, first_row, sent, sent_ref):
    lane, sublane, face = sent

    def body(step, carry):
        ends = gather_ends(src, (first_comp + step) * 3, lane, sublane, face)
        for d in range(2):
            for j in range(2):
                at = pl.multiple_of((first_row + step * 2 + j) * SUB, SUB)
                sent_ref[d, pl.ds(at, SUB), :] = ends[d][j]
        return carry

    lax.fori_loop(0, comps, body, 0)


def write_messages(sent_ref, messages):
    to_right, to_left, to_up, to_down = messages
    count = to_right.shape[1]
    for ref, direction in ((to_right, 6), (to_left, 1), (to_up, 4), (to_down, 3)):
        for block in range(2):
            ref[block] = sent_ref[block, pl.ds(direction, count, stride=SUB), :]
    for ref, direction in ((to_right, 5), (to_left, 2)):
        ref[2] = sent_ref[0, pl.ds(direction, count, stride=SUB), :]


def prepare_kernel(
    cot_ref,
    x_ref,
    area_ref,
    edge_ref,
    rough_ref,
    soil_ref,
    friction_ref,
    conduct_ref,
    wet_ref,
    zone_ref,
    send_ref,
    partner_ref,
    lam_ref,
    table_ref,
    stat_ref,
    index_ref,
    to_right,
    to_left,
    to_up,
    to_down,
    x_tiles,
    int_tiles,
    sent_ref,
):
    rows = cot_ref.shape[2]
    sections = x_ref.shape[0]
    rows_to_tiles(lambda b: cot_ref[0, 0, :, lanes_of(b)], lam_ref, rows)
    rows_to_tiles(lambda b: partner_ref[0, 0, :, lanes_of(b)], int_tiles, 3)
    face_total = 3 * SUB * LANES
    for f in range(3):
        partner = tile(int_tiles, f)
        beyond = partner - face_total
        direction = jnp.right_shift(beyond, 8)
        half = jnp.bitwise_and(jnp.right_shift(beyond, 7), 1)
        lane = jnp.bitwise_and(partner, LANES - 1)
        remote = jnp.where(beyond >= 0, 8, -1)
        remote = jnp.where((direction == 2) | (direction == 7), 9, remote)
        for number, first in ((1, 0), (6, 2), (3, 4), (4, 6)):
            remote = jnp.where(direction == number, first + half, remote)
        lane = jnp.where((direction == 0) | (direction == 7), jnp.bitwise_and(lane + 4, LANES - 1), lane)
        put(index_ref, f, lane)
        put(index_ref, 3 + f, jnp.bitwise_and(jnp.right_shift(partner, 7), SUB - 1))
        put(index_ref, 6 + f, jnp.right_shift(partner, 10))
        put(index_ref, 9 + f, remote)
    sub_iota = lax.broadcasted_iota(jnp.int32, (SUB, LANES), 0)
    lane_iota = lax.broadcasted_iota(jnp.int32, (SUB, LANES), 1)
    for d in range(2):
        slots = send_ref[0, 0, :, lanes_of(d)]
        if d == 0:
            moved = pltpu.roll(slots, 4, 1)
            second = (lane_iota >= 4) & (lane_iota < 8)
            slots = jnp.where(second & (sub_iota == 5), pltpu.roll(moved, 6, 0), slots)
            slots = jnp.where(second & (sub_iota == 2), pltpu.roll(moved, 2, 0), slots)
        put(index_ref, 12 + d, jnp.bitwise_and(slots, LANES - 1))
        put(index_ref, 14 + d, jnp.bitwise_and(jnp.right_shift(slots, 7), SUB - 1))
        put(index_ref, 16 + d, jnp.right_shift(slots, 10))
    zone = zone_ref[...]
    zone_lane = jnp.bitwise_and(zone, LANES - 1)
    zone_block = jnp.right_shift(zone, 7)
    factors = []
    for ref in (friction_ref, conduct_ref):
        found = None
        for block in range(ref.shape[0]):
            got = take(spread(ref, block), zone_lane)
            found = got if block == 0 else jnp.where(zone_block == block, got, found)
        factors.append(found)
    area = area_ref[...]
    wet = wet_ref[...].astype(jnp.float32)
    kappa = factors[1] * soil_ref[...]
    wet_area = wet * area
    half_kappa_area = LATERAL * kappa * area
    put(stat_ref, WET_AREA, wet_area)
    put(stat_ref, KAPPA, kappa)
    put(stat_ref, HALF_KAPPA_AREA, half_kappa_area)
    put(stat_ref, WET, wet)
    put(stat_ref, ZONE_FRICTION, factors[0])
    put(stat_ref, ZONE_ID, zone.astype(jnp.float32))
    rows_to_tiles(lambda b: edge_ref[0, 0, :, lanes_of(b)], stat_ref.at[EDGE * SUB : (EDGE + 3) * SUB], 3)
    for k in range(sections):
        rows_to_tiles(
            lambda b: x_ref[k, 0, 0, 0:16, lanes_of(b)].astype(jnp.float32), x_tiles, 16
        )
        squares = [tile(x_tiles, r) * tile(x_tiles, r) for r in range(12)]
        node_sum = [squares[i] + squares[3 + i] + squares[6 + i] + squares[9 + i] for i in range(3)]
        for f in range(3):
            first, second = FACE_NODES[f]
            put(table_ref, rows + 3 + 3 * k + f, node_sum[first] + node_sum[second])
        momentum = squares[3]
        for r in range(4, 9):
            momentum = momentum + squares[r]
        put(
            stat_ref,
            FRICTION_BASE + k,
            rough_ref[...] * jnp.sqrt(1.0 + momentum * (1.0 / 6.0)),
        )
    for f in range(3):
        put(table_ref, rows + f, tile(stat_ref, EDGE + f))
    put(table_ref, rows + 12, zone.astype(jnp.float32))
    for r in range(rows):
        put(table_ref, r, tile(lam_ref, r) * (wet_area if r < 12 else half_kappa_area))
    sent = sent_index(index_ref)
    comps = rows // 3
    send_states(table_ref, 0, comps, 0, sent, sent_ref)
    for group in range(4):
        values = gather_by_face(table_ref, rows + 3 * group, *sent)
        for d in range(2):
            at = (comps * 2 + group) * SUB
            sent_ref[d, at : at + SUB, :] = values[d]
    values = gather_tile(table_ref, rows + 12, sent[0], sent[1])
    for d in range(2):
        at = (comps * 2 + 4) * SUB
        sent_ref[d, at : at + SUB, :] = values[d]
    write_messages(sent_ref, (to_right, to_left, to_up, to_down))


def corner_kernel(left_ref, right_ref, up_in, down_in, up_ref, down_ref):
    first = lax.broadcasted_iota(jnp.int32, left_ref.shape, 2) < 4
    left, right = left_ref[...], right_ref[...]
    up_ref[...] = jnp.where(first, right, left)
    down_ref[...] = jnp.where(first, left, right)


def outer_states(src, first_comp, comps, first_row, received, index, out_ref):
    lane, sublane, face, remote = index

    def body(step, carry):
        ends = gather_ends(src, (first_comp + step) * 3, lane, sublane, face)
        for j in range(2):
            values = fill_remote(
                received, first_row + step * 2 + j, lane, remote, [ends[f][j] for f in range(3)]
            )
            for f in range(3):
                at = pl.multiple_of((f * comps * 2 + step * 2 + j) * SUB, SUB)
                out_ref[pl.ds(at, SUB), :] = values[f]
        return carry

    lax.fori_loop(0, comps, body, 0)


def transposed_section(
    section, lam_ref, y_ref, outer_ref, stat_ref, fact_ref, in_ref, out_ref, volume_ref, emit
):
    rows = lam_ref.shape[0] // SUB
    channels = rows // 3 * 2
    layers = (rows - 12) // 3
    edge = [tile(stat_ref, EDGE + f) for f in range(3)]
    outer_edge = [tile(fact_ref, OUTER_EDGE + f) for f in range(3)]
    half_speed = [tile(fact_ref, HALF_SPEED + 3 * section + f) for f in range(3)]
    kappa = tile(stat_ref, KAPPA)
    wet = tile(stat_ref, WET)
    own = [tile(y_ref, r) for r in range(12)]
    result = []
    for r in range(12):
        total = volume_ref[0, r] * own[0]
        for q in range(1, 12):
            total = total + volume_ref[q, r] * own[q]
        result.append(total)
    for f in range(3):
        ends = FACE_NODES[f]
        inner = [edge[f] * own[(ch // 2) * 3 + ends[ch % 2]] for ch in range(8)]
        outer = [outer_edge[f] * tile(outer_ref, f * channels + ch) for ch in range(8)]
        for b in range(8):
            total = half_speed[f] * (inner[b] - outer[b])
            for a in range(8):
                total = total + in_ref[a, b] * inner[a] - out_ref[a, b] * outer[a]
            at = (b // 2) * 3 + ends[b % 2]
            result[at] = result[at] + total
    friction = tile(stat_ref, ZONE_FRICTION) * tile(stat_ref, FRICTION_BASE + section) * wet
    for r in range(3, 9):
        result[r] = result[r] - friction * tile(lam_ref, r)
    exchange = []
    for i in range(3):
        top = tile(lam_ref, 12 + i) - SALT_RETURN * wet * tile(lam_ref, 9 + i)
        exchange.append(kappa * top)
        result[9 + i] = result[9 + i] + exchange[i]
    for r in range(12):
        emit(r, result[r])
    for i in range(3):
        (f0, j0), (f1, j1) = NODE_FACES[i]
        both = edge[f0] + edge[f1]
        from_above = exchange[i]
        for layer in range(layers):
            r = 12 + layer * 3 + i
            value = (
                outer_edge[f0] * tile(outer_ref, f0 * channels + 8 + layer * 2 + j0)
                + outer_edge[f1] * tile(outer_ref, f1 * channels + 8 + layer * 2 + j1)
                - both * tile(y_ref, r)
                - from_above
            )
            if layer + 1 < layers:
                from_above = kappa * (tile(lam_ref, r + 3) - tile(lam_ref, r))
                value = value + from_above
            emit(r, value)


def own_gradients(section, weight, lam_ref, y_ref, x_tiles, stat_ref):
    rows = lam_ref.shape[0] // SUB
    layers = (rows - 12) // 3
    wet = tile(stat_ref, WET)
    kappa = tile(stat_ref, KAPPA)
    momentum = tile(lam_ref, 3) * tile(x_tiles, 3)
    for r in range(4, 9):
        momentum = momentum + tile(lam_ref, r) * tile(x_tiles, r)
    friction = -(weight * wet * tile(stat_ref, FRICTION_BASE + section)) * momentum
    vertical = None
    lateral = None
    for i in range(3):
        (f0, _), (f1, _) = NODE_FACES[i]
        top = tile(lam_ref, 12 + i) - SALT_RETURN * wet * tile(lam_ref, 9 + i)
        total = top * (tile(x_tiles, 9 + i) - tile(x_tiles, 12 + i))
        dots = None
        for layer in range(layers):
            r = 12 + layer * 3 + i
            term = tile(y_ref, r) * tile(x_tiles, r)
            dots = term if dots is None else dots + term
            if layer + 1 < layers:
                total = total + (tile(lam_ref, r + 3) - tile(lam_ref, r)) * (
                    tile(x_tiles, r) - tile(x_tiles, r + 3)
                )
        side = (tile(stat_ref, EDGE + f0) + tile(stat_ref, EDGE + f1)) * dots
        vertical = total if vertical is None else vertical + total
        lateral = side if lateral is None else lateral + side
    return friction, weight * (kappa * vertical - lateral)


def outer_gradients(weight, outer_ref, x_tiles, fact_ref):
    channels = outer_ref.shape[0] // SUB // 3
    values = []
    for f in range(3):
        total = None
        for ch in range(8, channels):
            row = 12 + (ch - 8) // 2 * 3 + FACE_NODES[f][ch % 2]
            term = tile(outer_ref, f * channels + ch) * tile(x_tiles, row)
            total = term if total is None else total + term
        values.append(weight * tile(fact_ref, OUTER_EDGE + f) * total)
    return values


def x_to_tiles(x_ref, section, x_tiles):
    rows = x_ref.shape[3]
    rows_to_tiles(
        lambda b: x_ref[section, 0, 0, :, lanes_of(b)].astype(jnp.float32), x_tiles, rows
    )


def second_kernel(
    cot_ref,
    table_ref,
    stat_ref,
    index_ref,
    x_ref,
    in_ref,
    out_ref,
    volume_ref,
    from_left,
    from_right,
    from_down,
    from_up,
    lam_ref,
    y_ref,
    fact_ref,
    term_ref,
    to_right,
    to_left,
    to_up,
    to_down,
    outer_ref,
    x_tiles,
    sent_ref,
):
    received = (from_left, from_right, from_down, from_up)
    rows = cot_ref.shape[0] // SUB
    comps = rows // 3
    index = partner_index(index_ref)
    lane, sublane, face, remote = index
    outer_states(table_ref, 0, comps, 0, received, index, outer_ref)
    for group in range(4):
        values = gather_by_face(table_ref, rows + 3 * group, lane, sublane, face)
        values = fill_remote(received, comps * 2 + group, lane, remote, values)
        for f in range(3):
            if group == 0:
                put(fact_ref, OUTER_EDGE + f, values[f])
            else:
                k = group - 1
                both = tile(table_ref, rows + 3 * group + f) + values[f]
                put(
                    fact_ref,
                    HALF_SPEED + 3 * k + f,
                    0.5 * jnp.sqrt(1.0 + (0.25 / 8.0) * both),
                )
    values = gather_tile(table_ref, rows + 12, lane, sublane)
    values = fill_remote(received, comps * 2 + 4, lane, remote, values)
    for f in range(3):
        put(fact_ref, OUTER_ZONE + f, values[f])
    wet_area = tile(stat_ref, WET_AREA)
    half_kappa_area = tile(stat_ref, HALF_KAPPA_AREA)

    def emit(r, value):
        lam = (2.0 / 3.0) * (tile(cot_ref, r) + TIME_STEP * value)
        put(lam_ref, r, lam)
        put(y_ref, r, lam * (wet_area if r < 12 else half_kappa_area))

    transposed_section(
        2, cot_ref, table_ref, outer_ref, stat_ref, fact_ref, in_ref, out_ref, volume_ref, emit
    )
    x_to_tiles(x_ref, 0, x_tiles)
    sent = sent_index(index_ref)
    send_states(y_ref, 0, comps, 0, sent, sent_ref)
    send_states(x_tiles, 4, comps - 4, comps * 2, sent, sent_ref)
    write_messages(sent_ref, (to_right, to_left, to_up, to_down))
    x_to_tiles(x_ref, 2, x_tiles)
    weight = TIME_STEP * 2.0 / 3.0
    friction, conduct = own_gradients(2, weight, cot_ref, table_ref, x_tiles, stat_ref)
    put(term_ref, 0, friction)
    put(term_ref, 1, conduct)
    for f, value in enumerate(outer_gradients(weight, outer_ref, x_tiles, fact_ref)):
        put(term_ref, 2 + f, value)


def first_kernel(
    cot_ref,
    lam_ref,
    y_ref,
    stat_ref,
    index_ref,
    fact_ref,
    term_ref,
    x_ref,
    in_ref,
    out_ref,
    volume_ref,
    from_left,
    from_right,
    from_down,
    from_up,
    base_ref,
    next_ref,
    next_y_ref,
    new_term_ref,
    to_right,
    to_left,
    to_up,
    to_down,
    outer_ref,
    x_outer_ref,
    x_tiles,
    sent_ref,
):
    received = (from_left, from_right, from_down, from_up)
    rows = lam_ref.shape[0] // SUB
    comps = rows // 3
    index = partner_index(index_ref)
    outer_states(y_ref, 0, comps, 0, received, index, outer_ref)
    wet_area = tile(stat_ref, WET_AREA)
    half_kappa_area = tile(stat_ref, HALF_KAPPA_AREA)

    def emit(r, value):
        old = tile(lam_ref, r)
        lam = 0.25 * (old + TIME_STEP * value)
        put(next_ref, r, lam)
        put(next_y_ref, r, lam * (wet_area if r < 12 else half_kappa_area))
        put(base_ref, r, (1.0 / 3.0) * tile(cot_ref, r) + 0.75 * old + lam)

    transposed_section(
        1, lam_ref, y_ref, outer_ref, stat_ref, fact_ref, in_ref, out_ref, volume_ref, emit
    )
    send_states(next_y_ref, 0, comps, 0, sent_index(index_ref), sent_ref)
    write_messages(sent_ref, (to_right, to_left, to_up, to_down))
    x_to_tiles(x_ref, 1, x_tiles)
    weight = TIME_STEP * 0.25
    friction, conduct = own_gradients(1, weight, lam_ref, y_ref, x_tiles, stat_ref)
    for f, value in enumerate(outer_gradients(weight, outer_ref, x_tiles, fact_ref)):
        put(new_term_ref, 2 + f, tile(term_ref, 2 + f) + value)
    x_to_tiles(x_ref, 0, x_tiles)
    outer_states(x_tiles, 4, comps - 4, comps * 2, received, index, x_outer_ref)
    friction_0, conduct_0 = own_gradients(0, TIME_STEP, next_ref, next_y_ref, x_tiles, stat_ref)
    friction = friction + friction_0
    conduct = conduct + conduct_0
    channels = (comps - 4) * 2
    for f in range(3):
        total = None
        for ch in range(channels):
            row = 12 + ch // 2 * 3 + FACE_NODES[f][ch % 2]
            term = tile(x_outer_ref, f * channels + ch) * tile(next_y_ref, row)
            total = term if total is None else total + term
        conduct = conduct + TIME_STEP * tile(stat_ref, EDGE + f) * total
    put(new_term_ref, 0, tile(term_ref, 0) + friction)
    put(new_term_ref, 1, tile(term_ref, 1) + conduct)


def zone_kernel(term_ref, stat_ref, fact_ref, conduct_ref, out_ref):
    zones = out_ref.shape[1]
    zone_iota = lax.broadcasted_iota(jnp.int32, (zones, LANES), 0).astype(jnp.float32)
    sub_iota = lax.broadcasted_iota(jnp.int32, (SUB, zones), 0)

    def thirds(value):
        high = value.astype(jnp.bfloat16).astype(jnp.float32)
        rest = value - high
        middle = rest.astype(jnp.bfloat16).astype(jnp.float32)
        return [high, middle, rest - middle]

    def by_zone(values, zone_of, zone_row):
        pieces = sum([thirds(value) for value in values], [])
        left = jnp.concatenate(pieces, axis=0).astype(jnp.bfloat16)
        totals = [jnp.zeros((SUB, zones), jnp.float32) for _ in values]
        for sub in range(SUB):
            line = zone_of[pl.ds(zone_row * SUB + sub, 1), :]
            hot = (jnp.broadcast_to(line, (zones, LANES)) == zone_iota).astype(jnp.float32)
            dots = lax.dot_general(
                left,
                hot.astype(jnp.bfloat16),
                (((1,), (1,)), ((), ())),
                preferred_element_type=jnp.float32,
            )
            for n in range(len(values)):
                at = n * 3 * SUB
                three = dots[at : at + SUB] + dots[at + SUB : at + 2 * SUB]
                three = three + dots[at + 2 * SUB : at + 3 * SUB]
                totals[n] = totals[n] + jnp.where(sub_iota == sub, three, 0.0)
        return totals

    friction, conduct = by_zone([tile(term_ref, 0), tile(term_ref, 1)], stat_ref, ZONE_ID)
    for f in range(3):
        conduct = conduct + by_zone([tile(term_ref, 2 + f)], fact_ref, OUTER_ZONE + f)[0]
    out_ref[0:1, :] = GRAD_WEIGHT * jnp.sum(friction, axis=0, keepdims=True)
    out_ref[1:2, :] = (
        GRAD_WEIGHT * jnp.sum(conduct, axis=0, keepdims=True) / conduct_ref[...]
    )


def last_kernel(
    base_ref,
    lam_ref,
    y_ref,
    stat_ref,
    index_ref,
    fact_ref,
    in_ref,
    out_ref,
    volume_ref,
    from_left,
    from_right,
    from_down,
    from_up,
    adjoint_ref,
    outer_ref,
    sum_ref,
):
    received = (from_left, from_right, from_down, from_up)
    rows = lam_ref.shape[0] // SUB
    outer_states(y_ref, 0, rows // 3, 0, received, partner_index(index_ref), outer_ref)

    def emit(r, value):
        put(sum_ref, r, tile(base_ref, r) + TIME_STEP * value)

    transposed_section(
        0, lam_ref, y_ref, outer_ref, stat_ref, fact_ref, in_ref, out_ref, volume_ref, emit
    )
    for block in range(SUB):
        adjoint_ref[0, 0, :, lanes_of(block)] = sum_ref[pl.ds(block, rows, stride=SUB), :]


def exchange(messages):
    to_right, to_left, to_up, to_down = messages
    from_left = shifted(to_right, "gx", 1)
    from_right = shifted(to_left, "gx", -1)
    corner = pl.BlockSpec((1, to_right.shape[1], LANES), lambda i: (2, 0, 0))
    whole = pl.BlockSpec(memory_space=pl.ANY)
    to_up, to_down = pl.pallas_call(
        corner_kernel,
        grid=(1,),
        in_specs=[corner, corner, whole, whole],
        out_specs=[corner, corner],
        out_shape=[jax.ShapeDtypeStruct(to_up.shape, to_up.dtype)] * 2,
        input_output_aliases={2: 0, 3: 1},
        name="corners",
    )(from_left, from_right, to_up, to_down)
    from_down = shifted(to_up, "gy", 1)
    from_up = shifted(to_down, "gy", -1)
    return from_left, from_right, from_down, from_up


def call(kernel, name, outs, scratch, operands, scalars=()):
    in_memory = pl.BlockSpec(memory_space=pltpu.VMEM)
    in_scalar = pl.BlockSpec(memory_space=pltpu.SMEM)
    return pl.pallas_call(
        kernel,
        in_specs=[in_scalar if n in scalars else in_memory for n in range(len(operands))],
        out_specs=[in_memory] * len(outs),
        out_shape=outs,
        scratch_shapes=scratch,
        compiler_params=pltpu.CompilerParams(vmem_limit_bytes=32 * 1024 * 1024),
        name=name,
    )(*operands)


def local(
    cotangent,
    section_states,
    inverse_area,
    edge_length,
    roughness,
    soil_conductance,
    zone_friction,
    zone_conductivity,
    wet_mask,
    element_zone,
    send_face,
    send_count,
    face_partner,
    volume_matrix,
    flux_in,
    flux_out,
):
    rows = cotangent.shape[2]
    channels = rows // 3 * 2
    zones = zone_friction.shape[0]
    slots = send_face.shape[3]
    f32 = jnp.float32

    def tiles(count, dtype=f32):
        return jax.ShapeDtypeStruct((count * SUB, LANES), dtype)

    def tile_scratch(count, dtype=f32):
        return pltpu.VMEM((count * SUB, LANES), dtype)

    def messages(count):
        return [jax.ShapeDtypeStruct((slots // LANES + 1, count, LANES), f32)] * 4

    def sent_scratch(count):
        return pltpu.VMEM((slots // LANES, count * SUB, LANES), f32)

    square = lambda one: one.reshape(SUB, LANES)
    cot, table, stat, index, *to_send = call(
        prepare_kernel,
        "prepare",
        [tiles(rows), tiles(rows + 13), tiles(STAT_ROWS), tiles(INDEX_ROWS, jnp.int32)]
        + messages(channels + 5),
        [tile_scratch(16), tile_scratch(3, jnp.int32), sent_scratch(channels + 5)],
        [
            cotangent,
            section_states,
            square(inverse_area),
            edge_length,
            square(roughness),
            square(soil_conductance),
            zone_friction.reshape(-1, LANES),
            zone_conductivity.reshape(-1, LANES),
            square(wet_mask),
            square(element_zone),
            send_face,
            face_partner,
        ],
    )
    received = exchange(to_send)
    lam, y, fact, term, *to_send = call(
        second_kernel,
        "section_two",
        [tiles(rows), tiles(rows), tiles(FACT_ROWS), tiles(5)]
        + messages(channels + channels - 8),
        [tile_scratch(3 * channels), tile_scratch(rows), sent_scratch(2 * channels - 8)],
        [cot, table, stat, index, section_states, flux_in, flux_out, volume_matrix, *received],
        (5, 6, 7),
    )
    received = exchange(to_send)
    base, lam, y, term, *to_send = call(
        first_kernel,
        "section_one",
        [tiles(rows), tiles(rows), tiles(rows), tiles(5)] + messages(channels),
        [
            tile_scratch(3 * channels),
            tile_scratch(3 * (channels - 8)),
            tile_scratch(rows),
            sent_scratch(channels),
        ],
        [
            cot,
            lam,
            y,
            stat,
            index,
            fact,
            term,
            section_states,
            flux_in,
            flux_out,
            volume_matrix,
            *received,
        ],
        (8, 9, 10),
    )
    (zone_terms,) = call(
        zone_kernel,
        "zone_sums",
        [jax.ShapeDtypeStruct((2, zones), f32)],
        [],
        [term, stat, fact, zone_conductivity.reshape(1, zones)],
    )
    zone_grads = lax.psum(zone_terms, ("gx", "gy"))
    received = exchange(to_send)
    (adjoint,) = call(
        last_kernel,
        "section_zero",
        [jax.ShapeDtypeStruct(cotangent.shape, f32)],
        [tile_scratch(3 * channels), tile_scratch(rows)],
        [base, lam, y, stat, index, fact, flux_in, flux_out, volume_matrix, *received],
        (6, 7, 8),
    )
    return adjoint, zone_grads


def solution(mesh):
    placed = (
        P("gx", "gy", None, None),
        P(None, "gx", "gy", None, None),
        P("gx", "gy", None),
        P("gx", "gy", None, None),
        P("gx", "gy", None),
        P("gx", "gy", None),
        P(),
        P(),
        P("gx", "gy", None),
        P("gx", "gy", None),
        P("gx", "gy", None, None),
        P("gx", "gy", None),
        P("gx", "gy", None, None),
        P(),
        P(),
        P(),
    )
    return jax.shard_map(
        local,
        mesh=mesh,
        in_specs=placed,
        out_specs=(P("gx", "gy", None, None), P()),
        check_vma=False,
    )
```

```python
import functools
import jax
import jax.numpy as jnp
from jax import lax
from jax.experimental import pallas as pl
from jax.experimental.pallas import tpu as pltpu
from jax.sharding import PartitionSpec as P

TIME_STEP = 0.2
SALT_RETURN = 0.5
LATERAL = 0.5
GRAD_WEIGHT = 1.0 / 64.0
FACE_NODES = ((1, 2), (2, 0), (0, 1))
NODE_FACES = (((1, 1), (2, 0)), ((0, 0), (2, 1)), ((0, 1), (1, 0)))
SUB = 8
LANES = 128


WET_AREA, KAPPA, HALF_KAPPA_AREA, WET, EDGE, FRICTION_BASE, ZONE_FRICTION, ZONE_ID = (
    0,
    1,
    2,
    3,
    4,
    7,
    10,
    11,
)
STAT_ROWS = 12
OUTER_EDGE, OUTER_ZONE, HALF_SPEED = 0, 3, 6
FACT_ROWS = 15
REMOTE_BLOCKS = (
    (0, 0),
    (0, 1),
    (1, 0),
    (1, 1),
    (2, 0),
    (2, 1),
    (3, 0),
    (3, 1),
    (2, 2),
    (3, 2),
)


def shifted(x, axis, by):
    peers = lax.axis_size(axis)
    pairs = [(i, i + by) for i in range(peers) if 0 <= i + by < peers]
    return lax.ppermute(x, axis, pairs)


def tile(ref, row):
    return ref[row * SUB : (row + 1) * SUB, :]


def put(ref, row, value):
    ref[row * SUB : (row + 1) * SUB, :] = value


def take(row, lane_index):
    return jnp.take_along_axis(row, lane_index, axis=1, mode="promise_in_bounds")


def spread(ref, row):
    return jnp.broadcast_to(ref[pl.ds(row, 1), :], (SUB, LANES))


def rows_to_tiles(read, tiles_ref, count):
    for block in range(SUB):
        tiles_ref[pl.ds(block, count, stride=SUB), :] = read(block)


def lanes_of(block):
    return slice(block * LANES, (block + 1) * LANES)


def gather_tile(src, row, lane_index, sublane_index):
    found = [None] * len(lane_index)
    for sub in range(SUB):
        line = spread(src, row * SUB + sub)
        for d, lane in enumerate(lane_index):
            got = take(line, lane)
            found[d] = got if sub == 0 else jnp.where(sublane_index[d] == sub, got, found[d])
    return found


def pick(face, for_zero, for_one, for_two):
    return jnp.where(face == 0, for_zero, jnp.where(face == 1, for_one, for_two))


def gather_ends(src, row, lane_index, sublane_index, face):
    nodes = [gather_tile(src, row + i, lane_index, sublane_index) for i in range(3)]
    ends = []
    for d, which in enumerate(face):
        n0, n1, n2 = nodes[0][d], nodes[1][d], nodes[2][d]
        ends.append((pick(which, n1, n2, n0), pick(which, n2, n0, n1)))
    return ends


def gather_by_face(src, row, lane_index, sublane_index, face):
    faces = [gather_tile(src, row + i, lane_index, sublane_index) for i in range(3)]
    return [pick(which, faces[0][d], faces[1][d], faces[2][d]) for d, which in enumerate(face)]


def fill_remote(received, row, lane_index, remote_index, values):
    values = list(values)
    for number, (message, block) in enumerate(REMOTE_BLOCKS):
        line = spread(received[message].at[block], row)
        for d, lane in enumerate(lane_index):
            values[d] = jnp.where(remote_index[d] == number, take(line, lane), values[d])
    return values


def partner_index(index_ref):
    return [[tile(index_ref, part * 3 + f) for f in range(3)] for part in range(4)]


def sent_index(index_ref):
    return [[tile(index_ref, 12 + part * 2 + d) for d in range(2)] for part in range(3)]


INDEX_ROWS = 18


def send_states(src, first_comp, comps, first_row, sent, sent_ref):
    lane, sublane, face = sent

    def body(step, carry):
        ends = gather_ends(src, (first_comp + step) * 3, lane, sublane, face)
        for d in range(2):
            for j in range(2):
                at = pl.multiple_of((first_row + step * 2 + j) * SUB, SUB)
                sent_ref[d, pl.ds(at, SUB), :] = ends[d][j]
        return carry

    lax.fori_loop(0, comps, body, 0)


def write_messages(sent_ref, messages):
    to_right, to_left, to_up, to_down = messages
    count = to_right.shape[1]
    for ref, direction in ((to_right, 6), (to_left, 1), (to_up, 4), (to_down, 3)):
        for block in range(2):
            ref[block] = sent_ref.at[block][pl.ds(direction, count, stride=SUB), :]
    for ref, direction in ((to_right, 5), (to_left, 2)):
        ref[2] = sent_ref.at[0][pl.ds(direction, count, stride=SUB), :]


def prepare_kernel(
    cot_ref,
    x_ref,
    area_ref,
    edge_ref,
    rough_ref,
    soil_ref,
    friction_ref,
    conduct_ref,
    wet_ref,
    zone_ref,
    send_ref,
    partner_ref,
    table_ref,
    stat_ref,
    index_ref,
    to_right,
    to_left,
    to_up,
    to_down,
    x_tiles,
    sent_ref,
):
    rows = cot_ref.shape[0] // SUB
    sections = x_ref.shape[0]
    face_total = 3 * SUB * LANES
    for f in range(3):
        partner = tile(partner_ref, f)
        beyond = partner - face_total
        direction = jnp.right_shift(beyond, 8)
        half = jnp.bitwise_and(jnp.right_shift(beyond, 7), 1)
        lane = jnp.bitwise_and(partner, LANES - 1)
        remote = jnp.where(beyond >= 0, 8, -1)
        remote = jnp.where((direction == 2) | (direction == 7), 9, remote)
        for number, first in ((1, 0), (6, 2), (3, 4), (4, 6)):
            remote = jnp.where(direction == number, first + half, remote)
        lane = jnp.where((direction == 0) | (direction == 7), jnp.bitwise_and(lane + 4, LANES - 1), lane)
        put(index_ref, f, lane)
        put(index_ref, 3 + f, jnp.bitwise_and(jnp.right_shift(partner, 7), SUB - 1))
        put(index_ref, 6 + f, jnp.right_shift(partner, 10))
        put(index_ref, 9 + f, remote)
    sub_iota = lax.broadcasted_iota(jnp.int32, (SUB, LANES), 0)
    lane_iota = lax.broadcasted_iota(jnp.int32, (SUB, LANES), 1)
    for d in range(2):
        slots = send_ref[0, 0, :, lanes_of(d)]
        if d == 0:
            moved = pltpu.roll(slots, 4, 1)
            second = (lane_iota >= 4) & (lane_iota < 8)
            slots = jnp.where(second & (sub_iota == 5), pltpu.roll(moved, 6, 0), slots)
            slots = jnp.where(second & (sub_iota == 2), pltpu.roll(moved, 2, 0), slots)
        put(index_ref, 12 + d, jnp.bitwise_and(slots, LANES - 1))
        put(index_ref, 14 + d, jnp.bitwise_and(jnp.right_shift(slots, 7), SUB - 1))
        put(index_ref, 16 + d, jnp.right_shift(slots, 10))
    zone = zone_ref[...]
    zone_lane = jnp.bitwise_and(zone, LANES - 1)
    zone_block = jnp.right_shift(zone, 7)
    factors = []
    for ref in (friction_ref, conduct_ref):
        found = None
        for block in range(ref.shape[0]):
            got = take(spread(ref, block), zone_lane)
            found = got if block == 0 else jnp.where(zone_block == block, got, found)
        factors.append(found)
    area = area_ref[...]
    wet = wet_ref[...].astype(jnp.float32)
    kappa = factors[1] * soil_ref[...]
    wet_area = wet * area
    half_kappa_area = LATERAL * kappa * area
    put(stat_ref, WET_AREA, wet_area)
    put(stat_ref, KAPPA, kappa)
    put(stat_ref, HALF_KAPPA_AREA, half_kappa_area)
    put(stat_ref, WET, wet)
    put(stat_ref, ZONE_FRICTION, factors[0])
    put(stat_ref, ZONE_ID, zone.astype(jnp.float32))
    stat_ref[EDGE * SUB : (EDGE + 3) * SUB, :] = edge_ref[...]
    for k in range(sections):
        rows_to_tiles(
            lambda b: x_ref[k, 0, 0, 0:16, lanes_of(b)].astype(jnp.float32), x_tiles, 16
        )
        squares = [tile(x_tiles, r) * tile(x_tiles, r) for r in range(12)]
        node_sum = [squares[i] + squares[3 + i] + squares[6 + i] + squares[9 + i] for i in range(3)]
        for f in range(3):
            first, second = FACE_NODES[f]
            put(table_ref, rows + 3 + 3 * k + f, node_sum[first] + node_sum[second])
        momentum = squares[3]
        for r in range(4, 9):
            momentum = momentum + squares[r]
        put(
            stat_ref,
            FRICTION_BASE + k,
            rough_ref[...] * jnp.sqrt(1.0 + momentum * (1.0 / 6.0)),
        )
    for f in range(3):
        put(table_ref, rows + f, tile(stat_ref, EDGE + f))
    put(table_ref, rows + 12, zone.astype(jnp.float32))
    for r in range(rows):
        put(table_ref, r, tile(cot_ref, r) * (wet_area if r < 12 else half_kappa_area))
    sent = sent_index(index_ref)
    comps = rows // 3
    send_states(table_ref, 0, comps, 0, sent, sent_ref)
    for group in range(4):
        values = gather_by_face(table_ref, rows + 3 * group, *sent)
        for d in range(2):
            at = (comps * 2 + group) * SUB
            sent_ref[d, at : at + SUB, :] = values[d]
    values = gather_tile(table_ref, rows + 12, sent[0], sent[1])
    for d in range(2):
        at = (comps * 2 + 4) * SUB
        sent_ref[d, at : at + SUB, :] = values[d]
    write_messages(sent_ref, (to_right, to_left, to_up, to_down))


def corner_kernel(left_ref, right_ref, up_in, down_in, *rest):
    up_ref, down_ref = rest[-2:]
    first = lax.broadcasted_iota(jnp.int32, left_ref.shape, 2) < 4
    left, right = left_ref[...], right_ref[...]
    up_ref[...] = jnp.where(first, right, left)
    down_ref[...] = jnp.where(first, left, right)


def outer_states(src, first_comp, comps, first_row, received, index, out_ref):
    lane, sublane, face, remote = index

    def body(step, carry):
        ends = gather_ends(src, (first_comp + step) * 3, lane, sublane, face)
        for j in range(2):
            values = fill_remote(
                received, first_row + step * 2 + j, lane, remote, [ends[f][j] for f in range(3)]
            )
            for f in range(3):
                at = pl.multiple_of((f * comps * 2 + step * 2 + j) * SUB, SUB)
                out_ref[pl.ds(at, SUB), :] = values[f]
        return carry

    lax.fori_loop(0, comps, body, 0)


def transposed_section(
    section, lam_ref, y_ref, outer_ref, stat_ref, fact_ref, in_ref, out_ref, volume_ref, emit
):
    rows = lam_ref.shape[0] // SUB
    channels = rows // 3 * 2
    layers = (rows - 12) // 3
    edge = [tile(stat_ref, EDGE + f) for f in range(3)]
    outer_edge = [tile(fact_ref, OUTER_EDGE + f) for f in range(3)]
    half_speed = [tile(fact_ref, HALF_SPEED + 3 * section + f) for f in range(3)]
    kappa = tile(stat_ref, KAPPA)
    wet = tile(stat_ref, WET)
    own = [tile(y_ref, r) for r in range(12)]
    result = []
    for r in range(12):
        total = volume_ref[0, r] * own[0]
        for q in range(1, 12):
            total = total + volume_ref[q, r] * own[q]
        result.append(total)
    for f in range(3):
        ends = FACE_NODES[f]
        inner = [edge[f] * own[(ch // 2) * 3 + ends[ch % 2]] for ch in range(8)]
        outer = [outer_edge[f] * tile(outer_ref, f * channels + ch) for ch in range(8)]
        for b in range(8):
            total = half_speed[f] * (inner[b] - outer[b])
            for a in range(8):
                total = total + in_ref[a, b] * inner[a] - out_ref[a, b] * outer[a]
            at = (b // 2) * 3 + ends[b % 2]
            result[at] = result[at] + total
    friction = tile(stat_ref, ZONE_FRICTION) * tile(stat_ref, FRICTION_BASE + section) * wet
    for r in range(3, 9):
        result[r] = result[r] - friction * tile(lam_ref, r)
    exchange = []
    for i in range(3):
        top = tile(lam_ref, 12 + i) - SALT_RETURN * wet * tile(lam_ref, 9 + i)
        exchange.append(kappa * top)
        result[9 + i] = result[9 + i] + exchange[i]
    for r in range(12):
        emit(r, result[r])
    for i in range(3):
        (f0, j0), (f1, j1) = NODE_FACES[i]
        both = edge[f0] + edge[f1]
        from_above = exchange[i]
        for layer in range(layers):
            r = 12 + layer * 3 + i
            value = (
                outer_edge[f0] * tile(outer_ref, f0 * channels + 8 + layer * 2 + j0)
                + outer_edge[f1] * tile(outer_ref, f1 * channels + 8 + layer * 2 + j1)
                - both * tile(y_ref, r)
                - from_above
            )
            if layer + 1 < layers:
                from_above = kappa * (tile(lam_ref, r + 3) - tile(lam_ref, r))
                value = value + from_above
            emit(r, value)


def own_gradients(section, weight, lam_ref, y_ref, x_tiles, stat_ref):
    rows = lam_ref.shape[0] // SUB
    layers = (rows - 12) // 3
    wet = tile(stat_ref, WET)
    kappa = tile(stat_ref, KAPPA)
    momentum = tile(lam_ref, 3) * tile(x_tiles, 3)
    for r in range(4, 9):
        momentum = momentum + tile(lam_ref, r) * tile(x_tiles, r)
    friction = -(weight * wet * tile(stat_ref, FRICTION_BASE + section)) * momentum
    vertical = None
    lateral = None
    for i in range(3):
        (f0, _), (f1, _) = NODE_FACES[i]
        top = tile(lam_ref, 12 + i) - SALT_RETURN * wet * tile(lam_ref, 9 + i)
        total = top * (tile(x_tiles, 9 + i) - tile(x_tiles, 12 + i))
        dots = None
        for layer in range(layers):
            r = 12 + layer * 3 + i
            term = tile(y_ref, r) * tile(x_tiles, r)
            dots = term if dots is None else dots + term
            if layer + 1 < layers:
                total = total + (tile(lam_ref, r + 3) - tile(lam_ref, r)) * (
                    tile(x_tiles, r) - tile(x_tiles, r + 3)
                )
        side = (tile(stat_ref, EDGE + f0) + tile(stat_ref, EDGE + f1)) * dots
        vertical = total if vertical is None else vertical + total
        lateral = side if lateral is None else lateral + side
    return friction, weight * (kappa * vertical - lateral)


def outer_gradients(weight, outer_ref, x_tiles, fact_ref):
    channels = outer_ref.shape[0] // SUB // 3
    values = []
    for f in range(3):
        total = None
        for ch in range(8, channels):
            row = 12 + (ch - 8) // 2 * 3 + FACE_NODES[f][ch % 2]
            term = tile(outer_ref, f * channels + ch) * tile(x_tiles, row)
            total = term if total is None else total + term
        values.append(weight * tile(fact_ref, OUTER_EDGE + f) * total)
    return values


def x_to_tiles(x_ref, section, x_tiles):
    rows = x_ref.shape[3]
    rows_to_tiles(
        lambda b: x_ref[section, 0, 0, :, lanes_of(b)].astype(jnp.float32), x_tiles, rows
    )


def second_kernel(
    cot_ref,
    table_ref,
    stat_ref,
    index_ref,
    x_ref,
    in_ref,
    out_ref,
    volume_ref,
    from_left,
    from_right,
    from_down,
    from_up,
    lam_ref,
    y_ref,
    fact_ref,
    term_ref,
    to_right,
    to_left,
    to_up,
    to_down,
    outer_ref,
    x_tiles,
    sent_ref,
):
    received = (from_left, from_right, from_down, from_up)
    rows = cot_ref.shape[0] // SUB
    comps = rows // 3
    index = partner_index(index_ref)
    lane, sublane, face, remote = index
    outer_states(table_ref, 0, comps, 0, received, index, outer_ref)
    for group in range(4):
        values = gather_by_face(table_ref, rows + 3 * group, lane, sublane, face)
        values = fill_remote(received, comps * 2 + group, lane, remote, values)
        for f in range(3):
            if group == 0:
                put(fact_ref, OUTER_EDGE + f, values[f])
            else:
                k = group - 1
                both = tile(table_ref, rows + 3 * group + f) + values[f]
                put(
                    fact_ref,
                    HALF_SPEED + 3 * k + f,
                    0.5 * jnp.sqrt(1.0 + (0.25 / 8.0) * both),
                )
    values = gather_tile(table_ref, rows + 12, lane, sublane)
    values = fill_remote(received, comps * 2 + 4, lane, remote, values)
    for f in range(3):
        put(fact_ref, OUTER_ZONE + f, values[f])
    wet_area = tile(stat_ref, WET_AREA)
    half_kappa_area = tile(stat_ref, HALF_KAPPA_AREA)

    def emit(r, value):
        lam = (2.0 / 3.0) * (tile(cot_ref, r) + TIME_STEP * value)
        put(lam_ref, r, lam)
        put(y_ref, r, lam * (wet_area if r < 12 else half_kappa_area))

    transposed_section(
        2, cot_ref, table_ref, outer_ref, stat_ref, fact_ref, in_ref, out_ref, volume_ref, emit
    )
    x_to_tiles(x_ref, 0, x_tiles)
    sent = sent_index(index_ref)
    send_states(y_ref, 0, comps, 0, sent, sent_ref)
    send_states(x_tiles, 4, comps - 4, comps * 2, sent, sent_ref)
    write_messages(sent_ref, (to_right, to_left, to_up, to_down))
    x_to_tiles(x_ref, 2, x_tiles)
    weight = TIME_STEP * 2.0 / 3.0
    friction, conduct = own_gradients(2, weight, cot_ref, table_ref, x_tiles, stat_ref)
    put(term_ref, 0, friction)
    put(term_ref, 1, conduct)
    for f, value in enumerate(outer_gradients(weight, outer_ref, x_tiles, fact_ref)):
        put(term_ref, 2 + f, value)


def first_kernel(
    cot_ref,
    lam_ref,
    y_ref,
    stat_ref,
    index_ref,
    fact_ref,
    term_ref,
    x_ref,
    in_ref,
    out_ref,
    volume_ref,
    from_left,
    from_right,
    from_down,
    from_up,
    base_ref,
    next_ref,
    next_y_ref,
    new_term_ref,
    to_right,
    to_left,
    to_up,
    to_down,
    outer_ref,
    x_outer_ref,
    x_tiles,
    sent_ref,
):
    received = (from_left, from_right, from_down, from_up)
    rows = lam_ref.shape[0] // SUB
    comps = rows // 3
    index = partner_index(index_ref)
    outer_states(y_ref, 0, comps, 0, received, index, outer_ref)
    wet_area = tile(stat_ref, WET_AREA)
    half_kappa_area = tile(stat_ref, HALF_KAPPA_AREA)

    def emit(r, value):
        old = tile(lam_ref, r)
        lam = 0.25 * (old + TIME_STEP * value)
        put(next_ref, r, lam)
        put(next_y_ref, r, lam * (wet_area if r < 12 else half_kappa_area))
        put(base_ref, r, (1.0 / 3.0) * tile(cot_ref, r) + 0.75 * old + lam)

    transposed_section(
        1, lam_ref, y_ref, outer_ref, stat_ref, fact_ref, in_ref, out_ref, volume_ref, emit
    )
    send_states(next_y_ref, 0, comps, 0, sent_index(index_ref), sent_ref)
    write_messages(sent_ref, (to_right, to_left, to_up, to_down))
    x_to_tiles(x_ref, 1, x_tiles)
    weight = TIME_STEP * 0.25
    friction, conduct = own_gradients(1, weight, lam_ref, y_ref, x_tiles, stat_ref)
    for f, value in enumerate(outer_gradients(weight, outer_ref, x_tiles, fact_ref)):
        put(new_term_ref, 2 + f, tile(term_ref, 2 + f) + value)
    x_to_tiles(x_ref, 0, x_tiles)
    outer_states(x_tiles, 4, comps - 4, comps * 2, received, index, x_outer_ref)
    friction_0, conduct_0 = own_gradients(0, TIME_STEP, next_ref, next_y_ref, x_tiles, stat_ref)
    friction = friction + friction_0
    conduct = conduct + conduct_0
    channels = (comps - 4) * 2
    for f in range(3):
        total = None
        for ch in range(channels):
            row = 12 + ch // 2 * 3 + FACE_NODES[f][ch % 2]
            term = tile(x_outer_ref, f * channels + ch) * tile(next_y_ref, row)
            total = term if total is None else total + term
        conduct = conduct + TIME_STEP * tile(stat_ref, EDGE + f) * total
    put(new_term_ref, 0, tile(term_ref, 0) + friction)
    put(new_term_ref, 1, tile(term_ref, 1) + conduct)


def zone_kernel(term_ref, stat_ref, fact_ref, conduct_ref, out_ref):
    zones = out_ref.shape[1]
    zone_iota = lax.broadcasted_iota(jnp.int32, (zones, LANES), 0).astype(jnp.float32)
    sub_iota = lax.broadcasted_iota(jnp.int32, (SUB, zones), 0)

    def thirds(value):
        high = value.astype(jnp.bfloat16).astype(jnp.float32)
        rest = value - high
        middle = rest.astype(jnp.bfloat16).astype(jnp.float32)
        return [high, middle, rest - middle]

    def by_zone(values, zone_of, zone_row):
        pieces = sum([thirds(value) for value in values], [])
        left = jnp.concatenate(pieces, axis=0).astype(jnp.bfloat16)
        totals = [jnp.zeros((SUB, zones), jnp.float32) for _ in values]
        for sub in range(SUB):
            line = zone_of[pl.ds(zone_row * SUB + sub, 1), :]
            hot = (jnp.broadcast_to(line, (zones, LANES)) == zone_iota).astype(jnp.float32)
            dots = lax.dot_general(
                left,
                hot.astype(jnp.bfloat16),
                (((1,), (1,)), ((), ())),
                preferred_element_type=jnp.float32,
            )
            for n in range(len(values)):
                at = n * 3 * SUB
                three = dots[at : at + SUB] + dots[at + SUB : at + 2 * SUB]
                three = three + dots[at + 2 * SUB : at + 3 * SUB]
                totals[n] = totals[n] + jnp.where(sub_iota == sub, three, 0.0)
        return totals

    friction, conduct = by_zone([tile(term_ref, 0), tile(term_ref, 1)], stat_ref, ZONE_ID)
    for f in range(3):
        conduct = conduct + by_zone([tile(term_ref, 2 + f)], fact_ref, OUTER_ZONE + f)[0]
    out_ref[0:1, :] = GRAD_WEIGHT * jnp.sum(friction, axis=0, keepdims=True)
    out_ref[1:2, :] = (
        GRAD_WEIGHT * jnp.sum(conduct, axis=0, keepdims=True) / conduct_ref[...]
    )


def last_kernel(
    base_ref,
    lam_ref,
    y_ref,
    stat_ref,
    index_ref,
    fact_ref,
    in_ref,
    out_ref,
    volume_ref,
    from_left,
    from_right,
    from_down,
    from_up,
    adjoint_ref,
    outer_ref,
):
    received = (from_left, from_right, from_down, from_up)
    rows = lam_ref.shape[0] // SUB
    outer_states(y_ref, 0, rows // 3, 0, received, partner_index(index_ref), outer_ref)

    def emit(r, value):
        put(adjoint_ref, r, tile(base_ref, r) + TIME_STEP * value)

    transposed_section(
        0, lam_ref, y_ref, outer_ref, stat_ref, fact_ref, in_ref, out_ref, volume_ref, emit
    )


def total_kernel(zone_ref, adjoint_ref, grads_ref):
    grads_ref[...] = jnp.sum(zone_ref[...], axis=0)


def exchange(messages, *ahead):
    to_right, to_left, to_up, to_down = messages
    from_left = shifted(to_right, "gx", 1)
    from_right = shifted(to_left, "gx", -1)
    corner = pl.BlockSpec((1, to_right.shape[1], LANES), lambda i: (2, 0, 0))
    whole = pl.BlockSpec(memory_space=pl.ANY)
    to_up, to_down = pl.pallas_call(
        corner_kernel,
        grid=(1,),
        in_specs=[corner, corner, whole, whole] + [pl.BlockSpec(memory_space=pltpu.HBM)] * len(ahead),
        out_specs=[corner, corner],
        out_shape=[jax.ShapeDtypeStruct(to_up.shape, to_up.dtype)] * 2,
        input_output_aliases={2: 0, 3: 1},
        name="corners",
    )(from_left, from_right, to_up, to_down, *ahead)
    from_down = shifted(to_up, "gy", 1)
    from_up = shifted(to_down, "gy", -1)
    return from_left, from_right, from_down, from_up


def call(kernel, name, outs, scratch, operands, scalars=(), anywhere=()):
    in_memory = pl.BlockSpec(memory_space=pltpu.VMEM)
    in_scalar = pl.BlockSpec(memory_space=pltpu.SMEM)
    unread = pl.BlockSpec(memory_space=pltpu.HBM)
    specs = [
        in_scalar if n in scalars else unread if n in anywhere else in_memory
        for n in range(len(operands))
    ]
    return pl.pallas_call(
        kernel,
        in_specs=specs,
        out_specs=[in_memory] * len(outs),
        out_shape=outs,
        scratch_shapes=scratch,
        compiler_params=pltpu.CompilerParams(vmem_limit_bytes=32 * 1024 * 1024),
        name=name,
    )(*operands)


def local(
    cotangent,
    section_states,
    inverse_area,
    edge_length,
    roughness,
    soil_conductance,
    zone_friction,
    zone_conductivity,
    wet_mask,
    element_zone,
    send_face,
    send_count,
    face_partner,
    volume_matrix,
    flux_in,
    flux_out,
):
    rows = cotangent.shape[2]
    channels = rows // 3 * 2
    zones = zone_friction.shape[0]
    slots = send_face.shape[3]
    f32 = jnp.float32

    def tiles(count, dtype=f32):
        return jax.ShapeDtypeStruct((count * SUB, LANES), dtype)

    def tile_scratch(count, dtype=f32):
        return pltpu.VMEM((count * SUB, LANES), dtype)

    def messages(count):
        return [jax.ShapeDtypeStruct((slots // LANES + 1, count, LANES), f32)] * 4

    def sent_scratch(count):
        return pltpu.VMEM((slots // LANES, count * SUB, LANES), f32)

    square = lambda one: one.reshape(SUB, LANES)
    cot = cotangent.reshape(rows * SUB, LANES)
    table, stat, index, *to_send = call(
        prepare_kernel,
        "prepare",
        [tiles(rows + 13), tiles(STAT_ROWS), tiles(INDEX_ROWS, jnp.int32)]
        + messages(channels + 5),
        [tile_scratch(16), sent_scratch(channels + 5)],
        [
            cot,
            section_states,
            square(inverse_area),
            edge_length.reshape(3 * SUB, LANES),
            square(roughness),
            square(soil_conductance),
            zone_friction.reshape(-1, LANES),
            zone_conductivity.reshape(-1, LANES),
            square(wet_mask),
            square(element_zone),
            send_face,
            face_partner.reshape(3 * SUB, LANES),
        ],
    )
    received = exchange(to_send)
    lam, y, fact, term, *to_send = call(
        second_kernel,
        "section_two",
        [tiles(rows), tiles(rows), tiles(FACT_ROWS), tiles(5)]
        + messages(channels + channels - 8),
        [tile_scratch(3 * channels), tile_scratch(rows), sent_scratch(2 * channels - 8)],
        [cot, table, stat, index, section_states, flux_in, flux_out, volume_matrix, *received],
        (5, 6, 7),
    )
    received = exchange(to_send)
    base, lam, y, term, *to_send = call(
        first_kernel,
        "section_one",
        [tiles(rows), tiles(rows), tiles(rows), tiles(5)] + messages(channels),
        [
            tile_scratch(3 * channels),
            tile_scratch(3 * (channels - 8)),
            tile_scratch(rows),
            sent_scratch(channels),
        ],
        [
            cot,
            lam,
            y,
            stat,
            index,
            fact,
            term,
            section_states,
            flux_in,
            flux_out,
            volume_matrix,
            *received,
        ],
        (8, 9, 10),
    )
    (zone_terms,) = call(
        zone_kernel,
        "zone_sums",
        [jax.ShapeDtypeStruct((2, zones), f32)],
        [],
        [term, stat, fact, zone_conductivity.reshape(1, zones)],
    )
    all_terms = lax.all_gather(zone_terms, ("gx", "gy"))
    received = exchange(to_send, zone_terms)
    (adjoint,) = call(
        last_kernel,
        "section_zero",
        [tiles(rows)],
        [tile_scratch(3 * channels)],
        [
            base,
            lam,
            y,
            stat,
            index,
            fact,
            flux_in,
            flux_out,
            volume_matrix,
            *received,
        ],
        (6, 7, 8),
    )
    (zone_grads,) = call(
        total_kernel,
        "zone_total",
        [jax.ShapeDtypeStruct((2, zones), f32)],
        [],
        [all_terms, adjoint],
        anywhere=(1,),
    )
    return adjoint.reshape(cotangent.shape), zone_grads


def solution(mesh):
    placed = (
        P("gx", "gy", None, None),
        P(None, "gx", "gy", None, None),
        P("gx", "gy", None),
        P("gx", "gy", None, None),
        P("gx", "gy", None),
        P("gx", "gy", None),
        P(),
        P(),
        P("gx", "gy", None),
        P("gx", "gy", None),
        P("gx", "gy", None, None),
        P("gx", "gy", None),
        P("gx", "gy", None, None),
        P(),
        P(),
        P(),
    )
    return jax.shard_map(
        local,
        mesh=mesh,
        in_specs=placed,
        out_specs=(P("gx", "gy", None, None), P()),
        check_vma=False,
    )
```

```python
import functools
import jax
import jax.numpy as jnp
from jax import lax
from jax.experimental import pallas as pl
from jax.experimental.pallas import tpu as pltpu
from jax.sharding import PartitionSpec as P

TIME_STEP = 0.2
SALT_RETURN = 0.5
LATERAL = 0.5
GRAD_WEIGHT = 1.0 / 64.0
FACE_NODES = ((1, 2), (2, 0), (0, 1))
NODE_FACES = (((1, 1), (2, 0)), ((0, 0), (2, 1)), ((0, 1), (1, 0)))
SUB = 8
LANES = 128


WET_AREA, KAPPA, HALF_KAPPA_AREA, WET, EDGE, FRICTION_BASE, ZONE_FRICTION, ZONE_ID = (
    0,
    1,
    2,
    3,
    4,
    7,
    10,
    11,
)
STAT_ROWS = 12
NEAR_VMEM, FAR_VMEM = 32, 60
OUTER_EDGE, OUTER_ZONE, HALF_SPEED = 0, 3, 6
FACT_ROWS = 15
REMOTE_BLOCKS = (
    (0, 0),
    (0, 1),
    (1, 0),
    (1, 1),
    (2, 0),
    (2, 1),
    (3, 0),
    (3, 1),
    (2, 2),
    (3, 2),
)


def shifted(x, axis, by):
    peers = lax.axis_size(axis)
    pairs = [(i, i + by) for i in range(peers) if 0 <= i + by < peers]
    return lax.ppermute(x, axis, pairs)


def tile(ref, row):
    return ref[row * SUB : (row + 1) * SUB, :]


def put(ref, row, value):
    ref[row * SUB : (row + 1) * SUB, :] = value


def take(row, lane_index):
    return jnp.take_along_axis(row, lane_index, axis=1, mode="promise_in_bounds")


def spread(ref, row):
    return jnp.broadcast_to(ref[pl.ds(row, 1), :], (SUB, LANES))


def rows_to_tiles(read, tiles_ref, count):
    for block in range(SUB):
        tiles_ref[pl.ds(block, count, stride=SUB), :] = read(block)


def lanes_of(block):
    return slice(block * LANES, (block + 1) * LANES)


def gather_tile(src, row, lane_index, sublane_index):
    found = [None] * len(lane_index)
    for sub in range(SUB):
        line = spread(src, row * SUB + sub)
        for d, lane in enumerate(lane_index):
            got = take(line, lane)
            found[d] = got if sub == 0 else jnp.where(sublane_index[d] == sub, got, found[d])
    return found


def pick(face, for_zero, for_one, for_two):
    return jnp.where(face == 0, for_zero, jnp.where(face == 1, for_one, for_two))


def gather_ends(src, row, lane_index, sublane_index, face):
    nodes = [gather_tile(src, row + i, lane_index, sublane_index) for i in range(3)]
    ends = []
    for d, which in enumerate(face):
        n0, n1, n2 = nodes[0][d], nodes[1][d], nodes[2][d]
        ends.append((pick(which, n1, n2, n0), pick(which, n2, n0, n1)))
    return ends


def gather_by_face(src, row, lane_index, sublane_index, face):
    faces = [gather_tile(src, row + i, lane_index, sublane_index) for i in range(3)]
    return [pick(which, faces[0][d], faces[1][d], faces[2][d]) for d, which in enumerate(face)]


def fill_remote(received, row, lane_index, remote_index, values):
    values = list(values)
    for number, (message, block) in enumerate(REMOTE_BLOCKS):
        line = spread(received[message].at[block], row)
        for d, lane in enumerate(lane_index):
            values[d] = jnp.where(remote_index[d] == number, take(line, lane), values[d])
    return values


def partner_index(index_ref):
    return [[tile(index_ref, part * 3 + f) for f in range(3)] for part in range(4)]


def sent_index(index_ref):
    return [[tile(index_ref, 12 + part * 2 + d) for d in range(2)] for part in range(3)]


INDEX_ROWS = 18


def send_states(src, first_comp, comps, first_row, sent, sent_ref):
    lane, sublane, face = sent

    def body(step, carry):
        ends = gather_ends(src, (first_comp + step) * 3, lane, sublane, face)
        for d in range(2):
            for j in range(2):
                at = pl.multiple_of((first_row + step * 2 + j) * SUB, SUB)
                sent_ref[d, pl.ds(at, SUB), :] = ends[d][j]
        return carry

    lax.fori_loop(0, comps, body, 0)


def write_messages(sent_ref, messages):
    to_right, to_left, to_up, to_down = messages
    count = to_right.shape[1]
    for ref, direction in ((to_right, 6), (to_left, 1), (to_up, 4), (to_down, 3)):
        for block in range(2):
            ref[block] = sent_ref.at[block][pl.ds(direction, count, stride=SUB), :]
    for ref, direction in ((to_right, 5), (to_left, 2)):
        ref[2] = sent_ref.at[0][pl.ds(direction, count, stride=SUB), :]


def prepare_kernel(
    cot_ref,
    x_ref,
    area_ref,
    edge_ref,
    rough_ref,
    soil_ref,
    friction_ref,
    conduct_ref,
    wet_ref,
    zone_ref,
    send_ref,
    partner_ref,
    table_ref,
    stat_ref,
    index_ref,
    to_right,
    to_left,
    to_up,
    to_down,
    x_tiles,
    sent_ref,
    *fetched,
):
    *fetched, sems = fetched
    sources = [
        partner_ref,
        send_ref,
        cot_ref,
        x_ref.at[:, 0, 0, 0:16],
        area_ref,
        edge_ref,
        rough_ref,
        soil_ref,
        friction_ref,
        conduct_ref,
        wet_ref,
        zone_ref,
    ]
    copies = [
        pltpu.make_async_copy(source, target, sems.at[n])
        for n, (source, target) in enumerate(zip(sources, fetched))
    ]
    for copy in copies:
        copy.start()
    for copy in copies:
        copy.wait()
    (
        partner_ref,
        send_ref,
        cot_ref,
        x_ref,
        area_ref,
        edge_ref,
        rough_ref,
        soil_ref,
        friction_ref,
        conduct_ref,
        wet_ref,
        zone_ref,
    ) = fetched
    rows = cot_ref.shape[0] // SUB
    sections = x_ref.shape[0]
    face_total = 3 * SUB * LANES
    for f in range(3):
        partner = tile(partner_ref, f)
        beyond = partner - face_total
        direction = jnp.right_shift(beyond, 8)
        half = jnp.bitwise_and(jnp.right_shift(beyond, 7), 1)
        lane = jnp.bitwise_and(partner, LANES - 1)
        remote = jnp.where(beyond >= 0, 8, -1)
        remote = jnp.where((direction == 2) | (direction == 7), 9, remote)
        for number, first in ((1, 0), (6, 2), (3, 4), (4, 6)):
            remote = jnp.where(direction == number, first + half, remote)
        lane = jnp.where((direction == 0) | (direction == 7), jnp.bitwise_and(lane + 4, LANES - 1), lane)
        put(index_ref, f, lane)
        put(index_ref, 3 + f, jnp.bitwise_and(jnp.right_shift(partner, 7), SUB - 1))
        put(index_ref, 6 + f, jnp.right_shift(partner, 10))
        put(index_ref, 9 + f, remote)
    sub_iota = lax.broadcasted_iota(jnp.int32, (SUB, LANES), 0)
    lane_iota = lax.broadcasted_iota(jnp.int32, (SUB, LANES), 1)
    for d in range(2):
        slots = send_ref[0, 0, :, lanes_of(d)]
        if d == 0:
            moved = pltpu.roll(slots, 4, 1)
            second = (lane_iota >= 4) & (lane_iota < 8)
            slots = jnp.where(second & (sub_iota == 5), pltpu.roll(moved, 6, 0), slots)
            slots = jnp.where(second & (sub_iota == 2), pltpu.roll(moved, 2, 0), slots)
        put(index_ref, 12 + d, jnp.bitwise_and(slots, LANES - 1))
        put(index_ref, 14 + d, jnp.bitwise_and(jnp.right_shift(slots, 7), SUB - 1))
        put(index_ref, 16 + d, jnp.right_shift(slots, 10))
    zone = zone_ref[...]
    zone_lane = jnp.bitwise_and(zone, LANES - 1)
    zone_block = jnp.right_shift(zone, 7)
    factors = []
    for ref in (friction_ref, conduct_ref):
        found = None
        for block in range(ref.shape[0]):
            got = take(spread(ref, block), zone_lane)
            found = got if block == 0 else jnp.where(zone_block == block, got, found)
        factors.append(found)
    area = area_ref[...]
    wet = wet_ref[...].astype(jnp.float32)
    kappa = factors[1] * soil_ref[...]
    wet_area = wet * area
    half_kappa_area = LATERAL * kappa * area
    put(stat_ref, WET_AREA, wet_area)
    put(stat_ref, KAPPA, kappa)
    put(stat_ref, HALF_KAPPA_AREA, half_kappa_area)
    put(stat_ref, WET, wet)
    put(stat_ref, ZONE_FRICTION, factors[0])
    put(stat_ref, ZONE_ID, zone.astype(jnp.float32))
    stat_ref[EDGE * SUB : (EDGE + 3) * SUB, :] = edge_ref[...]
    for k in range(sections):
        rows_to_tiles(
            lambda b: x_ref[k, :, lanes_of(b)].astype(jnp.float32), x_tiles, 16
        )
        squares = [tile(x_tiles, r) * tile(x_tiles, r) for r in range(12)]
        node_sum = [squares[i] + squares[3 + i] + squares[6 + i] + squares[9 + i] for i in range(3)]
        for f in range(3):
            first, second = FACE_NODES[f]
            put(table_ref, rows + 3 + 3 * k + f, node_sum[first] + node_sum[second])
        momentum = squares[3]
        for r in range(4, 9):
            momentum = momentum + squares[r]
        put(
            stat_ref,
            FRICTION_BASE + k,
            rough_ref[...] * jnp.sqrt(1.0 + momentum * (1.0 / 6.0)),
        )
    for f in range(3):
        put(table_ref, rows + f, tile(stat_ref, EDGE + f))
    put(table_ref, rows + 12, zone.astype(jnp.float32))
    for r in range(rows):
        put(table_ref, r, tile(cot_ref, r) * (wet_area if r < 12 else half_kappa_area))
    sent = sent_index(index_ref)
    comps = rows // 3
    send_states(table_ref, 0, comps, 0, sent, sent_ref)
    for group in range(4):
        values = gather_by_face(table_ref, rows + 3 * group, *sent)
        for d in range(2):
            at = (comps * 2 + group) * SUB
            sent_ref[d, at : at + SUB, :] = values[d]
    values = gather_tile(table_ref, rows + 12, sent[0], sent[1])
    for d in range(2):
        at = (comps * 2 + 4) * SUB
        sent_ref[d, at : at + SUB, :] = values[d]
    write_messages(sent_ref, (to_right, to_left, to_up, to_down))


def corner_kernel(left_ref, right_ref, up_in, down_in, *rest):
    up_ref, down_ref = rest[-2:]
    left, right = left_ref[2], right_ref[2]
    first = lax.broadcasted_iota(jnp.int32, left.shape, 1) < 4
    up_ref[2] = jnp.where(first, right, left)
    down_ref[2] = jnp.where(first, left, right)


def outer_states(src, first_comp, comps, first_row, received, index, out_ref):
    lane, sublane, face, remote = index

    def body(step, carry):
        ends = gather_ends(src, (first_comp + step) * 3, lane, sublane, face)
        for j in range(2):
            values = fill_remote(
                received, first_row + step * 2 + j, lane, remote, [ends[f][j] for f in range(3)]
            )
            for f in range(3):
                at = pl.multiple_of((f * comps * 2 + step * 2 + j) * SUB, SUB)
                out_ref[pl.ds(at, SUB), :] = values[f]
        return carry

    lax.fori_loop(0, comps, body, 0)


def transposed_section(
    section, lam_ref, y_ref, outer_ref, stat_ref, fact_ref, in_ref, out_ref, volume_ref, emit
):
    rows = lam_ref.shape[0] // SUB
    channels = rows // 3 * 2
    layers = (rows - 12) // 3
    edge = [tile(stat_ref, EDGE + f) for f in range(3)]
    outer_edge = [tile(fact_ref, OUTER_EDGE + f) for f in range(3)]
    half_speed = [tile(fact_ref, HALF_SPEED + 3 * section + f) for f in range(3)]
    kappa = tile(stat_ref, KAPPA)
    wet = tile(stat_ref, WET)
    own = [tile(y_ref, r) for r in range(12)]
    result = []
    for r in range(12):
        total = volume_ref[0, r] * own[0]
        for q in range(1, 12):
            total = total + volume_ref[q, r] * own[q]
        result.append(total)
    for f in range(3):
        ends = FACE_NODES[f]
        inner = [edge[f] * own[(ch // 2) * 3 + ends[ch % 2]] for ch in range(8)]
        outer = [outer_edge[f] * tile(outer_ref, f * channels + ch) for ch in range(8)]
        for b in range(8):
            total = half_speed[f] * (inner[b] - outer[b])
            for a in range(8):
                total = total + in_ref[a, b] * inner[a] - out_ref[a, b] * outer[a]
            at = (b // 2) * 3 + ends[b % 2]
            result[at] = result[at] + total
    friction = tile(stat_ref, ZONE_FRICTION) * tile(stat_ref, FRICTION_BASE + section) * wet
    for r in range(3, 9):
        result[r] = result[r] - friction * tile(lam_ref, r)
    exchange = []
    for i in range(3):
        top = tile(lam_ref, 12 + i) - SALT_RETURN * wet * tile(lam_ref, 9 + i)
        exchange.append(kappa * top)
        result[9 + i] = result[9 + i] + exchange[i]
    for r in range(12):
        emit(r, result[r])
    for i in range(3):
        (f0, j0), (f1, j1) = NODE_FACES[i]
        both = edge[f0] + edge[f1]
        from_above = exchange[i]
        for layer in range(layers):
            r = 12 + layer * 3 + i
            value = (
                outer_edge[f0] * tile(outer_ref, f0 * channels + 8 + layer * 2 + j0)
                + outer_edge[f1] * tile(outer_ref, f1 * channels + 8 + layer * 2 + j1)
                - both * tile(y_ref, r)
                - from_above
            )
            if layer + 1 < layers:
                from_above = kappa * (tile(lam_ref, r + 3) - tile(lam_ref, r))
                value = value + from_above
            emit(r, value)


def own_gradients(section, weight, lam_ref, y_ref, x_tiles, stat_ref):
    rows = lam_ref.shape[0] // SUB
    layers = (rows - 12) // 3
    wet = tile(stat_ref, WET)
    kappa = tile(stat_ref, KAPPA)
    momentum = tile(lam_ref, 3) * tile(x_tiles, 3)
    for r in range(4, 9):
        momentum = momentum + tile(lam_ref, r) * tile(x_tiles, r)
    friction = -(weight * wet * tile(stat_ref, FRICTION_BASE + section)) * momentum
    vertical = None
    lateral = None
    for i in range(3):
        (f0, _), (f1, _) = NODE_FACES[i]
        top = tile(lam_ref, 12 + i) - SALT_RETURN * wet * tile(lam_ref, 9 + i)
        total = top * (tile(x_tiles, 9 + i) - tile(x_tiles, 12 + i))
        dots = None
        for layer in range(layers):
            r = 12 + layer * 3 + i
            term = tile(y_ref, r) * tile(x_tiles, r)
            dots = term if dots is None else dots + term
            if layer + 1 < layers:
                total = total + (tile(lam_ref, r + 3) - tile(lam_ref, r)) * (
                    tile(x_tiles, r) - tile(x_tiles, r + 3)
                )
        side = (tile(stat_ref, EDGE + f0) + tile(stat_ref, EDGE + f1)) * dots
        vertical = total if vertical is None else vertical + total
        lateral = side if lateral is None else lateral + side
    return friction, weight * (kappa * vertical - lateral)


def outer_gradients(weight, outer_ref, x_tiles, fact_ref):
    channels = outer_ref.shape[0] // SUB // 3
    values = []
    for f in range(3):
        total = None
        for ch in range(8, channels):
            row = 12 + (ch - 8) // 2 * 3 + FACE_NODES[f][ch % 2]
            term = tile(outer_ref, f * channels + ch) * tile(x_tiles, row)
            total = term if total is None else total + term
        values.append(weight * tile(fact_ref, OUTER_EDGE + f) * total)
    return values


def x_to_tiles(x_ref, section, x_tiles):
    rows = x_ref.shape[3]
    rows_to_tiles(
        lambda b: x_ref[section, 0, 0, :, lanes_of(b)].astype(jnp.float32), x_tiles, rows
    )


def second_kernel(
    cot_ref,
    table_ref,
    stat_ref,
    index_ref,
    x_ref,
    in_ref,
    out_ref,
    volume_ref,
    from_left,
    from_right,
    from_down,
    from_up,
    lam_ref,
    y_ref,
    fact_ref,
    term_ref,
    to_right,
    to_left,
    to_up,
    to_down,
    outer_ref,
    x_tiles,
    sent_ref,
):
    received = (from_left, from_right, from_down, from_up)
    rows = cot_ref.shape[0] // SUB
    comps = rows // 3
    index = partner_index(index_ref)
    lane, sublane, face, remote = index
    outer_states(table_ref, 0, comps, 0, received, index, outer_ref)
    for group in range(4):
        values = gather_by_face(table_ref, rows + 3 * group, lane, sublane, face)
        values = fill_remote(received, comps * 2 + group, lane, remote, values)
        for f in range(3):
            if group == 0:
                put(fact_ref, OUTER_EDGE + f, values[f])
            else:
                k = group - 1
                both = tile(table_ref, rows + 3 * group + f) + values[f]
                put(
                    fact_ref,
                    HALF_SPEED + 3 * k + f,
                    0.5 * jnp.sqrt(1.0 + (0.25 / 8.0) * both),
                )
    values = gather_tile(table_ref, rows + 12, lane, sublane)
    values = fill_remote(received, comps * 2 + 4, lane, remote, values)
    for f in range(3):
        put(fact_ref, OUTER_ZONE + f, values[f])
    wet_area = tile(stat_ref, WET_AREA)
    half_kappa_area = tile(stat_ref, HALF_KAPPA_AREA)

    def emit(r, value):
        lam = (2.0 / 3.0) * (tile(cot_ref, r) + TIME_STEP * value)
        put(lam_ref, r, lam)
        put(y_ref, r, lam * (wet_area if r < 12 else half_kappa_area))

    transposed_section(
        2, cot_ref, table_ref, outer_ref, stat_ref, fact_ref, in_ref, out_ref, volume_ref, emit
    )
    x_to_tiles(x_ref, 0, x_tiles)
    sent = sent_index(index_ref)
    send_states(y_ref, 0, comps, 0, sent, sent_ref)
    send_states(x_tiles, 4, comps - 4, comps * 2, sent, sent_ref)
    write_messages(sent_ref, (to_right, to_left, to_up, to_down))
    x_to_tiles(x_ref, 2, x_tiles)
    weight = TIME_STEP * 2.0 / 3.0
    friction, conduct = own_gradients(2, weight, cot_ref, table_ref, x_tiles, stat_ref)
    put(term_ref, 0, friction)
    put(term_ref, 1, conduct)
    for f, value in enumerate(outer_gradients(weight, outer_ref, x_tiles, fact_ref)):
        put(term_ref, 2 + f, value)


def first_kernel(
    cot_ref,
    lam_ref,
    y_ref,
    stat_ref,
    index_ref,
    fact_ref,
    term_ref,
    x_ref,
    in_ref,
    out_ref,
    volume_ref,
    from_left,
    from_right,
    from_down,
    from_up,
    base_ref,
    next_ref,
    next_y_ref,
    new_term_ref,
    to_right,
    to_left,
    to_up,
    to_down,
    outer_ref,
    x_outer_ref,
    x_tiles,
    sent_ref,
):
    received = (from_left, from_right, from_down, from_up)
    rows = lam_ref.shape[0] // SUB
    comps = rows // 3
    index = partner_index(index_ref)
    outer_states(y_ref, 0, comps, 0, received, index, outer_ref)
    wet_area = tile(stat_ref, WET_AREA)
    half_kappa_area = tile(stat_ref, HALF_KAPPA_AREA)

    def emit(r, value):
        old = tile(lam_ref, r)
        lam = 0.25 * (old + TIME_STEP * value)
        put(next_ref, r, lam)
        put(next_y_ref, r, lam * (wet_area if r < 12 else half_kappa_area))
        put(base_ref, r, (1.0 / 3.0) * tile(cot_ref, r) + 0.75 * old + lam)

    transposed_section(
        1, lam_ref, y_ref, outer_ref, stat_ref, fact_ref, in_ref, out_ref, volume_ref, emit
    )
    send_states(next_y_ref, 0, comps, 0, sent_index(index_ref), sent_ref)
    write_messages(sent_ref, (to_right, to_left, to_up, to_down))
    x_to_tiles(x_ref, 1, x_tiles)
    weight = TIME_STEP * 0.25
    friction, conduct = own_gradients(1, weight, lam_ref, y_ref, x_tiles, stat_ref)
    for f, value in enumerate(outer_gradients(weight, outer_ref, x_tiles, fact_ref)):
        put(new_term_ref, 2 + f, tile(term_ref, 2 + f) + value)
    x_to_tiles(x_ref, 0, x_tiles)
    outer_states(x_tiles, 4, comps - 4, comps * 2, received, index, x_outer_ref)
    friction_0, conduct_0 = own_gradients(0, TIME_STEP, next_ref, next_y_ref, x_tiles, stat_ref)
    friction = friction + friction_0
    conduct = conduct + conduct_0
    channels = (comps - 4) * 2
    for f in range(3):
        total = None
        for ch in range(channels):
            row = 12 + ch // 2 * 3 + FACE_NODES[f][ch % 2]
            term = tile(x_outer_ref, f * channels + ch) * tile(next_y_ref, row)
            total = term if total is None else total + term
        conduct = conduct + TIME_STEP * tile(stat_ref, EDGE + f) * total
    put(new_term_ref, 0, tile(term_ref, 0) + friction)
    put(new_term_ref, 1, tile(term_ref, 1) + conduct)


def zone_kernel(term_ref, stat_ref, fact_ref, conduct_ref, out_ref):
    zones = out_ref.shape[2]
    zone_iota = lax.broadcasted_iota(jnp.int32, (zones, LANES), 0).astype(jnp.float32)
    sub_iota = lax.broadcasted_iota(jnp.int32, (SUB, zones), 0)

    def thirds(value):
        high = value.astype(jnp.bfloat16).astype(jnp.float32)
        rest = value - high
        middle = rest.astype(jnp.bfloat16).astype(jnp.float32)
        return [high, middle, rest - middle]

    def by_zone(values, zone_of, zone_row):
        pieces = sum([thirds(value) for value in values], [])
        left = jnp.concatenate(pieces, axis=0).astype(jnp.bfloat16)
        totals = [jnp.zeros((SUB, zones), jnp.float32) for _ in values]
        for sub in range(SUB):
            line = zone_of[pl.ds(zone_row * SUB + sub, 1), :]
            hot = (jnp.broadcast_to(line, (zones, LANES)) == zone_iota).astype(jnp.float32)
            dots = lax.dot_general(
                left,
                hot.astype(jnp.bfloat16),
                (((1,), (1,)), ((), ())),
                preferred_element_type=jnp.float32,
            )
            for n in range(len(values)):
                at = n * 3 * SUB
                three = dots[at : at + SUB] + dots[at + SUB : at + 2 * SUB]
                three = three + dots[at + 2 * SUB : at + 3 * SUB]
                totals[n] = totals[n] + jnp.where(sub_iota == sub, three, 0.0)
        return totals

    friction, conduct = by_zone([tile(term_ref, 0), tile(term_ref, 1)], stat_ref, ZONE_ID)
    for f in range(3):
        conduct = conduct + by_zone([tile(term_ref, 2 + f)], fact_ref, OUTER_ZONE + f)[0]
    friction = GRAD_WEIGHT * jnp.sum(friction, axis=0, keepdims=True)
    conduct = GRAD_WEIGHT * jnp.sum(conduct, axis=0, keepdims=True) / conduct_ref[...]
    for device in range(out_ref.shape[0]):
        out_ref[device, 0:1, :] = friction
        out_ref[device, 1:2, :] = conduct


def last_kernel(
    base_ref,
    lam_ref,
    y_ref,
    stat_ref,
    index_ref,
    fact_ref,
    in_ref,
    out_ref,
    volume_ref,
    from_left,
    from_right,
    from_down,
    from_up,
    adjoint_ref,
    last_ref,
    outer_ref,
):
    received = (from_left, from_right, from_down, from_up)
    rows = lam_ref.shape[0] // SUB
    outer_states(y_ref, 0, rows // 3, 0, received, partner_index(index_ref), outer_ref)

    def emit(r, value):
        put(adjoint_ref, r, tile(base_ref, r) + TIME_STEP * value)

    transposed_section(
        0, lam_ref, y_ref, outer_ref, stat_ref, fact_ref, in_ref, out_ref, volume_ref, emit
    )
    last_ref[...] = tile(adjoint_ref, rows - 1)


def total_kernel(zone_ref, adjoint_ref, grads_ref):
    grads_ref[...] = jnp.sum(zone_ref[...], axis=0)


def exchange(messages, *ahead):
    to_right, to_left, to_up, to_down = messages
    from_left = shifted(to_right, "gx", 1)
    from_right = shifted(to_left, "gx", -1)
    to_up, to_down = call(
        corner_kernel,
        "corners",
        [jax.ShapeDtypeStruct(to_up.shape, to_up.dtype)] * 2,
        [],
        [from_left, from_right, to_up, to_down, *ahead],
        aliases={2: 0, 3: 1},
    )
    from_down = shifted(to_up, "gy", 1)
    from_up = shifted(to_down, "gy", -1)
    return from_left, from_right, from_down, from_up


def call(kernel, name, outs, scratch, operands, scalars=(), far=False, aliases={}):
    in_memory = pl.BlockSpec(memory_space=pltpu.VMEM)
    in_scalar = pl.BlockSpec(memory_space=pltpu.SMEM)
    in_place = pl.BlockSpec(memory_space=pl.ANY)
    return pl.pallas_call(
        kernel,
        in_specs=[
            in_place if far else in_scalar if n in scalars else in_memory
            for n in range(len(operands))
        ],
        out_specs=[in_memory] * len(outs),
        out_shape=outs,
        scratch_shapes=scratch,
        input_output_aliases=aliases,
        compiler_params=pltpu.CompilerParams(
            vmem_limit_bytes=(FAR_VMEM if far else NEAR_VMEM) * 1024 * 1024
        ),
        name=name,
    )(*operands)


def local(
    cotangent,
    section_states,
    inverse_area,
    edge_length,
    roughness,
    soil_conductance,
    zone_friction,
    zone_conductivity,
    wet_mask,
    element_zone,
    send_face,
    send_count,
    face_partner,
    volume_matrix,
    flux_in,
    flux_out,
):
    rows = cotangent.shape[2]
    channels = rows // 3 * 2
    zones = zone_friction.shape[0]
    slots = send_face.shape[3]
    devices = lax.axis_size("gx") * lax.axis_size("gy")
    f32 = jnp.float32

    def tiles(count, dtype=f32):
        return jax.ShapeDtypeStruct((count * SUB, LANES), dtype)

    def tile_scratch(count, dtype=f32):
        return pltpu.VMEM((count * SUB, LANES), dtype)

    def messages(count):
        return [jax.ShapeDtypeStruct((slots // LANES + 1, count, LANES), f32)] * 4

    def sent_scratch(count):
        return pltpu.VMEM((slots // LANES, count * SUB, LANES), f32)

    square = lambda one: one.reshape(SUB, LANES)
    cot = cotangent.reshape(rows * SUB, LANES)
    table, stat, index, *to_send = call(
        prepare_kernel,
        "prepare",
        [tiles(rows + 13), tiles(STAT_ROWS), tiles(INDEX_ROWS, jnp.int32)]
        + messages(channels + 5),
        [tile_scratch(16), sent_scratch(channels + 5)]
        + [
            tile_scratch(3, jnp.int32),
            pltpu.VMEM(send_face.shape, jnp.int32),
            tile_scratch(rows),
            pltpu.VMEM((section_states.shape[0], 16, SUB * LANES), section_states.dtype),
            tile_scratch(1),
            tile_scratch(3),
            tile_scratch(1),
            tile_scratch(1),
            pltpu.VMEM((zones // LANES, LANES), f32),
            pltpu.VMEM((zones // LANES, LANES), f32),
            tile_scratch(1, jnp.int32),
            tile_scratch(1, jnp.int32),
            pltpu.SemaphoreType.DMA((12,)),
        ],
        [
            cot,
            section_states,
            square(inverse_area),
            edge_length.reshape(3 * SUB, LANES),
            square(roughness),
            square(soil_conductance),
            zone_friction.reshape(-1, LANES),
            zone_conductivity.reshape(-1, LANES),
            square(wet_mask),
            square(element_zone),
            send_face,
            face_partner.reshape(3 * SUB, LANES),
        ],
        far=True,
    )
    received = exchange(to_send)
    lam, y, fact, term, *to_send = call(
        second_kernel,
        "section_two",
        [tiles(rows), tiles(rows), tiles(FACT_ROWS), tiles(5)]
        + messages(channels + channels - 8),
        [tile_scratch(3 * channels), tile_scratch(rows), sent_scratch(2 * channels - 8)],
        [cot, table, stat, index, section_states, flux_in, flux_out, volume_matrix, *received],
        (5, 6, 7),
    )
    received = exchange(to_send)
    base, lam, y, term, *to_send = call(
        first_kernel,
        "section_one",
        [tiles(rows), tiles(rows), tiles(rows), tiles(5)] + messages(channels),
        [
            tile_scratch(3 * channels),
            tile_scratch(3 * (channels - 8)),
            tile_scratch(rows),
            sent_scratch(channels),
        ],
        [
            cot,
            lam,
            y,
            stat,
            index,
            fact,
            term,
            section_states,
            flux_in,
            flux_out,
            volume_matrix,
            *received,
        ],
        (8, 9, 10),
    )
    (zone_terms,) = call(
        zone_kernel,
        "zone_sums",
        [jax.ShapeDtypeStruct((devices, 2, zones), f32)],
        [],
        [term, stat, fact, zone_conductivity.reshape(1, zones)],
    )
    all_terms = lax.all_to_all(zone_terms, ("gx", "gy"), 0, 0)
    received = exchange(to_send, zone_terms)
    adjoint, last = call(
        last_kernel,
        "section_zero",
        [tiles(rows), tiles(1)],
        [tile_scratch(3 * channels)],
        [
            base,
            lam,
            y,
            stat,
            index,
            fact,
            flux_in,
            flux_out,
            volume_matrix,
            *received,
        ],
        (6, 7, 8),
    )
    (zone_grads,) = call(
        total_kernel,
        "zone_total",
        [jax.ShapeDtypeStruct((2, zones), f32)],
        [],
        [all_terms, last],
    )
    return adjoint.reshape(cotangent.shape), zone_grads


def solution(mesh):
    placed = (
        P("gx", "gy", None, None),
        P(None, "gx", "gy", None, None),
        P("gx", "gy", None),
        P("gx", "gy", None, None),
        P("gx", "gy", None),
        P("gx", "gy", None),
        P(),
        P(),
        P("gx", "gy", None),
        P("gx", "gy", None),
        P("gx", "gy", None, None),
        P("gx", "gy", None),
        P("gx", "gy", None, None),
        P(),
        P(),
        P(),
    )
    return jax.shard_map(
        local,
        mesh=mesh,
        in_specs=placed,
        out_specs=(P("gx", "gy", None, None), P()),
        check_vma=False,
    )
```

```python
import functools
import jax
import jax.numpy as jnp
from jax import lax
from jax.experimental import pallas as pl
from jax.experimental.pallas import tpu as pltpu
from jax.sharding import PartitionSpec as P

TIME_STEP = 0.2
SALT_RETURN = 0.5
LATERAL = 0.5
GRAD_WEIGHT = 1.0 / 64.0
FACE_NODES = ((1, 2), (2, 0), (0, 1))
NODE_FACES = (((1, 1), (2, 0)), ((0, 0), (2, 1)), ((0, 1), (1, 0)))
SUB = 8
LANES = 128


WET_AREA, KAPPA, HALF_KAPPA_AREA, WET, EDGE, FRICTION_BASE, ZONE_FRICTION, ZONE_ID = (
    0,
    1,
    2,
    3,
    4,
    7,
    10,
    11,
)
STAT_ROWS = 12
NEAR_VMEM, FAR_VMEM = 32, 60
OUTER_EDGE, OUTER_ZONE, HALF_SPEED = 0, 3, 6
FACT_ROWS = 15
REMOTE_BLOCKS = (
    (0, 0),
    (0, 1),
    (1, 0),
    (1, 1),
    (2, 0),
    (2, 1),
    (3, 0),
    (3, 1),
    (2, 2),
    (3, 2),
)


def shifted(x, axis, by):
    peers = lax.axis_size(axis)
    pairs = [(i, i + by) for i in range(peers) if 0 <= i + by < peers]
    return lax.ppermute(x, axis, pairs)


def tile(ref, row):
    return ref[row * SUB : (row + 1) * SUB, :]


def put(ref, row, value):
    ref[row * SUB : (row + 1) * SUB, :] = value


def take(row, lane_index):
    return jnp.take_along_axis(row, lane_index, axis=1, mode="promise_in_bounds")


def spread(ref, row):
    return jnp.broadcast_to(ref[pl.ds(row, 1), :], (SUB, LANES))


def rows_to_tiles(read, tiles_ref, count):
    for block in range(SUB):
        tiles_ref[pl.ds(block, count, stride=SUB), :] = read(block)


def lanes_of(block):
    return slice(block * LANES, (block + 1) * LANES)


def gather_tile(src, row, lane_index, sublane_index):
    found = take(spread(src, row * SUB), lane_index)
    for sub in range(1, SUB):
        got = take(spread(src, row * SUB + sub), lane_index)
        found = jnp.where(sublane_index == sub, got, found)
    return found


def pick(face, for_zero, for_one, for_two):
    return jnp.where(face == 0, for_zero, jnp.where(face == 1, for_one, for_two))


def gather_ends(src, row, lane_index, sublane_index, face):
    n0, n1, n2 = [gather_tile(src, row + i, lane_index, sublane_index) for i in range(3)]
    return pick(face, n1, n2, n0), pick(face, n2, n0, n1)


def gather_by_face(src, row, lane_index, sublane_index, face):
    return pick(
        face, *[gather_tile(src, row + i, lane_index, sublane_index) for i in range(3)]
    )


def fill_remote(received, row, lane_index, remote_index, value):
    for number, (message, block) in enumerate(REMOTE_BLOCKS):
        got = take(spread(received[message].at[block], row), lane_index)
        value = jnp.where(remote_index == number, got, value)
    return value


def partner_index(index_ref, f):
    return [tile(index_ref, part * 3 + f) for part in range(4)]


def sent_index(index_ref, d):
    return [tile(index_ref, 12 + part * 2 + d) for part in range(3)]


INDEX_ROWS = 18


def send_states(src, first_comp, comps, first_row, index_ref, sent_ref):
    for d in range(2):
        lane, sublane, face = sent_index(index_ref, d)

        def body(step, carry):
            ends = gather_ends(src, (first_comp + step) * 3, lane, sublane, face)
            for j in range(2):
                at = pl.multiple_of((first_row + step * 2 + j) * SUB, SUB)
                sent_ref[d, pl.ds(at, SUB), :] = ends[j]
            return carry

        lax.fori_loop(0, comps, body, 0)


def write_messages(sent_ref, messages):
    to_right, to_left, to_up, to_down = messages
    count = to_right.shape[1]
    for ref, direction in ((to_right, 6), (to_left, 1), (to_up, 4), (to_down, 3)):
        for block in range(2):
            ref[block] = sent_ref.at[block][pl.ds(direction, count, stride=SUB), :]
    for ref, direction in ((to_right, 5), (to_left, 2)):
        ref[2] = sent_ref.at[0][pl.ds(direction, count, stride=SUB), :]


def prepare_kernel(
    cot_ref,
    x_ref,
    area_ref,
    edge_ref,
    rough_ref,
    soil_ref,
    friction_ref,
    conduct_ref,
    wet_ref,
    zone_ref,
    send_ref,
    partner_ref,
    table_ref,
    stat_ref,
    index_ref,
    to_right,
    to_left,
    to_up,
    to_down,
    x_tiles,
    sent_ref,
    *fetched,
):
    *fetched, sems = fetched
    sources = [
        partner_ref,
        send_ref,
        cot_ref,
        x_ref.at[:, 0, 0, 0:16],
        area_ref,
        edge_ref,
        rough_ref,
        soil_ref,
        friction_ref,
        conduct_ref,
        wet_ref,
        zone_ref,
    ]
    copies = [
        pltpu.make_async_copy(source, target, sems.at[n])
        for n, (source, target) in enumerate(zip(sources, fetched))
    ]
    for copy in copies:
        copy.start()
    for copy in copies:
        copy.wait()
    (
        partner_ref,
        send_ref,
        cot_ref,
        x_ref,
        area_ref,
        edge_ref,
        rough_ref,
        soil_ref,
        friction_ref,
        conduct_ref,
        wet_ref,
        zone_ref,
    ) = fetched
    rows = cot_ref.shape[0] // SUB
    sections = x_ref.shape[0]
    face_total = 3 * SUB * LANES
    for f in range(3):
        partner = tile(partner_ref, f)
        beyond = partner - face_total
        direction = jnp.right_shift(beyond, 8)
        half = jnp.bitwise_and(jnp.right_shift(beyond, 7), 1)
        lane = jnp.bitwise_and(partner, LANES - 1)
        remote = jnp.where(beyond >= 0, 8, -1)
        remote = jnp.where((direction == 2) | (direction == 7), 9, remote)
        for number, first in ((1, 0), (6, 2), (3, 4), (4, 6)):
            remote = jnp.where(direction == number, first + half, remote)
        lane = jnp.where((direction == 0) | (direction == 7), jnp.bitwise_and(lane + 4, LANES - 1), lane)
        put(index_ref, f, lane)
        put(index_ref, 3 + f, jnp.bitwise_and(jnp.right_shift(partner, 7), SUB - 1))
        put(index_ref, 6 + f, jnp.right_shift(partner, 10))
        put(index_ref, 9 + f, remote)
    sub_iota = lax.broadcasted_iota(jnp.int32, (SUB, LANES), 0)
    lane_iota = lax.broadcasted_iota(jnp.int32, (SUB, LANES), 1)
    for d in range(2):
        slots = send_ref[0, 0, :, lanes_of(d)]
        if d == 0:
            moved = pltpu.roll(slots, 4, 1)
            second = (lane_iota >= 4) & (lane_iota < 8)
            slots = jnp.where(second & (sub_iota == 5), pltpu.roll(moved, 6, 0), slots)
            slots = jnp.where(second & (sub_iota == 2), pltpu.roll(moved, 2, 0), slots)
        put(index_ref, 12 + d, jnp.bitwise_and(slots, LANES - 1))
        put(index_ref, 14 + d, jnp.bitwise_and(jnp.right_shift(slots, 7), SUB - 1))
        put(index_ref, 16 + d, jnp.right_shift(slots, 10))
    zone = zone_ref[...]
    zone_lane = jnp.bitwise_and(zone, LANES - 1)
    zone_block = jnp.right_shift(zone, 7)
    factors = []
    for ref in (friction_ref, conduct_ref):
        found = None
        for block in range(ref.shape[0]):
            got = take(spread(ref, block), zone_lane)
            found = got if block == 0 else jnp.where(zone_block == block, got, found)
        factors.append(found)
    area = area_ref[...]
    wet = wet_ref[...].astype(jnp.float32)
    kappa = factors[1] * soil_ref[...]
    wet_area = wet * area
    half_kappa_area = LATERAL * kappa * area
    put(stat_ref, WET_AREA, wet_area)
    put(stat_ref, KAPPA, kappa)
    put(stat_ref, HALF_KAPPA_AREA, half_kappa_area)
    put(stat_ref, WET, wet)
    put(stat_ref, ZONE_FRICTION, factors[0])
    put(stat_ref, ZONE_ID, zone.astype(jnp.float32))
    stat_ref[EDGE * SUB : (EDGE + 3) * SUB, :] = edge_ref[...]
    for k in range(sections):
        rows_to_tiles(
            lambda b: x_ref[k, :, lanes_of(b)].astype(jnp.float32), x_tiles, 16
        )
        squares = [tile(x_tiles, r) * tile(x_tiles, r) for r in range(12)]
        node_sum = [squares[i] + squares[3 + i] + squares[6 + i] + squares[9 + i] for i in range(3)]
        for f in range(3):
            first, second = FACE_NODES[f]
            put(table_ref, rows + 3 + 3 * k + f, node_sum[first] + node_sum[second])
        momentum = squares[3]
        for r in range(4, 9):
            momentum = momentum + squares[r]
        put(
            stat_ref,
            FRICTION_BASE + k,
            rough_ref[...] * jnp.sqrt(1.0 + momentum * (1.0 / 6.0)),
        )
    for f in range(3):
        put(table_ref, rows + f, tile(stat_ref, EDGE + f))
    put(table_ref, rows + 12, zone.astype(jnp.float32))
    for r in range(rows):
        put(table_ref, r, tile(cot_ref, r) * (wet_area if r < 12 else half_kappa_area))
    comps = rows // 3
    send_states(table_ref, 0, comps, 0, index_ref, sent_ref)
    for d in range(2):
        lane, sublane, face = sent_index(index_ref, d)
        at = comps * 2 * SUB
        for group in range(4):
            sent_ref[d, at : at + SUB, :] = gather_by_face(
                table_ref, rows + 3 * group, lane, sublane, face
            )
            at += SUB
        sent_ref[d, at : at + SUB, :] = gather_tile(table_ref, rows + 12, lane, sublane)
    write_messages(sent_ref, (to_right, to_left, to_up, to_down))


def corner_kernel(left_ref, right_ref, up_in, down_in, *rest):
    up_ref, down_ref = rest[-2:]
    left, right = left_ref[2], right_ref[2]
    first = lax.broadcasted_iota(jnp.int32, left.shape, 1) < 4
    up_ref[2] = jnp.where(first, right, left)
    down_ref[2] = jnp.where(first, left, right)


def outer_states(src, first_comp, comps, first_row, received, index_ref, out_ref):
    for f in range(3):
        lane, sublane, face, remote = partner_index(index_ref, f)

        def body(step, carry):
            ends = gather_ends(src, (first_comp + step) * 3, lane, sublane, face)
            for j in range(2):
                at = pl.multiple_of((f * comps * 2 + step * 2 + j) * SUB, SUB)
                out_ref[pl.ds(at, SUB), :] = fill_remote(
                    received, first_row + step * 2 + j, lane, remote, ends[j]
                )
            return carry

        lax.fori_loop(0, comps, body, 0)


def transposed_section(
    section, lam_ref, y_ref, outer_ref, stat_ref, fact_ref, in_ref, out_ref, volume_ref, emit
):
    rows = lam_ref.shape[0] // SUB
    channels = rows // 3 * 2
    layers = (rows - 12) // 3
    edge = [tile(stat_ref, EDGE + f) for f in range(3)]
    outer_edge = [tile(fact_ref, OUTER_EDGE + f) for f in range(3)]
    half_speed = [tile(fact_ref, HALF_SPEED + 3 * section + f) for f in range(3)]
    kappa = tile(stat_ref, KAPPA)
    wet = tile(stat_ref, WET)
    own = [tile(y_ref, r) for r in range(12)]
    result = []
    for r in range(12):
        total = volume_ref[0, r] * own[0]
        for q in range(1, 12):
            total = total + volume_ref[q, r] * own[q]
        result.append(total)
    for f in range(3):
        ends = FACE_NODES[f]
        inner = [edge[f] * own[(ch // 2) * 3 + ends[ch % 2]] for ch in range(8)]
        outer = [outer_edge[f] * tile(outer_ref, f * channels + ch) for ch in range(8)]
        for b in range(8):
            total = half_speed[f] * (inner[b] - outer[b])
            for a in range(8):
                total = total + in_ref[a, b] * inner[a] - out_ref[a, b] * outer[a]
            at = (b // 2) * 3 + ends[b % 2]
            result[at] = result[at] + total
    friction = tile(stat_ref, ZONE_FRICTION) * tile(stat_ref, FRICTION_BASE + section) * wet
    for r in range(3, 9):
        result[r] = result[r] - friction * tile(lam_ref, r)
    exchange = []
    for i in range(3):
        top = tile(lam_ref, 12 + i) - SALT_RETURN * wet * tile(lam_ref, 9 + i)
        exchange.append(kappa * top)
        result[9 + i] = result[9 + i] + exchange[i]
    for r in range(12):
        emit(r, result[r])
    for i in range(3):
        (f0, j0), (f1, j1) = NODE_FACES[i]
        both = edge[f0] + edge[f1]
        from_above = exchange[i]
        for layer in range(layers):
            r = 12 + layer * 3 + i
            value = (
                outer_edge[f0] * tile(outer_ref, f0 * channels + 8 + layer * 2 + j0)
                + outer_edge[f1] * tile(outer_ref, f1 * channels + 8 + layer * 2 + j1)
                - both * tile(y_ref, r)
                - from_above
            )
            if layer + 1 < layers:
                from_above = kappa * (tile(lam_ref, r + 3) - tile(lam_ref, r))
                value = value + from_above
            emit(r, value)


def own_gradients(section, weight, lam_ref, y_ref, x_tiles, stat_ref):
    rows = lam_ref.shape[0] // SUB
    layers = (rows - 12) // 3
    wet = tile(stat_ref, WET)
    kappa = tile(stat_ref, KAPPA)
    momentum = tile(lam_ref, 3) * tile(x_tiles, 3)
    for r in range(4, 9):
        momentum = momentum + tile(lam_ref, r) * tile(x_tiles, r)
    friction = -(weight * wet * tile(stat_ref, FRICTION_BASE + section)) * momentum
    vertical = None
    lateral = None
    for i in range(3):
        (f0, _), (f1, _) = NODE_FACES[i]
        top = tile(lam_ref, 12 + i) - SALT_RETURN * wet * tile(lam_ref, 9 + i)
        total = top * (tile(x_tiles, 9 + i) - tile(x_tiles, 12 + i))
        dots = None
        for layer in range(layers):
            r = 12 + layer * 3 + i
            term = tile(y_ref, r) * tile(x_tiles, r)
            dots = term if dots is None else dots + term
            if layer + 1 < layers:
                total = total + (tile(lam_ref, r + 3) - tile(lam_ref, r)) * (
                    tile(x_tiles, r) - tile(x_tiles, r + 3)
                )
        side = (tile(stat_ref, EDGE + f0) + tile(stat_ref, EDGE + f1)) * dots
        vertical = total if vertical is None else vertical + total
        lateral = side if lateral is None else lateral + side
    return friction, weight * (kappa * vertical - lateral)


def outer_gradients(weight, outer_ref, x_tiles, fact_ref):
    channels = outer_ref.shape[0] // SUB // 3
    values = []
    for f in range(3):
        total = None
        for ch in range(8, channels):
            row = 12 + (ch - 8) // 2 * 3 + FACE_NODES[f][ch % 2]
            term = tile(outer_ref, f * channels + ch) * tile(x_tiles, row)
            total = term if total is None else total + term
        values.append(weight * tile(fact_ref, OUTER_EDGE + f) * total)
    return values


def x_to_tiles(x_ref, section, x_tiles):
    rows = x_ref.shape[3]
    rows_to_tiles(
        lambda b: x_ref[section, 0, 0, :, lanes_of(b)].astype(jnp.float32), x_tiles, rows
    )


def second_kernel(
    cot_ref,
    table_ref,
    stat_ref,
    index_ref,
    x_ref,
    in_ref,
    out_ref,
    volume_ref,
    from_left,
    from_right,
    from_down,
    from_up,
    lam_ref,
    y_ref,
    fact_ref,
    term_ref,
    to_right,
    to_left,
    to_up,
    to_down,
    outer_ref,
    x_tiles,
    sent_ref,
):
    received = (from_left, from_right, from_down, from_up)
    rows = cot_ref.shape[0] // SUB
    comps = rows // 3
    outer_states(table_ref, 0, comps, 0, received, index_ref, outer_ref)
    for f in range(3):
        lane, sublane, face, remote = partner_index(index_ref, f)
        for group in range(4):
            value = gather_by_face(table_ref, rows + 3 * group, lane, sublane, face)
            value = fill_remote(received, comps * 2 + group, lane, remote, value)
            if group == 0:
                put(fact_ref, OUTER_EDGE + f, value)
            else:
                both = tile(table_ref, rows + 3 * group + f) + value
                put(
                    fact_ref,
                    HALF_SPEED + 3 * (group - 1) + f,
                    0.5 * jnp.sqrt(1.0 + (0.25 / 8.0) * both),
                )
        value = gather_tile(table_ref, rows + 12, lane, sublane)
        put(fact_ref, OUTER_ZONE + f, fill_remote(received, comps * 2 + 4, lane, remote, value))
    wet_area = tile(stat_ref, WET_AREA)
    half_kappa_area = tile(stat_ref, HALF_KAPPA_AREA)

    def emit(r, value):
        lam = (2.0 / 3.0) * (tile(cot_ref, r) + TIME_STEP * value)
        put(lam_ref, r, lam)
        put(y_ref, r, lam * (wet_area if r < 12 else half_kappa_area))

    transposed_section(
        2, cot_ref, table_ref, outer_ref, stat_ref, fact_ref, in_ref, out_ref, volume_ref, emit
    )
    x_to_tiles(x_ref, 0, x_tiles)
    send_states(y_ref, 0, comps, 0, index_ref, sent_ref)
    send_states(x_tiles, 4, comps - 4, comps * 2, index_ref, sent_ref)
    write_messages(sent_ref, (to_right, to_left, to_up, to_down))
    x_to_tiles(x_ref, 2, x_tiles)
    weight = TIME_STEP * 2.0 / 3.0
    friction, conduct = own_gradients(2, weight, cot_ref, table_ref, x_tiles, stat_ref)
    put(term_ref, 0, friction)
    put(term_ref, 1, conduct)
    for f, value in enumerate(outer_gradients(weight, outer_ref, x_tiles, fact_ref)):
        put(term_ref, 2 + f, value)


def first_kernel(
    cot_ref,
    lam_ref,
    y_ref,
    stat_ref,
    index_ref,
    fact_ref,
    term_ref,
    x_ref,
    in_ref,
    out_ref,
    volume_ref,
    from_left,
    from_right,
    from_down,
    from_up,
    base_ref,
    next_ref,
    next_y_ref,
    new_term_ref,
    to_right,
    to_left,
    to_up,
    to_down,
    outer_ref,
    x_outer_ref,
    x_tiles,
    sent_ref,
):
    received = (from_left, from_right, from_down, from_up)
    rows = lam_ref.shape[0] // SUB
    comps = rows // 3
    outer_states(y_ref, 0, comps, 0, received, index_ref, outer_ref)
    wet_area = tile(stat_ref, WET_AREA)
    half_kappa_area = tile(stat_ref, HALF_KAPPA_AREA)

    def emit(r, value):
        old = tile(lam_ref, r)
        lam = 0.25 * (old + TIME_STEP * value)
        put(next_ref, r, lam)
        put(next_y_ref, r, lam * (wet_area if r < 12 else half_kappa_area))
        put(base_ref, r, (1.0 / 3.0) * tile(cot_ref, r) + 0.75 * old + lam)

    transposed_section(
        1, lam_ref, y_ref, outer_ref, stat_ref, fact_ref, in_ref, out_ref, volume_ref, emit
    )
    send_states(next_y_ref, 0, comps, 0, index_ref, sent_ref)
    write_messages(sent_ref, (to_right, to_left, to_up, to_down))
    x_to_tiles(x_ref, 1, x_tiles)
    weight = TIME_STEP * 0.25
    friction, conduct = own_gradients(1, weight, lam_ref, y_ref, x_tiles, stat_ref)
    for f, value in enumerate(outer_gradients(weight, outer_ref, x_tiles, fact_ref)):
        put(new_term_ref, 2 + f, tile(term_ref, 2 + f) + value)
    x_to_tiles(x_ref, 0, x_tiles)
    outer_states(x_tiles, 4, comps - 4, comps * 2, received, index_ref, x_outer_ref)
    friction_0, conduct_0 = own_gradients(0, TIME_STEP, next_ref, next_y_ref, x_tiles, stat_ref)
    friction = friction + friction_0
    conduct = conduct + conduct_0
    channels = (comps - 4) * 2
    for f in range(3):
        total = None
        for ch in range(channels):
            row = 12 + ch // 2 * 3 + FACE_NODES[f][ch % 2]
            term = tile(x_outer_ref, f * channels + ch) * tile(next_y_ref, row)
            total = term if total is None else total + term
        conduct = conduct + TIME_STEP * tile(stat_ref, EDGE + f) * total
    put(new_term_ref, 0, tile(term_ref, 0) + friction)
    put(new_term_ref, 1, tile(term_ref, 1) + conduct)


def zone_kernel(term_ref, stat_ref, fact_ref, conduct_ref, out_ref):
    zones = out_ref.shape[2]
    zone_iota = lax.broadcasted_iota(jnp.int32, (zones, LANES), 0).astype(jnp.float32)
    sub_iota = lax.broadcasted_iota(jnp.int32, (SUB, zones), 0)

    def thirds(value):
        high = value.astype(jnp.bfloat16).astype(jnp.float32)
        rest = value - high
        middle = rest.astype(jnp.bfloat16).astype(jnp.float32)
        return [high, middle, rest - middle]

    def by_zone(values, zone_of, zone_row):
        pieces = sum([thirds(value) for value in values], [])
        left = jnp.concatenate(pieces, axis=0).astype(jnp.bfloat16)
        totals = [jnp.zeros((SUB, zones), jnp.float32) for _ in values]
        for sub in range(SUB):
            line = zone_of[pl.ds(zone_row * SUB + sub, 1), :]
            hot = (jnp.broadcast_to(line, (zones, LANES)) == zone_iota).astype(jnp.float32)
            dots = lax.dot_general(
                left,
                hot.astype(jnp.bfloat16),
                (((1,), (1,)), ((), ())),
                preferred_element_type=jnp.float32,
            )
            for n in range(len(values)):
                at = n * 3 * SUB
                three = dots[at : at + SUB] + dots[at + SUB : at + 2 * SUB]
                three = three + dots[at + 2 * SUB : at + 3 * SUB]
                totals[n] = totals[n] + jnp.where(sub_iota == sub, three, 0.0)
        return totals

    friction, conduct = by_zone([tile(term_ref, 0), tile(term_ref, 1)], stat_ref, ZONE_ID)
    for f in range(3):
        conduct = conduct + by_zone([tile(term_ref, 2 + f)], fact_ref, OUTER_ZONE + f)[0]
    friction = GRAD_WEIGHT * jnp.sum(friction, axis=0, keepdims=True)
    conduct = GRAD_WEIGHT * jnp.sum(conduct, axis=0, keepdims=True) / conduct_ref[...]
    for device in range(out_ref.shape[0]):
        out_ref[device, 0:1, :] = friction
        out_ref[device, 1:2, :] = conduct


def last_kernel(
    base_ref,
    lam_ref,
    y_ref,
    stat_ref,
    index_ref,
    fact_ref,
    in_ref,
    out_ref,
    volume_ref,
    from_left,
    from_right,
    from_down,
    from_up,
    adjoint_ref,
    last_ref,
    outer_ref,
):
    received = (from_left, from_right, from_down, from_up)
    rows = lam_ref.shape[0] // SUB
    outer_states(y_ref, 0, rows // 3, 0, received, index_ref, outer_ref)

    def emit(r, value):
        put(adjoint_ref, r, tile(base_ref, r) + TIME_STEP * value)

    transposed_section(
        0, lam_ref, y_ref, outer_ref, stat_ref, fact_ref, in_ref, out_ref, volume_ref, emit
    )
    last_ref[...] = tile(adjoint_ref, rows - 1)


def total_kernel(zone_ref, adjoint_ref, grads_ref):
    grads_ref[...] = jnp.sum(zone_ref[...], axis=0)


def exchange(messages, *ahead):
    to_right, to_left, to_up, to_down = messages
    from_left = shifted(to_right, "gx", 1)
    from_right = shifted(to_left, "gx", -1)
    to_up, to_down = call(
        corner_kernel,
        "corners",
        [jax.ShapeDtypeStruct(to_up.shape, to_up.dtype)] * 2,
        [],
        [from_left, from_right, to_up, to_down, *ahead],
        aliases={2: 0, 3: 1},
    )
    from_down = shifted(to_up, "gy", 1)
    from_up = shifted(to_down, "gy", -1)
    return from_left, from_right, from_down, from_up


def call(kernel, name, outs, scratch, operands, scalars=(), far=False, aliases={}):
    in_memory = pl.BlockSpec(memory_space=pltpu.VMEM)
    in_scalar = pl.BlockSpec(memory_space=pltpu.SMEM)
    in_place = pl.BlockSpec(memory_space=pl.ANY)
    return pl.pallas_call(
        kernel,
        in_specs=[
            in_place if far else in_scalar if n in scalars else in_memory
            for n in range(len(operands))
        ],
        out_specs=[in_memory] * len(outs),
        out_shape=outs,
        scratch_shapes=scratch,
        input_output_aliases=aliases,
        compiler_params=pltpu.CompilerParams(
            vmem_limit_bytes=(FAR_VMEM if far else NEAR_VMEM) * 1024 * 1024
        ),
        name=name,
    )(*operands)


def local(
    cotangent,
    section_states,
    inverse_area,
    edge_length,
    roughness,
    soil_conductance,
    zone_friction,
    zone_conductivity,
    wet_mask,
    element_zone,
    send_face,
    send_count,
    face_partner,
    volume_matrix,
    flux_in,
    flux_out,
):
    rows = cotangent.shape[2]
    channels = rows // 3 * 2
    zones = zone_friction.shape[0]
    slots = send_face.shape[3]
    devices = lax.axis_size("gx") * lax.axis_size("gy")
    f32 = jnp.float32

    def tiles(count, dtype=f32):
        return jax.ShapeDtypeStruct((count * SUB, LANES), dtype)

    def tile_scratch(count, dtype=f32):
        return pltpu.VMEM((count * SUB, LANES), dtype)

    def messages(count):
        return [jax.ShapeDtypeStruct((slots // LANES + 1, count, LANES), f32)] * 4

    def sent_scratch(count):
        return pltpu.VMEM((slots // LANES, count * SUB, LANES), f32)

    square = lambda one: one.reshape(SUB, LANES)
    cot = cotangent.reshape(rows * SUB, LANES)
    table, stat, index, *to_send = call(
        prepare_kernel,
        "prepare",
        [tiles(rows + 13), tiles(STAT_ROWS), tiles(INDEX_ROWS, jnp.int32)]
        + messages(channels + 5),
        [tile_scratch(16), sent_scratch(channels + 5)]
        + [
            tile_scratch(3, jnp.int32),
            pltpu.VMEM(send_face.shape, jnp.int32),
            tile_scratch(rows),
            pltpu.VMEM((section_states.shape[0], 16, SUB * LANES), section_states.dtype),
            tile_scratch(1),
            tile_scratch(3),
            tile_scratch(1),
            tile_scratch(1),
            pltpu.VMEM((zones // LANES, LANES), f32),
            pltpu.VMEM((zones // LANES, LANES), f32),
            tile_scratch(1, jnp.int32),
            tile_scratch(1, jnp.int32),
            pltpu.SemaphoreType.DMA((12,)),
        ],
        [
            cot,
            section_states,
            square(inverse_area),
            edge_length.reshape(3 * SUB, LANES),
            square(roughness),
            square(soil_conductance),
            zone_friction.reshape(-1, LANES),
            zone_conductivity.reshape(-1, LANES),
            square(wet_mask),
            square(element_zone),
            send_face,
            face_partner.reshape(3 * SUB, LANES),
        ],
        far=True,
    )
    received = exchange(to_send)
    lam, y, fact, term, *to_send = call(
        second_kernel,
        "section_two",
        [tiles(rows), tiles(rows), tiles(FACT_ROWS), tiles(5)]
        + messages(channels + channels - 8),
        [tile_scratch(3 * channels), tile_scratch(rows), sent_scratch(2 * channels - 8)],
        [cot, table, stat, index, section_states, flux_in, flux_out, volume_matrix, *received],
        (5, 6, 7),
    )
    received = exchange(to_send)
    base, lam, y, term, *to_send = call(
        first_kernel,
        "section_one",
        [tiles(rows), tiles(rows), tiles(rows), tiles(5)] + messages(channels),
        [
            tile_scratch(3 * channels),
            tile_scratch(3 * (channels - 8)),
            tile_scratch(rows),
            sent_scratch(channels),
        ],
        [
            cot,
            lam,
            y,
            stat,
            index,
            fact,
            term,
            section_states,
            flux_in,
            flux_out,
            volume_matrix,
            *received,
        ],
        (8, 9, 10),
    )
    (zone_terms,) = call(
        zone_kernel,
        "zone_sums",
        [jax.ShapeDtypeStruct((devices, 2, zones), f32)],
        [],
        [term, stat, fact, zone_conductivity.reshape(1, zones)],
    )
    all_terms = lax.all_to_all(zone_terms, ("gx", "gy"), 0, 0)
    received = exchange(to_send, zone_terms)
    adjoint, last = call(
        last_kernel,
        "section_zero",
        [tiles(rows), tiles(1)],
        [tile_scratch(3 * channels)],
        [
            base,
            lam,
            y,
            stat,
            index,
            fact,
            flux_in,
            flux_out,
            volume_matrix,
            *received,
        ],
        (6, 7, 8),
    )
    (zone_grads,) = call(
        total_kernel,
        "zone_total",
        [jax.ShapeDtypeStruct((2, zones), f32)],
        [],
        [all_terms, last],
    )
    return adjoint.reshape(cotangent.shape), zone_grads


def solution(mesh):
    placed = (
        P("gx", "gy", None, None),
        P(None, "gx", "gy", None, None),
        P("gx", "gy", None),
        P("gx", "gy", None, None),
        P("gx", "gy", None),
        P("gx", "gy", None),
        P(),
        P(),
        P("gx", "gy", None),
        P("gx", "gy", None),
        P("gx", "gy", None, None),
        P("gx", "gy", None),
        P("gx", "gy", None, None),
        P(),
        P(),
        P(),
    )
    return jax.shard_map(
        local,
        mesh=mesh,
        in_specs=placed,
        out_specs=(P("gx", "gy", None, None), P()),
        check_vma=False,
    )
```

```python
import functools
import jax
import jax.numpy as jnp
from jax import lax
from jax.experimental import pallas as pl
from jax.experimental.pallas import tpu as pltpu
from jax.sharding import PartitionSpec as P

TIME_STEP = 0.2
SALT_RETURN = 0.5
LATERAL = 0.5
GRAD_WEIGHT = 1.0 / 64.0
FACE_NODES = ((1, 2), (2, 0), (0, 1))
NODE_FACES = (((1, 1), (2, 0)), ((0, 0), (2, 1)), ((0, 1), (1, 0)))
SUB = 8
LANES = 128


WET_AREA, KAPPA, HALF_KAPPA_AREA, WET, EDGE, FRICTION_BASE, ZONE_FRICTION, ZONE_ID = (
    0,
    1,
    2,
    3,
    4,
    7,
    10,
    11,
)
STAT_ROWS = 12
NEAR_VMEM, FAR_VMEM = 32, 60
OUTER_EDGE, OUTER_ZONE, HALF_SPEED = 0, 3, 6
FACT_ROWS = 15
REMOTE_BLOCKS = (
    (0, 0),
    (0, 1),
    (1, 0),
    (1, 1),
    (2, 0),
    (2, 1),
    (3, 0),
    (3, 1),
    (2, 2),
    (3, 2),
)


def shifted(x, axis, by):
    peers = lax.axis_size(axis)
    pairs = [(i, i + by) for i in range(peers) if 0 <= i + by < peers]
    return lax.ppermute(x, axis, pairs)


def tile(ref, row):
    return ref[row * SUB : (row + 1) * SUB, :]


def put(ref, row, value):
    ref[row * SUB : (row + 1) * SUB, :] = value


def take(row, lane_index):
    return jnp.take_along_axis(row, lane_index, axis=1, mode="promise_in_bounds")


def spread(ref, row):
    return jnp.broadcast_to(ref[pl.ds(row, 1), :], (SUB, LANES))


def rows_to_tiles(read, tiles_ref, count):
    for block in range(SUB):
        tiles_ref[pl.ds(block, count, stride=SUB), :] = read(block)


def lanes_of(block):
    return slice(block * LANES, (block + 1) * LANES)


def gather_tile(src, row, lane_index, sublane_index):
    found = take(spread(src, row * SUB), lane_index)
    for sub in range(1, SUB):
        got = take(spread(src, row * SUB + sub), lane_index)
        found = jnp.where(sublane_index == sub, got, found)
    return found


def pick(face, for_zero, for_one, for_two):
    return jnp.where(face == 0, for_zero, jnp.where(face == 1, for_one, for_two))


def gather_ends(src, row, lane_index, sublane_index, face):
    n0, n1, n2 = [gather_tile(src, row + i, lane_index, sublane_index) for i in range(3)]
    return pick(face, n1, n2, n0), pick(face, n2, n0, n1)


def gather_by_face(src, row, lane_index, sublane_index, face):
    return pick(
        face, *[gather_tile(src, row + i, lane_index, sublane_index) for i in range(3)]
    )


def fill_remote(received, row, lane_index, remote_index, value):
    for number, (message, block) in enumerate(REMOTE_BLOCKS):
        got = take(spread(received[message].at[block], row), lane_index)
        value = jnp.where(remote_index == number, got, value)
    return value


def partner_index(index_ref, f):
    return [tile(index_ref, part * 3 + f) for part in range(4)]


def sent_index(index_ref, d):
    return [tile(index_ref, 12 + part * 2 + d) for part in range(3)]


INDEX_ROWS = 18


def turns(comps):
    width = 7 if comps % 7 == 0 else 5
    return width, comps // width


def tile_at(ref, row):
    return ref[pl.ds(pl.multiple_of(row * SUB, SUB), SUB), :]


def put_at(ref, row, value):
    ref[pl.ds(pl.multiple_of(row * SUB, SUB), SUB), :] = value


def send_states(src, first_comp, comps, first_row, index_ref, sent_ref):
    width, parts = turns(comps)

    def body(step, carry):
        d, part = step // parts, step % parts
        lane, sublane, face = [tile_at(index_ref, 12 + n * 2 + d) for n in range(3)]
        for w in range(width):
            comp = part * width + w
            ends = gather_ends(src, (first_comp + comp) * 3, lane, sublane, face)
            for j in range(2):
                put_at(sent_ref.at[d], first_row + comp * 2 + j, ends[j])
        return carry

    lax.fori_loop(0, 2 * parts, body, 0)


def write_messages(sent_ref, messages):
    to_right, to_left, to_up, to_down = messages
    count = to_right.shape[1]
    for ref, direction in ((to_right, 6), (to_left, 1), (to_up, 4), (to_down, 3)):
        for block in range(2):
            ref[block] = sent_ref.at[block][pl.ds(direction, count, stride=SUB), :]
    for ref, direction in ((to_right, 5), (to_left, 2)):
        ref[2] = sent_ref.at[0][pl.ds(direction, count, stride=SUB), :]


def prepare_kernel(
    cot_ref,
    x_ref,
    area_ref,
    edge_ref,
    rough_ref,
    soil_ref,
    friction_ref,
    conduct_ref,
    wet_ref,
    zone_ref,
    send_ref,
    partner_ref,
    table_ref,
    stat_ref,
    index_ref,
    to_right,
    to_left,
    to_up,
    to_down,
    x_tiles,
    sent_ref,
    *fetched,
):
    *fetched, sems = fetched
    sources = [
        partner_ref,
        send_ref,
        cot_ref,
        x_ref.at[:, 0, 0, 0:16],
        area_ref,
        edge_ref,
        rough_ref,
        soil_ref,
        friction_ref,
        conduct_ref,
        wet_ref,
        zone_ref,
    ]
    copies = [
        pltpu.make_async_copy(source, target, sems.at[n])
        for n, (source, target) in enumerate(zip(sources, fetched))
    ]
    for copy in copies:
        copy.start()
    for copy in copies:
        copy.wait()
    (
        partner_ref,
        send_ref,
        cot_ref,
        x_ref,
        area_ref,
        edge_ref,
        rough_ref,
        soil_ref,
        friction_ref,
        conduct_ref,
        wet_ref,
        zone_ref,
    ) = fetched
    rows = cot_ref.shape[0] // SUB
    sections = x_ref.shape[0]
    face_total = 3 * SUB * LANES
    for f in range(3):
        partner = tile(partner_ref, f)
        beyond = partner - face_total
        direction = jnp.right_shift(beyond, 8)
        half = jnp.bitwise_and(jnp.right_shift(beyond, 7), 1)
        lane = jnp.bitwise_and(partner, LANES - 1)
        remote = jnp.where(beyond >= 0, 8, -1)
        remote = jnp.where((direction == 2) | (direction == 7), 9, remote)
        for number, first in ((1, 0), (6, 2), (3, 4), (4, 6)):
            remote = jnp.where(direction == number, first + half, remote)
        lane = jnp.where((direction == 0) | (direction == 7), jnp.bitwise_and(lane + 4, LANES - 1), lane)
        put(index_ref, f, lane)
        put(index_ref, 3 + f, jnp.bitwise_and(jnp.right_shift(partner, 7), SUB - 1))
        put(index_ref, 6 + f, jnp.right_shift(partner, 10))
        put(index_ref, 9 + f, remote)
    sub_iota = lax.broadcasted_iota(jnp.int32, (SUB, LANES), 0)
    lane_iota = lax.broadcasted_iota(jnp.int32, (SUB, LANES), 1)
    for d in range(2):
        slots = send_ref[0, 0, :, lanes_of(d)]
        if d == 0:
            moved = pltpu.roll(slots, 4, 1)
            second = (lane_iota >= 4) & (lane_iota < 8)
            slots = jnp.where(second & (sub_iota == 5), pltpu.roll(moved, 6, 0), slots)
            slots = jnp.where(second & (sub_iota == 2), pltpu.roll(moved, 2, 0), slots)
        put(index_ref, 12 + d, jnp.bitwise_and(slots, LANES - 1))
        put(index_ref, 14 + d, jnp.bitwise_and(jnp.right_shift(slots, 7), SUB - 1))
        put(index_ref, 16 + d, jnp.right_shift(slots, 10))
    zone = zone_ref[...]
    zone_lane = jnp.bitwise_and(zone, LANES - 1)
    zone_block = jnp.right_shift(zone, 7)
    factors = []
    for ref in (friction_ref, conduct_ref):
        found = None
        for block in range(ref.shape[0]):
            got = take(spread(ref, block), zone_lane)
            found = got if block == 0 else jnp.where(zone_block == block, got, found)
        factors.append(found)
    area = area_ref[...]
    wet = wet_ref[...].astype(jnp.float32)
    kappa = factors[1] * soil_ref[...]
    wet_area = wet * area
    half_kappa_area = LATERAL * kappa * area
    put(stat_ref, WET_AREA, wet_area)
    put(stat_ref, KAPPA, kappa)
    put(stat_ref, HALF_KAPPA_AREA, half_kappa_area)
    put(stat_ref, WET, wet)
    put(stat_ref, ZONE_FRICTION, factors[0])
    put(stat_ref, ZONE_ID, zone.astype(jnp.float32))
    stat_ref[EDGE * SUB : (EDGE + 3) * SUB, :] = edge_ref[...]
    for k in range(sections):
        rows_to_tiles(
            lambda b: x_ref[k, :, lanes_of(b)].astype(jnp.float32), x_tiles, 16
        )
        squares = [tile(x_tiles, r) * tile(x_tiles, r) for r in range(12)]
        node_sum = [squares[i] + squares[3 + i] + squares[6 + i] + squares[9 + i] for i in range(3)]
        for f in range(3):
            first, second = FACE_NODES[f]
            put(table_ref, rows + 3 + 3 * k + f, node_sum[first] + node_sum[second])
        momentum = squares[3]
        for r in range(4, 9):
            momentum = momentum + squares[r]
        put(
            stat_ref,
            FRICTION_BASE + k,
            rough_ref[...] * jnp.sqrt(1.0 + momentum * (1.0 / 6.0)),
        )
    for f in range(3):
        put(table_ref, rows + f, tile(stat_ref, EDGE + f))
    put(table_ref, rows + 12, zone.astype(jnp.float32))
    for r in range(rows):
        put(table_ref, r, tile(cot_ref, r) * (wet_area if r < 12 else half_kappa_area))
    comps = rows // 3
    send_states(table_ref, 0, comps, 0, index_ref, sent_ref)
    for d in range(2):
        lane, sublane, face = sent_index(index_ref, d)
        at = comps * 2 * SUB
        for group in range(4):
            sent_ref[d, at : at + SUB, :] = gather_by_face(
                table_ref, rows + 3 * group, lane, sublane, face
            )
            at += SUB
        sent_ref[d, at : at + SUB, :] = gather_tile(table_ref, rows + 12, lane, sublane)
    write_messages(sent_ref, (to_right, to_left, to_up, to_down))


def corner_kernel(left_ref, right_ref, up_in, down_in, *rest):
    up_ref, down_ref = rest[-2:]
    left, right = left_ref[2], right_ref[2]
    first = lax.broadcasted_iota(jnp.int32, left.shape, 1) < 4
    up_ref[2] = jnp.where(first, right, left)
    down_ref[2] = jnp.where(first, left, right)


def outer_states(src, first_comp, comps, first_row, received, index_ref, out_ref):
    width, parts = turns(comps)

    def body(step, carry):
        f, part = step // parts, step % parts
        lane, sublane, face, remote = [tile_at(index_ref, n * 3 + f) for n in range(4)]
        for w in range(width):
            comp = part * width + w
            ends = gather_ends(src, (first_comp + comp) * 3, lane, sublane, face)
            for j in range(2):
                value = fill_remote(received, first_row + comp * 2 + j, lane, remote, ends[j])
                put_at(out_ref, f * comps * 2 + comp * 2 + j, value)
        return carry

    lax.fori_loop(0, 3 * parts, body, 0)


def transposed_section(
    section, lam_ref, y_ref, outer_ref, stat_ref, fact_ref, in_ref, out_ref, volume_ref, emit
):
    rows = lam_ref.shape[0] // SUB
    channels = rows // 3 * 2
    layers = (rows - 12) // 3
    edge = [tile(stat_ref, EDGE + f) for f in range(3)]
    outer_edge = [tile(fact_ref, OUTER_EDGE + f) for f in range(3)]
    half_speed = [tile(fact_ref, HALF_SPEED + 3 * section + f) for f in range(3)]
    kappa = tile(stat_ref, KAPPA)
    wet = tile(stat_ref, WET)
    own = [tile(y_ref, r) for r in range(12)]
    result = []
    for r in range(12):
        total = volume_ref[0, r] * own[0]
        for q in range(1, 12):
            total = total + volume_ref[q, r] * own[q]
        result.append(total)
    for f in range(3):
        ends = FACE_NODES[f]
        inner = [edge[f] * own[(ch // 2) * 3 + ends[ch % 2]] for ch in range(8)]
        outer = [outer_edge[f] * tile(outer_ref, f * channels + ch) for ch in range(8)]
        for b in range(8):
            total = half_speed[f] * (inner[b] - outer[b])
            for a in range(8):
                total = total + in_ref[a, b] * inner[a] - out_ref[a, b] * outer[a]
            at = (b // 2) * 3 + ends[b % 2]
            result[at] = result[at] + total
    friction = tile(stat_ref, ZONE_FRICTION) * tile(stat_ref, FRICTION_BASE + section) * wet
    for r in range(3, 9):
        result[r] = result[r] - friction * tile(lam_ref, r)
    exchange = []
    for i in range(3):
        top = tile(lam_ref, 12 + i) - SALT_RETURN * wet * tile(lam_ref, 9 + i)
        exchange.append(kappa * top)
        result[9 + i] = result[9 + i] + exchange[i]
    for r in range(12):
        emit(r, result[r])
    for i in range(3):
        (f0, j0), (f1, j1) = NODE_FACES[i]
        both = edge[f0] + edge[f1]
        from_above = exchange[i]
        for layer in range(layers):
            r = 12 + layer * 3 + i
            value = (
                outer_edge[f0] * tile(outer_ref, f0 * channels + 8 + layer * 2 + j0)
                + outer_edge[f1] * tile(outer_ref, f1 * channels + 8 + layer * 2 + j1)
                - both * tile(y_ref, r)
                - from_above
            )
            if layer + 1 < layers:
                from_above = kappa * (tile(lam_ref, r + 3) - tile(lam_ref, r))
                value = value + from_above
            emit(r, value)


def own_gradients(section, weight, lam_ref, y_ref, x_tiles, stat_ref):
    rows = lam_ref.shape[0] // SUB
    layers = (rows - 12) // 3
    wet = tile(stat_ref, WET)
    kappa = tile(stat_ref, KAPPA)
    momentum = tile(lam_ref, 3) * tile(x_tiles, 3)
    for r in range(4, 9):
        momentum = momentum + tile(lam_ref, r) * tile(x_tiles, r)
    friction = -(weight * wet * tile(stat_ref, FRICTION_BASE + section)) * momentum
    vertical = None
    lateral = None
    for i in range(3):
        (f0, _), (f1, _) = NODE_FACES[i]
        top = tile(lam_ref, 12 + i) - SALT_RETURN * wet * tile(lam_ref, 9 + i)
        total = top * (tile(x_tiles, 9 + i) - tile(x_tiles, 12 + i))
        dots = None
        for layer in range(layers):
            r = 12 + layer * 3 + i
            term = tile(y_ref, r) * tile(x_tiles, r)
            dots = term if dots is None else dots + term
            if layer + 1 < layers:
                total = total + (tile(lam_ref, r + 3) - tile(lam_ref, r)) * (
                    tile(x_tiles, r) - tile(x_tiles, r + 3)
                )
        side = (tile(stat_ref, EDGE + f0) + tile(stat_ref, EDGE + f1)) * dots
        vertical = total if vertical is None else vertical + total
        lateral = side if lateral is None else lateral + side
    return friction, weight * (kappa * vertical - lateral)


def outer_gradients(weight, outer_ref, x_tiles, fact_ref):
    channels = outer_ref.shape[0] // SUB // 3
    values = []
    for f in range(3):
        total = None
        for ch in range(8, channels):
            row = 12 + (ch - 8) // 2 * 3 + FACE_NODES[f][ch % 2]
            term = tile(outer_ref, f * channels + ch) * tile(x_tiles, row)
            total = term if total is None else total + term
        values.append(weight * tile(fact_ref, OUTER_EDGE + f) * total)
    return values


def x_to_tiles(x_ref, section, x_tiles):
    rows = x_ref.shape[3]
    rows_to_tiles(
        lambda b: x_ref[section, 0, 0, :, lanes_of(b)].astype(jnp.float32), x_tiles, rows
    )


def second_kernel(
    cot_ref,
    table_ref,
    stat_ref,
    index_ref,
    x_ref,
    in_ref,
    out_ref,
    volume_ref,
    from_left,
    from_right,
    from_down,
    from_up,
    lam_ref,
    y_ref,
    fact_ref,
    term_ref,
    to_right,
    to_left,
    to_up,
    to_down,
    outer_ref,
    x_tiles,
    sent_ref,
):
    received = (from_left, from_right, from_down, from_up)
    rows = cot_ref.shape[0] // SUB
    comps = rows // 3
    outer_states(table_ref, 0, comps, 0, received, index_ref, outer_ref)
    for f in range(3):
        lane, sublane, face, remote = partner_index(index_ref, f)
        for group in range(4):
            value = gather_by_face(table_ref, rows + 3 * group, lane, sublane, face)
            value = fill_remote(received, comps * 2 + group, lane, remote, value)
            if group == 0:
                put(fact_ref, OUTER_EDGE + f, value)
            else:
                both = tile(table_ref, rows + 3 * group + f) + value
                put(
                    fact_ref,
                    HALF_SPEED + 3 * (group - 1) + f,
                    0.5 * jnp.sqrt(1.0 + (0.25 / 8.0) * both),
                )
        value = gather_tile(table_ref, rows + 12, lane, sublane)
        put(fact_ref, OUTER_ZONE + f, fill_remote(received, comps * 2 + 4, lane, remote, value))
    wet_area = tile(stat_ref, WET_AREA)
    half_kappa_area = tile(stat_ref, HALF_KAPPA_AREA)

    def emit(r, value):
        lam = (2.0 / 3.0) * (tile(cot_ref, r) + TIME_STEP * value)
        put(lam_ref, r, lam)
        put(y_ref, r, lam * (wet_area if r < 12 else half_kappa_area))

    transposed_section(
        2, cot_ref, table_ref, outer_ref, stat_ref, fact_ref, in_ref, out_ref, volume_ref, emit
    )
    x_to_tiles(x_ref, 0, x_tiles)
    send_states(y_ref, 0, comps, 0, index_ref, sent_ref)
    send_states(x_tiles, 4, comps - 4, comps * 2, index_ref, sent_ref)
    write_messages(sent_ref, (to_right, to_left, to_up, to_down))
    x_to_tiles(x_ref, 2, x_tiles)
    weight = TIME_STEP * 2.0 / 3.0
    friction, conduct = own_gradients(2, weight, cot_ref, table_ref, x_tiles, stat_ref)
    put(term_ref, 0, friction)
    put(term_ref, 1, conduct)
    for f, value in enumerate(outer_gradients(weight, outer_ref, x_tiles, fact_ref)):
        put(term_ref, 2 + f, value)


def first_kernel(
    cot_ref,
    lam_ref,
    y_ref,
    stat_ref,
    index_ref,
    fact_ref,
    term_ref,
    x_ref,
    in_ref,
    out_ref,
    volume_ref,
    from_left,
    from_right,
    from_down,
    from_up,
    base_ref,
    next_ref,
    next_y_ref,
    new_term_ref,
    to_right,
    to_left,
    to_up,
    to_down,
    outer_ref,
    x_outer_ref,
    x_tiles,
    sent_ref,
):
    received = (from_left, from_right, from_down, from_up)
    rows = lam_ref.shape[0] // SUB
    comps = rows // 3
    outer_states(y_ref, 0, comps, 0, received, index_ref, outer_ref)
    wet_area = tile(stat_ref, WET_AREA)
    half_kappa_area = tile(stat_ref, HALF_KAPPA_AREA)

    def emit(r, value):
        old = tile(lam_ref, r)
        lam = 0.25 * (old + TIME_STEP * value)
        put(next_ref, r, lam)
        put(next_y_ref, r, lam * (wet_area if r < 12 else half_kappa_area))
        put(base_ref, r, (1.0 / 3.0) * tile(cot_ref, r) + 0.75 * old + lam)

    transposed_section(
        1, lam_ref, y_ref, outer_ref, stat_ref, fact_ref, in_ref, out_ref, volume_ref, emit
    )
    send_states(next_y_ref, 0, comps, 0, index_ref, sent_ref)
    write_messages(sent_ref, (to_right, to_left, to_up, to_down))
    x_to_tiles(x_ref, 1, x_tiles)
    weight = TIME_STEP * 0.25
    friction, conduct = own_gradients(1, weight, lam_ref, y_ref, x_tiles, stat_ref)
    for f, value in enumerate(outer_gradients(weight, outer_ref, x_tiles, fact_ref)):
        put(new_term_ref, 2 + f, tile(term_ref, 2 + f) + value)
    x_to_tiles(x_ref, 0, x_tiles)
    outer_states(x_tiles, 4, comps - 4, comps * 2, received, index_ref, x_outer_ref)
    friction_0, conduct_0 = own_gradients(0, TIME_STEP, next_ref, next_y_ref, x_tiles, stat_ref)
    friction = friction + friction_0
    conduct = conduct + conduct_0
    channels = (comps - 4) * 2
    for f in range(3):
        total = None
        for ch in range(channels):
            row = 12 + ch // 2 * 3 + FACE_NODES[f][ch % 2]
            term = tile(x_outer_ref, f * channels + ch) * tile(next_y_ref, row)
            total = term if total is None else total + term
        conduct = conduct + TIME_STEP * tile(stat_ref, EDGE + f) * total
    put(new_term_ref, 0, tile(term_ref, 0) + friction)
    put(new_term_ref, 1, tile(term_ref, 1) + conduct)


def zone_kernel(term_ref, stat_ref, fact_ref, conduct_ref, out_ref):
    zones = out_ref.shape[2]
    zone_iota = lax.broadcasted_iota(jnp.int32, (zones, LANES), 0).astype(jnp.float32)
    sub_iota = lax.broadcasted_iota(jnp.int32, (SUB, zones), 0)

    def thirds(value):
        high = value.astype(jnp.bfloat16).astype(jnp.float32)
        rest = value - high
        middle = rest.astype(jnp.bfloat16).astype(jnp.float32)
        return [high, middle, rest - middle]

    def by_zone(values, zone_of, zone_row):
        pieces = sum([thirds(value) for value in values], [])
        left = jnp.concatenate(pieces, axis=0).astype(jnp.bfloat16)
        totals = [jnp.zeros((SUB, zones), jnp.float32) for _ in values]
        for sub in range(SUB):
            line = zone_of[pl.ds(zone_row * SUB + sub, 1), :]
            hot = (jnp.broadcast_to(line, (zones, LANES)) == zone_iota).astype(jnp.float32)
            dots = lax.dot_general(
                left,
                hot.astype(jnp.bfloat16),
                (((1,), (1,)), ((), ())),
                preferred_element_type=jnp.float32,
            )
            for n in range(len(values)):
                at = n * 3 * SUB
                three = dots[at : at + SUB] + dots[at + SUB : at + 2 * SUB]
                three = three + dots[at + 2 * SUB : at + 3 * SUB]
                totals[n] = totals[n] + jnp.where(sub_iota == sub, three, 0.0)
        return totals

    friction, conduct = by_zone([tile(term_ref, 0), tile(term_ref, 1)], stat_ref, ZONE_ID)
    for f in range(3):
        conduct = conduct + by_zone([tile(term_ref, 2 + f)], fact_ref, OUTER_ZONE + f)[0]
    friction = GRAD_WEIGHT * jnp.sum(friction, axis=0, keepdims=True)
    conduct = GRAD_WEIGHT * jnp.sum(conduct, axis=0, keepdims=True) / conduct_ref[...]
    for device in range(out_ref.shape[0]):
        out_ref[device, 0:1, :] = friction
        out_ref[device, 1:2, :] = conduct


def last_kernel(
    base_ref,
    lam_ref,
    y_ref,
    stat_ref,
    index_ref,
    fact_ref,
    in_ref,
    out_ref,
    volume_ref,
    from_left,
    from_right,
    from_down,
    from_up,
    adjoint_ref,
    last_ref,
    outer_ref,
):
    received = (from_left, from_right, from_down, from_up)
    rows = lam_ref.shape[0] // SUB
    outer_states(y_ref, 0, rows // 3, 0, received, index_ref, outer_ref)

    def emit(r, value):
        put(adjoint_ref, r, tile(base_ref, r) + TIME_STEP * value)

    transposed_section(
        0, lam_ref, y_ref, outer_ref, stat_ref, fact_ref, in_ref, out_ref, volume_ref, emit
    )
    last_ref[...] = tile(adjoint_ref, rows - 1)


def total_kernel(zone_ref, adjoint_ref, grads_ref):
    grads_ref[...] = jnp.sum(zone_ref[...], axis=0)


def exchange(messages, *ahead):
    to_right, to_left, to_up, to_down = messages
    from_left = shifted(to_right, "gx", 1)
    from_right = shifted(to_left, "gx", -1)
    to_up, to_down = call(
        corner_kernel,
        "corners",
        [jax.ShapeDtypeStruct(to_up.shape, to_up.dtype)] * 2,
        [],
        [from_left, from_right, to_up, to_down, *ahead],
        aliases={2: 0, 3: 1},
    )
    from_down = shifted(to_up, "gy", 1)
    from_up = shifted(to_down, "gy", -1)
    return from_left, from_right, from_down, from_up


def call(kernel, name, outs, scratch, operands, scalars=(), far=False, aliases={}):
    in_memory = pl.BlockSpec(memory_space=pltpu.VMEM)
    in_scalar = pl.BlockSpec(memory_space=pltpu.SMEM)
    in_place = pl.BlockSpec(memory_space=pl.ANY)
    return pl.pallas_call(
        kernel,
        in_specs=[
            in_place if far else in_scalar if n in scalars else in_memory
            for n in range(len(operands))
        ],
        out_specs=[in_memory] * len(outs),
        out_shape=outs,
        scratch_shapes=scratch,
        input_output_aliases=aliases,
        compiler_params=pltpu.CompilerParams(
            vmem_limit_bytes=(FAR_VMEM if far else NEAR_VMEM) * 1024 * 1024
        ),
        name=name,
    )(*operands)


def local(
    cotangent,
    section_states,
    inverse_area,
    edge_length,
    roughness,
    soil_conductance,
    zone_friction,
    zone_conductivity,
    wet_mask,
    element_zone,
    send_face,
    send_count,
    face_partner,
    volume_matrix,
    flux_in,
    flux_out,
):
    rows = cotangent.shape[2]
    channels = rows // 3 * 2
    zones = zone_friction.shape[0]
    slots = send_face.shape[3]
    devices = lax.axis_size("gx") * lax.axis_size("gy")
    f32 = jnp.float32

    def tiles(count, dtype=f32):
        return jax.ShapeDtypeStruct((count * SUB, LANES), dtype)

    def tile_scratch(count, dtype=f32):
        return pltpu.VMEM((count * SUB, LANES), dtype)

    def messages(count):
        return [jax.ShapeDtypeStruct((slots // LANES + 1, count, LANES), f32)] * 4

    def sent_scratch(count):
        return pltpu.VMEM((slots // LANES, count * SUB, LANES), f32)

    square = lambda one: one.reshape(SUB, LANES)
    cot = cotangent.reshape(rows * SUB, LANES)
    table, stat, index, *to_send = call(
        prepare_kernel,
        "prepare",
        [tiles(rows + 13), tiles(STAT_ROWS), tiles(INDEX_ROWS, jnp.int32)]
        + messages(channels + 5),
        [tile_scratch(16), sent_scratch(channels + 5)]
        + [
            tile_scratch(3, jnp.int32),
            pltpu.VMEM(send_face.shape, jnp.int32),
            tile_scratch(rows),
            pltpu.VMEM((section_states.shape[0], 16, SUB * LANES), section_states.dtype),
            tile_scratch(1),
            tile_scratch(3),
            tile_scratch(1),
            tile_scratch(1),
            pltpu.VMEM((zones // LANES, LANES), f32),
            pltpu.VMEM((zones // LANES, LANES), f32),
            tile_scratch(1, jnp.int32),
            tile_scratch(1, jnp.int32),
            pltpu.SemaphoreType.DMA((12,)),
        ],
        [
            cot,
            section_states,
            square(inverse_area),
            edge_length.reshape(3 * SUB, LANES),
            square(roughness),
            square(soil_conductance),
            zone_friction.reshape(-1, LANES),
            zone_conductivity.reshape(-1, LANES),
            square(wet_mask),
            square(element_zone),
            send_face,
            face_partner.reshape(3 * SUB, LANES),
        ],
        far=True,
    )
    received = exchange(to_send)
    lam, y, fact, term, *to_send = call(
        second_kernel,
        "section_two",
        [tiles(rows), tiles(rows), tiles(FACT_ROWS), tiles(5)]
        + messages(channels + channels - 8),
        [tile_scratch(3 * channels), tile_scratch(rows), sent_scratch(2 * channels - 8)],
        [cot, table, stat, index, section_states, flux_in, flux_out, volume_matrix, *received],
        (5, 6, 7),
    )
    received = exchange(to_send)
    base, lam, y, term, *to_send = call(
        first_kernel,
        "section_one",
        [tiles(rows), tiles(rows), tiles(rows), tiles(5)] + messages(channels),
        [
            tile_scratch(3 * channels),
            tile_scratch(3 * (channels - 8)),
            tile_scratch(rows),
            sent_scratch(channels),
        ],
        [
            cot,
            lam,
            y,
            stat,
            index,
            fact,
            term,
            section_states,
            flux_in,
            flux_out,
            volume_matrix,
            *received,
        ],
        (8, 9, 10),
    )
    (zone_terms,) = call(
        zone_kernel,
        "zone_sums",
        [jax.ShapeDtypeStruct((devices, 2, zones), f32)],
        [],
        [term, stat, fact, zone_conductivity.reshape(1, zones)],
    )
    all_terms = lax.all_to_all(zone_terms, ("gx", "gy"), 0, 0)
    received = exchange(to_send, zone_terms)
    adjoint, last = call(
        last_kernel,
        "section_zero",
        [tiles(rows), tiles(1)],
        [tile_scratch(3 * channels)],
        [
            base,
            lam,
            y,
            stat,
            index,
            fact,
            flux_in,
            flux_out,
            volume_matrix,
            *received,
        ],
        (6, 7, 8),
    )
    (zone_grads,) = call(
        total_kernel,
        "zone_total",
        [jax.ShapeDtypeStruct((2, zones), f32)],
        [],
        [all_terms, last],
    )
    return adjoint.reshape(cotangent.shape), zone_grads


def solution(mesh):
    placed = (
        P("gx", "gy", None, None),
        P(None, "gx", "gy", None, None),
        P("gx", "gy", None),
        P("gx", "gy", None, None),
        P("gx", "gy", None),
        P("gx", "gy", None),
        P(),
        P(),
        P("gx", "gy", None),
        P("gx", "gy", None),
        P("gx", "gy", None, None),
        P("gx", "gy", None),
        P("gx", "gy", None, None),
        P(),
        P(),
        P(),
    )
    return jax.shard_map(
        local,
        mesh=mesh,
        in_specs=placed,
        out_specs=(P("gx", "gy", None, None), P()),
        check_vma=False,
    )
```

```python
import functools
import jax
import jax.numpy as jnp
from jax import lax
from jax.experimental import pallas as pl
from jax.experimental.pallas import tpu as pltpu
from jax.sharding import PartitionSpec as P

TIME_STEP = 0.2
SALT_RETURN = 0.5
LATERAL = 0.5
GRAD_WEIGHT = 1.0 / 64.0
FACE_NODES = ((1, 2), (2, 0), (0, 1))
NODE_FACES = (((1, 1), (2, 0)), ((0, 0), (2, 1)), ((0, 1), (1, 0)))
SUB = 8
LANES = 128


WET_AREA, KAPPA, HALF_KAPPA_AREA, WET, EDGE, FRICTION_BASE, ZONE_FRICTION, ZONE_ID = (
    0,
    1,
    2,
    3,
    4,
    7,
    10,
    11,
)
STAT_ROWS = 12
NEAR_VMEM, FAR_VMEM = 32, 60
OUTER_EDGE, OUTER_ZONE, HALF_SPEED = 0, 3, 6
FACT_ROWS = 15
CORNER_LANES = 16
CORNER_BLOCK = 8


def blocks_one(size_x, size_y):
    return [
        [(2 * i + u) * size_y + 2 * j + v for u in range(2) for v in range(2)]
        for i in range(size_x // 2)
        for j in range(size_y // 2)
    ]


def blocks_two(size_x, size_y):
    pairs = [(2 * j + 1, (2 * j + 2) % size_y) for j in range(size_y // 2)]
    blocks = [
        [(2 * i + 1 + u) * size_y + b for u in range(2) for b in pair]
        for i in range(size_x // 2 - 1)
        for pair in pairs
    ]
    for a in (0, size_x - 1):
        for j in range(0, len(pairs), 2):
            blocks.append([a * size_y + b for pair in pairs[j : j + 2] for b in pair])
    return blocks


def places():
    a, b = lax.axis_index("gx"), lax.axis_index("gy")
    size_x, size_y = lax.axis_size("gx"), lax.axis_size("gy")
    odd_a, odd_b = a % 2, b % 2
    one = odd_a * 2 + odd_b
    pair = (b + size_y - 1) % size_y // 2
    at_end = (a == 0) | (a == size_x - 1)
    two = jnp.where(at_end, pair % 2, 1 - odd_a) * 2 + 1 - odd_b
    return one, two, odd_a, odd_b


def slots_of(place):
    base = place - place % 2
    other = 1 - place % 2
    return (place + 2) % 4, base + other, (base + 2) % 4 + other


def tile(ref, row):
    return ref[row * SUB : (row + 1) * SUB, :]


def put(ref, row, value):
    ref[row * SUB : (row + 1) * SUB, :] = value


def take(row, lane_index):
    return jnp.take_along_axis(row, lane_index, axis=1, mode="promise_in_bounds")


def spread(ref, row):
    return jnp.broadcast_to(ref[pl.ds(row, 1), :], (SUB, LANES))


def rows_to_tiles(read, tiles_ref, count):
    for block in range(SUB):
        tiles_ref[pl.ds(block, count, stride=SUB), :] = read(block)


def lanes_of(block):
    return slice(block * LANES, (block + 1) * LANES)


def gather_tile(src, row, lane_index, sublane_index):
    found = take(spread(src, row * SUB), lane_index)
    for sub in range(1, SUB):
        got = take(spread(src, row * SUB + sub), lane_index)
        found = jnp.where(sublane_index == sub, got, found)
    return found


def pick(face, for_zero, for_one, for_two):
    return jnp.where(face == 0, for_zero, jnp.where(face == 1, for_one, for_two))


def gather_ends(src, row, lane_index, sublane_index, face):
    n0, n1, n2 = [gather_tile(src, row + i, lane_index, sublane_index) for i in range(3)]
    return pick(face, n1, n2, n0), pick(face, n2, n0, n1)


def gather_by_face(src, row, lane_index, sublane_index, face):
    return pick(
        face, *[gather_tile(src, row + i, lane_index, sublane_index) for i in range(3)]
    )


def corner_rows(channels):
    return (channels * CORNER_LANES + LANES - 1) // LANES


def message_rows(channels):
    return channels + corner_rows(channels)


class Received:
    def __init__(self, first, second, channels, corner_ref):
        one, two, _, _ = places()
        x1, y1, d11 = slots_of(one)
        x2, y2, d22 = slots_of(two)
        self.mains = [(first, x1), (first, y1), (second, x2), (second, y2)]
        self.corner_ref = corner_ref
        rows = slice(channels, message_rows(channels))
        lane = lax.broadcasted_iota(jnp.int32, (corner_rows(channels), LANES), 1) % CORNER_LANES
        far = jnp.where(lane < 12, second[y2, 0, rows, :], second[x2, 0, rows, :])
        near = jnp.where(lane < 4, first[d11, 0, rows, :], second[d22, 0, rows, :])
        corner_ref[0 : corner_rows(channels), :] = jnp.where(lane < 8, near, far)

    def fill(self, row, lane_index, remote_index, value):
        for number, (ref, slot) in enumerate(self.mains):
            for half in range(2):
                got = take(spread(ref.at[slot, half], row), lane_index)
                value = jnp.where(remote_index == 2 * number + half, got, value)
        channels_a_row = LANES // CORNER_LANES
        lane = lane_index + row % channels_a_row * CORNER_LANES
        line = spread(self.corner_ref, row // channels_a_row)
        got = take(line, jnp.bitwise_and(lane, LANES - 1))
        return jnp.where(remote_index == CORNER_BLOCK, got, value)


def partner_index(index_ref, f):
    return [tile(index_ref, part * 3 + f) for part in range(4)]


def sent_index(index_ref, d):
    return [tile(index_ref, 12 + part * 2 + d) for part in range(3)]


INDEX_ROWS = 18


def turns(comps):
    width = 7 if comps % 7 == 0 else 5
    return width, comps // width


def tile_at(ref, row):
    return ref[pl.ds(pl.multiple_of(row * SUB, SUB), SUB), :]


def put_at(ref, row, value):
    ref[pl.ds(pl.multiple_of(row * SUB, SUB), SUB), :] = value


def send_states(src, first_comp, comps, first_row, index_ref, sent_ref):
    width, parts = turns(comps)

    def body(step, carry):
        d, part = step // parts, step % parts
        lane, sublane, face = [tile_at(index_ref, 12 + n * 2 + d) for n in range(3)]
        for w in range(width):
            comp = part * width + w
            ends = gather_ends(src, (first_comp + comp) * 3, lane, sublane, face)
            for j in range(2):
                put_at(sent_ref.at[d], first_row + comp * 2 + j, ends[j])
        return carry

    lax.fori_loop(0, 2 * parts, body, 0)


def write_messages(sent_ref, channels, first_out, second_out):
    one, two, _, _ = places()
    lane = lax.broadcasted_iota(jnp.int32, (SUB, LANES), 1)
    sub = lax.broadcasted_iota(jnp.int32, (SUB, LANES), 0)
    packed = []
    for group in range(corner_rows(channels)):
        values = sent_ref.at[1][pl.ds(group * SUB * SUB, SUB, stride=SUB), :]
        moved = pltpu.roll(values, 0, 1, stride=CORNER_LANES, stride_axis=0)
        own = jnp.where(lane // CORNER_LANES == sub, moved, 0.0)
        packed.append(jnp.sum(own, axis=0, keepdims=True))
    x1, y1, d11 = slots_of(one)
    x2, y2, d22 = slots_of(two)
    for role, (out, slot) in enumerate(
        ((first_out, x1), (first_out, y1), (second_out, x2), (second_out, y2))
    ):
        for half in range(2):
            out[slot, half, 0:channels, :] = sent_ref.at[0][
                pl.ds(role * 2 + half, channels, stride=SUB), :
            ]
    for out, slot in ((first_out, x1), (first_out, y1), (first_out, d11), (second_out, d22)):
        for group, row in enumerate(packed):
            at = channels + group
            out[slot, 0, at : at + 1, :] = row


def prepare_kernel(
    cot_ref,
    x_ref,
    area_ref,
    edge_ref,
    rough_ref,
    soil_ref,
    friction_ref,
    conduct_ref,
    wet_ref,
    zone_ref,
    send_ref,
    partner_ref,
    table_ref,
    stat_ref,
    index_ref,
    first_out,
    second_out,
    x_tiles,
    sent_ref,
    *fetched,
):
    *fetched, sems = fetched
    sources = [
        partner_ref,
        send_ref,
        cot_ref,
        x_ref.at[:, 0, 0, 0:16],
        area_ref,
        edge_ref,
        rough_ref,
        soil_ref,
        friction_ref,
        conduct_ref,
        wet_ref,
        zone_ref,
    ]
    copies = [
        pltpu.make_async_copy(source, target, sems.at[n])
        for n, (source, target) in enumerate(zip(sources, fetched))
    ]
    for copy in copies:
        copy.start()
    for copy in copies:
        copy.wait()
    (
        partner_ref,
        send_ref,
        cot_ref,
        x_ref,
        area_ref,
        edge_ref,
        rough_ref,
        soil_ref,
        friction_ref,
        conduct_ref,
        wet_ref,
        zone_ref,
    ) = fetched
    rows = cot_ref.shape[0] // SUB
    sections = x_ref.shape[0]
    _, _, odd_a, odd_b = places()
    straight = (6 - 5 * odd_a, 4 - odd_b, 1 + 5 * odd_a, 3 + odd_b)
    right, up = 1 - odd_a, 1 - odd_b
    corners = (
        5 * right + 2 * up,
        7 - 5 * right - 2 * up,
        5 * right + 2 - 2 * up,
        5 - 5 * right + 2 * up,
    )
    face_total = 3 * SUB * LANES
    for f in range(3):
        partner = tile(partner_ref, f)
        beyond = partner - face_total
        direction = jnp.right_shift(beyond, 8)
        half = jnp.bitwise_and(jnp.right_shift(beyond, 7), 1)
        lane = jnp.bitwise_and(partner, LANES - 1)
        remote = jnp.where(beyond >= 0, CORNER_BLOCK, -1)
        for number, toward in enumerate(straight):
            remote = jnp.where(direction == toward, 2 * number + half, remote)
        for number, toward in enumerate(corners):
            lane = jnp.where(direction == toward, lane % 4 + 4 * number, lane)
        put(index_ref, f, lane)
        put(index_ref, 3 + f, jnp.bitwise_and(jnp.right_shift(partner, 7), SUB - 1))
        put(index_ref, 6 + f, jnp.right_shift(partner, 10))
        put(index_ref, 9 + f, remote)
    sub_iota = lax.broadcasted_iota(jnp.int32, (SUB, LANES), 0)
    lane_iota = lax.broadcasted_iota(jnp.int32, (SUB, LANES), 1)

    def slots_to(choices, choice, half):
        rows_of = [
            jnp.broadcast_to(send_ref[0, 0, n : n + 1, lanes_of(half)], (SUB, LANES))
            for n in choices
        ]
        found = rows_of[0]
        for n, row in zip(choices[1:], rows_of[1:]):
            found = jnp.where(choice == n, row, found)
        return found

    straight_slots = None
    for number, toward in enumerate(straight):
        for half in range(2):
            row = slots_to((1, 6) if number % 2 == 0 else (3, 4), toward, half)
            straight_slots = (
                row
                if straight_slots is None
                else jnp.where(sub_iota == 2 * number + half, row, straight_slots)
            )
    corner_slots = None
    for number, toward in enumerate(corners):
        row = slots_to((0, 2, 5, 7), toward, 0)
        if number == 0:
            corner_slots = row
        else:
            moved = pltpu.roll(row, 4 * number, 1)
            corner_slots = jnp.where(lane_iota // 4 == number, moved, corner_slots)
    for d, slots in enumerate((straight_slots, corner_slots)):
        put(index_ref, 12 + d, jnp.bitwise_and(slots, LANES - 1))
        put(index_ref, 14 + d, jnp.bitwise_and(jnp.right_shift(slots, 7), SUB - 1))
        put(index_ref, 16 + d, jnp.right_shift(slots, 10))
    zone = zone_ref[...]
    zone_lane = jnp.bitwise_and(zone, LANES - 1)
    zone_block = jnp.right_shift(zone, 7)
    factors = []
    for ref in (friction_ref, conduct_ref):
        found = None
        for block in range(ref.shape[0]):
            got = take(spread(ref, block), zone_lane)
            found = got if block == 0 else jnp.where(zone_block == block, got, found)
        factors.append(found)
    area = area_ref[...]
    wet = wet_ref[...].astype(jnp.float32)
    kappa = factors[1] * soil_ref[...]
    wet_area = wet * area
    half_kappa_area = LATERAL * kappa * area
    put(stat_ref, WET_AREA, wet_area)
    put(stat_ref, KAPPA, kappa)
    put(stat_ref, HALF_KAPPA_AREA, half_kappa_area)
    put(stat_ref, WET, wet)
    put(stat_ref, ZONE_FRICTION, factors[0])
    put(stat_ref, ZONE_ID, zone.astype(jnp.float32))
    stat_ref[EDGE * SUB : (EDGE + 3) * SUB, :] = edge_ref[...]
    for k in range(sections):
        rows_to_tiles(
            lambda b: x_ref[k, :, lanes_of(b)].astype(jnp.float32), x_tiles, 16
        )
        squares = [tile(x_tiles, r) * tile(x_tiles, r) for r in range(12)]
        node_sum = [squares[i] + squares[3 + i] + squares[6 + i] + squares[9 + i] for i in range(3)]
        for f in range(3):
            first, second = FACE_NODES[f]
            put(table_ref, rows + 3 + 3 * k + f, node_sum[first] + node_sum[second])
        momentum = squares[3]
        for r in range(4, 9):
            momentum = momentum + squares[r]
        put(
            stat_ref,
            FRICTION_BASE + k,
            rough_ref[...] * jnp.sqrt(1.0 + momentum * (1.0 / 6.0)),
        )
    for f in range(3):
        put(table_ref, rows + f, tile(stat_ref, EDGE + f))
    put(table_ref, rows + 12, zone.astype(jnp.float32))
    for r in range(rows):
        put(table_ref, r, tile(cot_ref, r) * (wet_area if r < 12 else half_kappa_area))
    comps = rows // 3
    send_states(table_ref, 0, comps, 0, index_ref, sent_ref)
    for d in range(2):
        lane, sublane, face = sent_index(index_ref, d)
        at = comps * 2 * SUB
        for group in range(4):
            sent_ref[d, at : at + SUB, :] = gather_by_face(
                table_ref, rows + 3 * group, lane, sublane, face
            )
            at += SUB
        sent_ref[d, at : at + SUB, :] = gather_tile(table_ref, rows + 12, lane, sublane)
    write_messages(sent_ref, comps * 2 + 5, first_out, second_out)


def corner_kernel(channels, first_in, second_old, *rest):
    second_out = rest[-1]
    one, two, _, _ = places()
    x1, y1, _ = slots_of(one)
    x2, y2, _ = slots_of(two)
    rows = slice(channels, message_rows(channels))
    second_out[x2, 0, rows, :] = first_in[y1, 0, rows, :]
    second_out[y2, 0, rows, :] = first_in[x1, 0, rows, :]


def outer_states(src, first_comp, comps, first_row, received, index_ref, out_ref):
    width, parts = turns(comps)

    def body(step, carry):
        f, part = step // parts, step % parts
        lane, sublane, face, remote = [tile_at(index_ref, n * 3 + f) for n in range(4)]
        for w in range(width):
            comp = part * width + w
            ends = gather_ends(src, (first_comp + comp) * 3, lane, sublane, face)
            for j in range(2):
                value = received.fill(first_row + comp * 2 + j, lane, remote, ends[j])
                put_at(out_ref, f * comps * 2 + comp * 2 + j, value)
        return carry

    lax.fori_loop(0, 3 * parts, body, 0)


def transposed_section(
    section, lam_ref, y_ref, outer_ref, stat_ref, fact_ref, in_ref, out_ref, volume_ref, emit
):
    rows = lam_ref.shape[0] // SUB
    channels = rows // 3 * 2
    layers = (rows - 12) // 3
    edge = [tile(stat_ref, EDGE + f) for f in range(3)]
    outer_edge = [tile(fact_ref, OUTER_EDGE + f) for f in range(3)]
    half_speed = [tile(fact_ref, HALF_SPEED + 3 * section + f) for f in range(3)]
    kappa = tile(stat_ref, KAPPA)
    wet = tile(stat_ref, WET)
    own = [tile(y_ref, r) for r in range(12)]
    result = []
    for r in range(12):
        total = volume_ref[0, r] * own[0]
        for q in range(1, 12):
            total = total + volume_ref[q, r] * own[q]
        result.append(total)
    for f in range(3):
        ends = FACE_NODES[f]
        inner = [edge[f] * own[(ch // 2) * 3 + ends[ch % 2]] for ch in range(8)]
        outer = [outer_edge[f] * tile(outer_ref, f * channels + ch) for ch in range(8)]
        for b in range(8):
            total = half_speed[f] * (inner[b] - outer[b])
            for a in range(8):
                total = total + in_ref[a, b] * inner[a] - out_ref[a, b] * outer[a]
            at = (b // 2) * 3 + ends[b % 2]
            result[at] = result[at] + total
    friction = tile(stat_ref, ZONE_FRICTION) * tile(stat_ref, FRICTION_BASE + section) * wet
    for r in range(3, 9):
        result[r] = result[r] - friction * tile(lam_ref, r)
    exchange = []
    for i in range(3):
        top = tile(lam_ref, 12 + i) - SALT_RETURN * wet * tile(lam_ref, 9 + i)
        exchange.append(kappa * top)
        result[9 + i] = result[9 + i] + exchange[i]
    for r in range(12):
        emit(r, result[r])
    for i in range(3):
        (f0, j0), (f1, j1) = NODE_FACES[i]
        both = edge[f0] + edge[f1]
        from_above = exchange[i]
        for layer in range(layers):
            r = 12 + layer * 3 + i
            value = (
                outer_edge[f0] * tile(outer_ref, f0 * channels + 8 + layer * 2 + j0)
                + outer_edge[f1] * tile(outer_ref, f1 * channels + 8 + layer * 2 + j1)
                - both * tile(y_ref, r)
                - from_above
            )
            if layer + 1 < layers:
                from_above = kappa * (tile(lam_ref, r + 3) - tile(lam_ref, r))
                value = value + from_above
            emit(r, value)


def own_gradients(section, weight, lam_ref, y_ref, x_tiles, stat_ref):
    rows = lam_ref.shape[0] // SUB
    layers = (rows - 12) // 3
    wet = tile(stat_ref, WET)
    kappa = tile(stat_ref, KAPPA)
    momentum = tile(lam_ref, 3) * tile(x_tiles, 3)
    for r in range(4, 9):
        momentum = momentum + tile(lam_ref, r) * tile(x_tiles, r)
    friction = -(weight * wet * tile(stat_ref, FRICTION_BASE + section)) * momentum
    vertical = None
    lateral = None
    for i in range(3):
        (f0, _), (f1, _) = NODE_FACES[i]
        top = tile(lam_ref, 12 + i) - SALT_RETURN * wet * tile(lam_ref, 9 + i)
        total = top * (tile(x_tiles, 9 + i) - tile(x_tiles, 12 + i))
        dots = None
        for layer in range(layers):
            r = 12 + layer * 3 + i
            term = tile(y_ref, r) * tile(x_tiles, r)
            dots = term if dots is None else dots + term
            if layer + 1 < layers:
                total = total + (tile(lam_ref, r + 3) - tile(lam_ref, r)) * (
                    tile(x_tiles, r) - tile(x_tiles, r + 3)
                )
        side = (tile(stat_ref, EDGE + f0) + tile(stat_ref, EDGE + f1)) * dots
        vertical = total if vertical is None else vertical + total
        lateral = side if lateral is None else lateral + side
    return friction, weight * (kappa * vertical - lateral)


def outer_gradients(weight, outer_ref, x_tiles, fact_ref):
    channels = outer_ref.shape[0] // SUB // 3
    values = []
    for f in range(3):
        total = None
        for ch in range(8, channels):
            row = 12 + (ch - 8) // 2 * 3 + FACE_NODES[f][ch % 2]
            term = tile(outer_ref, f * channels + ch) * tile(x_tiles, row)
            total = term if total is None else total + term
        values.append(weight * tile(fact_ref, OUTER_EDGE + f) * total)
    return values


def x_to_tiles(x_ref, section, x_tiles):
    rows = x_ref.shape[3]
    rows_to_tiles(
        lambda b: x_ref[section, 0, 0, :, lanes_of(b)].astype(jnp.float32), x_tiles, rows
    )


def second_kernel(
    cot_ref,
    table_ref,
    stat_ref,
    index_ref,
    x_ref,
    in_ref,
    out_ref,
    volume_ref,
    first_in,
    second_in,
    lam_ref,
    y_ref,
    fact_ref,
    term_ref,
    first_out,
    second_out,
    outer_ref,
    x_tiles,
    sent_ref,
    corner_ref,
):
    rows = cot_ref.shape[0] // SUB
    comps = rows // 3
    received = Received(first_in, second_in, comps * 2 + 5, corner_ref)
    outer_states(table_ref, 0, comps, 0, received, index_ref, outer_ref)
    for f in range(3):
        lane, sublane, face, remote = partner_index(index_ref, f)
        for group in range(4):
            value = gather_by_face(table_ref, rows + 3 * group, lane, sublane, face)
            value = received.fill(comps * 2 + group, lane, remote, value)
            if group == 0:
                put(fact_ref, OUTER_EDGE + f, value)
            else:
                both = tile(table_ref, rows + 3 * group + f) + value
                put(
                    fact_ref,
                    HALF_SPEED + 3 * (group - 1) + f,
                    0.5 * jnp.sqrt(1.0 + (0.25 / 8.0) * both),
                )
        value = gather_tile(table_ref, rows + 12, lane, sublane)
        put(fact_ref, OUTER_ZONE + f, received.fill(comps * 2 + 4, lane, remote, value))
    wet_area = tile(stat_ref, WET_AREA)
    half_kappa_area = tile(stat_ref, HALF_KAPPA_AREA)

    def emit(r, value):
        lam = (2.0 / 3.0) * (tile(cot_ref, r) + TIME_STEP * value)
        put(lam_ref, r, lam)
        put(y_ref, r, lam * (wet_area if r < 12 else half_kappa_area))

    transposed_section(
        2, cot_ref, table_ref, outer_ref, stat_ref, fact_ref, in_ref, out_ref, volume_ref, emit
    )
    x_to_tiles(x_ref, 0, x_tiles)
    send_states(y_ref, 0, comps, 0, index_ref, sent_ref)
    send_states(x_tiles, 4, comps - 4, comps * 2, index_ref, sent_ref)
    write_messages(sent_ref, comps * 4 - 8, first_out, second_out)
    x_to_tiles(x_ref, 2, x_tiles)
    weight = TIME_STEP * 2.0 / 3.0
    friction, conduct = own_gradients(2, weight, cot_ref, table_ref, x_tiles, stat_ref)
    put(term_ref, 0, friction)
    put(term_ref, 1, conduct)
    for f, value in enumerate(outer_gradients(weight, outer_ref, x_tiles, fact_ref)):
        put(term_ref, 2 + f, value)


def first_kernel(
    cot_ref,
    lam_ref,
    y_ref,
    stat_ref,
    index_ref,
    fact_ref,
    term_ref,
    x_ref,
    in_ref,
    out_ref,
    volume_ref,
    first_in,
    second_in,
    base_ref,
    next_ref,
    next_y_ref,
    new_term_ref,
    first_out,
    second_out,
    outer_ref,
    x_outer_ref,
    x_tiles,
    sent_ref,
    corner_ref,
):
    rows = lam_ref.shape[0] // SUB
    comps = rows // 3
    received = Received(first_in, second_in, comps * 4 - 8, corner_ref)
    outer_states(y_ref, 0, comps, 0, received, index_ref, outer_ref)
    wet_area = tile(stat_ref, WET_AREA)
    half_kappa_area = tile(stat_ref, HALF_KAPPA_AREA)

    def emit(r, value):
        old = tile(lam_ref, r)
        lam = 0.25 * (old + TIME_STEP * value)
        put(next_ref, r, lam)
        put(next_y_ref, r, lam * (wet_area if r < 12 else half_kappa_area))
        put(base_ref, r, (1.0 / 3.0) * tile(cot_ref, r) + 0.75 * old + lam)

    transposed_section(
        1, lam_ref, y_ref, outer_ref, stat_ref, fact_ref, in_ref, out_ref, volume_ref, emit
    )
    send_states(next_y_ref, 0, comps, 0, index_ref, sent_ref)
    write_messages(sent_ref, comps * 2, first_out, second_out)
    x_to_tiles(x_ref, 1, x_tiles)
    weight = TIME_STEP * 0.25
    friction, conduct = own_gradients(1, weight, lam_ref, y_ref, x_tiles, stat_ref)
    for f, value in enumerate(outer_gradients(weight, outer_ref, x_tiles, fact_ref)):
        put(new_term_ref, 2 + f, tile(term_ref, 2 + f) + value)
    x_to_tiles(x_ref, 0, x_tiles)
    outer_states(x_tiles, 4, comps - 4, comps * 2, received, index_ref, x_outer_ref)
    friction_0, conduct_0 = own_gradients(0, TIME_STEP, next_ref, next_y_ref, x_tiles, stat_ref)
    friction = friction + friction_0
    conduct = conduct + conduct_0
    channels = (comps - 4) * 2
    for f in range(3):
        total = None
        for ch in range(channels):
            row = 12 + ch // 2 * 3 + FACE_NODES[f][ch % 2]
            term = tile(x_outer_ref, f * channels + ch) * tile(next_y_ref, row)
            total = term if total is None else total + term
        conduct = conduct + TIME_STEP * tile(stat_ref, EDGE + f) * total
    put(new_term_ref, 0, tile(term_ref, 0) + friction)
    put(new_term_ref, 1, tile(term_ref, 1) + conduct)


def zone_kernel(term_ref, stat_ref, fact_ref, conduct_ref, out_ref):
    zones = out_ref.shape[2]
    zone_iota = lax.broadcasted_iota(jnp.int32, (zones, LANES), 0).astype(jnp.float32)
    sub_iota = lax.broadcasted_iota(jnp.int32, (SUB, zones), 0)

    def thirds(value):
        high = value.astype(jnp.bfloat16).astype(jnp.float32)
        rest = value - high
        middle = rest.astype(jnp.bfloat16).astype(jnp.float32)
        return [high, middle, rest - middle]

    def by_zone(values, zone_of, zone_row):
        pieces = sum([thirds(value) for value in values], [])
        left = jnp.concatenate(pieces, axis=0).astype(jnp.bfloat16)
        totals = [jnp.zeros((SUB, zones), jnp.float32) for _ in values]
        for sub in range(SUB):
            line = zone_of[pl.ds(zone_row * SUB + sub, 1), :]
            hot = (jnp.broadcast_to(line, (zones, LANES)) == zone_iota).astype(jnp.float32)
            dots = lax.dot_general(
                left,
                hot.astype(jnp.bfloat16),
                (((1,), (1,)), ((), ())),
                preferred_element_type=jnp.float32,
            )
            for n in range(len(values)):
                at = n * 3 * SUB
                three = dots[at : at + SUB] + dots[at + SUB : at + 2 * SUB]
                three = three + dots[at + 2 * SUB : at + 3 * SUB]
                totals[n] = totals[n] + jnp.where(sub_iota == sub, three, 0.0)
        return totals

    friction, conduct = by_zone([tile(term_ref, 0), tile(term_ref, 1)], stat_ref, ZONE_ID)
    for f in range(3):
        conduct = conduct + by_zone([tile(term_ref, 2 + f)], fact_ref, OUTER_ZONE + f)[0]
    friction = GRAD_WEIGHT * jnp.sum(friction, axis=0, keepdims=True)
    conduct = GRAD_WEIGHT * jnp.sum(conduct, axis=0, keepdims=True) / conduct_ref[...]
    for device in range(out_ref.shape[0]):
        out_ref[device, 0:1, :] = friction
        out_ref[device, 1:2, :] = conduct


def last_kernel(
    base_ref,
    lam_ref,
    y_ref,
    stat_ref,
    index_ref,
    fact_ref,
    in_ref,
    out_ref,
    volume_ref,
    first_in,
    second_in,
    adjoint_ref,
    last_ref,
    outer_ref,
    corner_ref,
):
    rows = lam_ref.shape[0] // SUB
    received = Received(first_in, second_in, rows // 3 * 2, corner_ref)
    outer_states(y_ref, 0, rows // 3, 0, received, index_ref, outer_ref)

    def emit(r, value):
        put(adjoint_ref, r, tile(base_ref, r) + TIME_STEP * value)

    transposed_section(
        0, lam_ref, y_ref, outer_ref, stat_ref, fact_ref, in_ref, out_ref, volume_ref, emit
    )
    last_ref[...] = tile(adjoint_ref, rows - 1)


def total_kernel(zone_ref, adjoint_ref, grads_ref):
    grads_ref[...] = jnp.sum(zone_ref[...], axis=0)


def exchange(channels, first, second, *ahead):
    sizes = lax.axis_size("gx"), lax.axis_size("gy")
    first = lax.all_to_all(first, ("gx", "gy"), 0, 0, axis_index_groups=blocks_one(*sizes))
    (second,) = call(
        functools.partial(corner_kernel, channels),
        "corners",
        [jax.ShapeDtypeStruct(second.shape, second.dtype)],
        [],
        [first, second, *ahead],
        aliases={1: 0},
    )
    second = lax.all_to_all(second, ("gx", "gy"), 0, 0, axis_index_groups=blocks_two(*sizes))
    return first, second


def call(kernel, name, outs, scratch, operands, scalars=(), far=False, aliases={}):
    in_memory = pl.BlockSpec(memory_space=pltpu.VMEM)
    in_scalar = pl.BlockSpec(memory_space=pltpu.SMEM)
    in_place = pl.BlockSpec(memory_space=pl.ANY)
    return pl.pallas_call(
        kernel,
        in_specs=[
            in_place if far else in_scalar if n in scalars else in_memory
            for n in range(len(operands))
        ],
        out_specs=[in_memory] * len(outs),
        out_shape=outs,
        scratch_shapes=scratch,
        input_output_aliases=aliases,
        compiler_params=pltpu.CompilerParams(
            vmem_limit_bytes=(FAR_VMEM if far else NEAR_VMEM) * 1024 * 1024
        ),
        name=name,
    )(*operands)


def local(
    cotangent,
    section_states,
    inverse_area,
    edge_length,
    roughness,
    soil_conductance,
    zone_friction,
    zone_conductivity,
    wet_mask,
    element_zone,
    send_face,
    send_count,
    face_partner,
    volume_matrix,
    flux_in,
    flux_out,
):
    rows = cotangent.shape[2]
    channels = rows // 3 * 2
    zones = zone_friction.shape[0]
    slots = send_face.shape[3]
    devices = lax.axis_size("gx") * lax.axis_size("gy")
    f32 = jnp.float32

    def tiles(count, dtype=f32):
        return jax.ShapeDtypeStruct((count * SUB, LANES), dtype)

    def tile_scratch(count, dtype=f32):
        return pltpu.VMEM((count * SUB, LANES), dtype)

    def messages(count):
        return [jax.ShapeDtypeStruct((4, slots // LANES, message_rows(count), LANES), f32)] * 2

    def sent_scratch(count):
        return pltpu.VMEM((slots // LANES, corner_rows(count) * SUB * SUB, LANES), f32)

    corner_scratch = pltpu.VMEM((SUB, LANES), f32)

    square = lambda one: one.reshape(SUB, LANES)
    cot = cotangent.reshape(rows * SUB, LANES)
    table, stat, index, *to_send = call(
        prepare_kernel,
        "prepare",
        [tiles(rows + 13), tiles(STAT_ROWS), tiles(INDEX_ROWS, jnp.int32)]
        + messages(channels + 5),
        [tile_scratch(16), sent_scratch(channels + 5)]
        + [
            tile_scratch(3, jnp.int32),
            pltpu.VMEM(send_face.shape, jnp.int32),
            tile_scratch(rows),
            pltpu.VMEM((section_states.shape[0], 16, SUB * LANES), section_states.dtype),
            tile_scratch(1),
            tile_scratch(3),
            tile_scratch(1),
            tile_scratch(1),
            pltpu.VMEM((zones // LANES, LANES), f32),
            pltpu.VMEM((zones // LANES, LANES), f32),
            tile_scratch(1, jnp.int32),
            tile_scratch(1, jnp.int32),
            pltpu.SemaphoreType.DMA((12,)),
        ],
        [
            cot,
            section_states,
            square(inverse_area),
            edge_length.reshape(3 * SUB, LANES),
            square(roughness),
            square(soil_conductance),
            zone_friction.reshape(-1, LANES),
            zone_conductivity.reshape(-1, LANES),
            square(wet_mask),
            square(element_zone),
            send_face,
            face_partner.reshape(3 * SUB, LANES),
        ],
        far=True,
    )
    received = exchange(channels + 5, *to_send)
    lam, y, fact, term, *to_send = call(
        second_kernel,
        "section_two",
        [tiles(rows), tiles(rows), tiles(FACT_ROWS), tiles(5)]
        + messages(channels + channels - 8),
        [
            tile_scratch(3 * channels),
            tile_scratch(rows),
            sent_scratch(2 * channels - 8),
            corner_scratch,
        ],
        [cot, table, stat, index, section_states, flux_in, flux_out, volume_matrix, *received],
        (5, 6, 7),
    )
    received = exchange(channels + channels - 8, *to_send)
    base, lam, y, term, *to_send = call(
        first_kernel,
        "section_one",
        [tiles(rows), tiles(rows), tiles(rows), tiles(5)] + messages(channels),
        [
            tile_scratch(3 * channels),
            tile_scratch(3 * (channels - 8)),
            tile_scratch(rows),
            sent_scratch(channels),
            corner_scratch,
        ],
        [
            cot,
            lam,
            y,
            stat,
            index,
            fact,
            term,
            section_states,
            flux_in,
            flux_out,
            volume_matrix,
            *received,
        ],
        (8, 9, 10),
    )
    (zone_terms,) = call(
        zone_kernel,
        "zone_sums",
        [jax.ShapeDtypeStruct((devices, 2, zones), f32)],
        [],
        [term, stat, fact, zone_conductivity.reshape(1, zones)],
    )
    all_terms = lax.all_to_all(zone_terms, ("gx", "gy"), 0, 0)
    received = exchange(channels, *to_send, zone_terms)
    adjoint, last = call(
        last_kernel,
        "section_zero",
        [tiles(rows), tiles(1)],
        [tile_scratch(3 * channels), corner_scratch],
        [
            base,
            lam,
            y,
            stat,
            index,
            fact,
            flux_in,
            flux_out,
            volume_matrix,
            *received,
        ],
        (6, 7, 8),
    )
    (zone_grads,) = call(
        total_kernel,
        "zone_total",
        [jax.ShapeDtypeStruct((2, zones), f32)],
        [],
        [all_terms, last],
    )
    return adjoint.reshape(cotangent.shape), zone_grads


def solution(mesh):
    placed = (
        P("gx", "gy", None, None),
        P(None, "gx", "gy", None, None),
        P("gx", "gy", None),
        P("gx", "gy", None, None),
        P("gx", "gy", None),
        P("gx", "gy", None),
        P(),
        P(),
        P("gx", "gy", None),
        P("gx", "gy", None),
        P("gx", "gy", None, None),
        P("gx", "gy", None),
        P("gx", "gy", None, None),
        P(),
        P(),
        P(),
    )
    return jax.shard_map(
        local,
        mesh=mesh,
        in_specs=placed,
        out_specs=(P("gx", "gy", None, None), P()),
        check_vma=False,
    )
```

```python
import functools
import jax
import jax.numpy as jnp
from jax import lax
from jax.experimental import pallas as pl
from jax.experimental.pallas import tpu as pltpu
from jax.sharding import PartitionSpec as P

TIME_STEP = 0.2
SALT_RETURN = 0.5
LATERAL = 0.5
GRAD_WEIGHT = 1.0 / 64.0
FACE_NODES = ((1, 2), (2, 0), (0, 1))
NODE_FACES = (((1, 1), (2, 0)), ((0, 0), (2, 1)), ((0, 1), (1, 0)))
SUB = 8
LANES = 128


WET_AREA, KAPPA, HALF_KAPPA_AREA, WET, EDGE, FRICTION_BASE, ZONE_FRICTION, ZONE_ID = (
    0,
    1,
    2,
    3,
    4,
    7,
    10,
    11,
)
STAT_ROWS = 12
NEAR_VMEM, FAR_VMEM = 32, 60
OUTER_EDGE, OUTER_ZONE, HALF_SPEED = 0, 3, 6
FACT_ROWS = 15
X_ROWS = 24
CORNER_LANES = 16
CORNER_BLOCK = 8


def swapped(x, axis, first):
    peers = lax.axis_size(axis)
    lows = range(first, peers - 1, 2)
    return lax.ppermute(x, axis, [(i, i + 1) for i in lows] + [(i + 1, i) for i in lows])


def tile(ref, row):
    return ref[row * SUB : (row + 1) * SUB, :]


def put(ref, row, value):
    ref[row * SUB : (row + 1) * SUB, :] = value


def take(row, lane_index):
    return jnp.take_along_axis(row, lane_index, axis=1, mode="promise_in_bounds")


def spread(ref, row):
    return jnp.broadcast_to(ref[pl.ds(row, 1), :], (SUB, LANES))


def rows_to_tiles(read, tiles_ref, count):
    for block in range(SUB):
        tiles_ref[pl.ds(block, count, stride=SUB), :] = read(block)


def lanes_of(block):
    return slice(block * LANES, (block + 1) * LANES)


def gather_tile(src, row, lane_index, sublane_index):
    found = take(spread(src, row * SUB), lane_index)
    for sub in range(1, SUB):
        got = take(spread(src, row * SUB + sub), lane_index)
        found = jnp.where(sublane_index == sub, got, found)
    return found


def pick(face, for_zero, for_one, for_two):
    return jnp.where(face == 0, for_zero, jnp.where(face == 1, for_one, for_two))


def gather_ends(src, row, lane_index, sublane_index, face):
    n0, n1, n2 = [gather_tile(src, row + i, lane_index, sublane_index) for i in range(3)]
    return pick(face, n1, n2, n0), pick(face, n2, n0, n1)


def gather_by_face(src, row, lane_index, sublane_index, face):
    return pick(
        face, *[gather_tile(src, row + i, lane_index, sublane_index) for i in range(3)]
    )


def corner_rows(channels):
    return (channels * CORNER_LANES + LANES - 1) // LANES


def message_rows(channels):
    return channels + corner_rows(channels)


def corner_lane(shape):
    return lax.broadcasted_iota(jnp.int32, shape, 1) % CORNER_LANES


class Received:
    def __init__(self, messages, channels, corner_ref):
        _, _, y1, y2 = messages
        self.mains = messages
        self.corner_ref = corner_ref
        rows = slice(channels, message_rows(channels))
        count = corner_rows(channels)
        lane = corner_lane((count, LANES))
        corner_ref[0:count, :] = jnp.where(
            jnp.bitwise_and(lane, 4) == 0, y1[0, rows, :], y2[0, rows, :]
        )

    def fill(self, row, lane_index, remote_index, value):
        for number, ref in enumerate(self.mains):
            for half in range(2):
                got = take(spread(ref.at[half], row), lane_index)
                value = jnp.where(remote_index == 2 * number + half, got, value)
        channels_a_row = LANES // CORNER_LANES
        lane = lane_index + row % channels_a_row * CORNER_LANES
        line = spread(self.corner_ref, row // channels_a_row)
        got = take(line, jnp.bitwise_and(lane, LANES - 1))
        return jnp.where(remote_index == CORNER_BLOCK, got, value)


def partner_index(index_ref, f):
    return [tile(index_ref, part * 3 + f) for part in range(4)]


def sent_index(index_ref, d):
    return [tile(index_ref, 12 + part * 2 + d) for part in range(3)]


INDEX_ROWS = 18


def tile_at(ref, row):
    return ref[pl.ds(pl.multiple_of(row * SUB, SUB), SUB), :]


def put_at(ref, row, value):
    ref[pl.ds(pl.multiple_of(row * SUB, SUB), SUB), :] = value


def send_states(src, first_comp, comps, index_ref, sent_ref):
    def body(d, carry):
        lane, sublane, face = [tile_at(index_ref, 12 + n * 2 + d) for n in range(3)]
        for comp in range(comps):
            ends = gather_ends(src, (first_comp + comp) * 3, lane, sublane, face)
            for j in range(2):
                put(sent_ref.at[d], comp * 2 + j, ends[j])
        return carry

    lax.fori_loop(0, 2, body, 0)


def write_messages(sent_ref, first, channels, outs, total):
    lane = lax.broadcasted_iota(jnp.int32, (SUB, LANES), 1)
    sub = lax.broadcasted_iota(jnp.int32, (SUB, LANES), 0)
    for role, out in enumerate(outs):
        for half in range(2):
            out[half, first : first + channels, :] = sent_ref.at[0][
                pl.ds(role * 2 + half, channels, stride=SUB), :
            ]
    for group in range(corner_rows(channels)):
        values = sent_ref.at[1][pl.ds(group * SUB * SUB, SUB, stride=SUB), :]
        moved = pltpu.roll(values, 0, 1, stride=CORNER_LANES, stride_axis=0)
        own = jnp.where(lane // CORNER_LANES == sub, moved, 0.0)
        row = jnp.sum(own, axis=0, keepdims=True)
        at = total + first // SUB + group
        for out in outs[:2]:
            out[0, at : at + 1, :] = row


def prepare_kernel(
    cot_ref,
    x_ref,
    area_ref,
    edge_ref,
    rough_ref,
    soil_ref,
    friction_ref,
    conduct_ref,
    wet_ref,
    zone_ref,
    send_ref,
    partner_ref,
    table_ref,
    stat_ref,
    index_ref,
    to_x1,
    to_x2,
    to_y1,
    to_y2,
    x_tiles,
    sent_ref,
    *fetched,
):
    *fetched, sems = fetched
    sources = [
        partner_ref,
        send_ref,
        cot_ref,
        x_ref.at[:, 0, 0, 0:16],
        area_ref,
        edge_ref,
        rough_ref,
        soil_ref,
        friction_ref,
        conduct_ref,
        wet_ref,
        zone_ref,
    ]
    copies = [
        pltpu.make_async_copy(source, target, sems.at[n])
        for n, (source, target) in enumerate(zip(sources, fetched))
    ]
    for copy in copies:
        copy.start()
    for copy in copies:
        copy.wait()
    (
        partner_ref,
        send_ref,
        cot_ref,
        x_ref,
        area_ref,
        edge_ref,
        rough_ref,
        soil_ref,
        friction_ref,
        conduct_ref,
        wet_ref,
        zone_ref,
    ) = fetched
    rows = cot_ref.shape[0] // SUB
    sections = x_ref.shape[0]
    odd_a, odd_b = lax.axis_index("gx") % 2, lax.axis_index("gy") % 2
    straight = (6 - 5 * odd_a, 1 + 5 * odd_a, 4 - odd_b, 3 + odd_b)
    right, up = 1 - odd_a, 1 - odd_b
    corners = (
        5 * right + 2 * up,
        5 * right + 2 - 2 * up,
        5 - 5 * right + 2 * up,
        7 - 5 * right - 2 * up,
    )
    face_total = 3 * SUB * LANES
    for f in range(3):
        partner = tile(partner_ref, f)
        beyond = partner - face_total
        direction = jnp.right_shift(beyond, 8)
        half = jnp.bitwise_and(jnp.right_shift(beyond, 7), 1)
        lane = jnp.bitwise_and(partner, LANES - 1)
        remote = jnp.where(beyond >= 0, CORNER_BLOCK, -1)
        for number, toward in enumerate(straight):
            remote = jnp.where(direction == toward, 2 * number + half, remote)
        for number, toward in enumerate(corners):
            lane = jnp.where(direction == toward, lane % 4 + 4 * number, lane)
        put(index_ref, f, lane)
        put(index_ref, 3 + f, jnp.bitwise_and(jnp.right_shift(partner, 7), SUB - 1))
        put(index_ref, 6 + f, jnp.right_shift(partner, 10))
        put(index_ref, 9 + f, remote)
    sub_iota = lax.broadcasted_iota(jnp.int32, (SUB, LANES), 0)
    lane_iota = lax.broadcasted_iota(jnp.int32, (SUB, LANES), 1)

    def slots_to(choices, choice, half):
        rows_of = [
            jnp.broadcast_to(send_ref[0, 0, n : n + 1, lanes_of(half)], (SUB, LANES))
            for n in choices
        ]
        found = rows_of[0]
        for n, row in zip(choices[1:], rows_of[1:]):
            found = jnp.where(choice == n, row, found)
        return found

    straight_slots = None
    for number, toward in enumerate(straight):
        for half in range(2):
            row = slots_to((1, 6) if number < 2 else (3, 4), toward, half)
            straight_slots = (
                row
                if straight_slots is None
                else jnp.where(sub_iota == 2 * number + half, row, straight_slots)
            )
    corner_slots = None
    for number, toward in enumerate(corners):
        row = slots_to((0, 2, 5, 7), toward, 0)
        if number == 0:
            corner_slots = row
        else:
            moved = pltpu.roll(row, 4 * number, 1)
            corner_slots = jnp.where(lane_iota // 4 == number, moved, corner_slots)
    for d, slots in enumerate((straight_slots, corner_slots)):
        put(index_ref, 12 + d, jnp.bitwise_and(slots, LANES - 1))
        put(index_ref, 14 + d, jnp.bitwise_and(jnp.right_shift(slots, 7), SUB - 1))
        put(index_ref, 16 + d, jnp.right_shift(slots, 10))
    zone = zone_ref[...]
    zone_lane = jnp.bitwise_and(zone, LANES - 1)
    zone_block = jnp.right_shift(zone, 7)
    factors = []
    for ref in (friction_ref, conduct_ref):
        found = None
        for block in range(ref.shape[0]):
            got = take(spread(ref, block), zone_lane)
            found = got if block == 0 else jnp.where(zone_block == block, got, found)
        factors.append(found)
    area = area_ref[...]
    wet = wet_ref[...].astype(jnp.float32)
    kappa = factors[1] * soil_ref[...]
    wet_area = wet * area
    half_kappa_area = LATERAL * kappa * area
    put(stat_ref, WET_AREA, wet_area)
    put(stat_ref, KAPPA, kappa)
    put(stat_ref, HALF_KAPPA_AREA, half_kappa_area)
    put(stat_ref, WET, wet)
    put(stat_ref, ZONE_FRICTION, factors[0])
    put(stat_ref, ZONE_ID, zone.astype(jnp.float32))
    stat_ref[EDGE * SUB : (EDGE + 3) * SUB, :] = edge_ref[...]
    for k in range(sections):
        rows_to_tiles(
            lambda b: x_ref[k, :, lanes_of(b)].astype(jnp.float32), x_tiles, 16
        )
        squares = [tile(x_tiles, r) * tile(x_tiles, r) for r in range(12)]
        node_sum = [squares[i] + squares[3 + i] + squares[6 + i] + squares[9 + i] for i in range(3)]
        for f in range(3):
            first, second = FACE_NODES[f]
            put(table_ref, rows + 3 + 3 * k + f, node_sum[first] + node_sum[second])
        momentum = squares[3]
        for r in range(4, 9):
            momentum = momentum + squares[r]
        put(
            stat_ref,
            FRICTION_BASE + k,
            rough_ref[...] * jnp.sqrt(1.0 + momentum * (1.0 / 6.0)),
        )
    for f in range(3):
        put(table_ref, rows + f, tile(stat_ref, EDGE + f))
    put(table_ref, rows + 12, zone.astype(jnp.float32))
    for r in range(rows):
        put(table_ref, r, tile(cot_ref, r) * (wet_area if r < 12 else half_kappa_area))
    comps = rows // 3
    send_states(table_ref, 0, comps, index_ref, sent_ref)
    for d in range(2):
        lane, sublane, face = sent_index(index_ref, d)
        at = comps * 2 * SUB
        for group in range(4):
            sent_ref[d, at : at + SUB, :] = gather_by_face(
                table_ref, rows + 3 * group, lane, sublane, face
            )
            at += SUB
        sent_ref[d, at : at + SUB, :] = gather_tile(table_ref, rows + 12, lane, sublane)
    channels = comps * 2 + 5
    write_messages(sent_ref, 0, channels, (to_x1, to_x2, to_y1, to_y2), channels)


def corner_kernel(channels, x1, x2, old_y1, old_y2, *rest):
    y1, y2 = rest[-2:]
    rows = slice(channels, message_rows(channels))
    lane = corner_lane((corner_rows(channels), LANES))
    merged = jnp.where(lane < 8, x1[0, rows, :], x2[0, rows, :])
    y1[0, rows, :] = merged
    y2[0, rows, :] = merged


def local_states(src, first_comp, comps, index_ref, out_ref):
    def body(f, carry):
        lane, sublane, face = [tile_at(index_ref, n * 3 + f) for n in range(3)]
        for comp in range(comps):
            ends = gather_ends(src, (first_comp + comp) * 3, lane, sublane, face)
            for j in range(2):
                put_at(out_ref, f * comps * 2 + comp * 2 + j, ends[j])
        return carry

    lax.fori_loop(0, 3, body, 0)


def remote_states(received, first_row, channels, index_ref, local_ref, out_ref):
    def body(f, carry):
        lane, remote = tile_at(index_ref, f), tile_at(index_ref, 9 + f)
        for ch in range(channels):
            value = tile_at(local_ref, f * channels + ch)
            put_at(
                out_ref, f * channels + ch, received.fill(first_row + ch, lane, remote, value)
            )
        return carry

    lax.fori_loop(0, 3, body, 0)


def transposed_section(
    section, lam_ref, y_ref, outer_ref, stat_ref, fact_ref, in_ref, out_ref, volume_ref, emit
):
    rows = lam_ref.shape[0] // SUB
    channels = rows // 3 * 2
    layers = (rows - 12) // 3
    edge = [tile(stat_ref, EDGE + f) for f in range(3)]
    outer_edge = [tile(fact_ref, OUTER_EDGE + f) for f in range(3)]
    half_speed = [tile(fact_ref, HALF_SPEED + 3 * section + f) for f in range(3)]
    kappa = tile(stat_ref, KAPPA)
    wet = tile(stat_ref, WET)
    own = [tile(y_ref, r) for r in range(12)]
    result = []
    for r in range(12):
        total = volume_ref[0, r] * own[0]
        for q in range(1, 12):
            total = total + volume_ref[q, r] * own[q]
        result.append(total)
    for f in range(3):
        ends = FACE_NODES[f]
        inner = [edge[f] * own[(ch // 2) * 3 + ends[ch % 2]] for ch in range(8)]
        outer = [outer_edge[f] * tile(outer_ref, f * channels + ch) for ch in range(8)]
        for b in range(8):
            total = half_speed[f] * (inner[b] - outer[b])
            for a in range(8):
                total = total + in_ref[a, b] * inner[a] - out_ref[a, b] * outer[a]
            at = (b // 2) * 3 + ends[b % 2]
            result[at] = result[at] + total
    friction = tile(stat_ref, ZONE_FRICTION) * tile(stat_ref, FRICTION_BASE + section) * wet
    for r in range(3, 9):
        result[r] = result[r] - friction * tile(lam_ref, r)
    exchange = []
    for i in range(3):
        top = tile(lam_ref, 12 + i) - SALT_RETURN * wet * tile(lam_ref, 9 + i)
        exchange.append(kappa * top)
        result[9 + i] = result[9 + i] + exchange[i]
    for r in range(12):
        emit(r, result[r])
    for i in range(3):
        (f0, j0), (f1, j1) = NODE_FACES[i]
        both = edge[f0] + edge[f1]
        from_above = exchange[i]
        for layer in range(layers):
            r = 12 + layer * 3 + i
            value = (
                outer_edge[f0] * tile(outer_ref, f0 * channels + 8 + layer * 2 + j0)
                + outer_edge[f1] * tile(outer_ref, f1 * channels + 8 + layer * 2 + j1)
                - both * tile(y_ref, r)
                - from_above
            )
            if layer + 1 < layers:
                from_above = kappa * (tile(lam_ref, r + 3) - tile(lam_ref, r))
                value = value + from_above
            emit(r, value)


def own_gradients(section, weight, lam_ref, y_ref, x_tiles, stat_ref):
    rows = lam_ref.shape[0] // SUB
    layers = (rows - 12) // 3
    wet = tile(stat_ref, WET)
    kappa = tile(stat_ref, KAPPA)
    momentum = tile(lam_ref, 3) * tile(x_tiles, 3)
    for r in range(4, 9):
        momentum = momentum + tile(lam_ref, r) * tile(x_tiles, r)
    friction = -(weight * wet * tile(stat_ref, FRICTION_BASE + section)) * momentum
    vertical = None
    lateral = None
    for i in range(3):
        (f0, _), (f1, _) = NODE_FACES[i]
        top = tile(lam_ref, 12 + i) - SALT_RETURN * wet * tile(lam_ref, 9 + i)
        total = top * (tile(x_tiles, 9 + i) - tile(x_tiles, 12 + i))
        dots = None
        for layer in range(layers):
            r = 12 + layer * 3 + i
            term = tile(y_ref, r) * tile(x_tiles, r)
            dots = term if dots is None else dots + term
            if layer + 1 < layers:
                total = total + (tile(lam_ref, r + 3) - tile(lam_ref, r)) * (
                    tile(x_tiles, r) - tile(x_tiles, r + 3)
                )
        side = (tile(stat_ref, EDGE + f0) + tile(stat_ref, EDGE + f1)) * dots
        vertical = total if vertical is None else vertical + total
        lateral = side if lateral is None else lateral + side
    return friction, weight * (kappa * vertical - lateral)


def outer_gradients(weight, outer_ref, x_tiles, fact_ref):
    channels = outer_ref.shape[0] // SUB // 3
    values = []
    for f in range(3):
        total = None
        for ch in range(8, channels):
            row = 12 + (ch - 8) // 2 * 3 + FACE_NODES[f][ch % 2]
            term = tile(outer_ref, f * channels + ch) * tile(x_tiles, row)
            total = term if total is None else total + term
        values.append(weight * tile(fact_ref, OUTER_EDGE + f) * total)
    return values


def x_to_tiles(x_ref, section, x_tiles):
    rows = x_ref.shape[3]
    rows_to_tiles(
        lambda b: x_ref[section, 0, 0, :, lanes_of(b)].astype(jnp.float32), x_tiles, rows
    )


def local_two_kernel(
    cot_ref, table_ref, stat_ref, index_ref, x_ref, outer_ref, near_ref, term_ref, x_tiles
):
    rows = cot_ref.shape[0] // SUB
    local_states(table_ref, 0, rows // 3, index_ref, outer_ref)
    for f in range(3):
        lane, sublane, face = [tile(index_ref, n * 3 + f) for n in range(3)]
        for group in range(4):
            value = gather_by_face(table_ref, rows + 3 * group, lane, sublane, face)
            put(near_ref, f * 5 + group, value)
        put(near_ref, f * 5 + 4, gather_tile(table_ref, rows + 12, lane, sublane))
    x_to_tiles(x_ref, 2, x_tiles)
    friction, conduct = own_gradients(
        2, TIME_STEP * 2.0 / 3.0, cot_ref, table_ref, x_tiles, stat_ref
    )
    put(term_ref, 0, friction)
    put(term_ref, 1, conduct)


def local_x_kernel(index_ref, x_ref, x_outer_ref, sent_ref, x_tiles):
    comps = x_ref.shape[3] // 3
    x_to_tiles(x_ref, 0, x_tiles)
    local_states(x_tiles, 4, comps - 4, index_ref, x_outer_ref)
    send_states(x_tiles, 4, comps - 4, index_ref, sent_ref)


def second_kernel(
    cot_ref,
    table_ref,
    stat_ref,
    index_ref,
    near_outer_ref,
    near_ref,
    x_sent_ref,
    in_ref,
    out_ref,
    volume_ref,
    from_x1,
    from_x2,
    from_y1,
    from_y2,
    lam_ref,
    y_ref,
    fact_ref,
    outer_ref,
    to_x1,
    to_x2,
    to_y1,
    to_y2,
    sent_ref,
    corner_ref,
):
    rows = cot_ref.shape[0] // SUB
    comps = rows // 3
    channels = comps * 2
    received = Received((from_x1, from_x2, from_y1, from_y2), channels + 5, corner_ref)
    remote_states(received, 0, channels, index_ref, near_outer_ref, outer_ref)
    for f in range(3):
        lane, remote = tile(index_ref, f), tile(index_ref, 9 + f)
        for group in range(5):
            value = received.fill(channels + group, lane, remote, tile(near_ref, f * 5 + group))
            if group == 0:
                put(fact_ref, OUTER_EDGE + f, value)
            elif group == 4:
                put(fact_ref, OUTER_ZONE + f, value)
            else:
                both = tile(table_ref, rows + 3 * group + f) + value
                put(
                    fact_ref,
                    HALF_SPEED + 3 * (group - 1) + f,
                    0.5 * jnp.sqrt(1.0 + (0.25 / 8.0) * both),
                )
    wet_area = tile(stat_ref, WET_AREA)
    half_kappa_area = tile(stat_ref, HALF_KAPPA_AREA)

    def emit(r, value):
        lam = (2.0 / 3.0) * (tile(cot_ref, r) + TIME_STEP * value)
        put(lam_ref, r, lam)
        put(y_ref, r, lam * (wet_area if r < 12 else half_kappa_area))

    transposed_section(
        2, cot_ref, table_ref, outer_ref, stat_ref, fact_ref, in_ref, out_ref, volume_ref, emit
    )
    send_states(y_ref, 0, comps, index_ref, sent_ref)
    outs = (to_x1, to_x2, to_y1, to_y2)
    write_messages(x_sent_ref, 0, channels - 8, outs, X_ROWS + channels)
    write_messages(sent_ref, X_ROWS, channels, outs, X_ROWS + channels)


def local_one_kernel(
    lam_ref,
    y_ref,
    stat_ref,
    index_ref,
    fact_ref,
    old_outer_ref,
    old_term_ref,
    x_ref,
    outer_ref,
    term_ref,
    x_tiles,
):
    local_states(y_ref, 0, lam_ref.shape[0] // SUB // 3, index_ref, outer_ref)
    x_to_tiles(x_ref, 2, x_tiles)
    weight = TIME_STEP * 2.0 / 3.0
    for f, value in enumerate(outer_gradients(weight, old_outer_ref, x_tiles, fact_ref)):
        put(term_ref, 2 + f, value)
    x_to_tiles(x_ref, 1, x_tiles)
    terms = own_gradients(1, TIME_STEP * 0.25, lam_ref, y_ref, x_tiles, stat_ref)
    for n in range(2):
        put(term_ref, n, tile(old_term_ref, n) + terms[n])


def first_kernel(
    cot_ref,
    lam_ref,
    y_ref,
    stat_ref,
    index_ref,
    fact_ref,
    near_outer_ref,
    in_ref,
    out_ref,
    volume_ref,
    from_x1,
    from_x2,
    from_y1,
    from_y2,
    base_ref,
    next_ref,
    next_y_ref,
    outer_ref,
    to_x1,
    to_x2,
    to_y1,
    to_y2,
    sent_ref,
    corner_ref,
):
    comps = lam_ref.shape[0] // SUB // 3
    channels = comps * 2
    received = Received((from_x1, from_x2, from_y1, from_y2), X_ROWS + channels, corner_ref)
    remote_states(received, X_ROWS, channels, index_ref, near_outer_ref, outer_ref)
    wet_area = tile(stat_ref, WET_AREA)
    half_kappa_area = tile(stat_ref, HALF_KAPPA_AREA)

    def emit(r, value):
        old = tile(lam_ref, r)
        lam = 0.25 * (old + TIME_STEP * value)
        put(next_ref, r, lam)
        put(next_y_ref, r, lam * (wet_area if r < 12 else half_kappa_area))
        put(base_ref, r, (1.0 / 3.0) * tile(cot_ref, r) + 0.75 * old + lam)

    transposed_section(
        1, lam_ref, y_ref, outer_ref, stat_ref, fact_ref, in_ref, out_ref, volume_ref, emit
    )
    send_states(next_y_ref, 0, comps, index_ref, sent_ref)
    write_messages(sent_ref, 0, channels, (to_x1, to_x2, to_y1, to_y2), channels)


def zone_kernel(
    lam_ref,
    y_ref,
    stat_ref,
    index_ref,
    fact_ref,
    old_outer_ref,
    term_ref,
    x_ref,
    x_near_ref,
    conduct_ref,
    from_x1,
    from_x2,
    from_y1,
    from_y2,
    out_ref,
    x_outer_ref,
    x_tiles,
    corner_ref,
):
    rows = lam_ref.shape[0] // SUB
    channels = rows // 3 * 2
    x_channels = channels - 8
    received = Received((from_x1, from_x2, from_y1, from_y2), X_ROWS + channels, corner_ref)
    remote_states(received, 0, x_channels, index_ref, x_near_ref, x_outer_ref)
    x_to_tiles(x_ref, 1, x_tiles)
    outer_terms = outer_gradients(TIME_STEP * 0.25, old_outer_ref, x_tiles, fact_ref)
    outer_terms = [tile(term_ref, 2 + f) + outer_terms[f] for f in range(3)]
    x_to_tiles(x_ref, 0, x_tiles)
    friction_term, conduct_term = own_gradients(
        0, TIME_STEP, lam_ref, y_ref, x_tiles, stat_ref
    )
    friction_term = friction_term + tile(term_ref, 0)
    conduct_term = conduct_term + tile(term_ref, 1)
    for f in range(3):
        total = None
        for ch in range(x_channels):
            row = 12 + ch // 2 * 3 + FACE_NODES[f][ch % 2]
            term = tile(x_outer_ref, f * x_channels + ch) * tile(y_ref, row)
            total = term if total is None else total + term
        conduct_term = conduct_term + TIME_STEP * tile(stat_ref, EDGE + f) * total

    zones = out_ref.shape[2]
    zone_iota = lax.broadcasted_iota(jnp.int32, (zones, LANES), 0).astype(jnp.float32)
    sub_iota = lax.broadcasted_iota(jnp.int32, (SUB, zones), 0)

    def thirds(value):
        high = value.astype(jnp.bfloat16).astype(jnp.float32)
        rest = value - high
        middle = rest.astype(jnp.bfloat16).astype(jnp.float32)
        return [high, middle, rest - middle]

    def by_zone(values, zone_of, zone_row):
        pieces = sum([thirds(value) for value in values], [])
        left = jnp.concatenate(pieces, axis=0).astype(jnp.bfloat16)
        totals = [jnp.zeros((SUB, zones), jnp.float32) for _ in values]
        for sub in range(SUB):
            line = zone_of[pl.ds(zone_row * SUB + sub, 1), :]
            hot = (jnp.broadcast_to(line, (zones, LANES)) == zone_iota).astype(jnp.float32)
            dots = lax.dot_general(
                left,
                hot.astype(jnp.bfloat16),
                (((1,), (1,)), ((), ())),
                preferred_element_type=jnp.float32,
            )
            for n in range(len(values)):
                at = n * 3 * SUB
                three = dots[at : at + SUB] + dots[at + SUB : at + 2 * SUB]
                three = three + dots[at + 2 * SUB : at + 3 * SUB]
                totals[n] = totals[n] + jnp.where(sub_iota == sub, three, 0.0)
        return totals

    friction, conduct = by_zone([friction_term, conduct_term], stat_ref, ZONE_ID)
    for f in range(3):
        conduct = conduct + by_zone([outer_terms[f]], fact_ref, OUTER_ZONE + f)[0]
    friction = GRAD_WEIGHT * jnp.sum(friction, axis=0, keepdims=True)
    conduct = GRAD_WEIGHT * jnp.sum(conduct, axis=0, keepdims=True) / conduct_ref[...]
    for device in range(out_ref.shape[0]):
        out_ref[device, 0:1, :] = friction
        out_ref[device, 1:2, :] = conduct


def local_zero_kernel(y_ref, index_ref, outer_ref):
    local_states(y_ref, 0, y_ref.shape[0] // SUB // 3, index_ref, outer_ref)


def last_kernel(
    base_ref,
    lam_ref,
    y_ref,
    stat_ref,
    index_ref,
    fact_ref,
    near_outer_ref,
    in_ref,
    out_ref,
    volume_ref,
    from_x1,
    from_x2,
    from_y1,
    from_y2,
    adjoint_ref,
    last_ref,
    outer_ref,
    corner_ref,
):
    rows = lam_ref.shape[0] // SUB
    channels = rows // 3 * 2
    received = Received((from_x1, from_x2, from_y1, from_y2), channels, corner_ref)
    remote_states(received, 0, channels, index_ref, near_outer_ref, outer_ref)

    def emit(r, value):
        put(adjoint_ref, r, tile(base_ref, r) + TIME_STEP * value)

    transposed_section(
        0, lam_ref, y_ref, outer_ref, stat_ref, fact_ref, in_ref, out_ref, volume_ref, emit
    )
    last_ref[...] = tile(adjoint_ref, rows - 1)


def total_kernel(zone_ref, adjoint_ref, grads_ref):
    grads_ref[...] = jnp.sum(zone_ref[...], axis=0)


def exchange(channels, messages, ahead=()):
    x1, x2, y1, y2 = messages
    x1, x2 = swapped(x1, "gx", 0), swapped(x2, "gx", 1)
    y1, y2 = call(
        functools.partial(corner_kernel, channels),
        "corners",
        [jax.ShapeDtypeStruct(y1.shape, y1.dtype)] * 2,
        [],
        [x1, x2, y1, y2, *ahead],
        aliases={2: 0, 3: 1},
    )
    return x1, x2, swapped(y1, "gy", 0), swapped(y2, "gy", 1)


def call(kernel, name, outs, scratch, operands, scalars=(), far=False, aliases={}):
    in_memory = pl.BlockSpec(memory_space=pltpu.VMEM)
    in_scalar = pl.BlockSpec(memory_space=pltpu.SMEM)
    in_place = pl.BlockSpec(memory_space=pl.ANY)
    return pl.pallas_call(
        kernel,
        in_specs=[
            in_place if far else in_scalar if n in scalars else in_memory
            for n in range(len(operands))
        ],
        out_specs=[in_memory] * len(outs),
        out_shape=outs,
        scratch_shapes=scratch,
        input_output_aliases=aliases,
        compiler_params=pltpu.CompilerParams(
            vmem_limit_bytes=(FAR_VMEM if far else NEAR_VMEM) * 1024 * 1024
        ),
        name=name,
    )(*operands)


def local(
    cotangent,
    section_states,
    inverse_area,
    edge_length,
    roughness,
    soil_conductance,
    zone_friction,
    zone_conductivity,
    wet_mask,
    element_zone,
    send_face,
    send_count,
    face_partner,
    volume_matrix,
    flux_in,
    flux_out,
):
    rows = cotangent.shape[2]
    channels = rows // 3 * 2
    zones = zone_friction.shape[0]
    slots = send_face.shape[3]
    devices = lax.axis_size("gx") * lax.axis_size("gy")
    f32 = jnp.float32

    def tiles(count, dtype=f32):
        return jax.ShapeDtypeStruct((count * SUB, LANES), dtype)

    def tile_scratch(count, dtype=f32):
        return pltpu.VMEM((count * SUB, LANES), dtype)

    def messages(count):
        return [jax.ShapeDtypeStruct((slots // LANES, message_rows(count), LANES), f32)] * 4

    def sent_scratch(count):
        return pltpu.VMEM(sent_shape(count), f32)

    def sent_shape(count):
        return (slots // LANES, corner_rows(count) * SUB * SUB, LANES)

    corner_scratch = pltpu.VMEM((SUB, LANES), f32)

    square = lambda one: one.reshape(SUB, LANES)
    cot = cotangent.reshape(rows * SUB, LANES)
    table, stat, index, *to_send = call(
        prepare_kernel,
        "prepare",
        [tiles(rows + 13), tiles(STAT_ROWS), tiles(INDEX_ROWS, jnp.int32)]
        + messages(channels + 5),
        [tile_scratch(16), sent_scratch(channels + 5)]
        + [
            tile_scratch(3, jnp.int32),
            pltpu.VMEM(send_face.shape, jnp.int32),
            tile_scratch(rows),
            pltpu.VMEM((section_states.shape[0], 16, SUB * LANES), section_states.dtype),
            tile_scratch(1),
            tile_scratch(3),
            tile_scratch(1),
            tile_scratch(1),
            pltpu.VMEM((zones // LANES, LANES), f32),
            pltpu.VMEM((zones // LANES, LANES), f32),
            tile_scratch(1, jnp.int32),
            tile_scratch(1, jnp.int32),
            pltpu.SemaphoreType.DMA((12,)),
        ],
        [
            cot,
            section_states,
            square(inverse_area),
            edge_length.reshape(3 * SUB, LANES),
            square(roughness),
            square(soil_conductance),
            zone_friction.reshape(-1, LANES),
            zone_conductivity.reshape(-1, LANES),
            square(wet_mask),
            square(element_zone),
            send_face,
            face_partner.reshape(3 * SUB, LANES),
        ],
        far=True,
    )
    matrices = [flux_in, flux_out, volume_matrix]
    near_outer, near, term = call(
        local_two_kernel,
        "local_two",
        [tiles(3 * channels), tiles(15), tiles(2)],
        [tile_scratch(rows)],
        [cot, table, stat, index, section_states],
    )
    x_near, x_sent = call(
        local_x_kernel,
        "local_x",
        [
            tiles(3 * (channels - 8)),
            jax.ShapeDtypeStruct(sent_shape(channels - 8), f32),
        ],
        [tile_scratch(rows)],
        [index, section_states],
    )
    received = exchange(channels + 5, to_send, [term])
    lam, y, fact, outer, *to_send = call(
        second_kernel,
        "section_two",
        [tiles(rows), tiles(rows), tiles(FACT_ROWS), tiles(3 * channels)]
        + messages(X_ROWS + channels),
        [sent_scratch(channels), corner_scratch],
        [cot, table, stat, index, near_outer, near, x_sent, *matrices, *received],
        (7, 8, 9),
    )
    near_outer, term = call(
        local_one_kernel,
        "local_one",
        [tiles(3 * channels), tiles(5)],
        [tile_scratch(rows)],
        [lam, y, stat, index, fact, outer, term, section_states],
    )
    received = exchange(X_ROWS + channels, to_send, [term])
    base, lam, y, outer, *to_send = call(
        first_kernel,
        "section_one",
        [tiles(rows), tiles(rows), tiles(rows), tiles(3 * channels)] + messages(channels),
        [sent_scratch(channels), corner_scratch],
        [cot, lam, y, stat, index, fact, near_outer, *matrices, *received],
        (7, 8, 9),
    )
    (zone_terms,) = call(
        zone_kernel,
        "zone_sums",
        [jax.ShapeDtypeStruct((devices, 2, zones), f32)],
        [tile_scratch(3 * (channels - 8)), tile_scratch(rows), corner_scratch],
        [
            lam,
            y,
            stat,
            index,
            fact,
            outer,
            term,
            section_states,
            x_near,
            zone_conductivity.reshape(1, zones),
            *received,
        ],
    )
    received = exchange(channels, to_send, [zone_terms])
    all_terms = lax.all_to_all(zone_terms, ("gx", "gy"), 0, 0)
    (near_outer,) = call(
        local_zero_kernel, "local_zero", [tiles(3 * channels)], [], [y, index]
    )
    adjoint, last = call(
        last_kernel,
        "section_zero",
        [tiles(rows), tiles(1)],
        [tile_scratch(3 * channels), corner_scratch],
        [base, lam, y, stat, index, fact, near_outer, *matrices, *received],
        (7, 8, 9),
    )
    (zone_grads,) = call(
        total_kernel,
        "zone_total",
        [jax.ShapeDtypeStruct((2, zones), f32)],
        [],
        [all_terms, last],
    )
    return adjoint.reshape(cotangent.shape), zone_grads


def solution(mesh):
    placed = (
        P("gx", "gy", None, None),
        P(None, "gx", "gy", None, None),
        P("gx", "gy", None),
        P("gx", "gy", None, None),
        P("gx", "gy", None),
        P("gx", "gy", None),
        P(),
        P(),
        P("gx", "gy", None),
        P("gx", "gy", None),
        P("gx", "gy", None, None),
        P("gx", "gy", None),
        P("gx", "gy", None, None),
        P(),
        P(),
        P(),
    )
    return jax.shard_map(
        local,
        mesh=mesh,
        in_specs=placed,
        out_specs=(P("gx", "gy", None, None), P()),
        check_vma=False,
    )
```

```python
import functools
import jax
import jax.numpy as jnp
from jax import lax
from jax.experimental import pallas as pl
from jax.experimental.pallas import tpu as pltpu
from jax.sharding import PartitionSpec as P

TIME_STEP = 0.2
SALT_RETURN = 0.5
LATERAL = 0.5
GRAD_WEIGHT = 1.0 / 64.0
FACE_NODES = ((1, 2), (2, 0), (0, 1))
NODE_FACES = (((1, 1), (2, 0)), ((0, 0), (2, 1)), ((0, 1), (1, 0)))
SUB = 8
LANES = 128


WET_AREA, KAPPA, HALF_KAPPA_AREA, WET, EDGE, FRICTION_BASE, ZONE_FRICTION, ZONE_ID = (
    0,
    1,
    2,
    3,
    4,
    7,
    10,
    11,
)
CONDUCTIVITY = 12
STAT_ROWS = 13
NEAR_VMEM, FAR_VMEM = 32, 60
OUTER_EDGE, OUTER_ZONE, HALF_SPEED = 0, 3, 6
FACT_ROWS = 15
X_ROWS = 24
CORNER_LANES = 16
CORNER_BLOCK = 8


def swapped(x, axis, first):
    peers = lax.axis_size(axis)
    lows = range(first, peers - 1, 2)
    return lax.ppermute(x, axis, [(i, i + 1) for i in lows] + [(i + 1, i) for i in lows])


def tile(ref, row):
    return ref[row * SUB : (row + 1) * SUB, :]


def put(ref, row, value):
    ref[row * SUB : (row + 1) * SUB, :] = value


def take(row, lane_index):
    return jnp.take_along_axis(row, lane_index, axis=1, mode="promise_in_bounds")


def spread(ref, row):
    return jnp.broadcast_to(ref[pl.ds(row, 1), :], (SUB, LANES))


def rows_to_tiles(read, tiles_ref, count):
    for block in range(SUB):
        tiles_ref[pl.ds(block, count, stride=SUB), :] = read(block)


def lanes_of(block):
    return slice(block * LANES, (block + 1) * LANES)


def gather_tile(src, row, lane_index, sublane_index):
    found = take(spread(src, row * SUB), lane_index)
    for sub in range(1, SUB):
        got = take(spread(src, row * SUB + sub), lane_index)
        found = jnp.where(sublane_index == sub, got, found)
    return found


def pick(face, for_zero, for_one, for_two):
    return jnp.where(face == 0, for_zero, jnp.where(face == 1, for_one, for_two))


def gather_ends(src, row, lane_index, sublane_index, face):
    n0, n1, n2 = [gather_tile(src, row + i, lane_index, sublane_index) for i in range(3)]
    return pick(face, n1, n2, n0), pick(face, n2, n0, n1)


def gather_by_face(src, row, lane_index, sublane_index, face):
    return pick(
        face, *[gather_tile(src, row + i, lane_index, sublane_index) for i in range(3)]
    )


def corner_rows(channels):
    return (channels * CORNER_LANES + LANES - 1) // LANES


def message_rows(channels):
    return channels + corner_rows(channels)


def corner_lane(shape):
    return lax.broadcasted_iota(jnp.int32, shape, 1) % CORNER_LANES


class Received:
    def __init__(self, messages, channels, corner_ref):
        _, _, y1, y2 = messages
        self.mains = messages
        self.corner_ref = corner_ref
        rows = slice(channels, message_rows(channels))
        count = corner_rows(channels)
        lane = corner_lane((count, LANES))
        corner_ref[0:count, :] = jnp.where(
            jnp.bitwise_and(lane, 4) == 0, y1[0, rows, :], y2[0, rows, :]
        )

    def fill(self, row, lane_index, remote_index, value):
        for number, ref in enumerate(self.mains):
            for half in range(2):
                got = take(spread(ref.at[half], row), lane_index)
                value = jnp.where(remote_index == 2 * number + half, got, value)
        channels_a_row = LANES // CORNER_LANES
        lane = lane_index + row % channels_a_row * CORNER_LANES
        line = spread(self.corner_ref, row // channels_a_row)
        got = take(line, jnp.bitwise_and(lane, LANES - 1))
        return jnp.where(remote_index == CORNER_BLOCK, got, value)


INDEX_ROWS = 18
MATRIX_ROWS = 4


def plan_rows(rows):
    return STAT_ROWS + INDEX_ROWS + MATRIX_ROWS + rows + 13


def plan_parts(plan_ref):
    parts, at = [], 0
    for count in (STAT_ROWS, INDEX_ROWS, MATRIX_ROWS):
        parts.append(plan_ref.at[at * SUB : (at + count) * SUB])
        at += count
    return (*parts, plan_ref.at[at * SUB :])


def tile_at(ref, row):
    return ref[pl.ds(pl.multiple_of(row * SUB, SUB), SUB), :]


def index_at(ref, row):
    return tile_at(ref, row).astype(jnp.int32)


def index_of(ref, row):
    return tile(ref, row).astype(jnp.int32)


def put_index(ref, row, value):
    put(ref, row, value.astype(jnp.float32))


def load_matrices(plan_ref, matrix_ref, sem):
    copy = pltpu.make_async_copy(plan_parts(plan_ref)[2], matrix_ref, sem.at[0])
    copy.start()
    return copy


def put_at(ref, row, value):
    ref[pl.ds(pl.multiple_of(row * SUB, SUB), SUB), :] = value


class Sender:
    def __init__(self, index_ref, sent_ref, packed_ref):
        self.straight = [index_of(index_ref, 12 + 2 * n) for n in range(3)]
        self.lane, sublane, self.face = [index_of(index_ref, 13 + 2 * n) for n in range(3)]
        sub = lax.broadcasted_iota(jnp.int32, (SUB, LANES), 0)
        slot = lax.broadcasted_iota(jnp.int32, (SUB, LANES), 1)
        self.own = (sub == sublane) & (slot < CORNER_LANES)
        self.sent_ref, self.packed_ref = sent_ref, packed_ref
        self.group = None

    def corner(self, src, row):
        return jnp.where(self.own, take(tile(src, row), self.lane), 0.0)

    def put(self, channel, value, corner):
        put(self.sent_ref, channel, value)
        place = channel % SUB
        moved = corner if place == 0 else pltpu.roll(corner, CORNER_LANES * place, 1)
        self.group = moved if place == 0 else self.group + moved
        if place == SUB - 1:
            self.flush(channel)

    def flush(self, channel):
        at = channel // SUB
        self.packed_ref[at : at + 1, :] = jnp.sum(self.group, axis=0, keepdims=True)

    def states(self, src, first_comp, comps):
        for comp in range(comps):
            row = (first_comp + comp) * 3
            ends = gather_ends(src, row, *self.straight)
            n0, n1, n2 = [self.corner(src, row + i) for i in range(3)]
            corners = pick(self.face, n1, n2, n0), pick(self.face, n2, n0, n1)
            for j in range(2):
                self.put(comp * 2 + j, ends[j], corners[j])

    def by_face(self, src, row, channel):
        corner = pick(self.face, *[self.corner(src, row + i) for i in range(3)])
        self.put(channel, gather_by_face(src, row, *self.straight), corner)

    def by_element(self, src, row, channel):
        self.put(channel, gather_tile(src, row, *self.straight[:2]), self.corner(src, row))


def write_messages(sent_ref, packed_ref, first, channels, outs, total):
    for role, out in enumerate(outs):
        for half in range(2):
            out[half, first : first + channels, :] = sent_ref[
                pl.ds(role * 2 + half, channels, stride=SUB), :
            ]
    count, at = corner_rows(channels), total + first // SUB
    for out in outs[:2]:
        out[0, at : at + count, :] = packed_ref[0:count, :]


def prepare_kernel(
    cot_ref,
    x_ref,
    area_ref,
    edge_ref,
    rough_ref,
    soil_ref,
    friction_ref,
    conduct_ref,
    wet_ref,
    zone_ref,
    send_ref,
    partner_ref,
    in_ref,
    out_ref,
    volume_ref,
    plan_ref,
    to_x1,
    to_x2,
    to_y1,
    to_y2,
    x_tiles,
    sent_ref,
    packed_ref,
    *fetched,
):
    *fetched, sems = fetched
    stat_ref, index_ref, matrix_ref, table_ref = plan_parts(plan_ref)
    sources = [
        partner_ref,
        send_ref,
        cot_ref,
        x_ref.at[:, 0, 0, 0:16],
        area_ref,
        edge_ref,
        rough_ref,
        soil_ref,
        friction_ref,
        conduct_ref,
        wet_ref,
        zone_ref,
        in_ref,
        out_ref,
        volume_ref,
    ]
    copies = [
        pltpu.make_async_copy(source, target, sems.at[n])
        for n, (source, target) in enumerate(zip(sources, fetched))
    ]
    for copy in copies:
        copy.start()
    for copy in copies:
        copy.wait()
    (
        partner_ref,
        send_ref,
        cot_ref,
        x_ref,
        area_ref,
        edge_ref,
        rough_ref,
        soil_ref,
        friction_ref,
        conduct_ref,
        wet_ref,
        zone_ref,
        in_ref,
        out_ref,
        volume_ref,
    ) = fetched
    matrix_ref[0:8, 0:8] = in_ref[...]
    matrix_ref[8:16, 0:8] = out_ref[...]
    matrix_ref[16:28, 0:12] = volume_ref[...]
    rows = cot_ref.shape[0] // SUB
    sections = x_ref.shape[0]
    odd_a, odd_b = lax.axis_index("gx") % 2, lax.axis_index("gy") % 2
    straight = (6 - 5 * odd_a, 1 + 5 * odd_a, 4 - odd_b, 3 + odd_b)
    right, up = 1 - odd_a, 1 - odd_b
    corners = (
        5 * right + 2 * up,
        5 * right + 2 - 2 * up,
        5 - 5 * right + 2 * up,
        7 - 5 * right - 2 * up,
    )
    face_total = 3 * SUB * LANES
    for f in range(3):
        partner = tile(partner_ref, f)
        beyond = partner - face_total
        direction = jnp.right_shift(beyond, 8)
        half = jnp.bitwise_and(jnp.right_shift(beyond, 7), 1)
        lane = jnp.bitwise_and(partner, LANES - 1)
        remote = jnp.where(beyond >= 0, CORNER_BLOCK, -1)
        for number, toward in enumerate(straight):
            remote = jnp.where(direction == toward, 2 * number + half, remote)
        for number, toward in enumerate(corners):
            lane = jnp.where(direction == toward, lane % 4 + 4 * number, lane)
        put_index(index_ref, f, lane)
        put_index(index_ref, 3 + f, jnp.bitwise_and(jnp.right_shift(partner, 7), SUB - 1))
        put_index(index_ref, 6 + f, jnp.right_shift(partner, 10))
        put_index(index_ref, 9 + f, remote)
    sub_iota = lax.broadcasted_iota(jnp.int32, (SUB, LANES), 0)
    lane_iota = lax.broadcasted_iota(jnp.int32, (SUB, LANES), 1)

    def slots_to(choices, choice, half):
        rows_of = [
            jnp.broadcast_to(send_ref[0, 0, n : n + 1, lanes_of(half)], (SUB, LANES))
            for n in choices
        ]
        found = rows_of[0]
        for n, row in zip(choices[1:], rows_of[1:]):
            found = jnp.where(choice == n, row, found)
        return found

    straight_slots = None
    for number, toward in enumerate(straight):
        for half in range(2):
            row = slots_to((1, 6) if number < 2 else (3, 4), toward, half)
            straight_slots = (
                row
                if straight_slots is None
                else jnp.where(sub_iota == 2 * number + half, row, straight_slots)
            )
    corner_slots = None
    for number, toward in enumerate(corners):
        row = slots_to((0, 2, 5, 7), toward, 0)
        if number == 0:
            corner_slots = row
        else:
            moved = pltpu.roll(row, 4 * number, 1)
            corner_slots = jnp.where(lane_iota // 4 == number, moved, corner_slots)
    for d, slots in enumerate((straight_slots, corner_slots)):
        put_index(index_ref, 12 + d, jnp.bitwise_and(slots, LANES - 1))
        put_index(index_ref, 14 + d, jnp.bitwise_and(jnp.right_shift(slots, 7), SUB - 1))
        put_index(index_ref, 16 + d, jnp.right_shift(slots, 10))
    zone = zone_ref[...]
    zone_lane = jnp.bitwise_and(zone, LANES - 1)
    zone_block = jnp.right_shift(zone, 7)
    factors = []
    for ref in (friction_ref, conduct_ref):
        found = None
        for block in range(ref.shape[0]):
            got = take(spread(ref, block), zone_lane)
            found = got if block == 0 else jnp.where(zone_block == block, got, found)
        factors.append(found)
    area = area_ref[...]
    wet = wet_ref[...].astype(jnp.float32)
    kappa = factors[1] * soil_ref[...]
    wet_area = wet * area
    half_kappa_area = LATERAL * kappa * area
    put(stat_ref, WET_AREA, wet_area)
    put(stat_ref, KAPPA, kappa)
    put(stat_ref, HALF_KAPPA_AREA, half_kappa_area)
    put(stat_ref, WET, wet)
    put(stat_ref, ZONE_FRICTION, factors[0])
    put(stat_ref, ZONE_ID, zone.astype(jnp.float32))
    stat_ref[CONDUCTIVITY * SUB : CONDUCTIVITY * SUB + conduct_ref.shape[0], :] = conduct_ref[...]
    stat_ref[EDGE * SUB : (EDGE + 3) * SUB, :] = edge_ref[...]
    for k in range(sections):
        rows_to_tiles(
            lambda b: x_ref[k, :, lanes_of(b)].astype(jnp.float32), x_tiles, 16
        )
        squares = [tile(x_tiles, r) * tile(x_tiles, r) for r in range(12)]
        node_sum = [squares[i] + squares[3 + i] + squares[6 + i] + squares[9 + i] for i in range(3)]
        for f in range(3):
            first, second = FACE_NODES[f]
            put(table_ref, rows + 3 + 3 * k + f, node_sum[first] + node_sum[second])
        momentum = squares[3]
        for r in range(4, 9):
            momentum = momentum + squares[r]
        put(
            stat_ref,
            FRICTION_BASE + k,
            rough_ref[...] * jnp.sqrt(1.0 + momentum * (1.0 / 6.0)),
        )
    for f in range(3):
        put(table_ref, rows + f, tile(stat_ref, EDGE + f))
    put(table_ref, rows + 12, zone.astype(jnp.float32))
    for r in range(rows):
        put(table_ref, r, tile(cot_ref, r) * (wet_area if r < 12 else half_kappa_area))
    comps = rows // 3
    channels = comps * 2 + 5
    sender = Sender(index_ref, sent_ref, packed_ref)
    sender.states(table_ref, 0, comps)
    for group in range(4):
        sender.by_face(table_ref, rows + 3 * group, comps * 2 + group)
    sender.by_element(table_ref, rows + 12, channels - 1)
    sender.flush(channels - 1)
    write_messages(sent_ref, packed_ref, 0, channels, (to_x1, to_x2, to_y1, to_y2), channels)


def corner_kernel(channels, x1, x2, old_y1, old_y2, *rest):
    y1, y2 = rest[1:3]
    rows = slice(channels, message_rows(channels))
    lane = corner_lane((corner_rows(channels), LANES))
    merged = jnp.where(lane < 8, x1[0, rows, :], x2[0, rows, :])
    y1[0, rows, :] = merged
    y2[0, rows, :] = merged


def local_states(src, first_comp, comps, index_ref, out_ref):
    def body(f, carry):
        lane, sublane, face = [index_at(index_ref, n * 3 + f) for n in range(3)]
        for comp in range(comps):
            ends = gather_ends(src, (first_comp + comp) * 3, lane, sublane, face)
            for j in range(2):
                put_at(out_ref, f * comps * 2 + comp * 2 + j, ends[j])
        return carry

    lax.fori_loop(0, 3, body, 0)


def remote_states(received, first_row, channels, index_ref, local_ref, out_ref):
    def body(f, carry):
        lane, remote = index_at(index_ref, f), index_at(index_ref, 9 + f)
        for ch in range(channels):
            value = tile_at(local_ref, f * channels + ch)
            put_at(
                out_ref, f * channels + ch, received.fill(first_row + ch, lane, remote, value)
            )
        return carry

    lax.fori_loop(0, 3, body, 0)


def transposed_section(
    section, lam_ref, y_ref, outer_ref, stat_ref, fact_ref, matrix_ref, emit
):
    rows = lam_ref.shape[0] // SUB
    channels = rows // 3 * 2
    layers = (rows - 12) // 3
    edge = [tile(stat_ref, EDGE + f) for f in range(3)]
    outer_edge = [tile(fact_ref, OUTER_EDGE + f) for f in range(3)]
    half_speed = [tile(fact_ref, HALF_SPEED + 3 * section + f) for f in range(3)]
    kappa = tile(stat_ref, KAPPA)
    wet = tile(stat_ref, WET)
    own = [tile(y_ref, r) for r in range(12)]
    result = []
    for r in range(12):
        total = matrix_ref[16, r] * own[0]
        for q in range(1, 12):
            total = total + matrix_ref[16 + q, r] * own[q]
        result.append(total)
    for f in range(3):
        ends = FACE_NODES[f]
        inner = [edge[f] * own[(ch // 2) * 3 + ends[ch % 2]] for ch in range(8)]
        outer = [outer_edge[f] * tile(outer_ref, f * channels + ch) for ch in range(8)]
        for b in range(8):
            total = half_speed[f] * (inner[b] - outer[b])
            for a in range(8):
                total = total + matrix_ref[a, b] * inner[a] - matrix_ref[8 + a, b] * outer[a]
            at = (b // 2) * 3 + ends[b % 2]
            result[at] = result[at] + total
    friction = tile(stat_ref, ZONE_FRICTION) * tile(stat_ref, FRICTION_BASE + section) * wet
    for r in range(3, 9):
        result[r] = result[r] - friction * tile(lam_ref, r)
    exchange = []
    for i in range(3):
        top = tile(lam_ref, 12 + i) - SALT_RETURN * wet * tile(lam_ref, 9 + i)
        exchange.append(kappa * top)
        result[9 + i] = result[9 + i] + exchange[i]
    for r in range(12):
        emit(r, result[r])
    for i in range(3):
        (f0, j0), (f1, j1) = NODE_FACES[i]
        both = edge[f0] + edge[f1]
        from_above = exchange[i]
        for layer in range(layers):
            r = 12 + layer * 3 + i
            value = (
                outer_edge[f0] * tile(outer_ref, f0 * channels + 8 + layer * 2 + j0)
                + outer_edge[f1] * tile(outer_ref, f1 * channels + 8 + layer * 2 + j1)
                - both * tile(y_ref, r)
                - from_above
            )
            if layer + 1 < layers:
                from_above = kappa * (tile(lam_ref, r + 3) - tile(lam_ref, r))
                value = value + from_above
            emit(r, value)


def own_gradients(section, weight, lam_ref, y_ref, x_tiles, stat_ref):
    rows = lam_ref.shape[0] // SUB
    layers = (rows - 12) // 3
    wet = tile(stat_ref, WET)
    kappa = tile(stat_ref, KAPPA)
    momentum = tile(lam_ref, 3) * tile(x_tiles, 3)
    for r in range(4, 9):
        momentum = momentum + tile(lam_ref, r) * tile(x_tiles, r)
    friction = -(weight * wet * tile(stat_ref, FRICTION_BASE + section)) * momentum
    vertical = None
    lateral = None
    for i in range(3):
        (f0, _), (f1, _) = NODE_FACES[i]
        top = tile(lam_ref, 12 + i) - SALT_RETURN * wet * tile(lam_ref, 9 + i)
        total = top * (tile(x_tiles, 9 + i) - tile(x_tiles, 12 + i))
        dots = None
        for layer in range(layers):
            r = 12 + layer * 3 + i
            term = tile(y_ref, r) * tile(x_tiles, r)
            dots = term if dots is None else dots + term
            if layer + 1 < layers:
                total = total + (tile(lam_ref, r + 3) - tile(lam_ref, r)) * (
                    tile(x_tiles, r) - tile(x_tiles, r + 3)
                )
        side = (tile(stat_ref, EDGE + f0) + tile(stat_ref, EDGE + f1)) * dots
        vertical = total if vertical is None else vertical + total
        lateral = side if lateral is None else lateral + side
    return friction, weight * (kappa * vertical - lateral)


def outer_gradients(weight, outer_ref, x_tiles, fact_ref):
    channels = outer_ref.shape[0] // SUB // 3
    values = []
    for f in range(3):
        total = None
        for ch in range(8, channels):
            row = 12 + (ch - 8) // 2 * 3 + FACE_NODES[f][ch % 2]
            term = tile(outer_ref, f * channels + ch) * tile(x_tiles, row)
            total = term if total is None else total + term
        values.append(weight * tile(fact_ref, OUTER_EDGE + f) * total)
    return values


def x_to_tiles(x_ref, section, x_tiles):
    rows = x_ref.shape[3]
    rows_to_tiles(
        lambda b: x_ref[section, 0, 0, :, lanes_of(b)].astype(jnp.float32), x_tiles, rows
    )


def local_two_kernel(
    cot_ref, plan_ref, x_ref, outer_ref, near_ref, term_ref, x_tiles
):
    stat_ref, index_ref, _, table_ref = plan_parts(plan_ref)
    rows = cot_ref.shape[0] // SUB
    local_states(table_ref, 0, rows // 3, index_ref, outer_ref)
    for f in range(3):
        lane, sublane, face = [index_of(index_ref, n * 3 + f) for n in range(3)]
        for group in range(4):
            value = gather_by_face(table_ref, rows + 3 * group, lane, sublane, face)
            put(near_ref, f * 5 + group, value)
        put(near_ref, f * 5 + 4, gather_tile(table_ref, rows + 12, lane, sublane))
    x_to_tiles(x_ref, 2, x_tiles)
    friction, conduct = own_gradients(
        2, TIME_STEP * 2.0 / 3.0, cot_ref, table_ref, x_tiles, stat_ref
    )
    put(term_ref, 0, friction)
    put(term_ref, 1, conduct)


def local_x_kernel(plan_ref, x_ref, x_outer_ref, sent_ref, packed_ref, x_tiles):
    index_ref = plan_parts(plan_ref)[1]
    comps = x_ref.shape[3] // 3
    x_to_tiles(x_ref, 0, x_tiles)
    local_states(x_tiles, 4, comps - 4, index_ref, x_outer_ref)
    sender = Sender(index_ref, sent_ref, packed_ref)
    sender.states(x_tiles, 4, comps - 4)
    sender.flush(comps * 2 - 9)


def second_kernel(
    cot_ref,
    plan_ref,
    near_outer_ref,
    near_ref,
    x_sent_ref,
    x_packed_ref,
    from_x1,
    from_x2,
    from_y1,
    from_y2,
    lam_ref,
    y_ref,
    fact_ref,
    outer_ref,
    to_x1,
    to_x2,
    to_y1,
    to_y2,
    sent_ref,
    packed_ref,
    corner_ref,
    matrix_ref,
    sem,
):
    matrices = load_matrices(plan_ref, matrix_ref, sem)
    stat_ref, index_ref, _, table_ref = plan_parts(plan_ref)
    rows = cot_ref.shape[0] // SUB
    comps = rows // 3
    channels = comps * 2
    received = Received((from_x1, from_x2, from_y1, from_y2), channels + 5, corner_ref)
    remote_states(received, 0, channels, index_ref, near_outer_ref, outer_ref)
    for f in range(3):
        lane, remote = index_of(index_ref, f), index_of(index_ref, 9 + f)
        for group in range(5):
            value = received.fill(channels + group, lane, remote, tile(near_ref, f * 5 + group))
            if group == 0:
                put(fact_ref, OUTER_EDGE + f, value)
            elif group == 4:
                put(fact_ref, OUTER_ZONE + f, value)
            else:
                both = tile(table_ref, rows + 3 * group + f) + value
                put(
                    fact_ref,
                    HALF_SPEED + 3 * (group - 1) + f,
                    0.5 * jnp.sqrt(1.0 + (0.25 / 8.0) * both),
                )
    wet_area = tile(stat_ref, WET_AREA)
    half_kappa_area = tile(stat_ref, HALF_KAPPA_AREA)

    def emit(r, value):
        lam = (2.0 / 3.0) * (tile(cot_ref, r) + TIME_STEP * value)
        put(lam_ref, r, lam)
        put(y_ref, r, lam * (wet_area if r < 12 else half_kappa_area))

    matrices.wait()
    transposed_section(
        2, cot_ref, table_ref, outer_ref, stat_ref, fact_ref, matrix_ref, emit
    )
    sender = Sender(index_ref, sent_ref, packed_ref)
    sender.states(y_ref, 0, comps)
    sender.flush(channels - 1)
    outs = (to_x1, to_x2, to_y1, to_y2)
    write_messages(x_sent_ref, x_packed_ref, 0, channels - 8, outs, X_ROWS + channels)
    write_messages(sent_ref, packed_ref, X_ROWS, channels, outs, X_ROWS + channels)


def local_one_kernel(
    lam_ref,
    y_ref,
    plan_ref,
    fact_ref,
    old_outer_ref,
    old_term_ref,
    x_ref,
    outer_ref,
    term_ref,
    x_tiles,
):
    stat_ref, index_ref, _, _ = plan_parts(plan_ref)
    local_states(y_ref, 0, lam_ref.shape[0] // SUB // 3, index_ref, outer_ref)
    x_to_tiles(x_ref, 2, x_tiles)
    weight = TIME_STEP * 2.0 / 3.0
    for f, value in enumerate(outer_gradients(weight, old_outer_ref, x_tiles, fact_ref)):
        put(term_ref, 2 + f, value)
    x_to_tiles(x_ref, 1, x_tiles)
    terms = own_gradients(1, TIME_STEP * 0.25, lam_ref, y_ref, x_tiles, stat_ref)
    for n in range(2):
        put(term_ref, n, tile(old_term_ref, n) + terms[n])


def first_kernel(
    cot_ref,
    lam_ref,
    y_ref,
    plan_ref,
    fact_ref,
    near_outer_ref,
    from_x1,
    from_x2,
    from_y1,
    from_y2,
    base_ref,
    next_ref,
    next_y_ref,
    outer_ref,
    to_x1,
    to_x2,
    to_y1,
    to_y2,
    sent_ref,
    packed_ref,
    corner_ref,
    matrix_ref,
    sem,
):
    matrices = load_matrices(plan_ref, matrix_ref, sem)
    stat_ref, index_ref, _, _ = plan_parts(plan_ref)
    comps = lam_ref.shape[0] // SUB // 3
    channels = comps * 2
    received = Received((from_x1, from_x2, from_y1, from_y2), X_ROWS + channels, corner_ref)
    remote_states(received, X_ROWS, channels, index_ref, near_outer_ref, outer_ref)
    wet_area = tile(stat_ref, WET_AREA)
    half_kappa_area = tile(stat_ref, HALF_KAPPA_AREA)

    def emit(r, value):
        old = tile(lam_ref, r)
        lam = 0.25 * (old + TIME_STEP * value)
        put(next_ref, r, lam)
        put(next_y_ref, r, lam * (wet_area if r < 12 else half_kappa_area))
        put(base_ref, r, (1.0 / 3.0) * tile(cot_ref, r) + 0.75 * old + lam)

    matrices.wait()
    transposed_section(
        1, lam_ref, y_ref, outer_ref, stat_ref, fact_ref, matrix_ref, emit
    )
    sender = Sender(index_ref, sent_ref, packed_ref)
    sender.states(next_y_ref, 0, comps)
    sender.flush(channels - 1)
    write_messages(sent_ref, packed_ref, 0, channels, (to_x1, to_x2, to_y1, to_y2), channels)


def zone_kernel(
    lam_ref,
    y_ref,
    plan_ref,
    fact_ref,
    old_outer_ref,
    term_ref,
    x_ref,
    x_near_ref,
    from_x1,
    from_x2,
    from_y1,
    from_y2,
    out_ref,
    x_outer_ref,
    x_tiles,
    corner_ref,
):
    stat_ref, index_ref, _, _ = plan_parts(plan_ref)
    rows = lam_ref.shape[0] // SUB
    channels = rows // 3 * 2
    x_channels = channels - 8
    received = Received((from_x1, from_x2, from_y1, from_y2), X_ROWS + channels, corner_ref)
    remote_states(received, 0, x_channels, index_ref, x_near_ref, x_outer_ref)
    x_to_tiles(x_ref, 1, x_tiles)
    outer_terms = outer_gradients(TIME_STEP * 0.25, old_outer_ref, x_tiles, fact_ref)
    outer_terms = [tile(term_ref, 2 + f) + outer_terms[f] for f in range(3)]
    x_to_tiles(x_ref, 0, x_tiles)
    friction_term, conduct_term = own_gradients(
        0, TIME_STEP, lam_ref, y_ref, x_tiles, stat_ref
    )
    friction_term = friction_term + tile(term_ref, 0)
    conduct_term = conduct_term + tile(term_ref, 1)
    for f in range(3):
        total = None
        for ch in range(x_channels):
            row = 12 + ch // 2 * 3 + FACE_NODES[f][ch % 2]
            term = tile(x_outer_ref, f * x_channels + ch) * tile(y_ref, row)
            total = term if total is None else total + term
        conduct_term = conduct_term + TIME_STEP * tile(stat_ref, EDGE + f) * total

    zones = out_ref.shape[2]
    zone_iota = lax.broadcasted_iota(jnp.int32, (zones, LANES), 0).astype(jnp.float32)
    sub_iota = lax.broadcasted_iota(jnp.int32, (SUB, zones), 0)

    def thirds(value):
        high = value.astype(jnp.bfloat16).astype(jnp.float32)
        rest = value - high
        middle = rest.astype(jnp.bfloat16).astype(jnp.float32)
        return [high, middle, rest - middle]

    def by_zone(values, zone_of, zone_row):
        pieces = sum([thirds(value) for value in values], [])
        left = jnp.concatenate(pieces, axis=0).astype(jnp.bfloat16)
        totals = [jnp.zeros((SUB, zones), jnp.float32) for _ in values]
        for sub in range(SUB):
            line = zone_of[pl.ds(zone_row * SUB + sub, 1), :]
            hot = (jnp.broadcast_to(line, (zones, LANES)) == zone_iota).astype(jnp.float32)
            dots = lax.dot_general(
                left,
                hot.astype(jnp.bfloat16),
                (((1,), (1,)), ((), ())),
                preferred_element_type=jnp.float32,
            )
            for n in range(len(values)):
                at = n * 3 * SUB
                three = dots[at : at + SUB] + dots[at + SUB : at + 2 * SUB]
                three = three + dots[at + 2 * SUB : at + 3 * SUB]
                totals[n] = totals[n] + jnp.where(sub_iota == sub, three, 0.0)
        return totals

    friction, conduct = by_zone([friction_term, conduct_term], stat_ref, ZONE_ID)
    for f in range(3):
        conduct = conduct + by_zone([outer_terms[f]], fact_ref, OUTER_ZONE + f)[0]
    friction = GRAD_WEIGHT * jnp.sum(friction, axis=0, keepdims=True)
    conduct = GRAD_WEIGHT * jnp.sum(conduct, axis=0, keepdims=True)
    factors = [
        stat_ref[CONDUCTIVITY * SUB + n : CONDUCTIVITY * SUB + n + 1, :]
        for n in range(zones // LANES)
    ]
    conduct = conduct / jnp.concatenate(factors, axis=1)
    for device in range(out_ref.shape[0]):
        out_ref[device, 0:1, :] = friction
        out_ref[device, 1:2, :] = conduct


def local_zero_kernel(y_ref, plan_ref, outer_ref):
    index_ref = plan_parts(plan_ref)[1]
    local_states(y_ref, 0, y_ref.shape[0] // SUB // 3, index_ref, outer_ref)


def last_kernel(
    base_ref,
    lam_ref,
    y_ref,
    plan_ref,
    fact_ref,
    near_outer_ref,
    from_x1,
    from_x2,
    from_y1,
    from_y2,
    adjoint_ref,
    last_ref,
    outer_ref,
    corner_ref,
    matrix_ref,
    sem,
):
    matrices = load_matrices(plan_ref, matrix_ref, sem)
    stat_ref, index_ref, _, _ = plan_parts(plan_ref)
    rows = lam_ref.shape[0] // SUB
    channels = rows // 3 * 2
    received = Received((from_x1, from_x2, from_y1, from_y2), channels, corner_ref)
    remote_states(received, 0, channels, index_ref, near_outer_ref, outer_ref)

    def emit(r, value):
        put(adjoint_ref, r, tile(base_ref, r) + TIME_STEP * value)

    matrices.wait()
    transposed_section(
        0, lam_ref, y_ref, outer_ref, stat_ref, fact_ref, matrix_ref, emit
    )
    last_ref[...] = tile(adjoint_ref, rows - 1)


def total_kernel(zone_ref, adjoint_ref, grads_ref):
    grads_ref[...] = jnp.sum(zone_ref[...], axis=0)


def exchange(channels, messages, ahead):
    x1, x2, y1, y2 = messages
    x1, x2 = swapped(x1, "gx", 0), swapped(x2, "gx", 1)
    y1, y2, ahead = call(
        functools.partial(corner_kernel, channels),
        "corners",
        [jax.ShapeDtypeStruct(one.shape, one.dtype) for one in (y1, y2, ahead)],
        [],
        [x1, x2, y1, y2, ahead],
        apart=(4,),
        aliases={2: 0, 3: 1, 4: 2},
    )
    return (x1, x2, swapped(y1, "gy", 0), swapped(y2, "gy", 1)), ahead


def call(kernel, name, outs, scratch, operands, far=False, apart=(), aliases={}):
    near = pl.BlockSpec(memory_space=pltpu.VMEM)
    in_place = pl.BlockSpec(memory_space=pl.ANY)
    specs = [in_place if far or n in apart else near for n in range(len(operands))]
    handed_on = [aliases[n] for n in apart]
    return pl.pallas_call(
        kernel,
        in_specs=specs,
        out_specs=[in_place if n in handed_on else near for n in range(len(outs))],
        out_shape=outs,
        scratch_shapes=scratch,
        input_output_aliases=aliases,
        compiler_params=pltpu.CompilerParams(
            vmem_limit_bytes=(FAR_VMEM if far else NEAR_VMEM) * 1024 * 1024
        ),
        name=name,
    )(*operands)


def local(
    cotangent,
    section_states,
    inverse_area,
    edge_length,
    roughness,
    soil_conductance,
    zone_friction,
    zone_conductivity,
    wet_mask,
    element_zone,
    send_face,
    send_count,
    face_partner,
    volume_matrix,
    flux_in,
    flux_out,
):
    rows = cotangent.shape[2]
    channels = rows // 3 * 2
    zones = zone_friction.shape[0]
    slots = send_face.shape[3]
    devices = lax.axis_size("gx") * lax.axis_size("gy")
    f32 = jnp.float32

    def tiles(count, dtype=f32):
        return jax.ShapeDtypeStruct((count * SUB, LANES), dtype)

    def tile_scratch(count, dtype=f32):
        return pltpu.VMEM((count * SUB, LANES), dtype)

    def messages(count):
        return [jax.ShapeDtypeStruct((slots // LANES, message_rows(count), LANES), f32)] * 4

    def sent_tiles(count):
        return corner_rows(count) * SUB

    section_scratch = [
        pltpu.VMEM((SUB, LANES), f32),
        pltpu.SMEM((MATRIX_ROWS * SUB, LANES), f32),
        pltpu.SemaphoreType.DMA((1,)),
    ]

    square = lambda one: one.reshape(SUB, LANES)
    cot = cotangent.reshape(rows * SUB, LANES)
    plan, *to_send = call(
        prepare_kernel,
        "prepare",
        [tiles(plan_rows(rows))] + messages(channels + 5),
        [
            tile_scratch(16),
            tile_scratch(sent_tiles(channels + 5)),
            tile_scratch(1),
            tile_scratch(3, jnp.int32),
            pltpu.VMEM(send_face.shape, jnp.int32),
            tile_scratch(rows),
            pltpu.VMEM((section_states.shape[0], 16, SUB * LANES), section_states.dtype),
            tile_scratch(1),
            tile_scratch(3),
            tile_scratch(1),
            tile_scratch(1),
            pltpu.VMEM((zones // LANES, LANES), f32),
            pltpu.VMEM((zones // LANES, LANES), f32),
            tile_scratch(1, jnp.int32),
            tile_scratch(1, jnp.int32),
            pltpu.VMEM(flux_in.shape, f32),
            pltpu.VMEM(flux_out.shape, f32),
            pltpu.VMEM(volume_matrix.shape, f32),
            pltpu.SemaphoreType.DMA((15,)),
        ],
        [
            cot,
            section_states,
            square(inverse_area),
            edge_length.reshape(3 * SUB, LANES),
            square(roughness),
            square(soil_conductance),
            zone_friction.reshape(-1, LANES),
            zone_conductivity.reshape(-1, LANES),
            square(wet_mask),
            square(element_zone),
            send_face,
            face_partner.reshape(3 * SUB, LANES),
            flux_in,
            flux_out,
            volume_matrix,
        ],
        far=True,
    )
    near_outer, near, term = call(
        local_two_kernel,
        "local_two",
        [tiles(3 * channels), tiles(15), tiles(2)],
        [tile_scratch(rows)],
        [cot, plan, section_states],
    )
    x_near, x_sent, x_packed = call(
        local_x_kernel,
        "local_x",
        [tiles(3 * (channels - 8)), tiles(sent_tiles(channels - 8)), tiles(1)],
        [tile_scratch(rows)],
        [plan, section_states],
    )
    received, term = exchange(channels + 5, to_send, term)
    lam, y, fact, outer, *to_send = call(
        second_kernel,
        "section_two",
        [tiles(rows), tiles(rows), tiles(FACT_ROWS), tiles(3 * channels)]
        + messages(X_ROWS + channels),
        [tile_scratch(sent_tiles(channels)), tile_scratch(1)] + section_scratch,
        [cot, plan, near_outer, near, x_sent, x_packed, *received],
    )
    near_outer, term = call(
        local_one_kernel,
        "local_one",
        [tiles(3 * channels), tiles(5)],
        [tile_scratch(rows)],
        [lam, y, plan, fact, outer, term, section_states],
    )
    received, term = exchange(X_ROWS + channels, to_send, term)
    base, lam, y, outer, *to_send = call(
        first_kernel,
        "section_one",
        [tiles(rows), tiles(rows), tiles(rows), tiles(3 * channels)] + messages(channels),
        [tile_scratch(sent_tiles(channels)), tile_scratch(1)] + section_scratch,
        [cot, lam, y, plan, fact, near_outer, *received],
    )
    (zone_terms,) = call(
        zone_kernel,
        "zone_sums",
        [jax.ShapeDtypeStruct((devices, 2, zones), f32)],
        [tile_scratch(3 * (channels - 8)), tile_scratch(rows), tile_scratch(1)],
        [lam, y, plan, fact, outer, term, section_states, x_near, *received],
    )
    received, zone_terms = exchange(channels, to_send, zone_terms)
    all_terms = lax.all_to_all(zone_terms, ("gx", "gy"), 0, 0)
    (near_outer,) = call(local_zero_kernel, "local_zero", [tiles(3 * channels)], [], [y, plan])
    adjoint, last = call(
        last_kernel,
        "section_zero",
        [tiles(rows), tiles(1)],
        [tile_scratch(3 * channels)] + section_scratch,
        [base, lam, y, plan, fact, near_outer, *received],
    )
    (zone_grads,) = call(
        total_kernel,
        "zone_total",
        [jax.ShapeDtypeStruct((2, zones), f32)],
        [],
        [all_terms, last],
    )
    return adjoint.reshape(cotangent.shape), zone_grads


def solution(mesh):
    placed = (
        P("gx", "gy", None, None),
        P(None, "gx", "gy", None, None),
        P("gx", "gy", None),
        P("gx", "gy", None, None),
        P("gx", "gy", None),
        P("gx", "gy", None),
        P(),
        P(),
        P("gx", "gy", None),
        P("gx", "gy", None),
        P("gx", "gy", None, None),
        P("gx", "gy", None),
        P("gx", "gy", None, None),
        P(),
        P(),
        P(),
    )
    return jax.shard_map(
        local,
        mesh=mesh,
        in_specs=placed,
        out_specs=(P("gx", "gy", None, None), P()),
        check_vma=False,
    )
```

```python
import functools
import jax
import jax.numpy as jnp
from jax import lax
from jax.experimental import pallas as pl
from jax.experimental.pallas import tpu as pltpu
from jax.sharding import PartitionSpec as P

TIME_STEP = 0.2
SALT_RETURN = 0.5
LATERAL = 0.5
GRAD_WEIGHT = 1.0 / 64.0
FACE_NODES = ((1, 2), (2, 0), (0, 1))
NODE_FACES = (((1, 1), (2, 0)), ((0, 0), (2, 1)), ((0, 1), (1, 0)))
SUB = 8
LANES = 128


WET_AREA, KAPPA, HALF_KAPPA_AREA, WET, EDGE, FRICTION_BASE, ZONE_FRICTION, ZONE_ID = (
    0,
    1,
    2,
    3,
    4,
    7,
    10,
    11,
)
CONDUCTIVITY = 12
STAT_ROWS = 13
NEAR_VMEM, FAR_VMEM = 32, 60
OUTER_EDGE, OUTER_ZONE, HALF_SPEED = 0, 3, 6
FACT_ROWS = 15
X_ROWS = 24
CORNER_LANES = 16
CORNER_BLOCK = 8


def swapped(x, axis, first):
    peers = lax.axis_size(axis)
    lows = range(first, peers - 1, 2)
    return lax.ppermute(x, axis, [(i, i + 1) for i in lows] + [(i + 1, i) for i in lows])


def tile(ref, row):
    return ref[row * SUB : (row + 1) * SUB, :]


def put(ref, row, value):
    ref[row * SUB : (row + 1) * SUB, :] = value


def take(row, lane_index):
    return jnp.take_along_axis(row, lane_index, axis=1, mode="promise_in_bounds")


def spread(ref, row):
    return jnp.broadcast_to(ref[pl.ds(row, 1), :], (SUB, LANES))


def rows_to_tiles(read, tiles_ref, count):
    for block in range(SUB):
        tiles_ref[pl.ds(block, count, stride=SUB), :] = read(block)


def lanes_of(block):
    return slice(block * LANES, (block + 1) * LANES)


def gather_tile(src, row, lane_index, sublane_index):
    found = take(spread(src, row * SUB), lane_index)
    for sub in range(1, SUB):
        got = take(spread(src, row * SUB + sub), lane_index)
        found = jnp.where(sublane_index == sub, got, found)
    return found


def pick(face, for_zero, for_one, for_two):
    return jnp.where(face == 0, for_zero, jnp.where(face == 1, for_one, for_two))


def gather_ends(src, row, lane_index, sublane_index, face):
    n0, n1, n2 = [gather_tile(src, row + i, lane_index, sublane_index) for i in range(3)]
    return pick(face, n1, n2, n0), pick(face, n2, n0, n1)


def gather_by_face(src, row, lane_index, sublane_index, face):
    return pick(
        face, *[gather_tile(src, row + i, lane_index, sublane_index) for i in range(3)]
    )


def corner_rows(channels):
    return (channels * CORNER_LANES + LANES - 1) // LANES


def message_rows(channels):
    return channels + corner_rows(channels)


def corner_lane(shape):
    return lax.broadcasted_iota(jnp.int32, shape, 1) % CORNER_LANES


class Received:
    def __init__(self, messages, channels, corner_ref):
        _, _, y1, y2 = messages
        self.mains = messages
        self.corner_ref = corner_ref
        rows = slice(channels, message_rows(channels))
        count = corner_rows(channels)
        lane = corner_lane((count, LANES))
        corner_ref[0:count, :] = jnp.where(
            jnp.bitwise_and(lane, 4) == 0, y1[0, rows, :], y2[0, rows, :]
        )

    def fill(self, row, lane_index, remote_index, value):
        for number, ref in enumerate(self.mains):
            for half in range(2):
                got = take(spread(ref.at[half], row), lane_index)
                value = jnp.where(remote_index == 2 * number + half, got, value)
        channels_a_row = LANES // CORNER_LANES
        lane = lane_index + row % channels_a_row * CORNER_LANES
        line = spread(self.corner_ref, row // channels_a_row)
        got = take(line, jnp.bitwise_and(lane, LANES - 1))
        return jnp.where(remote_index == CORNER_BLOCK, got, value)


INDEX_ROWS = 18
MATRIX_ROWS = 4


def plan_rows(rows):
    return STAT_ROWS + INDEX_ROWS + MATRIX_ROWS + rows + 13


def plan_parts(plan_ref):
    parts, at = [], 0
    for count in (STAT_ROWS, INDEX_ROWS, MATRIX_ROWS):
        parts.append(plan_ref.at[at * SUB : (at + count) * SUB])
        at += count
    return (*parts, plan_ref.at[at * SUB :])


def tile_at(ref, row):
    return ref[pl.ds(pl.multiple_of(row * SUB, SUB), SUB), :]


def index_at(ref, row):
    return tile_at(ref, row).astype(jnp.int32)


def index_of(ref, row):
    return tile(ref, row).astype(jnp.int32)


def put_index(ref, row, value):
    put(ref, row, value.astype(jnp.float32))


def load_matrices(plan_ref, matrix_ref, sem):
    copy = pltpu.make_async_copy(plan_parts(plan_ref)[2], matrix_ref, sem.at[0])
    copy.start()
    return copy


def put_at(ref, row, value):
    ref[pl.ds(pl.multiple_of(row * SUB, SUB), SUB), :] = value


class Sender:
    def __init__(self, index_ref, sent_ref, packed_ref):
        self.straight = [index_of(index_ref, 12 + 2 * n) for n in range(3)]
        self.lane, sublane, self.face = [index_of(index_ref, 13 + 2 * n) for n in range(3)]
        sub = lax.broadcasted_iota(jnp.int32, (SUB, LANES), 0)
        slot = lax.broadcasted_iota(jnp.int32, (SUB, LANES), 1)
        self.own = (sub == sublane) & (slot < CORNER_LANES)
        self.sent_ref, self.packed_ref = sent_ref, packed_ref
        self.group = None

    def corner(self, src, row):
        return jnp.where(self.own, take(tile(src, row), self.lane), 0.0)

    def put(self, channel, value, corner):
        put(self.sent_ref, channel, value)
        place = channel % SUB
        moved = corner if place == 0 else pltpu.roll(corner, CORNER_LANES * place, 1)
        self.group = moved if place == 0 else self.group + moved
        if place == SUB - 1:
            self.flush(channel)

    def flush(self, channel):
        at = channel // SUB
        self.packed_ref[at : at + 1, :] = jnp.sum(self.group, axis=0, keepdims=True)

    def states(self, src, first_comp, comps):
        for comp in range(comps):
            row = (first_comp + comp) * 3
            ends = gather_ends(src, row, *self.straight)
            n0, n1, n2 = [self.corner(src, row + i) for i in range(3)]
            corners = pick(self.face, n1, n2, n0), pick(self.face, n2, n0, n1)
            for j in range(2):
                self.put(comp * 2 + j, ends[j], corners[j])

    def by_face(self, src, row, channel):
        corner = pick(self.face, *[self.corner(src, row + i) for i in range(3)])
        self.put(channel, gather_by_face(src, row, *self.straight), corner)

    def by_element(self, src, row, channel):
        self.put(channel, gather_tile(src, row, *self.straight[:2]), self.corner(src, row))


def write_messages(sent_ref, packed_ref, first, channels, outs, total):
    for role, out in enumerate(outs):
        for half in range(2):
            out[half, first : first + channels, :] = sent_ref[
                pl.ds(role * 2 + half, channels, stride=SUB), :
            ]
    count, at = corner_rows(channels), total + first // SUB
    for out in outs[:2]:
        out[0, at : at + count, :] = packed_ref[0:count, :]


def prepare_kernel(
    cot_ref,
    x_ref,
    area_ref,
    edge_ref,
    rough_ref,
    soil_ref,
    friction_ref,
    conduct_ref,
    wet_ref,
    zone_ref,
    send_ref,
    partner_ref,
    in_ref,
    out_ref,
    volume_ref,
    plan_ref,
    to_x1,
    to_x2,
    to_y1,
    to_y2,
    x_tiles,
    sent_ref,
    packed_ref,
    *fetched,
):
    *fetched, sems = fetched
    stat_ref, index_ref, matrix_ref, table_ref = plan_parts(plan_ref)
    sources = [
        partner_ref,
        send_ref,
        cot_ref,
        x_ref.at[:, 0, 0, 0:16],
        area_ref,
        edge_ref,
        rough_ref,
        soil_ref,
        friction_ref,
        conduct_ref,
        wet_ref,
        zone_ref,
        in_ref,
        out_ref,
        volume_ref,
    ]
    copies = [
        pltpu.make_async_copy(source, target, sems.at[n])
        for n, (source, target) in enumerate(zip(sources, fetched))
    ]
    for copy in copies:
        copy.start()
    for copy in copies:
        copy.wait()
    (
        partner_ref,
        send_ref,
        cot_ref,
        x_ref,
        area_ref,
        edge_ref,
        rough_ref,
        soil_ref,
        friction_ref,
        conduct_ref,
        wet_ref,
        zone_ref,
        in_ref,
        out_ref,
        volume_ref,
    ) = fetched
    matrix_ref[0:8, 0:8] = in_ref[...]
    matrix_ref[8:16, 0:8] = out_ref[...]
    matrix_ref[16:28, 0:12] = volume_ref[...]
    rows = cot_ref.shape[0] // SUB
    sections = x_ref.shape[0]
    odd_a, odd_b = 1 - lax.axis_index("gx") % 2, 1 - lax.axis_index("gy") % 2
    straight = (6 - 5 * odd_a, 1 + 5 * odd_a, 4 - odd_b, 3 + odd_b)
    right, up = 1 - odd_a, 1 - odd_b
    corners = (
        5 * right + 2 * up,
        5 * right + 2 - 2 * up,
        5 - 5 * right + 2 * up,
        7 - 5 * right - 2 * up,
    )
    face_total = 3 * SUB * LANES
    for f in range(3):
        partner = tile(partner_ref, f)
        beyond = partner - face_total
        direction = jnp.right_shift(beyond, 8)
        half = jnp.bitwise_and(jnp.right_shift(beyond, 7), 1)
        lane = jnp.bitwise_and(partner, LANES - 1)
        remote = jnp.where(beyond >= 0, CORNER_BLOCK, -1)
        for number, toward in enumerate(straight):
            remote = jnp.where(direction == toward, 2 * number + half, remote)
        for number, toward in enumerate(corners):
            lane = jnp.where(direction == toward, lane % 4 + 4 * number, lane)
        put_index(index_ref, f, lane)
        put_index(index_ref, 3 + f, jnp.bitwise_and(jnp.right_shift(partner, 7), SUB - 1))
        put_index(index_ref, 6 + f, jnp.right_shift(partner, 10))
        put_index(index_ref, 9 + f, remote)
    sub_iota = lax.broadcasted_iota(jnp.int32, (SUB, LANES), 0)
    lane_iota = lax.broadcasted_iota(jnp.int32, (SUB, LANES), 1)

    def slots_to(choices, choice, half):
        rows_of = [
            jnp.broadcast_to(send_ref[0, 0, n : n + 1, lanes_of(half)], (SUB, LANES))
            for n in choices
        ]
        found = rows_of[0]
        for n, row in zip(choices[1:], rows_of[1:]):
            found = jnp.where(choice == n, row, found)
        return found

    straight_slots = None
    for number, toward in enumerate(straight):
        for half in range(2):
            row = slots_to((1, 6) if number < 2 else (3, 4), toward, half)
            straight_slots = (
                row
                if straight_slots is None
                else jnp.where(sub_iota == 2 * number + half, row, straight_slots)
            )
    corner_slots = None
    for number, toward in enumerate(corners):
        row = slots_to((0, 2, 5, 7), toward, 0)
        if number == 0:
            corner_slots = row
        else:
            moved = pltpu.roll(row, 4 * number, 1)
            corner_slots = jnp.where(lane_iota // 4 == number, moved, corner_slots)
    for d, slots in enumerate((straight_slots, corner_slots)):
        put_index(index_ref, 12 + d, jnp.bitwise_and(slots, LANES - 1))
        put_index(index_ref, 14 + d, jnp.bitwise_and(jnp.right_shift(slots, 7), SUB - 1))
        put_index(index_ref, 16 + d, jnp.right_shift(slots, 10))
    zone = zone_ref[...]
    zone_lane = jnp.bitwise_and(zone, LANES - 1)
    zone_block = jnp.right_shift(zone, 7)
    factors = []
    for ref in (friction_ref, conduct_ref):
        found = None
        for block in range(ref.shape[0]):
            got = take(spread(ref, block), zone_lane)
            found = got if block == 0 else jnp.where(zone_block == block, got, found)
        factors.append(found)
    area = area_ref[...]
    wet = wet_ref[...].astype(jnp.float32)
    kappa = factors[1] * soil_ref[...]
    wet_area = wet * area
    half_kappa_area = LATERAL * kappa * area
    put(stat_ref, WET_AREA, wet_area)
    put(stat_ref, KAPPA, kappa)
    put(stat_ref, HALF_KAPPA_AREA, half_kappa_area)
    put(stat_ref, WET, wet)
    put(stat_ref, ZONE_FRICTION, factors[0])
    put(stat_ref, ZONE_ID, zone.astype(jnp.float32))
    stat_ref[CONDUCTIVITY * SUB : CONDUCTIVITY * SUB + conduct_ref.shape[0], :] = conduct_ref[...]
    stat_ref[EDGE * SUB : (EDGE + 3) * SUB, :] = edge_ref[...]
    for k in range(sections):
        rows_to_tiles(
            lambda b: x_ref[k, :, lanes_of(b)].astype(jnp.float32), x_tiles, 16
        )
        squares = [tile(x_tiles, r) * tile(x_tiles, r) for r in range(12)]
        node_sum = [squares[i] + squares[3 + i] + squares[6 + i] + squares[9 + i] for i in range(3)]
        for f in range(3):
            first, second = FACE_NODES[f]
            put(table_ref, rows + 3 + 3 * k + f, node_sum[first] + node_sum[second])
        momentum = squares[3]
        for r in range(4, 9):
            momentum = momentum + squares[r]
        put(
            stat_ref,
            FRICTION_BASE + k,
            rough_ref[...] * jnp.sqrt(1.0 + momentum * (1.0 / 6.0)),
        )
    for f in range(3):
        put(table_ref, rows + f, tile(stat_ref, EDGE + f))
    put(table_ref, rows + 12, zone.astype(jnp.float32))
    for r in range(rows):
        put(table_ref, r, tile(cot_ref, r) * (wet_area if r < 12 else half_kappa_area))
    comps = rows // 3
    channels = comps * 2 + 5
    sender = Sender(index_ref, sent_ref, packed_ref)
    sender.states(table_ref, 0, comps)
    for group in range(4):
        sender.by_face(table_ref, rows + 3 * group, comps * 2 + group)
    sender.by_element(table_ref, rows + 12, channels - 1)
    sender.flush(channels - 1)
    write_messages(sent_ref, packed_ref, 0, channels, (to_x1, to_x2, to_y1, to_y2), channels)


def corner_kernel(channels, x1, x2, old_y1, old_y2, *rest):
    y1, y2 = rest[1:3]
    rows = slice(channels, message_rows(channels))
    lane = corner_lane((corner_rows(channels), LANES))
    merged = jnp.where(lane < 8, x1[0, rows, :], x2[0, rows, :])
    y1[0, rows, :] = merged
    y2[0, rows, :] = merged


def local_states(src, first_comp, comps, index_ref, out_ref):
    def body(f, carry):
        lane, sublane, face = [index_at(index_ref, n * 3 + f) for n in range(3)]
        for comp in range(comps):
            ends = gather_ends(src, (first_comp + comp) * 3, lane, sublane, face)
            for j in range(2):
                put_at(out_ref, f * comps * 2 + comp * 2 + j, ends[j])
        return carry

    lax.fori_loop(0, 3, body, 0)


def remote_states(received, first_row, channels, index_ref, local_ref, out_ref):
    def body(f, carry):
        lane, remote = index_at(index_ref, f), index_at(index_ref, 9 + f)
        for ch in range(channels):
            value = tile_at(local_ref, f * channels + ch)
            put_at(
                out_ref, f * channels + ch, received.fill(first_row + ch, lane, remote, value)
            )
        return carry

    lax.fori_loop(0, 3, body, 0)


def transposed_own(section, lam_ref, y_ref, stat_ref, matrix_ref, own_ref):
    rows = lam_ref.shape[0] // SUB
    layers = (rows - 12) // 3
    edge = [tile(stat_ref, EDGE + f) for f in range(3)]
    kappa = tile(stat_ref, KAPPA)
    wet = tile(stat_ref, WET)
    own = [tile(y_ref, r) for r in range(12)]
    result = []
    for r in range(12):
        total = matrix_ref[16, r] * own[0]
        for q in range(1, 12):
            total = total + matrix_ref[16 + q, r] * own[q]
        result.append(total)
    for f in range(3):
        ends = FACE_NODES[f]
        inner = [edge[f] * own[(ch // 2) * 3 + ends[ch % 2]] for ch in range(8)]
        for b in range(8):
            total = matrix_ref[0, b] * inner[0]
            for a in range(1, 8):
                total = total + matrix_ref[a, b] * inner[a]
            at = (b // 2) * 3 + ends[b % 2]
            result[at] = result[at] + total
    friction = tile(stat_ref, ZONE_FRICTION) * tile(stat_ref, FRICTION_BASE + section) * wet
    for r in range(3, 9):
        result[r] = result[r] - friction * tile(lam_ref, r)
    exchange = []
    for i in range(3):
        top = tile(lam_ref, 12 + i) - SALT_RETURN * wet * tile(lam_ref, 9 + i)
        exchange.append(kappa * top)
        result[9 + i] = result[9 + i] + exchange[i]
    for r in range(12):
        put(own_ref, r, result[r])
    for i in range(3):
        (f0, _), (f1, _) = NODE_FACES[i]
        both = edge[f0] + edge[f1]
        from_above = exchange[i]
        for layer in range(layers):
            r = 12 + layer * 3 + i
            value = -(both * tile(y_ref, r)) - from_above
            if layer + 1 < layers:
                from_above = kappa * (tile(lam_ref, r + 3) - tile(lam_ref, r))
                value = value + from_above
            put(own_ref, r, value)


def transposed_section(
    section, own_ref, y_ref, outer_ref, stat_ref, fact_ref, matrix_ref, emit
):
    rows = own_ref.shape[0] // SUB
    channels = rows // 3 * 2
    layers = (rows - 12) // 3
    outer_edge = [tile(fact_ref, OUTER_EDGE + f) for f in range(3)]
    result = [tile(own_ref, r) for r in range(12)]
    for f in range(3):
        edge = tile(stat_ref, EDGE + f)
        half_speed = tile(fact_ref, HALF_SPEED + 3 * section + f)
        ends = FACE_NODES[f]
        outer = [outer_edge[f] * tile(outer_ref, f * channels + ch) for ch in range(8)]
        for b in range(8):
            at = (b // 2) * 3 + ends[b % 2]
            total = half_speed * (edge * tile(y_ref, at) - outer[b])
            for a in range(8):
                total = total - matrix_ref[8 + a, b] * outer[a]
            result[at] = result[at] + total
    for r in range(12):
        emit(r, result[r])
    for i in range(3):
        (f0, j0), (f1, j1) = NODE_FACES[i]
        for layer in range(layers):
            r = 12 + layer * 3 + i
            emit(
                r,
                tile(own_ref, r)
                + outer_edge[f0] * tile(outer_ref, f0 * channels + 8 + layer * 2 + j0)
                + outer_edge[f1] * tile(outer_ref, f1 * channels + 8 + layer * 2 + j1),
            )


def own_gradients(section, weight, lam_ref, y_ref, x_tiles, stat_ref):
    rows = lam_ref.shape[0] // SUB
    layers = (rows - 12) // 3
    wet = tile(stat_ref, WET)
    kappa = tile(stat_ref, KAPPA)
    momentum = tile(lam_ref, 3) * tile(x_tiles, 3)
    for r in range(4, 9):
        momentum = momentum + tile(lam_ref, r) * tile(x_tiles, r)
    friction = -(weight * wet * tile(stat_ref, FRICTION_BASE + section)) * momentum
    vertical = None
    lateral = None
    for i in range(3):
        (f0, _), (f1, _) = NODE_FACES[i]
        top = tile(lam_ref, 12 + i) - SALT_RETURN * wet * tile(lam_ref, 9 + i)
        total = top * (tile(x_tiles, 9 + i) - tile(x_tiles, 12 + i))
        dots = None
        for layer in range(layers):
            r = 12 + layer * 3 + i
            term = tile(y_ref, r) * tile(x_tiles, r)
            dots = term if dots is None else dots + term
            if layer + 1 < layers:
                total = total + (tile(lam_ref, r + 3) - tile(lam_ref, r)) * (
                    tile(x_tiles, r) - tile(x_tiles, r + 3)
                )
        side = (tile(stat_ref, EDGE + f0) + tile(stat_ref, EDGE + f1)) * dots
        vertical = total if vertical is None else vertical + total
        lateral = side if lateral is None else lateral + side
    return friction, weight * (kappa * vertical - lateral)


def outer_gradients(weight, outer_ref, x_tiles, fact_ref):
    channels = outer_ref.shape[0] // SUB // 3
    values = []
    for f in range(3):
        total = None
        for ch in range(8, channels):
            row = 12 + (ch - 8) // 2 * 3 + FACE_NODES[f][ch % 2]
            term = tile(outer_ref, f * channels + ch) * tile(x_tiles, row)
            total = term if total is None else total + term
        values.append(weight * tile(fact_ref, OUTER_EDGE + f) * total)
    return values


def x_to_tiles(x_ref, section, x_tiles):
    rows = x_ref.shape[3]
    rows_to_tiles(
        lambda b: x_ref[section, 0, 0, :, lanes_of(b)].astype(jnp.float32), x_tiles, rows
    )


def local_two_kernel(
    cot_ref,
    plan_ref,
    x_ref,
    outer_ref,
    near_ref,
    term_ref,
    own_ref,
    x_tiles,
    matrix_ref,
    sem,
):
    matrices = load_matrices(plan_ref, matrix_ref, sem)
    stat_ref, index_ref, _, table_ref = plan_parts(plan_ref)
    rows = cot_ref.shape[0] // SUB
    local_states(table_ref, 0, rows // 3, index_ref, outer_ref)
    for f in range(3):
        lane, sublane, face = [index_of(index_ref, n * 3 + f) for n in range(3)]
        for group in range(4):
            value = gather_by_face(table_ref, rows + 3 * group, lane, sublane, face)
            put(near_ref, f * 5 + group, value)
        put(near_ref, f * 5 + 4, gather_tile(table_ref, rows + 12, lane, sublane))
    x_to_tiles(x_ref, 2, x_tiles)
    friction, conduct = own_gradients(
        2, TIME_STEP * 2.0 / 3.0, cot_ref, table_ref, x_tiles, stat_ref
    )
    put(term_ref, 0, friction)
    put(term_ref, 1, conduct)
    matrices.wait()
    transposed_own(2, cot_ref, table_ref, stat_ref, matrix_ref, own_ref)


def local_x_kernel(plan_ref, x_ref, x_outer_ref, sent_ref, packed_ref, x_tiles):
    index_ref = plan_parts(plan_ref)[1]
    comps = x_ref.shape[3] // 3
    x_to_tiles(x_ref, 0, x_tiles)
    local_states(x_tiles, 4, comps - 4, index_ref, x_outer_ref)
    sender = Sender(index_ref, sent_ref, packed_ref)
    sender.states(x_tiles, 4, comps - 4)
    sender.flush(comps * 2 - 9)


def second_kernel(
    cot_ref,
    plan_ref,
    own_ref,
    near_outer_ref,
    near_ref,
    x_sent_ref,
    x_packed_ref,
    from_x1,
    from_x2,
    from_y1,
    from_y2,
    lam_ref,
    y_ref,
    fact_ref,
    outer_ref,
    to_x1,
    to_x2,
    to_y1,
    to_y2,
    sent_ref,
    packed_ref,
    corner_ref,
    matrix_ref,
    sem,
):
    matrices = load_matrices(plan_ref, matrix_ref, sem)
    stat_ref, index_ref, _, table_ref = plan_parts(plan_ref)
    rows = cot_ref.shape[0] // SUB
    comps = rows // 3
    channels = comps * 2
    received = Received((from_x1, from_x2, from_y1, from_y2), channels + 5, corner_ref)
    remote_states(received, 0, channels, index_ref, near_outer_ref, outer_ref)
    for f in range(3):
        lane, remote = index_of(index_ref, f), index_of(index_ref, 9 + f)
        for group in range(5):
            value = received.fill(channels + group, lane, remote, tile(near_ref, f * 5 + group))
            if group == 0:
                put(fact_ref, OUTER_EDGE + f, value)
            elif group == 4:
                put(fact_ref, OUTER_ZONE + f, value)
            else:
                both = tile(table_ref, rows + 3 * group + f) + value
                put(
                    fact_ref,
                    HALF_SPEED + 3 * (group - 1) + f,
                    0.5 * jnp.sqrt(1.0 + (0.25 / 8.0) * both),
                )
    wet_area = tile(stat_ref, WET_AREA)
    half_kappa_area = tile(stat_ref, HALF_KAPPA_AREA)

    def emit(r, value):
        lam = (2.0 / 3.0) * (tile(cot_ref, r) + TIME_STEP * value)
        put(lam_ref, r, lam)
        put(y_ref, r, lam * (wet_area if r < 12 else half_kappa_area))

    matrices.wait()
    transposed_section(
        2, own_ref, table_ref, outer_ref, stat_ref, fact_ref, matrix_ref, emit
    )
    sender = Sender(index_ref, sent_ref, packed_ref)
    sender.states(y_ref, 0, comps)
    sender.flush(channels - 1)
    outs = (to_x1, to_x2, to_y1, to_y2)
    write_messages(x_sent_ref, x_packed_ref, 0, channels - 8, outs, X_ROWS + channels)
    write_messages(sent_ref, packed_ref, X_ROWS, channels, outs, X_ROWS + channels)


def local_one_kernel(
    lam_ref,
    y_ref,
    plan_ref,
    fact_ref,
    old_outer_ref,
    old_term_ref,
    x_ref,
    outer_ref,
    term_ref,
    own_ref,
    x_tiles,
    matrix_ref,
    sem,
):
    matrices = load_matrices(plan_ref, matrix_ref, sem)
    stat_ref, index_ref, _, _ = plan_parts(plan_ref)
    local_states(y_ref, 0, lam_ref.shape[0] // SUB // 3, index_ref, outer_ref)
    x_to_tiles(x_ref, 2, x_tiles)
    weight = TIME_STEP * 2.0 / 3.0
    for f, value in enumerate(outer_gradients(weight, old_outer_ref, x_tiles, fact_ref)):
        put(term_ref, 2 + f, value)
    x_to_tiles(x_ref, 1, x_tiles)
    terms = own_gradients(1, TIME_STEP * 0.25, lam_ref, y_ref, x_tiles, stat_ref)
    for n in range(2):
        put(term_ref, n, tile(old_term_ref, n) + terms[n])
    matrices.wait()
    transposed_own(1, lam_ref, y_ref, stat_ref, matrix_ref, own_ref)


def first_kernel(
    cot_ref,
    lam_ref,
    y_ref,
    plan_ref,
    fact_ref,
    own_ref,
    near_outer_ref,
    from_x1,
    from_x2,
    from_y1,
    from_y2,
    base_ref,
    next_ref,
    next_y_ref,
    outer_ref,
    to_x1,
    to_x2,
    to_y1,
    to_y2,
    sent_ref,
    packed_ref,
    corner_ref,
    matrix_ref,
    sem,
):
    matrices = load_matrices(plan_ref, matrix_ref, sem)
    stat_ref, index_ref, _, _ = plan_parts(plan_ref)
    comps = lam_ref.shape[0] // SUB // 3
    channels = comps * 2
    received = Received((from_x1, from_x2, from_y1, from_y2), X_ROWS + channels, corner_ref)
    remote_states(received, X_ROWS, channels, index_ref, near_outer_ref, outer_ref)
    wet_area = tile(stat_ref, WET_AREA)
    half_kappa_area = tile(stat_ref, HALF_KAPPA_AREA)

    def emit(r, value):
        old = tile(lam_ref, r)
        lam = 0.25 * (old + TIME_STEP * value)
        put(next_ref, r, lam)
        put(next_y_ref, r, lam * (wet_area if r < 12 else half_kappa_area))
        put(base_ref, r, (1.0 / 3.0) * tile(cot_ref, r) + 0.75 * old + lam)

    matrices.wait()
    transposed_section(
        1, own_ref, y_ref, outer_ref, stat_ref, fact_ref, matrix_ref, emit
    )
    sender = Sender(index_ref, sent_ref, packed_ref)
    sender.states(next_y_ref, 0, comps)
    sender.flush(channels - 1)
    write_messages(sent_ref, packed_ref, 0, channels, (to_x1, to_x2, to_y1, to_y2), channels)


def zone_kernel(
    lam_ref,
    y_ref,
    plan_ref,
    fact_ref,
    old_outer_ref,
    term_ref,
    x_ref,
    x_near_ref,
    from_x1,
    from_x2,
    from_y1,
    from_y2,
    out_ref,
    x_outer_ref,
    x_tiles,
    corner_ref,
):
    stat_ref, index_ref, _, _ = plan_parts(plan_ref)
    rows = lam_ref.shape[0] // SUB
    channels = rows // 3 * 2
    x_channels = channels - 8
    received = Received((from_x1, from_x2, from_y1, from_y2), X_ROWS + channels, corner_ref)
    remote_states(received, 0, x_channels, index_ref, x_near_ref, x_outer_ref)
    x_to_tiles(x_ref, 1, x_tiles)
    outer_terms = outer_gradients(TIME_STEP * 0.25, old_outer_ref, x_tiles, fact_ref)
    outer_terms = [tile(term_ref, 2 + f) + outer_terms[f] for f in range(3)]
    x_to_tiles(x_ref, 0, x_tiles)
    friction_term, conduct_term = own_gradients(
        0, TIME_STEP, lam_ref, y_ref, x_tiles, stat_ref
    )
    friction_term = friction_term + tile(term_ref, 0)
    conduct_term = conduct_term + tile(term_ref, 1)
    for f in range(3):
        total = None
        for ch in range(x_channels):
            row = 12 + ch // 2 * 3 + FACE_NODES[f][ch % 2]
            term = tile(x_outer_ref, f * x_channels + ch) * tile(y_ref, row)
            total = term if total is None else total + term
        conduct_term = conduct_term + TIME_STEP * tile(stat_ref, EDGE + f) * total

    zones = out_ref.shape[2]
    zone_iota = lax.broadcasted_iota(jnp.int32, (zones, LANES), 0).astype(jnp.float32)
    sub_iota = lax.broadcasted_iota(jnp.int32, (SUB, zones), 0)

    def thirds(value):
        high = value.astype(jnp.bfloat16).astype(jnp.float32)
        rest = value - high
        middle = rest.astype(jnp.bfloat16).astype(jnp.float32)
        return [high, middle, rest - middle]

    def by_zone(values, zone_of, zone_row):
        pieces = sum([thirds(value) for value in values], [])
        left = jnp.concatenate(pieces, axis=0).astype(jnp.bfloat16)
        totals = [jnp.zeros((SUB, zones), jnp.float32) for _ in values]
        for sub in range(SUB):
            line = zone_of[pl.ds(zone_row * SUB + sub, 1), :]
            hot = (jnp.broadcast_to(line, (zones, LANES)) == zone_iota).astype(jnp.float32)
            dots = lax.dot_general(
                left,
                hot.astype(jnp.bfloat16),
                (((1,), (1,)), ((), ())),
                preferred_element_type=jnp.float32,
            )
            for n in range(len(values)):
                at = n * 3 * SUB
                three = dots[at : at + SUB] + dots[at + SUB : at + 2 * SUB]
                three = three + dots[at + 2 * SUB : at + 3 * SUB]
                totals[n] = totals[n] + jnp.where(sub_iota == sub, three, 0.0)
        return totals

    friction, conduct = by_zone([friction_term, conduct_term], stat_ref, ZONE_ID)
    for f in range(3):
        conduct = conduct + by_zone([outer_terms[f]], fact_ref, OUTER_ZONE + f)[0]
    friction = GRAD_WEIGHT * jnp.sum(friction, axis=0, keepdims=True)
    conduct = GRAD_WEIGHT * jnp.sum(conduct, axis=0, keepdims=True)
    factors = [
        stat_ref[CONDUCTIVITY * SUB + n : CONDUCTIVITY * SUB + n + 1, :]
        for n in range(zones // LANES)
    ]
    conduct = conduct / jnp.concatenate(factors, axis=1)
    for device in range(out_ref.shape[0]):
        out_ref[device, 0:1, :] = friction
        out_ref[device, 1:2, :] = conduct


def local_zero_kernel(
    lam_ref, y_ref, plan_ref, zone_in, outer_ref, own_ref, zone_ref, matrix_ref, sem
):
    matrices = load_matrices(plan_ref, matrix_ref, sem)
    stat_ref, index_ref, _, _ = plan_parts(plan_ref)
    local_states(y_ref, 0, y_ref.shape[0] // SUB // 3, index_ref, outer_ref)
    matrices.wait()
    transposed_own(0, lam_ref, y_ref, stat_ref, matrix_ref, own_ref)


def last_kernel(
    base_ref,
    y_ref,
    plan_ref,
    fact_ref,
    own_ref,
    near_outer_ref,
    from_x1,
    from_x2,
    from_y1,
    from_y2,
    adjoint_ref,
    last_ref,
    outer_ref,
    corner_ref,
    matrix_ref,
    sem,
):
    matrices = load_matrices(plan_ref, matrix_ref, sem)
    stat_ref, index_ref, _, _ = plan_parts(plan_ref)
    rows = y_ref.shape[0] // SUB
    channels = rows // 3 * 2
    received = Received((from_x1, from_x2, from_y1, from_y2), channels, corner_ref)
    remote_states(received, 0, channels, index_ref, near_outer_ref, outer_ref)

    def emit(r, value):
        put(adjoint_ref, r, tile(base_ref, r) + TIME_STEP * value)

    matrices.wait()
    transposed_section(
        0, own_ref, y_ref, outer_ref, stat_ref, fact_ref, matrix_ref, emit
    )
    last_ref[...] = tile(adjoint_ref, rows - 1)


def total_kernel(zone_ref, adjoint_ref, grads_ref):
    grads_ref[...] = jnp.sum(zone_ref[...], axis=0)


def exchange(channels, messages, ahead):
    x1, x2, y1, y2 = messages
    x1, x2 = swapped(x1, "gx", 1), swapped(x2, "gx", 0)
    y1, y2, ahead = call(
        functools.partial(corner_kernel, channels),
        "corners",
        [jax.ShapeDtypeStruct(one.shape, one.dtype) for one in (y1, y2, ahead)],
        [],
        [x1, x2, y1, y2, ahead],
        apart=(4,),
        aliases={2: 0, 3: 1, 4: 2},
    )
    return (x1, x2, swapped(y1, "gy", 1), swapped(y2, "gy", 0)), ahead


def call(kernel, name, outs, scratch, operands, far=False, apart=(), aliases={}):
    near = pl.BlockSpec(memory_space=pltpu.VMEM)
    in_place = pl.BlockSpec(memory_space=pl.ANY)
    specs = [in_place if far or n in apart else near for n in range(len(operands))]
    handed_on = [aliases[n] for n in apart]
    return pl.pallas_call(
        kernel,
        in_specs=specs,
        out_specs=[in_place if n in handed_on else near for n in range(len(outs))],
        out_shape=outs,
        scratch_shapes=scratch,
        input_output_aliases=aliases,
        compiler_params=pltpu.CompilerParams(
            vmem_limit_bytes=(FAR_VMEM if far else NEAR_VMEM) * 1024 * 1024
        ),
        name=name,
    )(*operands)


def local(
    cotangent,
    section_states,
    inverse_area,
    edge_length,
    roughness,
    soil_conductance,
    zone_friction,
    zone_conductivity,
    wet_mask,
    element_zone,
    send_face,
    send_count,
    face_partner,
    volume_matrix,
    flux_in,
    flux_out,
):
    rows = cotangent.shape[2]
    channels = rows // 3 * 2
    zones = zone_friction.shape[0]
    slots = send_face.shape[3]
    devices = lax.axis_size("gx") * lax.axis_size("gy")
    f32 = jnp.float32

    def tiles(count, dtype=f32):
        return jax.ShapeDtypeStruct((count * SUB, LANES), dtype)

    def tile_scratch(count, dtype=f32):
        return pltpu.VMEM((count * SUB, LANES), dtype)

    def messages(count):
        return [jax.ShapeDtypeStruct((slots // LANES, message_rows(count), LANES), f32)] * 4

    def sent_tiles(count):
        return corner_rows(count) * SUB

    matrix_scratch = [
        pltpu.SMEM((MATRIX_ROWS * SUB, LANES), f32),
        pltpu.SemaphoreType.DMA((1,)),
    ]
    section_scratch = [pltpu.VMEM((SUB, LANES), f32)] + matrix_scratch

    square = lambda one: one.reshape(SUB, LANES)
    cot = cotangent.reshape(rows * SUB, LANES)
    plan, *to_send = call(
        prepare_kernel,
        "prepare",
        [tiles(plan_rows(rows))] + messages(channels + 5),
        [
            tile_scratch(16),
            tile_scratch(sent_tiles(channels + 5)),
            tile_scratch(1),
            tile_scratch(3, jnp.int32),
            pltpu.VMEM(send_face.shape, jnp.int32),
            tile_scratch(rows),
            pltpu.VMEM((section_states.shape[0], 16, SUB * LANES), section_states.dtype),
            tile_scratch(1),
            tile_scratch(3),
            tile_scratch(1),
            tile_scratch(1),
            pltpu.VMEM((zones // LANES, LANES), f32),
            pltpu.VMEM((zones // LANES, LANES), f32),
            tile_scratch(1, jnp.int32),
            tile_scratch(1, jnp.int32),
            pltpu.VMEM(flux_in.shape, f32),
            pltpu.VMEM(flux_out.shape, f32),
            pltpu.VMEM(volume_matrix.shape, f32),
            pltpu.SemaphoreType.DMA((15,)),
        ],
        [
            cot,
            section_states,
            square(inverse_area),
            edge_length.reshape(3 * SUB, LANES),
            square(roughness),
            square(soil_conductance),
            zone_friction.reshape(-1, LANES),
            zone_conductivity.reshape(-1, LANES),
            square(wet_mask),
            square(element_zone),
            send_face,
            face_partner.reshape(3 * SUB, LANES),
            flux_in,
            flux_out,
            volume_matrix,
        ],
        far=True,
    )
    near_outer, near, term, own = call(
        local_two_kernel,
        "local_two",
        [tiles(3 * channels), tiles(15), tiles(2), tiles(rows)],
        [tile_scratch(rows)] + matrix_scratch,
        [cot, plan, section_states],
    )
    x_near, x_sent, x_packed = call(
        local_x_kernel,
        "local_x",
        [tiles(3 * (channels - 8)), tiles(sent_tiles(channels - 8)), tiles(1)],
        [tile_scratch(rows)],
        [plan, section_states],
    )
    received, term = exchange(channels + 5, to_send, term)
    lam, y, fact, outer, *to_send = call(
        second_kernel,
        "section_two",
        [tiles(rows), tiles(rows), tiles(FACT_ROWS), tiles(3 * channels)]
        + messages(X_ROWS + channels),
        [tile_scratch(sent_tiles(channels)), tile_scratch(1)] + section_scratch,
        [cot, plan, own, near_outer, near, x_sent, x_packed, *received],
    )
    near_outer, term, own = call(
        local_one_kernel,
        "local_one",
        [tiles(3 * channels), tiles(5), tiles(rows)],
        [tile_scratch(rows)] + matrix_scratch,
        [lam, y, plan, fact, outer, term, section_states],
    )
    received, term = exchange(X_ROWS + channels, to_send, term)
    base, lam, y, outer, *to_send = call(
        first_kernel,
        "section_one",
        [tiles(rows), tiles(rows), tiles(rows), tiles(3 * channels)] + messages(channels),
        [tile_scratch(sent_tiles(channels)), tile_scratch(1)] + section_scratch,
        [cot, lam, y, plan, fact, own, near_outer, *received],
    )
    (zone_terms,) = call(
        zone_kernel,
        "zone_sums",
        [jax.ShapeDtypeStruct((devices, 2, zones), f32)],
        [tile_scratch(3 * (channels - 8)), tile_scratch(rows), tile_scratch(1)],
        [lam, y, plan, fact, outer, term, section_states, x_near, *received],
    )
    received, zone_terms = exchange(channels, to_send, zone_terms)
    near_outer, own, zone_terms = call(
        local_zero_kernel,
        "local_zero",
        [
            tiles(3 * channels),
            tiles(rows),
            jax.ShapeDtypeStruct(zone_terms.shape, f32),
        ],
        matrix_scratch,
        [lam, y, plan, zone_terms],
        apart=(3,),
        aliases={3: 2},
    )
    all_terms = lax.all_to_all(zone_terms, ("gx", "gy"), 0, 0)
    adjoint, last = call(
        last_kernel,
        "section_zero",
        [tiles(rows), tiles(1)],
        [tile_scratch(3 * channels)] + section_scratch,
        [base, y, plan, fact, own, near_outer, *received],
    )
    (zone_grads,) = call(
        total_kernel,
        "zone_total",
        [jax.ShapeDtypeStruct((2, zones), f32)],
        [],
        [all_terms, last],
    )
    return adjoint.reshape(cotangent.shape), zone_grads


def solution(mesh):
    placed = (
        P("gx", "gy", None, None),
        P(None, "gx", "gy", None, None),
        P("gx", "gy", None),
        P("gx", "gy", None, None),
        P("gx", "gy", None),
        P("gx", "gy", None),
        P(),
        P(),
        P("gx", "gy", None),
        P("gx", "gy", None),
        P("gx", "gy", None, None),
        P("gx", "gy", None),
        P("gx", "gy", None, None),
        P(),
        P(),
        P(),
    )
    return jax.shard_map(
        local,
        mesh=mesh,
        in_specs=placed,
        out_specs=(P("gx", "gy", None, None), P()),
        check_vma=False,
    )
```

```python
import functools
import jax
import jax.numpy as jnp
from jax import lax
from jax.experimental import pallas as pl
from jax.experimental.pallas import tpu as pltpu
from jax.sharding import PartitionSpec as P

TIME_STEP = 0.2
SALT_RETURN = 0.5
LATERAL = 0.5
GRAD_WEIGHT = 1.0 / 64.0
FACE_NODES = ((1, 2), (2, 0), (0, 1))
NODE_FACES = (((1, 1), (2, 0)), ((0, 0), (2, 1)), ((0, 1), (1, 0)))
SUB = 8
LANES = 128


WET_AREA, KAPPA, HALF_KAPPA_AREA, WET, EDGE, FRICTION_BASE, ZONE_FRICTION, ZONE_ID = (
    0,
    1,
    2,
    3,
    4,
    7,
    10,
    11,
)
CONDUCTIVITY = 12
STAT_ROWS = 13
NEAR_VMEM, FAR_VMEM = 32, 60
OUTER_EDGE, OUTER_ZONE, HALF_SPEED = 0, 3, 6
FACT_ROWS = 15
X_ROWS = 24
CORNER_LANES = 16
CORNER_BLOCK = 8


def swapped(x, axis, first):
    peers = lax.axis_size(axis)
    lows = range(first, peers - 1, 2)
    return lax.ppermute(x, axis, [(i, i + 1) for i in lows] + [(i + 1, i) for i in lows])


def tile(ref, row):
    return ref[row * SUB : (row + 1) * SUB, :]


def put(ref, row, value):
    ref[row * SUB : (row + 1) * SUB, :] = value


def take(row, lane_index):
    return jnp.take_along_axis(row, lane_index, axis=1, mode="promise_in_bounds")


def spread(ref, row):
    return jnp.broadcast_to(ref[pl.ds(row, 1), :], (SUB, LANES))


def rows_to_tiles(read, tiles_ref, count):
    for block in range(SUB):
        tiles_ref[pl.ds(block, count, stride=SUB), :] = read(block)


def lanes_of(block):
    return slice(block * LANES, (block + 1) * LANES)


def gather_tile(src, row, lane_index, sublane_index):
    found = take(spread(src, row * SUB), lane_index)
    for sub in range(1, SUB):
        got = take(spread(src, row * SUB + sub), lane_index)
        found = jnp.where(sublane_index == sub, got, found)
    return found


def pick(face, for_zero, for_one, for_two):
    return jnp.where(face == 0, for_zero, jnp.where(face == 1, for_one, for_two))


def gather_ends(src, row, lane_index, sublane_index, face):
    n0, n1, n2 = [gather_tile(src, row + i, lane_index, sublane_index) for i in range(3)]
    return pick(face, n1, n2, n0), pick(face, n2, n0, n1)


def gather_by_face(src, row, lane_index, sublane_index, face):
    return pick(
        face, *[gather_tile(src, row + i, lane_index, sublane_index) for i in range(3)]
    )


def corner_rows(channels):
    return (channels * CORNER_LANES + LANES - 1) // LANES


def message_rows(channels):
    return channels + corner_rows(channels)


def corner_lane(shape):
    return lax.broadcasted_iota(jnp.int32, shape, 1) % CORNER_LANES


class Received:
    def __init__(self, messages, channels, corner_ref):
        _, _, y1, y2 = messages
        self.mains = messages
        self.corner_ref = corner_ref
        rows = slice(channels, message_rows(channels))
        count = corner_rows(channels)
        lane = corner_lane((count, LANES))
        corner_ref[0:count, :] = jnp.where(
            jnp.bitwise_and(lane, 4) == 0, y1[0, rows, :], y2[0, rows, :]
        )

    def fill(self, row, lane_index, remote_index, value):
        for number, ref in enumerate(self.mains):
            for half in range(2):
                got = take(spread(ref.at[half], row), lane_index)
                value = jnp.where(remote_index == 2 * number + half, got, value)
        channels_a_row = LANES // CORNER_LANES
        lane = lane_index + row % channels_a_row * CORNER_LANES
        line = spread(self.corner_ref, row // channels_a_row)
        got = take(line, jnp.bitwise_and(lane, LANES - 1))
        return jnp.where(remote_index == CORNER_BLOCK, got, value)


INDEX_ROWS = 18
MATRIX_ROWS = 4


def plan_rows(rows):
    return STAT_ROWS + INDEX_ROWS + MATRIX_ROWS + rows + 13


def plan_parts(plan_ref):
    parts, at = [], 0
    for count in (STAT_ROWS, INDEX_ROWS, MATRIX_ROWS):
        parts.append(plan_ref.at[at * SUB : (at + count) * SUB])
        at += count
    return (*parts, plan_ref.at[at * SUB :])


def tile_at(ref, row):
    return ref[pl.ds(pl.multiple_of(row * SUB, SUB), SUB), :]


def index_at(ref, row):
    return tile_at(ref, row).astype(jnp.int32)


def index_of(ref, row):
    return tile(ref, row).astype(jnp.int32)


def put_index(ref, row, value):
    put(ref, row, value.astype(jnp.float32))


def load_matrices(plan_ref, matrix_ref, sem):
    copy = pltpu.make_async_copy(plan_parts(plan_ref)[2], matrix_ref, sem.at[0])
    copy.start()
    return copy


def put_at(ref, row, value):
    ref[pl.ds(pl.multiple_of(row * SUB, SUB), SUB), :] = value


class Sender:
    def __init__(self, index_ref, sent_ref, packed_ref):
        self.straight = [index_of(index_ref, 12 + 2 * n) for n in range(3)]
        self.lane, sublane, self.face = [index_of(index_ref, 13 + 2 * n) for n in range(3)]
        sub = lax.broadcasted_iota(jnp.int32, (SUB, LANES), 0)
        slot = lax.broadcasted_iota(jnp.int32, (SUB, LANES), 1)
        self.own = (sub == sublane) & (slot < CORNER_LANES)
        self.sent_ref, self.packed_ref = sent_ref, packed_ref
        self.group = None

    def corner(self, src, row):
        return jnp.where(self.own, take(tile(src, row), self.lane), 0.0)

    def put(self, channel, value, corner):
        put(self.sent_ref, channel, value)
        place = channel % SUB
        moved = corner if place == 0 else pltpu.roll(corner, CORNER_LANES * place, 1)
        self.group = moved if place == 0 else self.group + moved
        if place == SUB - 1:
            self.flush(channel)

    def flush(self, channel):
        at = channel // SUB
        self.packed_ref[at : at + 1, :] = jnp.sum(self.group, axis=0, keepdims=True)

    def states(self, src, first_comp, comps):
        for comp in range(comps):
            row = (first_comp + comp) * 3
            ends = gather_ends(src, row, *self.straight)
            n0, n1, n2 = [self.corner(src, row + i) for i in range(3)]
            corners = pick(self.face, n1, n2, n0), pick(self.face, n2, n0, n1)
            for j in range(2):
                self.put(comp * 2 + j, ends[j], corners[j])

    def by_face(self, src, row, channel):
        corner = pick(self.face, *[self.corner(src, row + i) for i in range(3)])
        self.put(channel, gather_by_face(src, row, *self.straight), corner)

    def by_element(self, src, row, channel):
        self.put(channel, gather_tile(src, row, *self.straight[:2]), self.corner(src, row))


def write_messages(sent_ref, packed_ref, first, channels, outs, total):
    for role, out in enumerate(outs):
        for half in range(2):
            out[half, first : first + channels, :] = sent_ref[
                pl.ds(role * 2 + half, channels, stride=SUB), :
            ]
    count, at = corner_rows(channels), total + first // SUB
    for out in outs[:2]:
        out[0, at : at + count, :] = packed_ref[0:count, :]


def prepare_kernel(
    cot_ref,
    x_ref,
    area_ref,
    edge_ref,
    rough_ref,
    soil_ref,
    friction_ref,
    conduct_ref,
    wet_ref,
    zone_ref,
    send_ref,
    partner_ref,
    in_ref,
    out_ref,
    volume_ref,
    plan_ref,
    to_x1,
    to_x2,
    to_y1,
    to_y2,
    x_tiles,
    sent_ref,
    packed_ref,
    *fetched,
):
    *fetched, sems = fetched
    stat_ref, index_ref, matrix_ref, table_ref = plan_parts(plan_ref)
    sources = [
        partner_ref,
        send_ref,
        cot_ref,
        x_ref.at[:, 0, 0, 0:16],
        area_ref,
        edge_ref,
        rough_ref,
        soil_ref,
        friction_ref,
        conduct_ref,
        wet_ref,
        zone_ref,
        in_ref,
        out_ref,
        volume_ref,
    ]
    copies = [
        pltpu.make_async_copy(source, target, sems.at[n])
        for n, (source, target) in enumerate(zip(sources, fetched))
    ]
    for copy in copies:
        copy.start()
    for copy in copies[:2]:
        copy.wait()
    (
        partner_ref,
        send_ref,
        cot_ref,
        x_ref,
        area_ref,
        edge_ref,
        rough_ref,
        soil_ref,
        friction_ref,
        conduct_ref,
        wet_ref,
        zone_ref,
        in_ref,
        out_ref,
        volume_ref,
    ) = fetched
    rows = cot_ref.shape[0] // SUB
    sections = x_ref.shape[0]
    odd_a, odd_b = 1 - lax.axis_index("gx") % 2, 1 - lax.axis_index("gy") % 2
    straight = (6 - 5 * odd_a, 1 + 5 * odd_a, 4 - odd_b, 3 + odd_b)
    right, up = 1 - odd_a, 1 - odd_b
    corners = (
        5 * right + 2 * up,
        5 * right + 2 - 2 * up,
        5 - 5 * right + 2 * up,
        7 - 5 * right - 2 * up,
    )
    face_total = 3 * SUB * LANES
    for f in range(3):
        partner = tile(partner_ref, f)
        beyond = partner - face_total
        direction = jnp.right_shift(beyond, 8)
        half = jnp.bitwise_and(jnp.right_shift(beyond, 7), 1)
        lane = jnp.bitwise_and(partner, LANES - 1)
        remote = jnp.where(beyond >= 0, CORNER_BLOCK, -1)
        for number, toward in enumerate(straight):
            remote = jnp.where(direction == toward, 2 * number + half, remote)
        for number, toward in enumerate(corners):
            lane = jnp.where(direction == toward, lane % 4 + 4 * number, lane)
        put_index(index_ref, f, lane)
        put_index(index_ref, 3 + f, jnp.bitwise_and(jnp.right_shift(partner, 7), SUB - 1))
        put_index(index_ref, 6 + f, jnp.right_shift(partner, 10))
        put_index(index_ref, 9 + f, remote)
    sub_iota = lax.broadcasted_iota(jnp.int32, (SUB, LANES), 0)
    lane_iota = lax.broadcasted_iota(jnp.int32, (SUB, LANES), 1)

    def slots_to(choices, choice, half):
        rows_of = [
            jnp.broadcast_to(send_ref[0, 0, n : n + 1, lanes_of(half)], (SUB, LANES))
            for n in choices
        ]
        found = rows_of[0]
        for n, row in zip(choices[1:], rows_of[1:]):
            found = jnp.where(choice == n, row, found)
        return found

    straight_slots = None
    for number, toward in enumerate(straight):
        for half in range(2):
            row = slots_to((1, 6) if number < 2 else (3, 4), toward, half)
            straight_slots = (
                row
                if straight_slots is None
                else jnp.where(sub_iota == 2 * number + half, row, straight_slots)
            )
    corner_slots = None
    for number, toward in enumerate(corners):
        row = slots_to((0, 2, 5, 7), toward, 0)
        if number == 0:
            corner_slots = row
        else:
            moved = pltpu.roll(row, 4 * number, 1)
            corner_slots = jnp.where(lane_iota // 4 == number, moved, corner_slots)
    for d, slots in enumerate((straight_slots, corner_slots)):
        put_index(index_ref, 12 + d, jnp.bitwise_and(slots, LANES - 1))
        put_index(index_ref, 14 + d, jnp.bitwise_and(jnp.right_shift(slots, 7), SUB - 1))
        put_index(index_ref, 16 + d, jnp.right_shift(slots, 10))
    for copy in copies[2:]:
        copy.wait()
    matrix_ref[0:8, 0:8] = in_ref[...]
    matrix_ref[8:16, 0:8] = out_ref[...]
    matrix_ref[16:28, 0:12] = volume_ref[...]
    zone = zone_ref[...]
    zone_lane = jnp.bitwise_and(zone, LANES - 1)
    zone_block = jnp.right_shift(zone, 7)
    factors = []
    for ref in (friction_ref, conduct_ref):
        found = None
        for block in range(ref.shape[0]):
            got = take(spread(ref, block), zone_lane)
            found = got if block == 0 else jnp.where(zone_block == block, got, found)
        factors.append(found)
    area = area_ref[...]
    wet = wet_ref[...].astype(jnp.float32)
    kappa = factors[1] * soil_ref[...]
    wet_area = wet * area
    half_kappa_area = LATERAL * kappa * area
    put(stat_ref, WET_AREA, wet_area)
    put(stat_ref, KAPPA, kappa)
    put(stat_ref, HALF_KAPPA_AREA, half_kappa_area)
    put(stat_ref, WET, wet)
    put(stat_ref, ZONE_FRICTION, factors[0])
    put(stat_ref, ZONE_ID, zone.astype(jnp.float32))
    stat_ref[CONDUCTIVITY * SUB : CONDUCTIVITY * SUB + conduct_ref.shape[0], :] = conduct_ref[...]
    stat_ref[EDGE * SUB : (EDGE + 3) * SUB, :] = edge_ref[...]
    for k in range(sections):
        rows_to_tiles(
            lambda b: x_ref[k, :, lanes_of(b)].astype(jnp.float32), x_tiles, 16
        )
        squares = [tile(x_tiles, r) * tile(x_tiles, r) for r in range(12)]
        node_sum = [squares[i] + squares[3 + i] + squares[6 + i] + squares[9 + i] for i in range(3)]
        for f in range(3):
            first, second = FACE_NODES[f]
            put(table_ref, rows + 3 + 3 * k + f, node_sum[first] + node_sum[second])
        momentum = squares[3]
        for r in range(4, 9):
            momentum = momentum + squares[r]
        put(
            stat_ref,
            FRICTION_BASE + k,
            rough_ref[...] * jnp.sqrt(1.0 + momentum * (1.0 / 6.0)),
        )
    for f in range(3):
        put(table_ref, rows + f, tile(stat_ref, EDGE + f))
    put(table_ref, rows + 12, zone.astype(jnp.float32))
    for r in range(rows):
        put(table_ref, r, tile(cot_ref, r) * (wet_area if r < 12 else half_kappa_area))
    comps = rows // 3
    channels = comps * 2 + 5
    sender = Sender(index_ref, sent_ref, packed_ref)
    sender.states(table_ref, 0, comps)
    for group in range(4):
        sender.by_face(table_ref, rows + 3 * group, comps * 2 + group)
    sender.by_element(table_ref, rows + 12, channels - 1)
    sender.flush(channels - 1)
    write_messages(sent_ref, packed_ref, 0, channels, (to_x1, to_x2, to_y1, to_y2), channels)


def corner_kernel(channels, x1, x2, old_y1, old_y2, *rest):
    y1, y2 = rest[1:3]
    rows = slice(channels, message_rows(channels))
    lane = corner_lane((corner_rows(channels), LANES))
    merged = jnp.where(lane < 8, x1[0, rows, :], x2[0, rows, :])
    y1[0, rows, :] = merged
    y2[0, rows, :] = merged


def local_states(src, first_comp, comps, index_ref, out_ref):
    def body(f, carry):
        lane, sublane, face = [index_at(index_ref, n * 3 + f) for n in range(3)]
        for comp in range(comps):
            ends = gather_ends(src, (first_comp + comp) * 3, lane, sublane, face)
            for j in range(2):
                put_at(out_ref, f * comps * 2 + comp * 2 + j, ends[j])
        return carry

    lax.fori_loop(0, 3, body, 0)


def remote_states(received, first_row, channels, index_ref, local_ref, out_ref):
    def body(f, carry):
        lane, remote = index_at(index_ref, f), index_at(index_ref, 9 + f)
        for ch in range(channels):
            value = tile_at(local_ref, f * channels + ch)
            put_at(
                out_ref, f * channels + ch, received.fill(first_row + ch, lane, remote, value)
            )
        return carry

    lax.fori_loop(0, 3, body, 0)


def transposed_own(section, lam_ref, y_ref, stat_ref, matrix_ref, own_ref):
    rows = lam_ref.shape[0] // SUB
    layers = (rows - 12) // 3
    edge = [tile(stat_ref, EDGE + f) for f in range(3)]
    kappa = tile(stat_ref, KAPPA)
    wet = tile(stat_ref, WET)
    own = [tile(y_ref, r) for r in range(12)]
    result = []
    for r in range(12):
        total = matrix_ref[16, r] * own[0]
        for q in range(1, 12):
            total = total + matrix_ref[16 + q, r] * own[q]
        result.append(total)
    for f in range(3):
        ends = FACE_NODES[f]
        inner = [edge[f] * own[(ch // 2) * 3 + ends[ch % 2]] for ch in range(8)]
        for b in range(8):
            total = matrix_ref[0, b] * inner[0]
            for a in range(1, 8):
                total = total + matrix_ref[a, b] * inner[a]
            at = (b // 2) * 3 + ends[b % 2]
            result[at] = result[at] + total
    friction = tile(stat_ref, ZONE_FRICTION) * tile(stat_ref, FRICTION_BASE + section) * wet
    for r in range(3, 9):
        result[r] = result[r] - friction * tile(lam_ref, r)
    exchange = []
    for i in range(3):
        top = tile(lam_ref, 12 + i) - SALT_RETURN * wet * tile(lam_ref, 9 + i)
        exchange.append(kappa * top)
        result[9 + i] = result[9 + i] + exchange[i]
    for r in range(12):
        put(own_ref, r, result[r])
    for i in range(3):
        (f0, _), (f1, _) = NODE_FACES[i]
        both = edge[f0] + edge[f1]
        from_above = exchange[i]
        for layer in range(layers):
            r = 12 + layer * 3 + i
            value = -(both * tile(y_ref, r)) - from_above
            if layer + 1 < layers:
                from_above = kappa * (tile(lam_ref, r + 3) - tile(lam_ref, r))
                value = value + from_above
            put(own_ref, r, value)


def transposed_section(
    section, own_ref, y_ref, outer_ref, stat_ref, fact_ref, matrix_ref, emit
):
    rows = own_ref.shape[0] // SUB
    channels = rows // 3 * 2
    layers = (rows - 12) // 3
    outer_edge = [tile(fact_ref, OUTER_EDGE + f) for f in range(3)]
    result = [tile(own_ref, r) for r in range(12)]
    for f in range(3):
        edge = tile(stat_ref, EDGE + f)
        half_speed = tile(fact_ref, HALF_SPEED + 3 * section + f)
        ends = FACE_NODES[f]
        outer = [outer_edge[f] * tile(outer_ref, f * channels + ch) for ch in range(8)]
        for b in range(8):
            at = (b // 2) * 3 + ends[b % 2]
            total = half_speed * (edge * tile(y_ref, at) - outer[b])
            for a in range(8):
                total = total - matrix_ref[8 + a, b] * outer[a]
            result[at] = result[at] + total
    for r in range(12):
        emit(r, result[r])
    for i in range(3):
        (f0, j0), (f1, j1) = NODE_FACES[i]
        for layer in range(layers):
            r = 12 + layer * 3 + i
            emit(
                r,
                tile(own_ref, r)
                + outer_edge[f0] * tile(outer_ref, f0 * channels + 8 + layer * 2 + j0)
                + outer_edge[f1] * tile(outer_ref, f1 * channels + 8 + layer * 2 + j1),
            )


def own_gradients(section, weight, lam_ref, y_ref, x_tiles, stat_ref):
    rows = lam_ref.shape[0] // SUB
    layers = (rows - 12) // 3
    wet = tile(stat_ref, WET)
    kappa = tile(stat_ref, KAPPA)
    momentum = tile(lam_ref, 3) * tile(x_tiles, 3)
    for r in range(4, 9):
        momentum = momentum + tile(lam_ref, r) * tile(x_tiles, r)
    friction = -(weight * wet * tile(stat_ref, FRICTION_BASE + section)) * momentum
    vertical = None
    lateral = None
    for i in range(3):
        (f0, _), (f1, _) = NODE_FACES[i]
        top = tile(lam_ref, 12 + i) - SALT_RETURN * wet * tile(lam_ref, 9 + i)
        total = top * (tile(x_tiles, 9 + i) - tile(x_tiles, 12 + i))
        dots = None
        for layer in range(layers):
            r = 12 + layer * 3 + i
            term = tile(y_ref, r) * tile(x_tiles, r)
            dots = term if dots is None else dots + term
            if layer + 1 < layers:
                total = total + (tile(lam_ref, r + 3) - tile(lam_ref, r)) * (
                    tile(x_tiles, r) - tile(x_tiles, r + 3)
                )
        side = (tile(stat_ref, EDGE + f0) + tile(stat_ref, EDGE + f1)) * dots
        vertical = total if vertical is None else vertical + total
        lateral = side if lateral is None else lateral + side
    return friction, weight * (kappa * vertical - lateral)


def outer_gradients(weight, outer_ref, x_tiles, fact_ref):
    channels = outer_ref.shape[0] // SUB // 3
    values = []
    for f in range(3):
        total = None
        for ch in range(8, channels):
            row = 12 + (ch - 8) // 2 * 3 + FACE_NODES[f][ch % 2]
            term = tile(outer_ref, f * channels + ch) * tile(x_tiles, row)
            total = term if total is None else total + term
        values.append(weight * tile(fact_ref, OUTER_EDGE + f) * total)
    return values


def x_to_tiles(x_ref, section, x_tiles):
    rows = x_ref.shape[3]
    rows_to_tiles(
        lambda b: x_ref[section, 0, 0, :, lanes_of(b)].astype(jnp.float32), x_tiles, rows
    )


def local_two_kernel(
    cot_ref,
    plan_ref,
    x_ref,
    outer_ref,
    near_ref,
    term_ref,
    own_ref,
    x_tiles,
    matrix_ref,
    sem,
):
    matrices = load_matrices(plan_ref, matrix_ref, sem)
    stat_ref, index_ref, _, table_ref = plan_parts(plan_ref)
    rows = cot_ref.shape[0] // SUB
    local_states(table_ref, 0, rows // 3, index_ref, outer_ref)
    for f in range(3):
        lane, sublane, face = [index_of(index_ref, n * 3 + f) for n in range(3)]
        for group in range(4):
            value = gather_by_face(table_ref, rows + 3 * group, lane, sublane, face)
            put(near_ref, f * 5 + group, value)
        put(near_ref, f * 5 + 4, gather_tile(table_ref, rows + 12, lane, sublane))
    x_to_tiles(x_ref, 2, x_tiles)
    friction, conduct = own_gradients(
        2, TIME_STEP * 2.0 / 3.0, cot_ref, table_ref, x_tiles, stat_ref
    )
    put(term_ref, 0, friction)
    put(term_ref, 1, conduct)
    matrices.wait()
    transposed_own(2, cot_ref, table_ref, stat_ref, matrix_ref, own_ref)


def local_x_kernel(plan_ref, x_ref, x_outer_ref, sent_ref, packed_ref, x_tiles):
    index_ref = plan_parts(plan_ref)[1]
    comps = x_ref.shape[3] // 3
    x_to_tiles(x_ref, 0, x_tiles)
    local_states(x_tiles, 4, comps - 4, index_ref, x_outer_ref)
    sender = Sender(index_ref, sent_ref, packed_ref)
    sender.states(x_tiles, 4, comps - 4)
    sender.flush(comps * 2 - 9)


def second_kernel(
    cot_ref,
    plan_ref,
    own_ref,
    near_outer_ref,
    near_ref,
    x_sent_ref,
    x_packed_ref,
    from_x1,
    from_x2,
    from_y1,
    from_y2,
    lam_ref,
    y_ref,
    fact_ref,
    outer_ref,
    to_x1,
    to_x2,
    to_y1,
    to_y2,
    sent_ref,
    packed_ref,
    corner_ref,
    matrix_ref,
    sem,
):
    matrices = load_matrices(plan_ref, matrix_ref, sem)
    stat_ref, index_ref, _, table_ref = plan_parts(plan_ref)
    rows = cot_ref.shape[0] // SUB
    comps = rows // 3
    channels = comps * 2
    received = Received((from_x1, from_x2, from_y1, from_y2), channels + 5, corner_ref)
    remote_states(received, 0, channels, index_ref, near_outer_ref, outer_ref)
    for f in range(3):
        lane, remote = index_of(index_ref, f), index_of(index_ref, 9 + f)
        for group in range(5):
            value = received.fill(channels + group, lane, remote, tile(near_ref, f * 5 + group))
            if group == 0:
                put(fact_ref, OUTER_EDGE + f, value)
            elif group == 4:
                put(fact_ref, OUTER_ZONE + f, value)
            else:
                both = tile(table_ref, rows + 3 * group + f) + value
                put(
                    fact_ref,
                    HALF_SPEED + 3 * (group - 1) + f,
                    0.5 * jnp.sqrt(1.0 + (0.25 / 8.0) * both),
                )
    wet_area = tile(stat_ref, WET_AREA)
    half_kappa_area = tile(stat_ref, HALF_KAPPA_AREA)

    def emit(r, value):
        lam = (2.0 / 3.0) * (tile(cot_ref, r) + TIME_STEP * value)
        put(lam_ref, r, lam)
        put(y_ref, r, lam * (wet_area if r < 12 else half_kappa_area))

    matrices.wait()
    transposed_section(
        2, own_ref, table_ref, outer_ref, stat_ref, fact_ref, matrix_ref, emit
    )
    sender = Sender(index_ref, sent_ref, packed_ref)
    sender.states(y_ref, 0, comps)
    sender.flush(channels - 1)
    outs = (to_x1, to_x2, to_y1, to_y2)
    write_messages(x_sent_ref, x_packed_ref, 0, channels - 8, outs, X_ROWS + channels)
    write_messages(sent_ref, packed_ref, X_ROWS, channels, outs, X_ROWS + channels)


def local_one_kernel(
    lam_ref,
    y_ref,
    plan_ref,
    fact_ref,
    old_outer_ref,
    old_term_ref,
    x_ref,
    outer_ref,
    term_ref,
    own_ref,
    x_tiles,
    matrix_ref,
    sem,
):
    matrices = load_matrices(plan_ref, matrix_ref, sem)
    stat_ref, index_ref, _, _ = plan_parts(plan_ref)
    local_states(y_ref, 0, lam_ref.shape[0] // SUB // 3, index_ref, outer_ref)
    x_to_tiles(x_ref, 2, x_tiles)
    weight = TIME_STEP * 2.0 / 3.0
    for f, value in enumerate(outer_gradients(weight, old_outer_ref, x_tiles, fact_ref)):
        put(term_ref, 2 + f, value)
    x_to_tiles(x_ref, 1, x_tiles)
    terms = own_gradients(1, TIME_STEP * 0.25, lam_ref, y_ref, x_tiles, stat_ref)
    for n in range(2):
        put(term_ref, n, tile(old_term_ref, n) + terms[n])
    matrices.wait()
    transposed_own(1, lam_ref, y_ref, stat_ref, matrix_ref, own_ref)


def first_kernel(
    cot_ref,
    lam_ref,
    y_ref,
    plan_ref,
    fact_ref,
    own_ref,
    near_outer_ref,
    from_x1,
    from_x2,
    from_y1,
    from_y2,
    base_ref,
    next_ref,
    next_y_ref,
    outer_ref,
    to_x1,
    to_x2,
    to_y1,
    to_y2,
    sent_ref,
    packed_ref,
    corner_ref,
    matrix_ref,
    sem,
):
    matrices = load_matrices(plan_ref, matrix_ref, sem)
    stat_ref, index_ref, _, _ = plan_parts(plan_ref)
    comps = lam_ref.shape[0] // SUB // 3
    channels = comps * 2
    received = Received((from_x1, from_x2, from_y1, from_y2), X_ROWS + channels, corner_ref)
    remote_states(received, X_ROWS, channels, index_ref, near_outer_ref, outer_ref)
    wet_area = tile(stat_ref, WET_AREA)
    half_kappa_area = tile(stat_ref, HALF_KAPPA_AREA)

    def emit(r, value):
        old = tile(lam_ref, r)
        lam = 0.25 * (old + TIME_STEP * value)
        put(next_ref, r, lam)
        put(next_y_ref, r, lam * (wet_area if r < 12 else half_kappa_area))
        put(base_ref, r, (1.0 / 3.0) * tile(cot_ref, r) + 0.75 * old + lam)

    matrices.wait()
    transposed_section(
        1, own_ref, y_ref, outer_ref, stat_ref, fact_ref, matrix_ref, emit
    )
    sender = Sender(index_ref, sent_ref, packed_ref)
    sender.states(next_y_ref, 0, comps)
    sender.flush(channels - 1)
    write_messages(sent_ref, packed_ref, 0, channels, (to_x1, to_x2, to_y1, to_y2), channels)


def zone_kernel(
    lam_ref,
    y_ref,
    plan_ref,
    fact_ref,
    old_outer_ref,
    term_ref,
    x_ref,
    x_near_ref,
    from_x1,
    from_x2,
    from_y1,
    from_y2,
    out_ref,
    x_outer_ref,
    x_tiles,
    corner_ref,
):
    stat_ref, index_ref, _, _ = plan_parts(plan_ref)
    rows = lam_ref.shape[0] // SUB
    channels = rows // 3 * 2
    x_channels = channels - 8
    received = Received((from_x1, from_x2, from_y1, from_y2), X_ROWS + channels, corner_ref)
    remote_states(received, 0, x_channels, index_ref, x_near_ref, x_outer_ref)
    x_to_tiles(x_ref, 1, x_tiles)
    outer_terms = outer_gradients(TIME_STEP * 0.25, old_outer_ref, x_tiles, fact_ref)
    outer_terms = [tile(term_ref, 2 + f) + outer_terms[f] for f in range(3)]
    x_to_tiles(x_ref, 0, x_tiles)
    friction_term, conduct_term = own_gradients(
        0, TIME_STEP, lam_ref, y_ref, x_tiles, stat_ref
    )
    friction_term = friction_term + tile(term_ref, 0)
    conduct_term = conduct_term + tile(term_ref, 1)
    for f in range(3):
        total = None
        for ch in range(x_channels):
            row = 12 + ch // 2 * 3 + FACE_NODES[f][ch % 2]
            term = tile(x_outer_ref, f * x_channels + ch) * tile(y_ref, row)
            total = term if total is None else total + term
        conduct_term = conduct_term + TIME_STEP * tile(stat_ref, EDGE + f) * total

    zones = out_ref.shape[2]
    zone_iota = lax.broadcasted_iota(jnp.int32, (zones, LANES), 0).astype(jnp.float32)
    sub_iota = lax.broadcasted_iota(jnp.int32, (SUB, zones), 0)

    def thirds(value):
        high = value.astype(jnp.bfloat16).astype(jnp.float32)
        rest = value - high
        middle = rest.astype(jnp.bfloat16).astype(jnp.float32)
        return [high, middle, rest - middle]

    def by_zone(values, zone_of, zone_row):
        pieces = sum([thirds(value) for value in values], [])
        left = jnp.concatenate(pieces, axis=0).astype(jnp.bfloat16)
        totals = [jnp.zeros((SUB, zones), jnp.float32) for _ in values]
        for sub in range(SUB):
            line = zone_of[pl.ds(zone_row * SUB + sub, 1), :]
            hot = (jnp.broadcast_to(line, (zones, LANES)) == zone_iota).astype(jnp.float32)
            dots = lax.dot_general(
                left,
                hot.astype(jnp.bfloat16),
                (((1,), (1,)), ((), ())),
                preferred_element_type=jnp.float32,
            )
            for n in range(len(values)):
                at = n * 3 * SUB
                three = dots[at : at + SUB] + dots[at + SUB : at + 2 * SUB]
                three = three + dots[at + 2 * SUB : at + 3 * SUB]
                totals[n] = totals[n] + jnp.where(sub_iota == sub, three, 0.0)
        return totals

    friction, conduct = by_zone([friction_term, conduct_term], stat_ref, ZONE_ID)
    for f in range(3):
        conduct = conduct + by_zone([outer_terms[f]], fact_ref, OUTER_ZONE + f)[0]
    friction = GRAD_WEIGHT * jnp.sum(friction, axis=0, keepdims=True)
    conduct = GRAD_WEIGHT * jnp.sum(conduct, axis=0, keepdims=True)
    factors = [
        stat_ref[CONDUCTIVITY * SUB + n : CONDUCTIVITY * SUB + n + 1, :]
        for n in range(zones // LANES)
    ]
    conduct = conduct / jnp.concatenate(factors, axis=1)
    for device in range(out_ref.shape[0]):
        out_ref[device, 0:1, :] = friction
        out_ref[device, 1:2, :] = conduct


def after_kernel(zone_in, message_ref, zone_ref):
    pass


def local_zero_kernel(lam_ref, y_ref, plan_ref, outer_ref, own_ref, matrix_ref, sem):
    matrices = load_matrices(plan_ref, matrix_ref, sem)
    stat_ref, index_ref, _, _ = plan_parts(plan_ref)
    local_states(y_ref, 0, y_ref.shape[0] // SUB // 3, index_ref, outer_ref)
    matrices.wait()
    transposed_own(0, lam_ref, y_ref, stat_ref, matrix_ref, own_ref)


def last_kernel(
    base_ref,
    y_ref,
    plan_ref,
    fact_ref,
    own_ref,
    near_outer_ref,
    from_x1,
    from_x2,
    from_y1,
    from_y2,
    adjoint_ref,
    last_ref,
    outer_ref,
    corner_ref,
    matrix_ref,
    sem,
):
    matrices = load_matrices(plan_ref, matrix_ref, sem)
    stat_ref, index_ref, _, _ = plan_parts(plan_ref)
    rows = y_ref.shape[0] // SUB
    channels = rows // 3 * 2
    received = Received((from_x1, from_x2, from_y1, from_y2), channels, corner_ref)
    remote_states(received, 0, channels, index_ref, near_outer_ref, outer_ref)

    def emit(r, value):
        put(adjoint_ref, r, tile(base_ref, r) + TIME_STEP * value)

    matrices.wait()
    transposed_section(
        0, own_ref, y_ref, outer_ref, stat_ref, fact_ref, matrix_ref, emit
    )
    last_ref[...] = tile(adjoint_ref, rows - 1)


def total_kernel(zone_ref, adjoint_ref, grads_ref):
    grads_ref[...] = jnp.sum(zone_ref[...], axis=0)


def exchange(channels, messages, ahead):
    x1, x2, y1, y2 = messages
    x1, x2 = swapped(x1, "gx", 1), swapped(x2, "gx", 0)
    y1, y2, ahead = call(
        functools.partial(corner_kernel, channels),
        "corners",
        [jax.ShapeDtypeStruct(one.shape, one.dtype) for one in (y1, y2, ahead)],
        [],
        [x1, x2, y1, y2, ahead],
        apart=(4,),
        aliases={2: 0, 3: 1, 4: 2},
    )
    return (x1, x2, swapped(y1, "gy", 1), swapped(y2, "gy", 0)), ahead


def call(kernel, name, outs, scratch, operands, far=False, apart=(), aliases={}):
    near = pl.BlockSpec(memory_space=pltpu.VMEM)
    in_place = pl.BlockSpec(memory_space=pl.ANY)
    specs = [in_place if far or n in apart else near for n in range(len(operands))]
    handed_on = [aliases[n] for n in apart if n in aliases]
    return pl.pallas_call(
        kernel,
        in_specs=specs,
        out_specs=[in_place if n in handed_on else near for n in range(len(outs))],
        out_shape=outs,
        scratch_shapes=scratch,
        input_output_aliases=aliases,
        compiler_params=pltpu.CompilerParams(
            vmem_limit_bytes=(FAR_VMEM if far else NEAR_VMEM) * 1024 * 1024
        ),
        name=name,
    )(*operands)


def local(
    cotangent,
    section_states,
    inverse_area,
    edge_length,
    roughness,
    soil_conductance,
    zone_friction,
    zone_conductivity,
    wet_mask,
    element_zone,
    send_face,
    send_count,
    face_partner,
    volume_matrix,
    flux_in,
    flux_out,
):
    rows = cotangent.shape[2]
    channels = rows // 3 * 2
    zones = zone_friction.shape[0]
    slots = send_face.shape[3]
    devices = lax.axis_size("gx") * lax.axis_size("gy")
    f32 = jnp.float32

    def tiles(count, dtype=f32):
        return jax.ShapeDtypeStruct((count * SUB, LANES), dtype)

    def tile_scratch(count, dtype=f32):
        return pltpu.VMEM((count * SUB, LANES), dtype)

    def messages(count):
        return [jax.ShapeDtypeStruct((slots // LANES, message_rows(count), LANES), f32)] * 4

    def sent_tiles(count):
        return corner_rows(count) * SUB

    matrix_scratch = [
        pltpu.SMEM((MATRIX_ROWS * SUB, LANES), f32),
        pltpu.SemaphoreType.DMA((1,)),
    ]
    section_scratch = [pltpu.VMEM((SUB, LANES), f32)] + matrix_scratch

    square = lambda one: one.reshape(SUB, LANES)
    cot = cotangent.reshape(rows * SUB, LANES)
    plan, *to_send = call(
        prepare_kernel,
        "prepare",
        [tiles(plan_rows(rows))] + messages(channels + 5),
        [
            tile_scratch(16),
            tile_scratch(sent_tiles(channels + 5)),
            tile_scratch(1),
            tile_scratch(3, jnp.int32),
            pltpu.VMEM(send_face.shape, jnp.int32),
            tile_scratch(rows),
            pltpu.VMEM((section_states.shape[0], 16, SUB * LANES), section_states.dtype),
            tile_scratch(1),
            tile_scratch(3),
            tile_scratch(1),
            tile_scratch(1),
            pltpu.VMEM((zones // LANES, LANES), f32),
            pltpu.VMEM((zones // LANES, LANES), f32),
            tile_scratch(1, jnp.int32),
            tile_scratch(1, jnp.int32),
            pltpu.VMEM(flux_in.shape, f32),
            pltpu.VMEM(flux_out.shape, f32),
            pltpu.VMEM(volume_matrix.shape, f32),
            pltpu.SemaphoreType.DMA((15,)),
        ],
        [
            cot,
            section_states,
            square(inverse_area),
            edge_length.reshape(3 * SUB, LANES),
            square(roughness),
            square(soil_conductance),
            zone_friction.reshape(-1, LANES),
            zone_conductivity.reshape(-1, LANES),
            square(wet_mask),
            square(element_zone),
            send_face,
            face_partner.reshape(3 * SUB, LANES),
            flux_in,
            flux_out,
            volume_matrix,
        ],
        far=True,
    )
    near_outer, near, term, own = call(
        local_two_kernel,
        "local_two",
        [tiles(3 * channels), tiles(15), tiles(2), tiles(rows)],
        [tile_scratch(rows)] + matrix_scratch,
        [cot, plan, section_states],
    )
    x_near, x_sent, x_packed = call(
        local_x_kernel,
        "local_x",
        [tiles(3 * (channels - 8)), tiles(sent_tiles(channels - 8)), tiles(1)],
        [tile_scratch(rows)],
        [plan, section_states],
    )
    received, term = exchange(channels + 5, to_send, term)
    lam, y, fact, outer, *to_send = call(
        second_kernel,
        "section_two",
        [tiles(rows), tiles(rows), tiles(FACT_ROWS), tiles(3 * channels)]
        + messages(X_ROWS + channels),
        [tile_scratch(sent_tiles(channels)), tile_scratch(1)] + section_scratch,
        [cot, plan, own, near_outer, near, x_sent, x_packed, *received],
    )
    near_outer, term, own = call(
        local_one_kernel,
        "local_one",
        [tiles(3 * channels), tiles(5), tiles(rows)],
        [tile_scratch(rows)] + matrix_scratch,
        [lam, y, plan, fact, outer, term, section_states],
    )
    received, term = exchange(X_ROWS + channels, to_send, term)
    base, lam, y, outer, *to_send = call(
        first_kernel,
        "section_one",
        [tiles(rows), tiles(rows), tiles(rows), tiles(3 * channels)] + messages(channels),
        [tile_scratch(sent_tiles(channels)), tile_scratch(1)] + section_scratch,
        [cot, lam, y, plan, fact, own, near_outer, *received],
    )
    (zone_terms,) = call(
        zone_kernel,
        "zone_sums",
        [jax.ShapeDtypeStruct((devices, 2, zones), f32)],
        [tile_scratch(3 * (channels - 8)), tile_scratch(rows), tile_scratch(1)],
        [lam, y, plan, fact, outer, term, section_states, x_near, *received],
    )
    received, zone_terms = exchange(channels, to_send, zone_terms)
    (zone_terms,) = call(
        after_kernel,
        "after",
        [jax.ShapeDtypeStruct(zone_terms.shape, f32)],
        [],
        [zone_terms, received[3]],
        apart=(0, 1),
        aliases={0: 0},
    )
    all_terms = lax.all_to_all(zone_terms, ("gx", "gy"), 0, 0)
    near_outer, own = call(
        local_zero_kernel,
        "local_zero",
        [tiles(3 * channels), tiles(rows)],
        matrix_scratch,
        [lam, y, plan],
    )
    adjoint, last = call(
        last_kernel,
        "section_zero",
        [tiles(rows), tiles(1)],
        [tile_scratch(3 * channels)] + section_scratch,
        [base, y, plan, fact, own, near_outer, *received],
    )
    (zone_grads,) = call(
        total_kernel,
        "zone_total",
        [jax.ShapeDtypeStruct((2, zones), f32)],
        [],
        [all_terms, last],
    )
    return adjoint.reshape(cotangent.shape), zone_grads


def solution(mesh):
    placed = (
        P("gx", "gy", None, None),
        P(None, "gx", "gy", None, None),
        P("gx", "gy", None),
        P("gx", "gy", None, None),
        P("gx", "gy", None),
        P("gx", "gy", None),
        P(),
        P(),
        P("gx", "gy", None),
        P("gx", "gy", None),
        P("gx", "gy", None, None),
        P("gx", "gy", None),
        P("gx", "gy", None, None),
        P(),
        P(),
        P(),
    )
    return jax.shard_map(
        local,
        mesh=mesh,
        in_specs=placed,
        out_specs=(P("gx", "gy", None, None), P()),
        check_vma=False,
    )
```

```python
import functools
import jax
import jax.numpy as jnp
from jax import lax
from jax.experimental import pallas as pl
from jax.experimental.pallas import tpu as pltpu
from jax.sharding import PartitionSpec as P

TIME_STEP = 0.2
SALT_RETURN = 0.5
LATERAL = 0.5
GRAD_WEIGHT = 1.0 / 64.0
FACE_NODES = ((1, 2), (2, 0), (0, 1))
NODE_FACES = (((1, 1), (2, 0)), ((0, 0), (2, 1)), ((0, 1), (1, 0)))
SUB = 8
LANES = 128


WET_AREA, KAPPA, HALF_KAPPA_AREA, WET, EDGE, FRICTION_BASE, ZONE_FRICTION, ZONE_ID = (
    0,
    1,
    2,
    3,
    4,
    7,
    10,
    11,
)
CONDUCTIVITY = 12
STAT_ROWS = 13
NEAR_VMEM, FAR_VMEM = 32, 60
OUTER_EDGE, OUTER_ZONE, HALF_SPEED = 0, 3, 6
FACT_ROWS = 15
X_ROWS = 24
CORNER_LANES = 16
CORNER_BLOCK = 8


def swapped(x, axis, first):
    peers = lax.axis_size(axis)
    lows = range(first, peers - 1, 2)
    return lax.ppermute(x, axis, [(i, i + 1) for i in lows] + [(i + 1, i) for i in lows])


def tile(ref, row):
    return ref[row * SUB : (row + 1) * SUB, :]


def put(ref, row, value):
    ref[row * SUB : (row + 1) * SUB, :] = value


def take(row, lane_index):
    return jnp.take_along_axis(row, lane_index, axis=1, mode="promise_in_bounds")


def spread(ref, row):
    return jnp.broadcast_to(ref[pl.ds(row, 1), :], (SUB, LANES))


def rows_to_tiles(read, tiles_ref, count):
    for block in range(SUB):
        tiles_ref[pl.ds(block, count, stride=SUB), :] = read(block)


def lanes_of(block):
    return slice(block * LANES, (block + 1) * LANES)


def gather_tile(src, row, lane_index, sublane_index):
    found = take(spread(src, row * SUB), lane_index)
    for sub in range(1, SUB):
        got = take(spread(src, row * SUB + sub), lane_index)
        found = jnp.where(sublane_index == sub, got, found)
    return found


def pick(face, for_zero, for_one, for_two):
    return jnp.where(face == 0, for_zero, jnp.where(face == 1, for_one, for_two))


def gather_ends(src, row, lane_index, sublane_index, face):
    n0, n1, n2 = [gather_tile(src, row + i, lane_index, sublane_index) for i in range(3)]
    return pick(face, n1, n2, n0), pick(face, n2, n0, n1)


def gather_by_face(src, row, lane_index, sublane_index, face):
    return pick(
        face, *[gather_tile(src, row + i, lane_index, sublane_index) for i in range(3)]
    )


def corner_rows(channels):
    return (channels * CORNER_LANES + LANES - 1) // LANES


def message_rows(channels):
    return channels + corner_rows(channels)


def corner_lane(shape):
    return lax.broadcasted_iota(jnp.int32, shape, 1) % CORNER_LANES


class Received:
    def __init__(self, messages, channels, corner_ref):
        _, _, y1, y2 = messages
        self.mains = messages
        self.corner_ref = corner_ref
        rows = slice(channels, message_rows(channels))
        count = corner_rows(channels)
        lane = corner_lane((count, LANES))
        corner_ref[0:count, :] = jnp.where(
            jnp.bitwise_and(lane, 4) == 0, y1[0, rows, :], y2[0, rows, :]
        )

    def fill(self, row, lane_index, remote_index, value):
        for number, ref in enumerate(self.mains):
            for half in range(2):
                got = take(spread(ref.at[half], row), lane_index)
                value = jnp.where(remote_index == 2 * number + half, got, value)
        channels_a_row = LANES // CORNER_LANES
        lane = lane_index + row % channels_a_row * CORNER_LANES
        line = spread(self.corner_ref, row // channels_a_row)
        got = take(line, jnp.bitwise_and(lane, LANES - 1))
        return jnp.where(remote_index == CORNER_BLOCK, got, value)


INDEX_ROWS = 18
MATRIX_ROWS = 4


def plan_rows(rows):
    return STAT_ROWS + INDEX_ROWS + MATRIX_ROWS + rows + 13


def plan_parts(plan_ref):
    parts, at = [], 0
    for count in (STAT_ROWS, INDEX_ROWS, MATRIX_ROWS):
        parts.append(plan_ref.at[at * SUB : (at + count) * SUB])
        at += count
    return (*parts, plan_ref.at[at * SUB :])


def tile_at(ref, row):
    return ref[pl.ds(pl.multiple_of(row * SUB, SUB), SUB), :]


def index_at(ref, row):
    return tile_at(ref, row).astype(jnp.int32)


def index_of(ref, row):
    return tile(ref, row).astype(jnp.int32)


def put_index(ref, row, value):
    put(ref, row, value.astype(jnp.float32))


def load_matrices(plan_ref, matrix_ref, sem):
    copy = pltpu.make_async_copy(plan_parts(plan_ref)[2], matrix_ref, sem.at[0])
    copy.start()
    return copy


def put_at(ref, row, value):
    ref[pl.ds(pl.multiple_of(row * SUB, SUB), SUB), :] = value


class Sender:
    def __init__(self, index_ref, sent_ref, packed_ref):
        self.straight = [index_of(index_ref, 12 + 2 * n) for n in range(3)]
        self.lane, sublane, self.face = [index_of(index_ref, 13 + 2 * n) for n in range(3)]
        sub = lax.broadcasted_iota(jnp.int32, (SUB, LANES), 0)
        slot = lax.broadcasted_iota(jnp.int32, (SUB, LANES), 1)
        self.own = (sub == sublane) & (slot < CORNER_LANES)
        self.sent_ref, self.packed_ref = sent_ref, packed_ref
        self.group = None

    def corner(self, src, row):
        return jnp.where(self.own, take(tile(src, row), self.lane), 0.0)

    def put(self, channel, value, corner):
        put(self.sent_ref, channel, value)
        place = channel % SUB
        moved = corner if place == 0 else pltpu.roll(corner, CORNER_LANES * place, 1)
        self.group = moved if place == 0 else self.group + moved
        if place == SUB - 1:
            self.flush(channel)

    def flush(self, channel):
        at = channel // SUB
        self.packed_ref[at : at + 1, :] = jnp.sum(self.group, axis=0, keepdims=True)

    def states(self, src, first_comp, comps):
        for comp in range(comps):
            row = (first_comp + comp) * 3
            ends = gather_ends(src, row, *self.straight)
            n0, n1, n2 = [self.corner(src, row + i) for i in range(3)]
            corners = pick(self.face, n1, n2, n0), pick(self.face, n2, n0, n1)
            for j in range(2):
                self.put(comp * 2 + j, ends[j], corners[j])

    def by_face(self, src, row, channel):
        corner = pick(self.face, *[self.corner(src, row + i) for i in range(3)])
        self.put(channel, gather_by_face(src, row, *self.straight), corner)

    def by_element(self, src, row, channel):
        self.put(channel, gather_tile(src, row, *self.straight[:2]), self.corner(src, row))


def write_messages(sent_ref, packed_ref, first, channels, outs, total):
    for role, out in enumerate(outs):
        for half in range(2):
            out[half, first : first + channels, :] = sent_ref[
                pl.ds(role * 2 + half, channels, stride=SUB), :
            ]
    count, at = corner_rows(channels), total + first // SUB
    for out in outs[:2]:
        out[0, at : at + count, :] = packed_ref[0:count, :]


def prepare_kernel(
    cot_ref,
    x_ref,
    area_ref,
    edge_ref,
    rough_ref,
    soil_ref,
    friction_ref,
    conduct_ref,
    wet_ref,
    zone_ref,
    send_ref,
    partner_ref,
    in_ref,
    out_ref,
    volume_ref,
    plan_ref,
    to_x1,
    to_x2,
    to_y1,
    to_y2,
    x_tiles,
    sent_ref,
    packed_ref,
    *fetched,
):
    *fetched, sems = fetched
    stat_ref, index_ref, matrix_ref, table_ref = plan_parts(plan_ref)
    sources = [
        partner_ref,
        send_ref,
        cot_ref,
        x_ref.at[:, 0, 0, 0:16],
        area_ref,
        edge_ref,
        rough_ref,
        soil_ref,
        friction_ref,
        conduct_ref,
        wet_ref,
        zone_ref,
        in_ref,
        out_ref,
        volume_ref,
    ]
    copies = [
        pltpu.make_async_copy(source, target, sems.at[n])
        for n, (source, target) in enumerate(zip(sources, fetched))
    ]
    for copy in copies:
        copy.start()
    for copy in copies[:2]:
        copy.wait()
    (
        partner_ref,
        send_ref,
        cot_ref,
        x_ref,
        area_ref,
        edge_ref,
        rough_ref,
        soil_ref,
        friction_ref,
        conduct_ref,
        wet_ref,
        zone_ref,
        in_ref,
        out_ref,
        volume_ref,
    ) = fetched
    rows = cot_ref.shape[0] // SUB
    sections = x_ref.shape[0]
    odd_a, odd_b = 1 - lax.axis_index("gx") % 2, 1 - lax.axis_index("gy") % 2
    straight = (6 - 5 * odd_a, 1 + 5 * odd_a, 4 - odd_b, 3 + odd_b)
    right, up = 1 - odd_a, 1 - odd_b
    corners = (
        5 * right + 2 * up,
        5 * right + 2 - 2 * up,
        5 - 5 * right + 2 * up,
        7 - 5 * right - 2 * up,
    )
    face_total = 3 * SUB * LANES
    for f in range(3):
        partner = tile(partner_ref, f)
        beyond = partner - face_total
        direction = jnp.right_shift(beyond, 8)
        half = jnp.bitwise_and(jnp.right_shift(beyond, 7), 1)
        lane = jnp.bitwise_and(partner, LANES - 1)
        remote = jnp.where(beyond >= 0, CORNER_BLOCK, -1)
        for number, toward in enumerate(straight):
            remote = jnp.where(direction == toward, 2 * number + half, remote)
        for number, toward in enumerate(corners):
            lane = jnp.where(direction == toward, lane % 4 + 4 * number, lane)
        put_index(index_ref, f, lane)
        put_index(index_ref, 3 + f, jnp.bitwise_and(jnp.right_shift(partner, 7), SUB - 1))
        put_index(index_ref, 6 + f, jnp.right_shift(partner, 10))
        put_index(index_ref, 9 + f, remote)
    sub_iota = lax.broadcasted_iota(jnp.int32, (SUB, LANES), 0)
    lane_iota = lax.broadcasted_iota(jnp.int32, (SUB, LANES), 1)

    def slots_to(choices, choice, half):
        rows_of = [
            jnp.broadcast_to(send_ref[0, 0, n : n + 1, lanes_of(half)], (SUB, LANES))
            for n in choices
        ]
        found = rows_of[0]
        for n, row in zip(choices[1:], rows_of[1:]):
            found = jnp.where(choice == n, row, found)
        return found

    straight_slots = None
    for number, toward in enumerate(straight):
        for half in range(2):
            row = slots_to((1, 6) if number < 2 else (3, 4), toward, half)
            straight_slots = (
                row
                if straight_slots is None
                else jnp.where(sub_iota == 2 * number + half, row, straight_slots)
            )
    corner_slots = None
    for number, toward in enumerate(corners):
        row = slots_to((0, 2, 5, 7), toward, 0)
        if number == 0:
            corner_slots = row
        else:
            moved = pltpu.roll(row, 4 * number, 1)
            corner_slots = jnp.where(lane_iota // 4 == number, moved, corner_slots)
    for d, slots in enumerate((straight_slots, corner_slots)):
        put_index(index_ref, 12 + d, jnp.bitwise_and(slots, LANES - 1))
        put_index(index_ref, 14 + d, jnp.bitwise_and(jnp.right_shift(slots, 7), SUB - 1))
        put_index(index_ref, 16 + d, jnp.right_shift(slots, 10))
    for copy in copies[2:]:
        copy.wait()
    matrix_ref[0:8, 0:8] = in_ref[...]
    matrix_ref[8:16, 0:8] = out_ref[...]
    matrix_ref[16:28, 0:12] = volume_ref[...]
    zone = zone_ref[...]
    zone_lane = jnp.bitwise_and(zone, LANES - 1)
    zone_block = jnp.right_shift(zone, 7)
    factors = []
    for ref in (friction_ref, conduct_ref):
        found = None
        for block in range(ref.shape[0]):
            got = take(spread(ref, block), zone_lane)
            found = got if block == 0 else jnp.where(zone_block == block, got, found)
        factors.append(found)
    area = area_ref[...]
    wet = wet_ref[...].astype(jnp.float32)
    kappa = factors[1] * soil_ref[...]
    wet_area = wet * area
    half_kappa_area = LATERAL * kappa * area
    put(stat_ref, WET_AREA, wet_area)
    put(stat_ref, KAPPA, kappa)
    put(stat_ref, HALF_KAPPA_AREA, half_kappa_area)
    put(stat_ref, WET, wet)
    put(stat_ref, ZONE_FRICTION, factors[0])
    put(stat_ref, ZONE_ID, zone.astype(jnp.float32))
    stat_ref[CONDUCTIVITY * SUB : CONDUCTIVITY * SUB + conduct_ref.shape[0], :] = conduct_ref[...]
    stat_ref[EDGE * SUB : (EDGE + 3) * SUB, :] = edge_ref[...]
    for k in range(sections):
        rows_to_tiles(
            lambda b: x_ref[k, :, lanes_of(b)].astype(jnp.float32), x_tiles, 16
        )
        squares = [tile(x_tiles, r) * tile(x_tiles, r) for r in range(12)]
        node_sum = [squares[i] + squares[3 + i] + squares[6 + i] + squares[9 + i] for i in range(3)]
        for f in range(3):
            first, second = FACE_NODES[f]
            put(table_ref, rows + 3 + 3 * k + f, node_sum[first] + node_sum[second])
        momentum = squares[3]
        for r in range(4, 9):
            momentum = momentum + squares[r]
        put(
            stat_ref,
            FRICTION_BASE + k,
            rough_ref[...] * jnp.sqrt(1.0 + momentum * (1.0 / 6.0)),
        )
    for f in range(3):
        put(table_ref, rows + f, tile(stat_ref, EDGE + f))
    put(table_ref, rows + 12, zone.astype(jnp.float32))
    for r in range(rows):
        put(table_ref, r, tile(cot_ref, r) * (wet_area if r < 12 else half_kappa_area))
    comps = rows // 3
    channels = comps * 2 + 5
    sender = Sender(index_ref, sent_ref, packed_ref)
    sender.states(table_ref, 0, comps)
    for group in range(4):
        sender.by_face(table_ref, rows + 3 * group, comps * 2 + group)
    sender.by_element(table_ref, rows + 12, channels - 1)
    sender.flush(channels - 1)
    write_messages(sent_ref, packed_ref, 0, channels, (to_x1, to_x2, to_y1, to_y2), channels)


def corner_kernel(channels, x1, x2, old_y1, old_y2, *rest):
    y1, y2 = rest[1:3]
    rows = slice(channels, message_rows(channels))
    lane = corner_lane((corner_rows(channels), LANES))
    merged = jnp.where(lane < 8, x1[0, rows, :], x2[0, rows, :])
    y1[0, rows, :] = merged
    y2[0, rows, :] = merged


def local_states(src, first_comp, comps, index_ref, out_ref):
    def body(f, carry):
        lane, sublane, face = [index_at(index_ref, n * 3 + f) for n in range(3)]
        for comp in range(comps):
            ends = gather_ends(src, (first_comp + comp) * 3, lane, sublane, face)
            for j in range(2):
                put_at(out_ref, f * comps * 2 + comp * 2 + j, ends[j])
        return carry

    lax.fori_loop(0, 3, body, 0)


def remote_states(received, first_row, channels, index_ref, local_ref, out_ref):
    def body(f, carry):
        lane, remote = index_at(index_ref, f), index_at(index_ref, 9 + f)
        for ch in range(channels):
            value = tile_at(local_ref, f * channels + ch)
            put_at(
                out_ref, f * channels + ch, received.fill(first_row + ch, lane, remote, value)
            )
        return carry

    lax.fori_loop(0, 3, body, 0)


def transposed_own(section, lam_ref, y_ref, stat_ref, matrix_ref, own_ref):
    rows = lam_ref.shape[0] // SUB
    layers = (rows - 12) // 3
    edge = [tile(stat_ref, EDGE + f) for f in range(3)]
    kappa = tile(stat_ref, KAPPA)
    wet = tile(stat_ref, WET)
    own = [tile(y_ref, r) for r in range(12)]
    result = []
    for r in range(12):
        total = matrix_ref[16, r] * own[0]
        for q in range(1, 12):
            total = total + matrix_ref[16 + q, r] * own[q]
        result.append(total)
    for f in range(3):
        ends = FACE_NODES[f]
        inner = [edge[f] * own[(ch // 2) * 3 + ends[ch % 2]] for ch in range(8)]
        for b in range(8):
            total = matrix_ref[0, b] * inner[0]
            for a in range(1, 8):
                total = total + matrix_ref[a, b] * inner[a]
            at = (b // 2) * 3 + ends[b % 2]
            result[at] = result[at] + total
    friction = tile(stat_ref, ZONE_FRICTION) * tile(stat_ref, FRICTION_BASE + section) * wet
    for r in range(3, 9):
        result[r] = result[r] - friction * tile(lam_ref, r)
    exchange = []
    for i in range(3):
        top = tile(lam_ref, 12 + i) - SALT_RETURN * wet * tile(lam_ref, 9 + i)
        exchange.append(kappa * top)
        result[9 + i] = result[9 + i] + exchange[i]
    for r in range(12):
        put(own_ref, r, result[r])
    for i in range(3):
        (f0, _), (f1, _) = NODE_FACES[i]
        both = edge[f0] + edge[f1]
        from_above = exchange[i]
        for layer in range(layers):
            r = 12 + layer * 3 + i
            value = -(both * tile(y_ref, r)) - from_above
            if layer + 1 < layers:
                from_above = kappa * (tile(lam_ref, r + 3) - tile(lam_ref, r))
                value = value + from_above
            put(own_ref, r, value)


def transposed_section(
    section, own_ref, y_ref, outer_ref, stat_ref, fact_ref, matrix_ref, emit
):
    rows = own_ref.shape[0] // SUB
    channels = rows // 3 * 2
    layers = (rows - 12) // 3
    outer_edge = [tile(fact_ref, OUTER_EDGE + f) for f in range(3)]
    result = [tile(own_ref, r) for r in range(12)]
    for f in range(3):
        edge = tile(stat_ref, EDGE + f)
        half_speed = tile(fact_ref, HALF_SPEED + 3 * section + f)
        ends = FACE_NODES[f]
        outer = [outer_edge[f] * tile(outer_ref, f * channels + ch) for ch in range(8)]
        for b in range(8):
            at = (b // 2) * 3 + ends[b % 2]
            total = half_speed * (edge * tile(y_ref, at) - outer[b])
            for a in range(8):
                total = total - matrix_ref[8 + a, b] * outer[a]
            result[at] = result[at] + total
    for r in range(12):
        emit(r, result[r])
    for i in range(3):
        (f0, j0), (f1, j1) = NODE_FACES[i]
        for layer in range(layers):
            r = 12 + layer * 3 + i
            emit(
                r,
                tile(own_ref, r)
                + outer_edge[f0] * tile(outer_ref, f0 * channels + 8 + layer * 2 + j0)
                + outer_edge[f1] * tile(outer_ref, f1 * channels + 8 + layer * 2 + j1),
            )


def own_gradients(section, weight, lam_ref, y_ref, x_tiles, stat_ref):
    rows = lam_ref.shape[0] // SUB
    layers = (rows - 12) // 3
    wet = tile(stat_ref, WET)
    kappa = tile(stat_ref, KAPPA)
    momentum = tile(lam_ref, 3) * tile(x_tiles, 3)
    for r in range(4, 9):
        momentum = momentum + tile(lam_ref, r) * tile(x_tiles, r)
    friction = -(weight * wet * tile(stat_ref, FRICTION_BASE + section)) * momentum
    vertical = None
    lateral = None
    for i in range(3):
        (f0, _), (f1, _) = NODE_FACES[i]
        top = tile(lam_ref, 12 + i) - SALT_RETURN * wet * tile(lam_ref, 9 + i)
        total = top * (tile(x_tiles, 9 + i) - tile(x_tiles, 12 + i))
        dots = None
        for layer in range(layers):
            r = 12 + layer * 3 + i
            term = tile(y_ref, r) * tile(x_tiles, r)
            dots = term if dots is None else dots + term
            if layer + 1 < layers:
                total = total + (tile(lam_ref, r + 3) - tile(lam_ref, r)) * (
                    tile(x_tiles, r) - tile(x_tiles, r + 3)
                )
        side = (tile(stat_ref, EDGE + f0) + tile(stat_ref, EDGE + f1)) * dots
        vertical = total if vertical is None else vertical + total
        lateral = side if lateral is None else lateral + side
    return friction, weight * (kappa * vertical - lateral)


def outer_gradients(weight, outer_ref, x_tiles, fact_ref):
    channels = outer_ref.shape[0] // SUB // 3
    values = []
    for f in range(3):
        total = None
        for ch in range(8, channels):
            row = 12 + (ch - 8) // 2 * 3 + FACE_NODES[f][ch % 2]
            term = tile(outer_ref, f * channels + ch) * tile(x_tiles, row)
            total = term if total is None else total + term
        values.append(weight * tile(fact_ref, OUTER_EDGE + f) * total)
    return values


def x_to_tiles(x_ref, section, x_tiles):
    rows = x_ref.shape[3]
    rows_to_tiles(
        lambda b: x_ref[section, 0, 0, :, lanes_of(b)].astype(jnp.float32), x_tiles, rows
    )


def local_two_kernel(
    cot_ref,
    plan_ref,
    x_ref,
    outer_ref,
    near_ref,
    term_ref,
    own_ref,
    x_tiles,
    matrix_ref,
    sem,
):
    matrices = load_matrices(plan_ref, matrix_ref, sem)
    stat_ref, index_ref, _, table_ref = plan_parts(plan_ref)
    rows = cot_ref.shape[0] // SUB
    local_states(table_ref, 0, rows // 3, index_ref, outer_ref)
    for f in range(3):
        lane, sublane, face = [index_of(index_ref, n * 3 + f) for n in range(3)]
        for group in range(4):
            value = gather_by_face(table_ref, rows + 3 * group, lane, sublane, face)
            put(near_ref, f * 5 + group, value)
        put(near_ref, f * 5 + 4, gather_tile(table_ref, rows + 12, lane, sublane))
    x_to_tiles(x_ref, 2, x_tiles)
    friction, conduct = own_gradients(
        2, TIME_STEP * 2.0 / 3.0, cot_ref, table_ref, x_tiles, stat_ref
    )
    put(term_ref, 0, friction)
    put(term_ref, 1, conduct)
    matrices.wait()
    transposed_own(2, cot_ref, table_ref, stat_ref, matrix_ref, own_ref)


def local_x_kernel(plan_ref, x_ref, x_outer_ref, sent_ref, packed_ref, x_tiles):
    index_ref = plan_parts(plan_ref)[1]
    comps = x_ref.shape[3] // 3
    x_to_tiles(x_ref, 0, x_tiles)
    local_states(x_tiles, 4, comps - 4, index_ref, x_outer_ref)
    sender = Sender(index_ref, sent_ref, packed_ref)
    sender.states(x_tiles, 4, comps - 4)
    sender.flush(comps * 2 - 9)


def second_kernel(
    cot_ref,
    plan_ref,
    own_ref,
    near_outer_ref,
    near_ref,
    x_sent_ref,
    x_packed_ref,
    from_x1,
    from_x2,
    from_y1,
    from_y2,
    lam_ref,
    y_ref,
    fact_ref,
    outer_ref,
    to_x1,
    to_x2,
    to_y1,
    to_y2,
    sent_ref,
    packed_ref,
    corner_ref,
    matrix_ref,
    sem,
):
    matrices = load_matrices(plan_ref, matrix_ref, sem)
    stat_ref, index_ref, _, table_ref = plan_parts(plan_ref)
    rows = cot_ref.shape[0] // SUB
    comps = rows // 3
    channels = comps * 2
    received = Received((from_x1, from_x2, from_y1, from_y2), channels + 5, corner_ref)
    remote_states(received, 0, channels, index_ref, near_outer_ref, outer_ref)
    for f in range(3):
        lane, remote = index_of(index_ref, f), index_of(index_ref, 9 + f)
        for group in range(5):
            value = received.fill(channels + group, lane, remote, tile(near_ref, f * 5 + group))
            if group == 0:
                put(fact_ref, OUTER_EDGE + f, value)
            elif group == 4:
                put(fact_ref, OUTER_ZONE + f, value)
            else:
                both = tile(table_ref, rows + 3 * group + f) + value
                put(
                    fact_ref,
                    HALF_SPEED + 3 * (group - 1) + f,
                    0.5 * jnp.sqrt(1.0 + (0.25 / 8.0) * both),
                )
    wet_area = tile(stat_ref, WET_AREA)
    half_kappa_area = tile(stat_ref, HALF_KAPPA_AREA)

    def emit(r, value):
        lam = (2.0 / 3.0) * (tile(cot_ref, r) + TIME_STEP * value)
        put(lam_ref, r, lam)
        put(y_ref, r, lam * (wet_area if r < 12 else half_kappa_area))

    matrices.wait()
    transposed_section(
        2, own_ref, table_ref, outer_ref, stat_ref, fact_ref, matrix_ref, emit
    )
    sender = Sender(index_ref, sent_ref, packed_ref)
    sender.states(y_ref, 0, comps)
    sender.flush(channels - 1)
    outs = (to_x1, to_x2, to_y1, to_y2)
    write_messages(x_sent_ref, x_packed_ref, 0, channels - 8, outs, X_ROWS + channels)
    write_messages(sent_ref, packed_ref, X_ROWS, channels, outs, X_ROWS + channels)


def local_one_kernel(
    lam_ref,
    y_ref,
    plan_ref,
    fact_ref,
    old_outer_ref,
    old_term_ref,
    x_ref,
    outer_ref,
    term_ref,
    own_ref,
    x_tiles,
    matrix_ref,
    sem,
):
    matrices = load_matrices(plan_ref, matrix_ref, sem)
    stat_ref, index_ref, _, _ = plan_parts(plan_ref)
    local_states(y_ref, 0, lam_ref.shape[0] // SUB // 3, index_ref, outer_ref)
    x_to_tiles(x_ref, 2, x_tiles)
    weight = TIME_STEP * 2.0 / 3.0
    for f, value in enumerate(outer_gradients(weight, old_outer_ref, x_tiles, fact_ref)):
        put(term_ref, 2 + f, value)
    x_to_tiles(x_ref, 1, x_tiles)
    terms = own_gradients(1, TIME_STEP * 0.25, lam_ref, y_ref, x_tiles, stat_ref)
    for n in range(2):
        put(term_ref, n, tile(old_term_ref, n) + terms[n])
    matrices.wait()
    transposed_own(1, lam_ref, y_ref, stat_ref, matrix_ref, own_ref)


def first_kernel(
    cot_ref,
    lam_ref,
    y_ref,
    plan_ref,
    fact_ref,
    own_ref,
    near_outer_ref,
    from_x1,
    from_x2,
    from_y1,
    from_y2,
    base_ref,
    next_ref,
    next_y_ref,
    outer_ref,
    to_x1,
    to_x2,
    to_y1,
    to_y2,
    sent_ref,
    packed_ref,
    corner_ref,
    matrix_ref,
    sem,
):
    matrices = load_matrices(plan_ref, matrix_ref, sem)
    stat_ref, index_ref, _, _ = plan_parts(plan_ref)
    comps = lam_ref.shape[0] // SUB // 3
    channels = comps * 2
    received = Received((from_x1, from_x2, from_y1, from_y2), X_ROWS + channels, corner_ref)
    remote_states(received, X_ROWS, channels, index_ref, near_outer_ref, outer_ref)
    wet_area = tile(stat_ref, WET_AREA)
    half_kappa_area = tile(stat_ref, HALF_KAPPA_AREA)

    def emit(r, value):
        old = tile(lam_ref, r)
        lam = 0.25 * (old + TIME_STEP * value)
        put(next_ref, r, lam)
        put(next_y_ref, r, lam * (wet_area if r < 12 else half_kappa_area))
        put(base_ref, r, (1.0 / 3.0) * tile(cot_ref, r) + 0.75 * old + lam)

    matrices.wait()
    transposed_section(
        1, own_ref, y_ref, outer_ref, stat_ref, fact_ref, matrix_ref, emit
    )
    sender = Sender(index_ref, sent_ref, packed_ref)
    sender.states(next_y_ref, 0, comps)
    sender.flush(channels - 1)
    write_messages(sent_ref, packed_ref, 0, channels, (to_x1, to_x2, to_y1, to_y2), channels)


def zone_kernel(
    lam_ref,
    y_ref,
    plan_ref,
    fact_ref,
    old_outer_ref,
    term_ref,
    x_ref,
    x_near_ref,
    from_x1,
    from_x2,
    from_y1,
    from_y2,
    out_ref,
    x_outer_ref,
    x_tiles,
    corner_ref,
):
    stat_ref, index_ref, _, _ = plan_parts(plan_ref)
    rows = lam_ref.shape[0] // SUB
    channels = rows // 3 * 2
    x_channels = channels - 8
    received = Received((from_x1, from_x2, from_y1, from_y2), X_ROWS + channels, corner_ref)
    remote_states(received, 0, x_channels, index_ref, x_near_ref, x_outer_ref)
    x_to_tiles(x_ref, 1, x_tiles)
    outer_terms = outer_gradients(TIME_STEP * 0.25, old_outer_ref, x_tiles, fact_ref)
    outer_terms = [tile(term_ref, 2 + f) + outer_terms[f] for f in range(3)]
    x_to_tiles(x_ref, 0, x_tiles)
    friction_term, conduct_term = own_gradients(
        0, TIME_STEP, lam_ref, y_ref, x_tiles, stat_ref
    )
    friction_term = friction_term + tile(term_ref, 0)
    conduct_term = conduct_term + tile(term_ref, 1)
    for f in range(3):
        total = None
        for ch in range(x_channels):
            row = 12 + ch // 2 * 3 + FACE_NODES[f][ch % 2]
            term = tile(x_outer_ref, f * x_channels + ch) * tile(y_ref, row)
            total = term if total is None else total + term
        conduct_term = conduct_term + TIME_STEP * tile(stat_ref, EDGE + f) * total

    zones = out_ref.shape[2]
    zone_iota = lax.broadcasted_iota(jnp.int32, (zones, LANES), 0).astype(jnp.float32)
    sub_iota = lax.broadcasted_iota(jnp.int32, (SUB, zones), 0)

    def thirds(value):
        high = value.astype(jnp.bfloat16).astype(jnp.float32)
        rest = value - high
        middle = rest.astype(jnp.bfloat16).astype(jnp.float32)
        return [high, middle, rest - middle]

    def by_zone(values, zone_of, zone_row):
        pieces = sum([thirds(value) for value in values], [])
        left = jnp.concatenate(pieces, axis=0).astype(jnp.bfloat16)
        totals = [jnp.zeros((SUB, zones), jnp.float32) for _ in values]
        for sub in range(SUB):
            line = zone_of[pl.ds(zone_row * SUB + sub, 1), :]
            hot = (jnp.broadcast_to(line, (zones, LANES)) == zone_iota).astype(jnp.float32)
            dots = lax.dot_general(
                left,
                hot.astype(jnp.bfloat16),
                (((1,), (1,)), ((), ())),
                preferred_element_type=jnp.float32,
            )
            for n in range(len(values)):
                at = n * 3 * SUB
                three = dots[at : at + SUB] + dots[at + SUB : at + 2 * SUB]
                three = three + dots[at + 2 * SUB : at + 3 * SUB]
                totals[n] = totals[n] + jnp.where(sub_iota == sub, three, 0.0)
        return totals

    friction, conduct = by_zone([friction_term, conduct_term], stat_ref, ZONE_ID)
    for f in range(3):
        conduct = conduct + by_zone([outer_terms[f]], fact_ref, OUTER_ZONE + f)[0]
    friction = GRAD_WEIGHT * jnp.sum(friction, axis=0, keepdims=True)
    conduct = GRAD_WEIGHT * jnp.sum(conduct, axis=0, keepdims=True)
    factors = [
        stat_ref[CONDUCTIVITY * SUB + n : CONDUCTIVITY * SUB + n + 1, :]
        for n in range(zones // LANES)
    ]
    conduct = conduct / jnp.concatenate(factors, axis=1)
    for device in range(out_ref.shape[0]):
        out_ref[device, 0:1, :] = friction
        out_ref[device, 1:2, :] = conduct


def after_kernel(zone_in, message_ref, zone_ref):
    pass


def local_zero_kernel(lam_ref, y_ref, plan_ref, outer_ref, own_ref, matrix_ref, sem):
    matrices = load_matrices(plan_ref, matrix_ref, sem)
    stat_ref, index_ref, _, _ = plan_parts(plan_ref)
    local_states(y_ref, 0, y_ref.shape[0] // SUB // 3, index_ref, outer_ref)
    matrices.wait()
    transposed_own(0, lam_ref, y_ref, stat_ref, matrix_ref, own_ref)


def last_kernel(
    base_ref,
    y_ref,
    plan_ref,
    fact_ref,
    own_ref,
    near_outer_ref,
    from_x1,
    from_x2,
    from_y1,
    from_y2,
    adjoint_ref,
    last_ref,
    outer_ref,
    corner_ref,
    matrix_ref,
    sem,
):
    matrices = load_matrices(plan_ref, matrix_ref, sem)
    stat_ref, index_ref, _, _ = plan_parts(plan_ref)
    rows = y_ref.shape[0] // SUB
    channels = rows // 3 * 2
    received = Received((from_x1, from_x2, from_y1, from_y2), channels, corner_ref)
    remote_states(received, 0, channels, index_ref, near_outer_ref, outer_ref)

    def emit(r, value):
        put(adjoint_ref, r, tile(base_ref, r) + TIME_STEP * value)

    matrices.wait()
    transposed_section(
        0, own_ref, y_ref, outer_ref, stat_ref, fact_ref, matrix_ref, emit
    )
    last_ref[...] = tile(adjoint_ref, rows - 1)


def total_kernel(zone_ref, adjoint_ref, grads_ref):
    grads_ref[...] = jnp.sum(zone_ref[...], axis=0)


def exchange(channels, messages, ahead):
    x1, x2, y1, y2 = messages
    x1, x2 = swapped(x1, "gx", 1), swapped(x2, "gx", 0)
    y1, y2, ahead = call(
        functools.partial(corner_kernel, channels),
        "corners",
        [jax.ShapeDtypeStruct(one.shape, one.dtype) for one in (y1, y2, ahead)],
        [],
        [x1, x2, y1, y2, ahead],
        apart=(4,),
        aliases={2: 0, 3: 1, 4: 2},
    )
    return (x1, x2, swapped(y1, "gy", 1), swapped(y2, "gy", 0)), ahead


def call(kernel, name, outs, scratch, operands, far=False, apart=(), aliases={}):
    near = pl.BlockSpec(memory_space=pltpu.VMEM)
    in_place = pl.BlockSpec(memory_space=pl.ANY)
    specs = [in_place if far or n in apart else near for n in range(len(operands))]
    handed_on = [aliases[n] for n in apart if n in aliases]
    return pl.pallas_call(
        kernel,
        in_specs=specs,
        out_specs=[in_place if n in handed_on else near for n in range(len(outs))],
        out_shape=outs,
        scratch_shapes=scratch,
        input_output_aliases=aliases,
        compiler_params=pltpu.CompilerParams(
            vmem_limit_bytes=(FAR_VMEM if far else NEAR_VMEM) * 1024 * 1024
        ),
        name=name,
    )(*operands)


def local(
    cotangent,
    section_states,
    inverse_area,
    edge_length,
    roughness,
    soil_conductance,
    zone_friction,
    zone_conductivity,
    wet_mask,
    element_zone,
    send_face,
    send_count,
    face_partner,
    volume_matrix,
    flux_in,
    flux_out,
):
    rows = cotangent.shape[2]
    channels = rows // 3 * 2
    zones = zone_friction.shape[0]
    slots = send_face.shape[3]
    devices = lax.axis_size("gx") * lax.axis_size("gy")
    f32 = jnp.float32

    def tiles(count, dtype=f32):
        return jax.ShapeDtypeStruct((count * SUB, LANES), dtype)

    def tile_scratch(count, dtype=f32):
        return pltpu.VMEM((count * SUB, LANES), dtype)

    def messages(count):
        return [jax.ShapeDtypeStruct((slots // LANES, message_rows(count), LANES), f32)] * 4

    def sent_tiles(count):
        return corner_rows(count) * SUB

    matrix_scratch = [
        pltpu.SMEM((MATRIX_ROWS * SUB, LANES), f32),
        pltpu.SemaphoreType.DMA((1,)),
    ]
    section_scratch = [pltpu.VMEM((SUB, LANES), f32)] + matrix_scratch

    square = lambda one: one.reshape(SUB, LANES)
    cot = cotangent.reshape(rows * SUB, LANES)
    plan, *to_send = call(
        prepare_kernel,
        "prepare",
        [tiles(plan_rows(rows))] + messages(channels + 5),
        [
            tile_scratch(16),
            tile_scratch(sent_tiles(channels + 5)),
            tile_scratch(1),
            tile_scratch(3, jnp.int32),
            pltpu.VMEM(send_face.shape, jnp.int32),
            tile_scratch(rows),
            pltpu.VMEM((section_states.shape[0], 16, SUB * LANES), section_states.dtype),
            tile_scratch(1),
            tile_scratch(3),
            tile_scratch(1),
            tile_scratch(1),
            pltpu.VMEM((zones // LANES, LANES), f32),
            pltpu.VMEM((zones // LANES, LANES), f32),
            tile_scratch(1, jnp.int32),
            tile_scratch(1, jnp.int32),
            pltpu.VMEM(flux_in.shape, f32),
            pltpu.VMEM(flux_out.shape, f32),
            pltpu.VMEM(volume_matrix.shape, f32),
            pltpu.SemaphoreType.DMA((15,)),
        ],
        [
            cot,
            section_states,
            square(inverse_area),
            edge_length.reshape(3 * SUB, LANES),
            square(roughness),
            square(soil_conductance),
            zone_friction.reshape(-1, LANES),
            zone_conductivity.reshape(-1, LANES),
            square(wet_mask),
            square(element_zone),
            send_face,
            face_partner.reshape(3 * SUB, LANES),
            flux_in,
            flux_out,
            volume_matrix,
        ],
        far=True,
    )
    near_outer, near, term, own = call(
        local_two_kernel,
        "local_two",
        [tiles(3 * channels), tiles(15), tiles(2), tiles(rows)],
        [tile_scratch(rows)] + matrix_scratch,
        [cot, plan, section_states],
    )
    x_near, x_sent, x_packed = call(
        local_x_kernel,
        "local_x",
        [tiles(3 * (channels - 8)), tiles(sent_tiles(channels - 8)), tiles(1)],
        [tile_scratch(rows)],
        [plan, section_states],
    )
    received, term = exchange(channels + 5, to_send, term)
    lam, y, fact, outer, *to_send = call(
        second_kernel,
        "section_two",
        [tiles(rows), tiles(rows), tiles(FACT_ROWS), tiles(3 * channels)]
        + messages(X_ROWS + channels),
        [tile_scratch(sent_tiles(channels)), tile_scratch(1)] + section_scratch,
        [cot, plan, own, near_outer, near, x_sent, x_packed, *received],
    )
    near_outer, term, own = call(
        local_one_kernel,
        "local_one",
        [tiles(3 * channels), tiles(5), tiles(rows)],
        [tile_scratch(rows)] + matrix_scratch,
        [lam, y, plan, fact, outer, term, section_states],
    )
    received, term = exchange(X_ROWS + channels, to_send, term)
    base, lam, y, outer, *to_send = call(
        first_kernel,
        "section_one",
        [tiles(rows), tiles(rows), tiles(rows), tiles(3 * channels)] + messages(channels),
        [tile_scratch(sent_tiles(channels)), tile_scratch(1)] + section_scratch,
        [cot, lam, y, plan, fact, own, near_outer, *received],
    )
    (zone_terms,) = call(
        zone_kernel,
        "zone_sums",
        [jax.ShapeDtypeStruct((devices, 2, zones), f32)],
        [tile_scratch(3 * (channels - 8)), tile_scratch(rows), tile_scratch(1)],
        [lam, y, plan, fact, outer, term, section_states, x_near, *received],
    )
    received, zone_terms = exchange(channels, to_send, zone_terms)
    (zone_terms,) = call(
        after_kernel,
        "after",
        [jax.ShapeDtypeStruct(zone_terms.shape, f32)],
        [],
        [zone_terms, received[2]],
        apart=(0, 1),
        aliases={0: 0},
    )
    all_terms = lax.all_to_all(zone_terms, ("gx", "gy"), 0, 0)
    near_outer, own = call(
        local_zero_kernel,
        "local_zero",
        [tiles(3 * channels), tiles(rows)],
        matrix_scratch,
        [lam, y, plan],
    )
    adjoint, last = call(
        last_kernel,
        "section_zero",
        [tiles(rows), tiles(1)],
        [tile_scratch(3 * channels)] + section_scratch,
        [base, y, plan, fact, own, near_outer, *received],
    )
    (zone_grads,) = call(
        total_kernel,
        "zone_total",
        [jax.ShapeDtypeStruct((2, zones), f32)],
        [],
        [all_terms, last],
    )
    return adjoint.reshape(cotangent.shape), zone_grads


def solution(mesh):
    placed = (
        P("gx", "gy", None, None),
        P(None, "gx", "gy", None, None),
        P("gx", "gy", None),
        P("gx", "gy", None, None),
        P("gx", "gy", None),
        P("gx", "gy", None),
        P(),
        P(),
        P("gx", "gy", None),
        P("gx", "gy", None),
        P("gx", "gy", None, None),
        P("gx", "gy", None),
        P("gx", "gy", None, None),
        P(),
        P(),
        P(),
    )
    return jax.shard_map(
        local,
        mesh=mesh,
        in_specs=placed,
        out_specs=(P("gx", "gy", None, None), P()),
        check_vma=False,
    )
```

```python
import functools
import jax
import jax.numpy as jnp
from jax import lax
from jax.experimental import pallas as pl
from jax.experimental.pallas import tpu as pltpu
from jax.sharding import PartitionSpec as P

TIME_STEP = 0.2
SALT_RETURN = 0.5
LATERAL = 0.5
GRAD_WEIGHT = 1.0 / 64.0
FACE_NODES = ((1, 2), (2, 0), (0, 1))
NODE_FACES = (((1, 1), (2, 0)), ((0, 0), (2, 1)), ((0, 1), (1, 0)))
SUB = 8
LANES = 128


WET_AREA, KAPPA, HALF_KAPPA_AREA, WET, EDGE, FRICTION_BASE, ZONE_FRICTION, ZONE_ID = (
    0,
    1,
    2,
    3,
    4,
    7,
    10,
    11,
)
CONDUCTIVITY = 12
STAT_ROWS = 13
NEAR_VMEM, FAR_VMEM = 32, 60
OUTER_EDGE, OUTER_ZONE, HALF_SPEED = 0, 3, 6
FACT_ROWS = 15
X_ROWS = 24
CORNER_LANES = 16
CORNER_BLOCK = 8


def swapped(x, axis, first):
    peers = lax.axis_size(axis)
    lows = range(first, peers - 1, 2)
    return lax.ppermute(x, axis, [(i, i + 1) for i in lows] + [(i + 1, i) for i in lows])


def tile(ref, row):
    return ref[row * SUB : (row + 1) * SUB, :]


def put(ref, row, value):
    ref[row * SUB : (row + 1) * SUB, :] = value


def take(row, lane_index):
    return jnp.take_along_axis(row, lane_index, axis=1, mode="promise_in_bounds")


def spread(ref, row):
    return jnp.broadcast_to(ref[pl.ds(row, 1), :], (SUB, LANES))


def rows_to_tiles(read, tiles_ref, count):
    for block in range(SUB):
        tiles_ref[pl.ds(block, count, stride=SUB), :] = read(block)


def lanes_of(block):
    return slice(block * LANES, (block + 1) * LANES)


def gather_tile(src, row, lane_index, sublane_index):
    found = take(spread(src, row * SUB), lane_index)
    for sub in range(1, SUB):
        got = take(spread(src, row * SUB + sub), lane_index)
        found = jnp.where(sublane_index == sub, got, found)
    return found


def pick(face, for_zero, for_one, for_two):
    return jnp.where(face == 0, for_zero, jnp.where(face == 1, for_one, for_two))


def gather_ends(src, row, lane_index, sublane_index, face):
    n0, n1, n2 = [gather_tile(src, row + i, lane_index, sublane_index) for i in range(3)]
    return pick(face, n1, n2, n0), pick(face, n2, n0, n1)


def gather_by_face(src, row, lane_index, sublane_index, face):
    return pick(
        face, *[gather_tile(src, row + i, lane_index, sublane_index) for i in range(3)]
    )


def corner_rows(channels):
    return (channels * CORNER_LANES + LANES - 1) // LANES


def message_rows(channels):
    return channels + corner_rows(channels)


def corner_lane(shape):
    return lax.broadcasted_iota(jnp.int32, shape, 1) % CORNER_LANES


class Received:
    def __init__(self, messages, channels, corner_ref):
        _, _, y1, y2 = messages
        self.mains = messages
        self.corner_ref = corner_ref
        rows = slice(channels, message_rows(channels))
        count = corner_rows(channels)
        lane = corner_lane((count, LANES))
        corner_ref[0:count, :] = jnp.where(
            jnp.bitwise_and(lane, 4) == 0, y1[0, rows, :], y2[0, rows, :]
        )

    def fill(self, row, lane_index, remote_index, value):
        for number, ref in enumerate(self.mains):
            for half in range(2):
                got = take(spread(ref.at[half], row), lane_index)
                value = jnp.where(remote_index == 2 * number + half, got, value)
        channels_a_row = LANES // CORNER_LANES
        lane = lane_index + row % channels_a_row * CORNER_LANES
        line = spread(self.corner_ref, row // channels_a_row)
        got = take(line, jnp.bitwise_and(lane, LANES - 1))
        return jnp.where(remote_index == CORNER_BLOCK, got, value)


INDEX_ROWS = 18
MATRIX_ROWS = 4


def plan_rows(rows):
    return STAT_ROWS + INDEX_ROWS + MATRIX_ROWS + rows + 13


def plan_parts(plan_ref):
    parts, at = [], 0
    for count in (STAT_ROWS, INDEX_ROWS, MATRIX_ROWS):
        parts.append(plan_ref.at[at * SUB : (at + count) * SUB])
        at += count
    return (*parts, plan_ref.at[at * SUB :])


def tile_at(ref, row):
    return ref[pl.ds(pl.multiple_of(row * SUB, SUB), SUB), :]


def index_at(ref, row):
    return tile_at(ref, row).astype(jnp.int32)


def index_of(ref, row):
    return tile(ref, row).astype(jnp.int32)


def put_index(ref, row, value):
    put(ref, row, value.astype(jnp.float32))


def load_matrices(plan_ref, matrix_ref, sem):
    copy = pltpu.make_async_copy(plan_parts(plan_ref)[2], matrix_ref, sem.at[0])
    copy.start()
    return copy


def put_at(ref, row, value):
    ref[pl.ds(pl.multiple_of(row * SUB, SUB), SUB), :] = value


class Sender:
    def __init__(self, index_ref, sent_ref, packed_ref):
        self.straight = [index_of(index_ref, 12 + 2 * n) for n in range(3)]
        self.lane, sublane, self.face = [index_of(index_ref, 13 + 2 * n) for n in range(3)]
        sub = lax.broadcasted_iota(jnp.int32, (SUB, LANES), 0)
        slot = lax.broadcasted_iota(jnp.int32, (SUB, LANES), 1)
        self.own = (sub == sublane) & (slot < CORNER_LANES)
        self.sent_ref, self.packed_ref = sent_ref, packed_ref
        self.group = None

    def corner(self, src, row):
        return jnp.where(self.own, take(tile(src, row), self.lane), 0.0)

    def put(self, channel, value, corner):
        put(self.sent_ref, channel, value)
        place = channel % SUB
        moved = corner if place == 0 else pltpu.roll(corner, CORNER_LANES * place, 1)
        self.group = moved if place == 0 else self.group + moved
        if place == SUB - 1:
            self.flush(channel)

    def flush(self, channel):
        at = channel // SUB
        self.packed_ref[at : at + 1, :] = jnp.sum(self.group, axis=0, keepdims=True)

    def states(self, src, first_comp, comps):
        for comp in range(comps):
            row = (first_comp + comp) * 3
            ends = gather_ends(src, row, *self.straight)
            n0, n1, n2 = [self.corner(src, row + i) for i in range(3)]
            corners = pick(self.face, n1, n2, n0), pick(self.face, n2, n0, n1)
            for j in range(2):
                self.put(comp * 2 + j, ends[j], corners[j])

    def by_face(self, src, row, channel):
        corner = pick(self.face, *[self.corner(src, row + i) for i in range(3)])
        self.put(channel, gather_by_face(src, row, *self.straight), corner)

    def by_element(self, src, row, channel):
        self.put(channel, gather_tile(src, row, *self.straight[:2]), self.corner(src, row))


def write_messages(sent_ref, packed_ref, first, channels, outs, total):
    for role, out in enumerate(outs):
        for half in range(2):
            out[half, first : first + channels, :] = sent_ref[
                pl.ds(role * 2 + half, channels, stride=SUB), :
            ]
    count, at = corner_rows(channels), total + first // SUB
    for out in outs[:2]:
        out[0, at : at + count, :] = packed_ref[0:count, :]


def prepare_kernel(
    cot_ref,
    x_ref,
    area_ref,
    edge_ref,
    rough_ref,
    soil_ref,
    friction_ref,
    conduct_ref,
    wet_ref,
    zone_ref,
    send_ref,
    partner_ref,
    in_ref,
    out_ref,
    volume_ref,
    plan_ref,
    to_x1,
    to_x2,
    to_y1,
    to_y2,
    x_tiles,
    sent_ref,
    packed_ref,
    *fetched,
):
    *fetched, sems = fetched
    stat_ref, index_ref, matrix_ref, table_ref = plan_parts(plan_ref)
    sources = [
        partner_ref,
        send_ref,
        cot_ref,
        x_ref.at[:, 0, 0, 0:16],
        area_ref,
        edge_ref,
        rough_ref,
        soil_ref,
        friction_ref,
        conduct_ref,
        wet_ref,
        zone_ref,
        in_ref,
        out_ref,
        volume_ref,
    ]
    copies = [
        pltpu.make_async_copy(source, target, sems.at[n])
        for n, (source, target) in enumerate(zip(sources, fetched))
    ]
    for copy in copies:
        copy.start()
    for copy in copies[:2]:
        copy.wait()
    (
        partner_ref,
        send_ref,
        cot_ref,
        x_ref,
        area_ref,
        edge_ref,
        rough_ref,
        soil_ref,
        friction_ref,
        conduct_ref,
        wet_ref,
        zone_ref,
        in_ref,
        out_ref,
        volume_ref,
    ) = fetched
    rows = cot_ref.shape[0] // SUB
    sections = x_ref.shape[0]
    odd_a, odd_b = 1 - lax.axis_index("gx") % 2, 1 - lax.axis_index("gy") % 2
    straight = (6 - 5 * odd_a, 1 + 5 * odd_a, 4 - odd_b, 3 + odd_b)
    right, up = 1 - odd_a, 1 - odd_b
    corners = (
        5 * right + 2 * up,
        5 * right + 2 - 2 * up,
        5 - 5 * right + 2 * up,
        7 - 5 * right - 2 * up,
    )
    face_total = 3 * SUB * LANES
    for f in range(3):
        partner = tile(partner_ref, f)
        beyond = partner - face_total
        direction = jnp.right_shift(beyond, 8)
        half = jnp.bitwise_and(jnp.right_shift(beyond, 7), 1)
        lane = jnp.bitwise_and(partner, LANES - 1)
        remote = jnp.where(beyond >= 0, CORNER_BLOCK, -1)
        for number, toward in enumerate(straight):
            remote = jnp.where(direction == toward, 2 * number + half, remote)
        for number, toward in enumerate(corners):
            lane = jnp.where(direction == toward, lane % 4 + 4 * number, lane)
        put_index(index_ref, f, lane)
        put_index(index_ref, 3 + f, jnp.bitwise_and(jnp.right_shift(partner, 7), SUB - 1))
        put_index(index_ref, 6 + f, jnp.right_shift(partner, 10))
        put_index(index_ref, 9 + f, remote)
    sub_iota = lax.broadcasted_iota(jnp.int32, (SUB, LANES), 0)
    lane_iota = lax.broadcasted_iota(jnp.int32, (SUB, LANES), 1)

    def slots_to(choices, choice, half):
        rows_of = [
            jnp.broadcast_to(send_ref[0, 0, n : n + 1, lanes_of(half)], (SUB, LANES))
            for n in choices
        ]
        found = rows_of[0]
        for n, row in zip(choices[1:], rows_of[1:]):
            found = jnp.where(choice == n, row, found)
        return found

    straight_slots = None
    for number, toward in enumerate(straight):
        for half in range(2):
            row = slots_to((1, 6) if number < 2 else (3, 4), toward, half)
            straight_slots = (
                row
                if straight_slots is None
                else jnp.where(sub_iota == 2 * number + half, row, straight_slots)
            )
    corner_slots = None
    for number, toward in enumerate(corners):
        row = slots_to((0, 2, 5, 7), toward, 0)
        if number == 0:
            corner_slots = row
        else:
            moved = pltpu.roll(row, 4 * number, 1)
            corner_slots = jnp.where(lane_iota // 4 == number, moved, corner_slots)
    for d, slots in enumerate((straight_slots, corner_slots)):
        put_index(index_ref, 12 + d, jnp.bitwise_and(slots, LANES - 1))
        put_index(index_ref, 14 + d, jnp.bitwise_and(jnp.right_shift(slots, 7), SUB - 1))
        put_index(index_ref, 16 + d, jnp.right_shift(slots, 10))
    for copy in copies[2:]:
        copy.wait()
    matrix_ref[0:8, 0:8] = in_ref[...]
    matrix_ref[8:16, 0:8] = out_ref[...]
    matrix_ref[16:28, 0:12] = volume_ref[...]
    zone = zone_ref[...]
    zone_lane = jnp.bitwise_and(zone, LANES - 1)
    zone_block = jnp.right_shift(zone, 7)
    factors = []
    for ref in (friction_ref, conduct_ref):
        found = None
        for block in range(ref.shape[0]):
            got = take(spread(ref, block), zone_lane)
            found = got if block == 0 else jnp.where(zone_block == block, got, found)
        factors.append(found)
    area = area_ref[...]
    wet = wet_ref[...].astype(jnp.float32)
    kappa = factors[1] * soil_ref[...]
    wet_area = wet * area
    half_kappa_area = LATERAL * kappa * area
    put(stat_ref, WET_AREA, wet_area)
    put(stat_ref, KAPPA, kappa)
    put(stat_ref, HALF_KAPPA_AREA, half_kappa_area)
    put(stat_ref, WET, wet)
    put(stat_ref, ZONE_FRICTION, factors[0])
    put(stat_ref, ZONE_ID, zone.astype(jnp.float32))
    stat_ref[CONDUCTIVITY * SUB : CONDUCTIVITY * SUB + conduct_ref.shape[0], :] = conduct_ref[...]
    stat_ref[EDGE * SUB : (EDGE + 3) * SUB, :] = edge_ref[...]
    for k in range(sections):
        rows_to_tiles(
            lambda b: x_ref[k, :, lanes_of(b)].astype(jnp.float32), x_tiles, 16
        )
        squares = [tile(x_tiles, r) * tile(x_tiles, r) for r in range(12)]
        node_sum = [squares[i] + squares[3 + i] + squares[6 + i] + squares[9 + i] for i in range(3)]
        for f in range(3):
            first, second = FACE_NODES[f]
            put(table_ref, rows + 3 + 3 * k + f, node_sum[first] + node_sum[second])
        momentum = squares[3]
        for r in range(4, 9):
            momentum = momentum + squares[r]
        put(
            stat_ref,
            FRICTION_BASE + k,
            rough_ref[...] * jnp.sqrt(1.0 + momentum * (1.0 / 6.0)),
        )
    for f in range(3):
        put(table_ref, rows + f, tile(stat_ref, EDGE + f))
    put(table_ref, rows + 12, zone.astype(jnp.float32))
    for r in range(rows):
        put(table_ref, r, tile(cot_ref, r) * (wet_area if r < 12 else half_kappa_area))
    comps = rows // 3
    channels = comps * 2 + 5
    sender = Sender(index_ref, sent_ref, packed_ref)
    sender.states(table_ref, 0, comps)
    for group in range(4):
        sender.by_face(table_ref, rows + 3 * group, comps * 2 + group)
    sender.by_element(table_ref, rows + 12, channels - 1)
    sender.flush(channels - 1)
    write_messages(sent_ref, packed_ref, 0, channels, (to_x1, to_x2, to_y1, to_y2), channels)


def corner_kernel(channels, x1, x2, old_y1, old_y2, *rest):
    y1, y2 = rest[1:3]
    rows = slice(channels, message_rows(channels))
    lane = corner_lane((corner_rows(channels), LANES))
    merged = jnp.where(lane < 8, x1[0, rows, :], x2[0, rows, :])
    y1[0, rows, :] = merged
    y2[0, rows, :] = merged


def local_states(src, first_comp, comps, index_ref, out_ref):
    def body(f, carry):
        lane, sublane, face = [index_at(index_ref, n * 3 + f) for n in range(3)]
        for comp in range(comps):
            ends = gather_ends(src, (first_comp + comp) * 3, lane, sublane, face)
            for j in range(2):
                put_at(out_ref, f * comps * 2 + comp * 2 + j, ends[j])
        return carry

    lax.fori_loop(0, 3, body, 0)


def remote_states(received, first_row, channels, index_ref, local_ref, out_ref):
    def body(f, carry):
        lane, remote = index_at(index_ref, f), index_at(index_ref, 9 + f)
        for ch in range(channels):
            value = tile_at(local_ref, f * channels + ch)
            put_at(
                out_ref, f * channels + ch, received.fill(first_row + ch, lane, remote, value)
            )
        return carry

    lax.fori_loop(0, 3, body, 0)


def transposed_own(section, lam_ref, y_ref, stat_ref, matrix_ref, own_ref):
    rows = lam_ref.shape[0] // SUB
    layers = (rows - 12) // 3
    edge = [tile(stat_ref, EDGE + f) for f in range(3)]
    kappa = tile(stat_ref, KAPPA)
    wet = tile(stat_ref, WET)
    own = [tile(y_ref, r) for r in range(12)]
    result = []
    for r in range(12):
        total = matrix_ref[16, r] * own[0]
        for q in range(1, 12):
            total = total + matrix_ref[16 + q, r] * own[q]
        result.append(total)
    for f in range(3):
        ends = FACE_NODES[f]
        inner = [edge[f] * own[(ch // 2) * 3 + ends[ch % 2]] for ch in range(8)]
        for b in range(8):
            total = matrix_ref[0, b] * inner[0]
            for a in range(1, 8):
                total = total + matrix_ref[a, b] * inner[a]
            at = (b // 2) * 3 + ends[b % 2]
            result[at] = result[at] + total
    friction = tile(stat_ref, ZONE_FRICTION) * tile(stat_ref, FRICTION_BASE + section) * wet
    for r in range(3, 9):
        result[r] = result[r] - friction * tile(lam_ref, r)
    exchange = []
    for i in range(3):
        top = tile(lam_ref, 12 + i) - SALT_RETURN * wet * tile(lam_ref, 9 + i)
        exchange.append(kappa * top)
        result[9 + i] = result[9 + i] + exchange[i]
    for r in range(12):
        put(own_ref, r, result[r])
    for i in range(3):
        (f0, _), (f1, _) = NODE_FACES[i]
        both = edge[f0] + edge[f1]
        from_above = exchange[i]
        for layer in range(layers):
            r = 12 + layer * 3 + i
            value = -(both * tile(y_ref, r)) - from_above
            if layer + 1 < layers:
                from_above = kappa * (tile(lam_ref, r + 3) - tile(lam_ref, r))
                value = value + from_above
            put(own_ref, r, value)


def transposed_section(
    section, own_ref, y_ref, outer_ref, stat_ref, fact_ref, matrix_ref, emit
):
    rows = own_ref.shape[0] // SUB
    channels = rows // 3 * 2
    layers = (rows - 12) // 3
    outer_edge = [tile(fact_ref, OUTER_EDGE + f) for f in range(3)]
    result = [tile(own_ref, r) for r in range(12)]
    for f in range(3):
        edge = tile(stat_ref, EDGE + f)
        half_speed = tile(fact_ref, HALF_SPEED + 3 * section + f)
        ends = FACE_NODES[f]
        outer = [outer_edge[f] * tile(outer_ref, f * channels + ch) for ch in range(8)]
        for b in range(8):
            at = (b // 2) * 3 + ends[b % 2]
            total = half_speed * (edge * tile(y_ref, at) - outer[b])
            for a in range(8):
                total = total - matrix_ref[8 + a, b] * outer[a]
            result[at] = result[at] + total
    for r in range(12):
        emit(r, result[r])
    for i in range(3):
        (f0, j0), (f1, j1) = NODE_FACES[i]
        for layer in range(layers):
            r = 12 + layer * 3 + i
            emit(
                r,
                tile(own_ref, r)
                + outer_edge[f0] * tile(outer_ref, f0 * channels + 8 + layer * 2 + j0)
                + outer_edge[f1] * tile(outer_ref, f1 * channels + 8 + layer * 2 + j1),
            )


def own_gradients(section, weight, lam_ref, y_ref, x_tiles, stat_ref):
    rows = lam_ref.shape[0] // SUB
    layers = (rows - 12) // 3
    wet = tile(stat_ref, WET)
    kappa = tile(stat_ref, KAPPA)
    momentum = tile(lam_ref, 3) * tile(x_tiles, 3)
    for r in range(4, 9):
        momentum = momentum + tile(lam_ref, r) * tile(x_tiles, r)
    friction = -(weight * wet * tile(stat_ref, FRICTION_BASE + section)) * momentum
    vertical = None
    lateral = None
    for i in range(3):
        (f0, _), (f1, _) = NODE_FACES[i]
        top = tile(lam_ref, 12 + i) - SALT_RETURN * wet * tile(lam_ref, 9 + i)
        total = top * (tile(x_tiles, 9 + i) - tile(x_tiles, 12 + i))
        dots = None
        for layer in range(layers):
            r = 12 + layer * 3 + i
            term = tile(y_ref, r) * tile(x_tiles, r)
            dots = term if dots is None else dots + term
            if layer + 1 < layers:
                total = total + (tile(lam_ref, r + 3) - tile(lam_ref, r)) * (
                    tile(x_tiles, r) - tile(x_tiles, r + 3)
                )
        side = (tile(stat_ref, EDGE + f0) + tile(stat_ref, EDGE + f1)) * dots
        vertical = total if vertical is None else vertical + total
        lateral = side if lateral is None else lateral + side
    return friction, weight * (kappa * vertical - lateral)


def outer_gradients(weight, outer_ref, x_tiles, fact_ref):
    channels = outer_ref.shape[0] // SUB // 3
    values = []
    for f in range(3):
        total = None
        for ch in range(8, channels):
            row = 12 + (ch - 8) // 2 * 3 + FACE_NODES[f][ch % 2]
            term = tile(outer_ref, f * channels + ch) * tile(x_tiles, row)
            total = term if total is None else total + term
        values.append(weight * tile(fact_ref, OUTER_EDGE + f) * total)
    return values


def x_to_tiles(x_ref, section, x_tiles):
    rows = x_ref.shape[3]
    rows_to_tiles(
        lambda b: x_ref[section, 0, 0, :, lanes_of(b)].astype(jnp.float32), x_tiles, rows
    )


def local_two_kernel(
    cot_ref,
    plan_ref,
    x_ref,
    outer_ref,
    near_ref,
    term_ref,
    own_ref,
    x_tiles,
    matrix_ref,
    sem,
):
    matrices = load_matrices(plan_ref, matrix_ref, sem)
    stat_ref, index_ref, _, table_ref = plan_parts(plan_ref)
    rows = cot_ref.shape[0] // SUB
    local_states(table_ref, 0, rows // 3, index_ref, outer_ref)
    for f in range(3):
        lane, sublane, face = [index_of(index_ref, n * 3 + f) for n in range(3)]
        for group in range(4):
            value = gather_by_face(table_ref, rows + 3 * group, lane, sublane, face)
            put(near_ref, f * 5 + group, value)
        put(near_ref, f * 5 + 4, gather_tile(table_ref, rows + 12, lane, sublane))
    x_to_tiles(x_ref, 2, x_tiles)
    friction, conduct = own_gradients(
        2, TIME_STEP * 2.0 / 3.0, cot_ref, table_ref, x_tiles, stat_ref
    )
    put(term_ref, 0, friction)
    put(term_ref, 1, conduct)
    matrices.wait()
    transposed_own(2, cot_ref, table_ref, stat_ref, matrix_ref, own_ref)


def local_x_kernel(plan_ref, x_ref, x_outer_ref, sent_ref, packed_ref, x_tiles):
    index_ref = plan_parts(plan_ref)[1]
    comps = x_ref.shape[3] // 3
    x_to_tiles(x_ref, 0, x_tiles)
    local_states(x_tiles, 4, comps - 4, index_ref, x_outer_ref)
    sender = Sender(index_ref, sent_ref, packed_ref)
    sender.states(x_tiles, 4, comps - 4)
    sender.flush(comps * 2 - 9)


def second_kernel(
    cot_ref,
    plan_ref,
    own_ref,
    near_outer_ref,
    near_ref,
    x_sent_ref,
    x_packed_ref,
    from_x1,
    from_x2,
    from_y1,
    from_y2,
    lam_ref,
    y_ref,
    fact_ref,
    outer_ref,
    to_x1,
    to_x2,
    to_y1,
    to_y2,
    sent_ref,
    packed_ref,
    corner_ref,
    matrix_ref,
    sem,
):
    matrices = load_matrices(plan_ref, matrix_ref, sem)
    stat_ref, index_ref, _, table_ref = plan_parts(plan_ref)
    rows = cot_ref.shape[0] // SUB
    comps = rows // 3
    channels = comps * 2
    received = Received((from_x1, from_x2, from_y1, from_y2), channels + 5, corner_ref)
    remote_states(received, 0, channels, index_ref, near_outer_ref, outer_ref)
    for f in range(3):
        lane, remote = index_of(index_ref, f), index_of(index_ref, 9 + f)
        for group in range(5):
            value = received.fill(channels + group, lane, remote, tile(near_ref, f * 5 + group))
            if group == 0:
                put(fact_ref, OUTER_EDGE + f, value)
            elif group == 4:
                put(fact_ref, OUTER_ZONE + f, value)
            else:
                both = tile(table_ref, rows + 3 * group + f) + value
                put(
                    fact_ref,
                    HALF_SPEED + 3 * (group - 1) + f,
                    0.5 * jnp.sqrt(1.0 + (0.25 / 8.0) * both),
                )
    wet_area = tile(stat_ref, WET_AREA)
    half_kappa_area = tile(stat_ref, HALF_KAPPA_AREA)

    def emit(r, value):
        lam = (2.0 / 3.0) * (tile(cot_ref, r) + TIME_STEP * value)
        put(lam_ref, r, lam)
        put(y_ref, r, lam * (wet_area if r < 12 else half_kappa_area))

    matrices.wait()
    transposed_section(
        2, own_ref, table_ref, outer_ref, stat_ref, fact_ref, matrix_ref, emit
    )
    sender = Sender(index_ref, sent_ref, packed_ref)
    sender.states(y_ref, 0, comps)
    sender.flush(channels - 1)
    outs = (to_x1, to_x2, to_y1, to_y2)
    write_messages(x_sent_ref, x_packed_ref, 0, channels - 8, outs, X_ROWS + channels)
    write_messages(sent_ref, packed_ref, X_ROWS, channels, outs, X_ROWS + channels)


def local_one_kernel(
    lam_ref,
    y_ref,
    plan_ref,
    fact_ref,
    old_outer_ref,
    old_term_ref,
    x_ref,
    outer_ref,
    term_ref,
    own_ref,
    x_tiles,
    matrix_ref,
    sem,
):
    matrices = load_matrices(plan_ref, matrix_ref, sem)
    stat_ref, index_ref, _, _ = plan_parts(plan_ref)
    local_states(y_ref, 0, lam_ref.shape[0] // SUB // 3, index_ref, outer_ref)
    x_to_tiles(x_ref, 2, x_tiles)
    weight = TIME_STEP * 2.0 / 3.0
    for f, value in enumerate(outer_gradients(weight, old_outer_ref, x_tiles, fact_ref)):
        put(term_ref, 2 + f, value)
    x_to_tiles(x_ref, 1, x_tiles)
    terms = own_gradients(1, TIME_STEP * 0.25, lam_ref, y_ref, x_tiles, stat_ref)
    for n in range(2):
        put(term_ref, n, tile(old_term_ref, n) + terms[n])
    matrices.wait()
    transposed_own(1, lam_ref, y_ref, stat_ref, matrix_ref, own_ref)


def first_kernel(
    cot_ref,
    lam_ref,
    y_ref,
    plan_ref,
    fact_ref,
    own_ref,
    near_outer_ref,
    from_x1,
    from_x2,
    from_y1,
    from_y2,
    base_ref,
    next_ref,
    next_y_ref,
    outer_ref,
    to_x1,
    to_x2,
    to_y1,
    to_y2,
    sent_ref,
    packed_ref,
    corner_ref,
    matrix_ref,
    sem,
):
    matrices = load_matrices(plan_ref, matrix_ref, sem)
    stat_ref, index_ref, _, _ = plan_parts(plan_ref)
    comps = lam_ref.shape[0] // SUB // 3
    channels = comps * 2
    received = Received((from_x1, from_x2, from_y1, from_y2), X_ROWS + channels, corner_ref)
    remote_states(received, X_ROWS, channels, index_ref, near_outer_ref, outer_ref)
    wet_area = tile(stat_ref, WET_AREA)
    half_kappa_area = tile(stat_ref, HALF_KAPPA_AREA)

    def emit(r, value):
        old = tile(lam_ref, r)
        lam = 0.25 * (old + TIME_STEP * value)
        put(next_ref, r, lam)
        put(next_y_ref, r, lam * (wet_area if r < 12 else half_kappa_area))
        put(base_ref, r, (1.0 / 3.0) * tile(cot_ref, r) + 0.75 * old + lam)

    matrices.wait()
    transposed_section(
        1, own_ref, y_ref, outer_ref, stat_ref, fact_ref, matrix_ref, emit
    )
    sender = Sender(index_ref, sent_ref, packed_ref)
    sender.states(next_y_ref, 0, comps)
    sender.flush(channels - 1)
    write_messages(sent_ref, packed_ref, 0, channels, (to_x1, to_x2, to_y1, to_y2), channels)


def zone_kernel(
    lam_ref,
    y_ref,
    plan_ref,
    fact_ref,
    old_outer_ref,
    term_ref,
    x_ref,
    x_near_ref,
    from_x1,
    from_x2,
    from_y1,
    from_y2,
    out_ref,
    x_outer_ref,
    x_tiles,
    corner_ref,
):
    stat_ref, index_ref, _, _ = plan_parts(plan_ref)
    rows = lam_ref.shape[0] // SUB
    channels = rows // 3 * 2
    x_channels = channels - 8
    received = Received((from_x1, from_x2, from_y1, from_y2), X_ROWS + channels, corner_ref)
    remote_states(received, 0, x_channels, index_ref, x_near_ref, x_outer_ref)
    x_to_tiles(x_ref, 1, x_tiles)
    outer_terms = outer_gradients(TIME_STEP * 0.25, old_outer_ref, x_tiles, fact_ref)
    outer_terms = [tile(term_ref, 2 + f) + outer_terms[f] for f in range(3)]
    x_to_tiles(x_ref, 0, x_tiles)
    friction_term, conduct_term = own_gradients(
        0, TIME_STEP, lam_ref, y_ref, x_tiles, stat_ref
    )
    friction_term = friction_term + tile(term_ref, 0)
    conduct_term = conduct_term + tile(term_ref, 1)
    for f in range(3):
        total = None
        for ch in range(x_channels):
            row = 12 + ch // 2 * 3 + FACE_NODES[f][ch % 2]
            term = tile(x_outer_ref, f * x_channels + ch) * tile(y_ref, row)
            total = term if total is None else total + term
        conduct_term = conduct_term + TIME_STEP * tile(stat_ref, EDGE + f) * total

    zones = out_ref.shape[2]
    zone_iota = lax.broadcasted_iota(jnp.int32, (zones, LANES), 0).astype(jnp.float32)
    sub_iota = lax.broadcasted_iota(jnp.int32, (SUB, zones), 0)

    def thirds(value):
        high = value.astype(jnp.bfloat16).astype(jnp.float32)
        rest = value - high
        middle = rest.astype(jnp.bfloat16).astype(jnp.float32)
        return [high, middle, rest - middle]

    def by_zone(values, zone_of, zone_row):
        pieces = sum([thirds(value) for value in values], [])
        left = jnp.concatenate(pieces, axis=0).astype(jnp.bfloat16)
        totals = [jnp.zeros((SUB, zones), jnp.float32) for _ in values]
        for sub in range(SUB):
            line = zone_of[pl.ds(zone_row * SUB + sub, 1), :]
            hot = (jnp.broadcast_to(line, (zones, LANES)) == zone_iota).astype(jnp.float32)
            dots = lax.dot_general(
                left,
                hot.astype(jnp.bfloat16),
                (((1,), (1,)), ((), ())),
                preferred_element_type=jnp.float32,
            )
            for n in range(len(values)):
                at = n * 3 * SUB
                three = dots[at : at + SUB] + dots[at + SUB : at + 2 * SUB]
                three = three + dots[at + 2 * SUB : at + 3 * SUB]
                totals[n] = totals[n] + jnp.where(sub_iota == sub, three, 0.0)
        return totals

    friction, conduct = by_zone([friction_term, conduct_term], stat_ref, ZONE_ID)
    for f in range(3):
        conduct = conduct + by_zone([outer_terms[f]], fact_ref, OUTER_ZONE + f)[0]
    friction = GRAD_WEIGHT * jnp.sum(friction, axis=0, keepdims=True)
    conduct = GRAD_WEIGHT * jnp.sum(conduct, axis=0, keepdims=True)
    factors = [
        stat_ref[CONDUCTIVITY * SUB + n : CONDUCTIVITY * SUB + n + 1, :]
        for n in range(zones // LANES)
    ]
    conduct = conduct / jnp.concatenate(factors, axis=1)
    for device in range(out_ref.shape[0]):
        out_ref[device, 0:1, :] = friction
        out_ref[device, 1:2, :] = conduct


def local_zero_kernel(lam_ref, y_ref, plan_ref, outer_ref, own_ref, matrix_ref, sem):
    matrices = load_matrices(plan_ref, matrix_ref, sem)
    stat_ref, index_ref, _, _ = plan_parts(plan_ref)
    local_states(y_ref, 0, y_ref.shape[0] // SUB // 3, index_ref, outer_ref)
    matrices.wait()
    transposed_own(0, lam_ref, y_ref, stat_ref, matrix_ref, own_ref)


def last_kernel(
    base_ref,
    y_ref,
    plan_ref,
    fact_ref,
    own_ref,
    near_outer_ref,
    from_x1,
    from_x2,
    from_y1,
    from_y2,
    adjoint_ref,
    last_ref,
    outer_ref,
    corner_ref,
    matrix_ref,
    sem,
):
    matrices = load_matrices(plan_ref, matrix_ref, sem)
    stat_ref, index_ref, _, _ = plan_parts(plan_ref)
    rows = y_ref.shape[0] // SUB
    channels = rows // 3 * 2
    received = Received((from_x1, from_x2, from_y1, from_y2), channels, corner_ref)
    remote_states(received, 0, channels, index_ref, near_outer_ref, outer_ref)

    def emit(r, value):
        put(adjoint_ref, r, tile(base_ref, r) + TIME_STEP * value)

    matrices.wait()
    transposed_section(
        0, own_ref, y_ref, outer_ref, stat_ref, fact_ref, matrix_ref, emit
    )
    last_ref[...] = tile(adjoint_ref, rows - 1)


def total_kernel(zone_ref, adjoint_ref, grads_ref):
    grads_ref[...] = jnp.sum(zone_ref[...], axis=0)


def exchange(channels, messages, ahead):
    x1, x2, y1, y2 = messages
    x1, x2 = swapped(x1, "gx", 1), swapped(x2, "gx", 0)
    y1, y2, ahead = call(
        functools.partial(corner_kernel, channels),
        "corners",
        [jax.ShapeDtypeStruct(one.shape, one.dtype) for one in (y1, y2, ahead)],
        [],
        [x1, x2, y1, y2, ahead],
        apart=(4,),
        aliases={2: 0, 3: 1, 4: 2},
    )
    return (x1, x2, swapped(y1, "gy", 1), swapped(y2, "gy", 0)), ahead


def call(kernel, name, outs, scratch, operands, far=False, apart=(), aliases={}):
    near = pl.BlockSpec(memory_space=pltpu.VMEM)
    in_place = pl.BlockSpec(memory_space=pl.ANY)
    specs = [in_place if far or n in apart else near for n in range(len(operands))]
    handed_on = [aliases[n] for n in apart if n in aliases]
    return pl.pallas_call(
        kernel,
        in_specs=specs,
        out_specs=[in_place if n in handed_on else near for n in range(len(outs))],
        out_shape=outs,
        scratch_shapes=scratch,
        input_output_aliases=aliases,
        compiler_params=pltpu.CompilerParams(
            vmem_limit_bytes=(FAR_VMEM if far else NEAR_VMEM) * 1024 * 1024
        ),
        name=name,
    )(*operands)


def local(
    cotangent,
    section_states,
    inverse_area,
    edge_length,
    roughness,
    soil_conductance,
    zone_friction,
    zone_conductivity,
    wet_mask,
    element_zone,
    send_face,
    send_count,
    face_partner,
    volume_matrix,
    flux_in,
    flux_out,
):
    rows = cotangent.shape[2]
    channels = rows // 3 * 2
    zones = zone_friction.shape[0]
    slots = send_face.shape[3]
    devices = lax.axis_size("gx") * lax.axis_size("gy")
    f32 = jnp.float32

    def tiles(count, dtype=f32):
        return jax.ShapeDtypeStruct((count * SUB, LANES), dtype)

    def tile_scratch(count, dtype=f32):
        return pltpu.VMEM((count * SUB, LANES), dtype)

    def messages(count):
        return [jax.ShapeDtypeStruct((slots // LANES, message_rows(count), LANES), f32)] * 4

    def sent_tiles(count):
        return corner_rows(count) * SUB

    matrix_scratch = [
        pltpu.SMEM((MATRIX_ROWS * SUB, LANES), f32),
        pltpu.SemaphoreType.DMA((1,)),
    ]
    section_scratch = [pltpu.VMEM((SUB, LANES), f32)] + matrix_scratch

    square = lambda one: one.reshape(SUB, LANES)
    cot = cotangent.reshape(rows * SUB, LANES)
    plan, *to_send = call(
        prepare_kernel,
        "prepare",
        [tiles(plan_rows(rows))] + messages(channels + 5),
        [
            tile_scratch(16),
            tile_scratch(sent_tiles(channels + 5)),
            tile_scratch(1),
            tile_scratch(3, jnp.int32),
            pltpu.VMEM(send_face.shape, jnp.int32),
            tile_scratch(rows),
            pltpu.VMEM((section_states.shape[0], 16, SUB * LANES), section_states.dtype),
            tile_scratch(1),
            tile_scratch(3),
            tile_scratch(1),
            tile_scratch(1),
            pltpu.VMEM((zones // LANES, LANES), f32),
            pltpu.VMEM((zones // LANES, LANES), f32),
            tile_scratch(1, jnp.int32),
            tile_scratch(1, jnp.int32),
            pltpu.VMEM(flux_in.shape, f32),
            pltpu.VMEM(flux_out.shape, f32),
            pltpu.VMEM(volume_matrix.shape, f32),
            pltpu.SemaphoreType.DMA((15,)),
        ],
        [
            cot,
            section_states,
            square(inverse_area),
            edge_length.reshape(3 * SUB, LANES),
            square(roughness),
            square(soil_conductance),
            zone_friction.reshape(-1, LANES),
            zone_conductivity.reshape(-1, LANES),
            square(wet_mask),
            square(element_zone),
            send_face,
            face_partner.reshape(3 * SUB, LANES),
            flux_in,
            flux_out,
            volume_matrix,
        ],
        far=True,
    )
    near_outer, near, term, own = call(
        local_two_kernel,
        "local_two",
        [tiles(3 * channels), tiles(15), tiles(2), tiles(rows)],
        [tile_scratch(rows)] + matrix_scratch,
        [cot, plan, section_states],
    )
    x_near, x_sent, x_packed = call(
        local_x_kernel,
        "local_x",
        [tiles(3 * (channels - 8)), tiles(sent_tiles(channels - 8)), tiles(1)],
        [tile_scratch(rows)],
        [plan, section_states],
    )
    received, term = exchange(channels + 5, to_send, term)
    lam, y, fact, outer, *to_send = call(
        second_kernel,
        "section_two",
        [tiles(rows), tiles(rows), tiles(FACT_ROWS), tiles(3 * channels)]
        + messages(X_ROWS + channels),
        [tile_scratch(sent_tiles(channels)), tile_scratch(1)] + section_scratch,
        [cot, plan, own, near_outer, near, x_sent, x_packed, *received],
    )
    near_outer, term, own = call(
        local_one_kernel,
        "local_one",
        [tiles(3 * channels), tiles(5), tiles(rows)],
        [tile_scratch(rows)] + matrix_scratch,
        [lam, y, plan, fact, outer, term, section_states],
    )
    received, term = exchange(X_ROWS + channels, to_send, term)
    base, lam, y, outer, *to_send = call(
        first_kernel,
        "section_one",
        [tiles(rows), tiles(rows), tiles(rows), tiles(3 * channels)] + messages(channels),
        [tile_scratch(sent_tiles(channels)), tile_scratch(1)] + section_scratch,
        [cot, lam, y, plan, fact, own, near_outer, *received],
    )
    (zone_terms,) = call(
        zone_kernel,
        "zone_sums",
        [jax.ShapeDtypeStruct((devices, 2, zones), f32)],
        [tile_scratch(3 * (channels - 8)), tile_scratch(rows), tile_scratch(1)],
        [lam, y, plan, fact, outer, term, section_states, x_near, *received],
    )
    received, zone_terms = exchange(channels, to_send, zone_terms)
    all_terms = lax.all_to_all(zone_terms, ("gx", "gy"), 0, 0)
    near_outer, own = call(
        local_zero_kernel,
        "local_zero",
        [tiles(3 * channels), tiles(rows)],
        matrix_scratch,
        [lam, y, plan],
    )
    adjoint, last = call(
        last_kernel,
        "section_zero",
        [tiles(rows), tiles(1)],
        [tile_scratch(3 * channels)] + section_scratch,
        [base, y, plan, fact, own, near_outer, *received],
    )
    (zone_grads,) = call(
        total_kernel,
        "zone_total",
        [jax.ShapeDtypeStruct((2, zones), f32)],
        [],
        [all_terms, last],
    )
    return adjoint.reshape(cotangent.shape), zone_grads


def solution(mesh):
    placed = (
        P("gx", "gy", None, None),
        P(None, "gx", "gy", None, None),
        P("gx", "gy", None),
        P("gx", "gy", None, None),
        P("gx", "gy", None),
        P("gx", "gy", None),
        P(),
        P(),
        P("gx", "gy", None),
        P("gx", "gy", None),
        P("gx", "gy", None, None),
        P("gx", "gy", None),
        P("gx", "gy", None, None),
        P(),
        P(),
        P(),
    )
    return jax.shard_map(
        local,
        mesh=mesh,
        in_specs=placed,
        out_specs=(P("gx", "gy", None, None), P()),
        check_vma=False,
    )
```
